32 devices in a mesh: dp: 8 (over y, x, core), tensor: 4 (over z).
Axes of the slice: x: 2, y: 2, z: 4, core: 2. Of those that a mesh axis runs over, the one named last changes fastest.
Arguments:
- tokens: bfloat16 [24576, 1024], P(('dp', 'tensor')), may hold values from -6 to 6
- cotangent: bfloat16 [24576, 1024], P(('dp', 'tensor')), may hold values from -6 to 6
- item_len: int32 [8, 2], P('dp'), may hold values from 0 to 3072, as said below
- bucket_table: int32 [3072], replicated, may hold values from 0 to 31, as said below
- w_qkv: float32 [3, 1024, 1024], P(None, 'dp', 'tensor'), may hold values from -0.1875 to 0.1875
- w_proj: float32 [1024, 1024], P('tensor', 'dp'), may hold values from -2 to 2
- w_up: float32 [1024, 4096], P('dp', 'tensor'), may hold values from -0.1875 to 0.1875
- w_down: float32 [4096, 1024], P('tensor', 'dp'), may hold values from -0.09375 to 0.09375
- rel_bias: float32 [512], P(('dp', 'tensor')), may hold values from -4 to 4
- ln_gain: float32 [2, 1024], P(None, ('dp', 'tensor')), may hold values from 0.25 to 1.75
- ln_shift: float32 [2, 1024], P(None, ('dp', 'tensor')), may hold values from -2 to 2
- mean_qkv: float32 [3, 1024, 1024], P(None, 'dp', 'tensor'), may hold values from -0.002 to 0.002
- mean_proj: float32 [1024, 1024], P('tensor', 'dp'), may hold values from -0.002 to 0.002
- mean_up: float32 [1024, 4096], P('dp', 'tensor'), may hold values from -0.002 to 0.002
- mean_down: float32 [4096, 1024], P('tensor', 'dp'), may hold values from -0.002 to 0.002
- mean_bias: float32 [512], P(('dp', 'tensor')), may hold values from -0.002 to 0.002
- mean_gain: float32 [2, 1024], P(None, ('dp', 'tensor')), may hold values from -0.002 to 0.002
- mean_shift: float32 [2, 1024], P(None, ('dp', 'tensor')), may hold values from -0.002 to 0.002
- square_qkv: float32 [3, 1024, 1024], P(None, 'dp', 'tensor'), may hold values from 1e-08 to 1e-06
- square_proj: float32 [1024, 1024], P('tensor', 'dp'), may hold values from 5e-10 to 5e-08
- square_up: float32 [1024, 4096], P('dp', 'tensor'), may hold values from 5e-10 to 5e-08
- square_down: float32 [4096, 1024], P('tensor', 'dp'), may hold values from 1e-08 to 1e-06
- square_bias: float32 [512], P(('dp', 'tensor')), may hold values from 1e-08 to 1e-06
- square_gain: float32 [2, 1024], P(None, ('dp', 'tensor')), may hold values from 1e-08 to 1e-06
- square_shift: float32 [2, 1024], P(None, ('dp', 'tensor')), may hold values from 1e-08 to 1e-06
Outputs:
- block_out: bfloat16 [24576, 1024], P(('dp', 'tensor'))
- grad_tokens: bfloat16 [24576, 1024], P(('dp', 'tensor'))
- grad_norm: float32 [], replicated
- param_norms: float32 [2, 11], replicated
- new_w_qkv: float32 [3, 1024, 1024], P(None, 'dp', 'tensor')
- new_w_proj: float32 [1024, 1024], P('tensor', 'dp')
- new_w_up: float32 [1024, 4096], P('dp', 'tensor')
- new_w_down: float32 [4096, 1024], P('tensor', 'dp')
- new_rel_bias: float32 [512], P(('dp', 'tensor'))
- new_ln_gain: float32 [2, 1024], P(None, ('dp', 'tensor'))
- new_ln_shift: float32 [2, 1024], P(None, ('dp', 'tensor'))
- new_mean_qkv: float32 [3, 1024, 1024], P(None, 'dp', 'tensor')
- new_mean_proj: float32 [1024, 1024], P('tensor', 'dp')
- new_mean_up: float32 [1024, 4096], P('dp', 'tensor')
- new_mean_down: float32 [4096, 1024], P('tensor', 'dp')
- new_mean_bias: float32 [512], P(('dp', 'tensor'))
- new_mean_gain: float32 [2, 1024], P(None, ('dp', 'tensor'))
- new_mean_shift: float32 [2, 1024], P(None, ('dp', 'tensor'))
- new_square_qkv: float32 [3, 1024, 1024], P(None, 'dp', 'tensor')
- new_square_proj: float32 [1024, 1024], P('tensor', 'dp')
- new_square_up: float32 [1024, 4096], P('dp', 'tensor')
- new_square_down: float32 [4096, 1024], P('tensor', 'dp')
- new_square_bias: float32 [512], P(('dp', 'tensor'))
- new_square_gain: float32 [2, 1024], P(None, ('dp', 'tensor'))
- new_square_shift: float32 [2, 1024], P(None, ('dp', 'tensor'))
The draws below stay inside these ranges and needn't reach their ends.
Inputs may be any that keep to these rules, and one draw needn't show every extreme that they name: `item_len`: row g holds the lengths of the items packed in group g: either one item of 3072 tokens and an empty second, or two items of 1536 tokens; every draw has groups of both kinds. `bucket_table`: entry d is the bucket of distance d: d itself for d < 16, non-decreasing in d, reaching 31.
All inputs are finite; a program needn't handle non-finite values.
Results may differ from the reference program's by a relative error of at most 0.018.
Values may be sent and summed in bfloat16 or wider, within the bound.
A program may use at most 512 MiB of HBM per device.

```python
import math
import jax
import jax.numpy as jnp
from jax import lax

D = 1024
H = 16
DH = 64
FF = 4096
BUCKETS = 32
TOK_DEV = 3072
TOKENS = 24576
N_DP = 8


def draw_item_len(key, part):
    choose_key, long_key, short_key = jax.random.split(jax.random.fold_in(key, 11), 3)
    longs = jax.random.randint(choose_key, (N_DP,), 0, 2)
    sure_long = jax.random.randint(long_key, (), 0, N_DP)
    sure_short = (sure_long + 1 + jax.random.randint(short_key, (), 0, N_DP - 1)) % N_DP
    positions = jnp.arange(N_DP)
    longs = jnp.where(positions == sure_long, 1, longs)
    longs = jnp.where(positions == sure_short, 0, longs)
    first_length = jnp.where(longs == 1, TOK_DEV, TOK_DEV // 2)
    return jnp.stack([first_length, TOK_DEV - first_length], axis=1).astype(jnp.int32)


def draw_bucket_table(key, part):
    span_size = max(1, (TOK_DEV // 4 - 16) // 15)
    increments = jax.random.randint(jax.random.fold_in(key, 23), (15,), 1, 2 * span_size + 1)
    bounds = 16 + jnp.cumsum(increments)
    distance = jnp.arange(TOK_DEV)
    far_bucket = 16 + jnp.sum((distance[:, None] >= bounds[None, :]).astype(jnp.int32), axis=1)
    return jnp.where(distance < 16, distance, far_bucket).astype(jnp.int32)


def levels(stream_key, shape, cuts, least, top_value):
    level, own = 1.0, jax.random.fold_in(stream_key, 6)
    for position, blocks in cuts:
        heights = jnp.exp(jax.random.uniform(jax.random.fold_in(own, position), (blocks,), jnp.float32, least / len(cuts), top_value / len(cuts)))
        level = level * jnp.repeat(heights, shape[position] // blocks).reshape([-1 if axis == position else 1 for axis in range(len(shape))])
    return level


def bell_draw(own_key, extent, scale, reach, pieces=(), held_as=jnp.bfloat16):
    entries = scale * jax.random.normal(own_key, extent, jnp.float32)
    if pieces:
        entries = entries * levels(own_key, extent, pieces, -0.22, 0.18)
    return jnp.clip(entries, -reach, reach).astype(held_as)


def setup_inputs(seed: int = 0) -> dict:
    arg_keys = jax.random.split(jax.random.key(seed), 26)
    return {
        "tokens": bell_draw(arg_keys[0], (TOKENS, D), 1.0, 6.0, ((0, 32),)),
        "cotangent": bell_draw(arg_keys[1], (TOKENS, D), 1.0, 6.0, ((0, 32),)),
        "item_len": draw_item_len(jax.random.fold_in(arg_keys[25], 71), 0),
        "bucket_table": draw_bucket_table(jax.random.fold_in(arg_keys[25], 71), 0),
        "w_qkv": bell_draw(arg_keys[4], (3, D, H * DH), D ** -0.5, 0.1875, ((1, 8), (2, 4)), jnp.float32),
        "w_proj": bell_draw(arg_keys[5], (H * DH, D), (max(1, H * DH // 128)) ** -0.5, 2.0, ((0, 4), (1, 8)), jnp.float32),
        "w_up": bell_draw(arg_keys[6], (D, FF), D ** -0.5, 0.1875, ((0, 8), (1, 4)), jnp.float32),
        "w_down": bell_draw(arg_keys[7], (FF, D), FF ** -0.5, 0.09375, ((0, 4), (1, 8)), jnp.float32),
        "rel_bias": bell_draw(arg_keys[8], (BUCKETS * H,), 1.0, 4.0, ((0, 32),), jnp.float32),
        "ln_gain": jnp.clip(1.0 + 0.15 * jax.random.normal(arg_keys[9], (2, D), jnp.float32), 0.25, 1.75),
        "ln_shift": bell_draw(arg_keys[10], (2, D), 0.3, 2.0, ((1, 32),), jnp.float32),
        "mean_qkv": bell_draw(arg_keys[11], (3, D, H * DH), 0.0003, 0.002, ((1, 8), (2, 4)), jnp.float32),
        "mean_proj": bell_draw(arg_keys[12], (H * DH, D), 0.0003, 0.002, ((0, 4), (1, 8)), jnp.float32),
        "mean_up": bell_draw(arg_keys[13], (D, FF), 0.0003, 0.002, ((0, 8), (1, 4)), jnp.float32),
        "mean_down": bell_draw(arg_keys[14], (FF, D), 0.0003, 0.002, ((0, 4), (1, 8)), jnp.float32),
        "mean_bias": bell_draw(arg_keys[15], (BUCKETS * H,), 0.0003, 0.002, ((0, 32),), jnp.float32),
        "mean_gain": bell_draw(arg_keys[16], (2, D), 0.0003, 0.002, ((1, 32),), jnp.float32),
        "mean_shift": bell_draw(arg_keys[17], (2, D), 0.0003, 0.002, ((1, 32),), jnp.float32),
        "square_qkv": jnp.clip(jnp.exp(math.log(9.999999974752427e-07) - 4.6051702 * jax.random.uniform(arg_keys[18], (3, D, H * DH), jnp.float32) ** levels(arg_keys[18], (3, D, H * DH), ((1, 8), (2, 4)), -0.2, 0.2)), 9.99999993922529e-09, 9.999999974752427e-07),
        "square_proj": jnp.clip(jnp.exp(math.log(5.000000058430487e-08) - 4.6051702 * jax.random.uniform(arg_keys[19], (H * DH, D), jnp.float32) ** levels(arg_keys[19], (H * DH, D), ((0, 4), (1, 8)), -0.2, 0.2)), 4.999999858590343e-10, 5.000000058430487e-08),
        "square_up": jnp.clip(jnp.exp(math.log(5.000000058430487e-08) - 4.6051702 * jax.random.uniform(arg_keys[20], (D, FF), jnp.float32) ** levels(arg_keys[20], (D, FF), ((0, 8), (1, 4)), -0.2, 0.2)), 4.999999858590343e-10, 5.000000058430487e-08),
        "square_down": jnp.clip(jnp.exp(math.log(9.999999974752427e-07) - 4.6051702 * jax.random.uniform(arg_keys[21], (FF, D), jnp.float32) ** levels(arg_keys[21], (FF, D), ((0, 4), (1, 8)), -0.2, 0.2)), 9.99999993922529e-09, 9.999999974752427e-07),
        "square_bias": jnp.clip(jnp.exp(math.log(9.999999974752427e-07) - 4.6051702 * jax.random.uniform(arg_keys[22], (BUCKETS * H,), jnp.float32) ** levels(arg_keys[22], (BUCKETS * H,), ((0, 32),), -0.2, 0.2)), 9.99999993922529e-09, 9.999999974752427e-07),
        "square_gain": jnp.clip(jnp.exp(math.log(9.999999974752427e-07) - 4.6051702 * jax.random.uniform(arg_keys[23], (2, D), jnp.float32) ** levels(arg_keys[23], (2, D), ((1, 32),), -0.2, 0.2)), 9.99999993922529e-09, 9.999999974752427e-07),
        "square_shift": jnp.clip(jnp.exp(math.log(9.999999974752427e-07) - 4.6051702 * jax.random.uniform(arg_keys[24], (2, D), jnp.float32) ** levels(arg_keys[24], (2, D), ((1, 32),), -0.2, 0.2)), 9.99999993922529e-09, 9.999999974752427e-07),
    }


HIGHEST = lax.Precision.HIGHEST

@jax.custom_vjp
def low(v):
    return lax.optimization_barrier(v.astype(jnp.bfloat16)).astype(jnp.float32)

@jax.custom_vjp
def low_back(v):
    return v

def low_keep(v):
    return (low(v), None)

def low_pass(kept, grad):
    return (grad,)

def back_keep(v):
    return (v, None)

def back_low(kept, grad):
    return (low(grad),)
low.defvjp(low_keep, low_pass)
low_back.defvjp(back_keep, back_low)

def matmul(left, right):
    return jnp.dot(left, right, precision=HIGHEST, preferred_element_type=jnp.float32)

def layer_norm(values, gain, shift):
    center = values - lax.optimization_barrier(jnp.mean(values, axis=-1, keepdims=True))
    spread = lax.optimization_barrier(jnp.mean(center * center, axis=-1, keepdims=True))
    return center * lax.rsqrt(spread + 1e-05) * gain + shift

def layer(block_in, lengths, bucket_table, params):
    w_qkv, w_proj, w_up, w_down, rel_bias, ln_gain, ln_shift = params
    a_first = low(layer_norm(block_in, ln_gain[0], ln_shift[0]))
    qkv_low = low(w_qkv)
    queries = low_back(low(matmul(a_first, qkv_low[0])))
    keys = low_back(low(matmul(a_first, qkv_low[1])))
    values = low_back(low(matmul(a_first, qkv_low[2])))
    positions = jnp.arange(TOK_DEV).astype(jnp.int32)
    distance = positions[:, None] - positions[None, :]
    segment = positions >= lengths[0]
    allowed = (distance >= 0) & (segment[:, None] == segment[None, :])
    buckets = jnp.take(bucket_table, jnp.maximum(distance, 0))
    table = rel_bias.reshape(BUCKETS, H)

    def one_head(inputs):
        head_q, head_k, head_v, head_bias = inputs
        scores = low_back(matmul(head_q, head_k.T) * DH ** (-0.5) + jnp.take(head_bias, buckets))
        scores = jnp.where(allowed, scores, -jnp.inf)
        row_max = lax.optimization_barrier(jnp.max(scores, axis=-1, keepdims=True))
        weights = jnp.exp(scores - row_max)
        shares = weights / lax.optimization_barrier(jnp.sum(weights, axis=-1, keepdims=True))
        return matmul(low(shares), head_v)

    def split_heads(matrix):
        return matrix.reshape(TOK_DEV, H, DH).transpose(1, 0, 2)
    heads_out = lax.map(jax.checkpoint(one_head), (split_heads(queries), split_heads(keys), split_heads(values), table.T))
    attn_out = low_back(low(heads_out.transpose(1, 0, 2).reshape(TOK_DEV, H * DH)))
    mixed = low_back(matmul(attn_out, low(w_proj)))
    middle = block_in + mixed
    a_second = low(layer_norm(middle, ln_gain[1], ln_shift[1]))
    hidden_pre = low_back(matmul(a_second, low(w_up)))
    hidden = low(jax.nn.gelu(hidden_pre, approximate=False))
    return middle + matmul(hidden, low(w_down))

def param_squares(arrays):
    qkv, proj, up, down, table, gain, shift = arrays
    parts = [lax.optimization_barrier(jnp.sum(qkv * qkv, axis=(1, 2))), jnp.stack([jnp.sum(proj * proj), jnp.sum(up * up), jnp.sum(down * down), jnp.sum(table * table)]), lax.optimization_barrier(jnp.sum(gain * gain, axis=1)), lax.optimization_barrier(jnp.sum(shift * shift, axis=1))]
    return jnp.concatenate(parts)

def expand(values):
    return (values[0:3][:, None, None], values[3], values[4], values[5], values[6], values[7:9][:, None], values[9:11][:, None])

def reference(tokens, cotangent, item_len, bucket_table, w_qkv, w_proj, w_up, w_down, rel_bias, ln_gain, ln_shift, mean_qkv, mean_proj, mean_up, mean_down, mean_bias, mean_gain, mean_shift, square_qkv, square_proj, square_up, square_down, square_bias, square_gain, square_shift):
    params = (w_qkv, w_proj, w_up, w_down, rel_bias, ln_gain, ln_shift)
    means = (mean_qkv, mean_proj, mean_up, mean_down, mean_bias, mean_gain, mean_shift)
    squares = (square_qkv, square_proj, square_up, square_down, square_bias, square_gain, square_shift)
    step = jax.checkpoint(layer)

    def forward(block_in, weights):
        groups = block_in.reshape(N_DP, TOK_DEV, D)

        def scan_step(carry, inputs):
            return (carry, step(inputs[0], inputs[1], bucket_table, weights))
        _, outputs = lax.scan(scan_step, jnp.zeros((), jnp.float32), (groups, item_len))
        return outputs.reshape(N_DP * TOK_DEV, D)
    block_out, pull_back = jax.vjp(forward, tokens.astype(jnp.float32), params)
    grad_in, grads = pull_back(cotangent.astype(jnp.float32))
    sq_grad = param_squares(grads)
    sq_weight = param_squares(params)
    grad_norm = jnp.sqrt(jnp.sum(sq_grad))
    clip = jnp.minimum(1.0, 1.0 / grad_norm)
    new_means = [0.5 * m + 0.5 * (clip * g) for m, g in zip(means, grads)]
    new_squares = [0.5 * s + 0.5 * (clip * g) * (clip * g) for s, g in zip(squares, grads)]
    updates = [nm / (jnp.sqrt(ns) + 1e-06) + 0.01 * w for nm, ns, w in zip(new_means, new_squares, params)]
    sq_update = param_squares(updates)
    trust = jnp.sqrt(sq_weight) / jnp.sqrt(sq_update)
    factors = expand(trust)
    new_weights = [w - 0.3 * f * u for w, f, u in zip(params, factors, updates)]
    param_norms = jnp.stack([jnp.sqrt(sq_weight), jnp.sqrt(sq_update)])
    return (block_out.astype(jnp.bfloat16), grad_in.astype(jnp.bfloat16), grad_norm, param_norms, new_weights[0], new_weights[1], new_weights[2], new_weights[3], new_weights[4], new_weights[5], new_weights[6], new_means[0], new_means[1], new_means[2], new_means[3], new_means[4], new_means[5], new_means[6], new_squares[0], new_squares[1], new_squares[2], new_squares[3], new_squares[4], new_squares[5], new_squares[6])
```

```python
import functools

import jax
import jax.numpy as jnp
from jax import lax
from jax.experimental import pallas as pl
from jax.experimental.pallas import tpu as pltpu
from jax.sharding import Mesh
from jax.sharding import PartitionSpec as P

H = 16
DH = 64
BUCKETS = 32
BLK = 512
NEG = -1e30
LOG2E = 1.4426950408889634
F32 = jnp.float32
BF = jnp.bfloat16
MESH = pl.DeviceIdType.MESH
HIGHEST = lax.Precision.HIGHEST
ALL = ("xy", "core", "zh", "zl")
DP = ("xy", "core")
TENSOR = ("zh", "zl")


def dot(left, right, left_dim, right_dim):
    return lax.dot_general(
        left, right, (((left_dim,), (right_dim,)), ((), ())), preferred_element_type=F32
    )


def make_slab(pattern, slab):
    width = slab.shape[1]
    slab[0:8, :] = pltpu.roll(jnp.broadcast_to(pattern, (8, width)), 0, 1, stride=1, stride_axis=0)
    done = 8
    while done < slab.shape[0]:
        slab[done : 2 * done, :] = pltpu.roll(slab[0:done, :], done, 1)
        done *= 2


def fold_slab(slab):
    width = slab.shape[1]
    half = slab.shape[0] // 2
    while half >= 8:
        slab[0:half, :] = slab[0:half, :] + pltpu.roll(slab[half : 2 * half, :], width - half, 1)
        half //= 2
    total = slab[0:1, :]
    for row in range(1, 8):
        total = total + pltpu.roll(slab[row : row + 1, :], width - row, 1)
    return total


def split_three(values):
    high = values.astype(BF).astype(F32)
    rest = values - high
    middle = rest.astype(BF).astype(F32)
    return high, middle, (rest - middle).astype(BF).astype(F32)


def put_queries(queries, split, minus, tok, dst):
    scaled = queries.astype(F32) * (DH**-0.5 * LOG2E)
    high = scaled.astype(BF)
    dst[0:DH, :] = high
    dst[DH : 2 * DH, :] = (scaled - high.astype(F32)).astype(BF)
    position = lax.broadcasted_iota(jnp.int32, (16, tok), 1)
    row = lax.broadcasted_iota(jnp.int32, (16, tok), 0)
    extra = jnp.where((row == 0) & (position >= split), 1.0, 0.0)
    if minus is not None:
        first, second, third = split_three(minus)
        extra = jnp.where(
            row == 1, first, jnp.where(row == 2, second, jnp.where(row == 3, third, extra))
        )
    dst[2 * DH : 2 * DH + 16, :] = extra.astype(BF)


def put_keys(keys, split, tok, dst):
    for start in range(0, tok, BLK):
        position = start + lax.broadcasted_iota(jnp.int32, (16, BLK), 1)
        row = lax.broadcasted_iota(jnp.int32, (16, BLK), 0)
        extra = jnp.where(
            row == 0, jnp.where(position < split, NEG, 0.0), jnp.where(row < 4, 1.0, 0.0)
        )
        block = keys[:, start : start + BLK].astype(F32)
        whole = jnp.concatenate([block, block, extra], axis=0)
        dst[start : start + BLK, :] = whole.T.astype(BF)


def block_at(index):
    return pl.ds(pl.multiple_of(index * BLK, BLK), BLK)


def attend_kernel(split_ref, pattern_ref, q_ref, k_ref, v_ref, o_ref, lse_ref, slab, kx, qx):
    tok = q_ref.shape[1]
    split = split_ref[0]
    make_slab(pattern_ref[0], slab)
    put_queries(q_ref[...], split, None, tok, qx)
    put_keys(k_ref, split, tok, kx)

    def step(i, j, top, total, out):
        scores = dot(kx[block_at(j), :], qx[:, block_at(i)], 1, 0) + slab[:, block_at(i - j)]
        new_top = jnp.maximum(top, jnp.max(scores, axis=0, keepdims=True))
        weights = jnp.exp2(scores - new_top)
        scale = jnp.exp2(top - new_top)
        total = total * scale + jnp.sum(weights, axis=0, keepdims=True)
        out = out * scale + dot(v_ref[:, block_at(j)], weights.astype(BF), 1, 0)
        return new_top, total, out

    def row(i, carry):
        start = (
            jnp.full((1, BLK), NEG, F32),
            jnp.zeros((1, BLK), F32),
            jnp.zeros((DH, BLK), F32),
        )
        top, total, out = lax.fori_loop(0, i + 1, lambda t, c: step(i, i - t, *c), start)
        o_ref[:, block_at(i)] = (out / total).astype(BF)
        lse_ref[0, :, block_at(i)] = top + jnp.log2(total)
        return carry

    lax.fori_loop(0, tok // BLK, row, 0)


def attend(qkv, pattern, split, heads):
    tok = qkv.shape[1]
    width = pattern.shape[-1]
    return pl.pallas_call(
        attend_kernel,
        grid=(heads,),
        in_specs=[
            pl.BlockSpec(memory_space=pltpu.SMEM),
            pl.BlockSpec((1, 1, width), lambda h: (h, 0, 0)),
            pl.BlockSpec((DH, tok), lambda h: (h, 0)),
            pl.BlockSpec((DH, tok), lambda h: (h + heads, 0)),
            pl.BlockSpec((DH, tok), lambda h: (h + 2 * heads, 0)),
        ],
        out_specs=[
            pl.BlockSpec((DH, tok), lambda h: (h, 0)),
            pl.BlockSpec((1, 1, tok), lambda h: (h, 0, 0)),
        ],
        out_shape=[
            jax.ShapeDtypeStruct((heads * DH, tok), BF),
            jax.ShapeDtypeStruct((heads, 1, tok), F32),
        ],
        scratch_shapes=[
            pltpu.VMEM((BLK, width), F32),
            pltpu.VMEM((tok, 2 * DH + 16), BF),
            pltpu.VMEM((2 * DH + 16, tok), BF),
        ],
        compiler_params=pltpu.CompilerParams(vmem_limit_bytes=56 * 2**20),
        cost_estimate=pl.CostEstimate(
            flops=heads * tok * tok * 800, bytes_accessed=8 * heads * DH * tok, transcendentals=0
        ),
        name="attend",
    )(split, pattern, qkv, qkv, qkv)


def attend_back_kernel(
    split_ref, pattern_ref, q_ref, k_ref, v_ref, o_ref, do_ref, lse_ref,
    dq_ref, dk_ref, dv_ref, dpattern_ref,
    slab, dslab, kx, qx, vx, dox, qn, don, dk, dv,
):
    tok = q_ref.shape[1]
    split = split_ref[0]
    make_slab(pattern_ref[0], slab)
    put_queries(q_ref[...], split, -lse_ref[0], tok, qx)
    put_keys(k_ref, split, tok, kx)
    dslab[...] = jnp.zeros_like(dslab)
    dk[...] = jnp.zeros_like(dk)
    dv[...] = jnp.zeros_like(dv)
    row = lax.broadcasted_iota(jnp.int32, (16, BLK), 0)
    ones = jnp.where(row < 3, 1.0, 0.0)
    for start in range(0, tok, BLK):
        here = slice(start, start + BLK)
        grad = do_ref[:, here].astype(F32)
        inner = jnp.sum(grad * o_ref[:, here].astype(F32), axis=0, keepdims=True)
        first, second, third = split_three(-inner)
        extra = jnp.where(
            row == 0, first, jnp.where(row == 1, second, jnp.where(row == 2, third, 0.0))
        )
        dox[0:DH, here] = do_ref[:, here]
        dox[DH : DH + 16, here] = extra.astype(BF)
        vx[here, :] = jnp.concatenate([v_ref[:, here].astype(F32), ones], axis=0).T.astype(BF)
        both = jnp.concatenate([q_ref[:, here].astype(F32), grad], axis=0).T
        qn[here, :] = both[:, 0:DH].astype(BF)
        don[here, :] = both[:, DH : 2 * DH].astype(BF)

    def tile(i, j):
        qs, ks, diagonal = block_at(i), block_at(j), block_at(i - j)
        shares = jnp.exp2(dot(kx[ks, :], qx[:, qs], 1, 0) + slab[:, diagonal])
        grad_scores = shares * dot(vx[ks, :], dox[:, qs], 1, 0)
        dslab[:, diagonal] += grad_scores
        low = grad_scores.astype(BF)
        dv[ks, :] += dot(shares.astype(BF), don[qs, :], 1, 0)
        dk[ks, :] += dot(low, qn[qs, :], 1, 0)
        return dot(k_ref[:, ks], low, 1, 0)

    def query_row(i, carry):
        total = lax.fori_loop(
            0, i + 1, lambda t, c: c + tile(i, i - t), jnp.zeros((DH, BLK), F32)
        )
        dq_ref[:, block_at(i)] = (total * DH**-0.5).astype(BF)
        return carry

    lax.fori_loop(0, tok // BLK, query_row, 0)
    for start in range(0, tok, BLK):
        here = slice(start, start + BLK)
        dk_ref[:, here] = (dk[here, :] * DH**-0.5).T.astype(BF)
        dv_ref[:, here] = dv[here, :].T.astype(BF)
    dpattern_ref[0] = fold_slab(dslab)


def attend_back(qkv, out, grad, lse, pattern, split, heads):
    tok = qkv.shape[1]
    width = pattern.shape[-1]
    flat = pl.BlockSpec((DH, tok), lambda h: (h, 0))
    return pl.pallas_call(
        attend_back_kernel,
        grid=(heads,),
        in_specs=[
            pl.BlockSpec(memory_space=pltpu.SMEM),
            pl.BlockSpec((1, 1, width), lambda h: (h, 0, 0)),
            flat,
            pl.BlockSpec((DH, tok), lambda h: (h + heads, 0)),
            pl.BlockSpec((DH, tok), lambda h: (h + 2 * heads, 0)),
            flat,
            flat,
            pl.BlockSpec((1, 1, tok), lambda h: (h, 0, 0)),
        ],
        out_specs=[flat] * 3 + [pl.BlockSpec((1, 1, width), lambda h: (h, 0, 0))],
        out_shape=[jax.ShapeDtypeStruct((heads * DH, tok), BF)] * 3
        + [jax.ShapeDtypeStruct((heads, 1, width), F32)],
        scratch_shapes=[
            pltpu.VMEM((BLK, width), F32),
            pltpu.VMEM((BLK, width), F32),
            pltpu.VMEM((tok, 2 * DH + 16), BF),
            pltpu.VMEM((2 * DH + 16, tok), BF),
            pltpu.VMEM((tok, DH + 16), BF),
            pltpu.VMEM((DH + 16, tok), BF),
            pltpu.VMEM((tok, DH), BF),
            pltpu.VMEM((tok, DH), BF),
            pltpu.VMEM((tok, DH), F32),
            pltpu.VMEM((tok, DH), F32),
        ],
        compiler_params=pltpu.CompilerParams(vmem_limit_bytes=60 * 2**20),
        cost_estimate=pl.CostEstimate(
            flops=heads * tok * tok * 1200, bytes_accessed=16 * heads * DH * tok, transcendentals=0
        ),
        name="attend_back",
    )(split, pattern, qkv, qkv, qkv, out, grad, lse)


def place():
    return tuple(lax.axis_index(axis) for axis in ALL)


def exchange_kernel(shape, to_owners, src_ref, dst_ref, send_sem, recv_sem, local_sem):
    places = shape["zl"]
    parts = shape["zh"] * places
    rows = dst_ref.shape[-1] if to_owners else src_ref.shape[-1]
    xy, core, zh, zl = place()
    mine_row = zh * places + zl
    mine_head = zl * 2 + core

    def owner(group, n):
        return (xy, group, n // places, n % places)

    def header(group, n):
        return (xy, n % 2, group, n // 2)

    def is_me(device):
        return (device[1] == core) & (device[2] == zh) & (device[3] == zl)

    if to_owners:
        def target(n):
            return owner(zh, n)

        def source(n):
            return header(core, n)

        mine = mine_head
    else:
        def target(n):
            return header(core, n)

        def source(n):
            return owner(zh, n)

        mine = mine_row
    barrier = pltpu.get_barrier_semaphore()
    for n in range(parts):
        device = source(n)

        @pl.when(jnp.logical_not(is_me(device)))
        def _():
            pl.semaphore_signal(barrier, inc=1, device_id=device, device_id_type=MESH)

    has_self = (zh == core).astype(jnp.int32)
    pl.semaphore_wait(barrier, parts - has_self)

    def piece(n):
        if to_owners:
            return src_ref.at[:, pl.ds(n * rows, rows)]
        return src_ref.at[n]

    def slot(n):
        if to_owners:
            return dst_ref.at[n]
        return dst_ref.at[:, pl.ds(pl.multiple_of(n * rows, rows), rows)]

    def remote(n, device):
        return pltpu.make_async_remote_copy(
            src_ref=piece(n),
            dst_ref=slot(mine),
            send_sem=send_sem.at[n],
            recv_sem=recv_sem.at[mine],
            device_id=device,
            device_id_type=MESH,
        )

    for n in range(parts):
        device = target(n)

        @pl.when(is_me(device))
        def _():
            pltpu.make_async_copy(piece(n), slot(mine), local_sem).start()

        @pl.when(jnp.logical_not(is_me(device)))
        def _():
            remote(n, device).start()

    for n in range(parts):
        device = target(n)

        @pl.when(is_me(device))
        def _():
            pltpu.make_async_copy(piece(n), slot(mine), local_sem).wait()

        @pl.when(jnp.logical_not(is_me(device)))
        def _():
            remote(n, device).wait_send()

    for n in range(parts):
        device = source(n)

        @pl.when(jnp.logical_not(is_me(device)))
        def _():
            pltpu.make_async_remote_copy(
                src_ref=piece(n),
                dst_ref=slot(n),
                send_sem=send_sem.at[n],
                recv_sem=recv_sem.at[n],
                device_id=device,
                device_id_type=MESH,
            ).wait_recv()


def exchange(shape, pieces, to_owners, collective_id):
    parts = shape["zh"] * shape["zl"]
    if to_owners:
        depth, rows = pieces.shape[0], pieces.shape[1] // parts
        out = (parts, depth, rows)
    else:
        depth, rows = pieces.shape[1], pieces.shape[2]
        out = (depth, parts * rows)
    return pl.pallas_call(
        functools.partial(exchange_kernel, shape, to_owners),
        out_shape=jax.ShapeDtypeStruct(out, pieces.dtype),
        in_specs=[pl.BlockSpec(memory_space=pl.ANY)],
        out_specs=pl.BlockSpec(memory_space=pl.ANY),
        scratch_shapes=[
            pltpu.SemaphoreType.DMA((parts,)),
            pltpu.SemaphoreType.DMA((parts,)),
            pltpu.SemaphoreType.DMA,
        ],
        compiler_params=pltpu.CompilerParams(collective_id=collective_id, has_side_effects=True),
        name="exchange",
    )(pieces)


def norm_parts(values):
    center = values - jnp.mean(values, axis=-1, keepdims=True)
    inverse = lax.rsqrt(jnp.mean(center * center, axis=-1, keepdims=True) + 1e-05)
    return center * inverse, inverse


def norm_back(normed, inverse, gain, grad):
    inner = grad * gain
    return inverse * (
        inner
        - jnp.mean(inner, axis=-1, keepdims=True)
        - normed * jnp.mean(inner * normed, axis=-1, keepdims=True)
    )


def gelu_exact(values):
    return jax.nn.gelu(values, approximate=False)


def squares_of(arrays):
    qkv, proj, up, down = arrays
    return jnp.concatenate(
        [
            jnp.sum(qkv * qkv, axis=(1, 2)),
            jnp.stack([jnp.sum(proj * proj), jnp.sum(up * up), jnp.sum(down * down)]),
        ]
    )


def small_squares(table, gain, shift):
    return jnp.concatenate(
        [jnp.sum(table * table)[None], jnp.sum(gain * gain, axis=1), jnp.sum(shift * shift, axis=1)]
    )


def expand(values):
    return (
        values[0:3][:, None, None],
        values[3],
        values[4],
        values[5],
        values[6],
        values[7:9][:, None],
        values[9:11][:, None],
    )


def per_device(
    shape,
    tokens, cotangent, item_len, bucket_table,
    w_qkv, w_proj, w_up, w_down, rel_bias, ln_gain, ln_shift,
    mean_qkv, mean_proj, mean_up, mean_down, mean_bias, mean_gain, mean_shift,
    square_qkv, square_proj, square_up, square_down, square_bias, square_gain, square_shift,
):
    columns, places = shape["xy"], shape["zl"]
    parts = 2 * places
    devices = columns * 2 * parts
    rows, width = tokens.shape
    heads = w_qkv.shape[2] // DH
    tok = rows * parts
    xy, core, zh, zl = place()
    me = ((xy * 2 + core) * 2 + zh) * places + zl
    head_block = zl * 2 + core

    to_heads = [
        (((c * 2 + k) * parts + z), ((c * 2 + z % 2) * 2 + k) * places + z // 2)
        for c in range(columns)
        for k in range(2)
        for z in range(parts)
    ]
    to_owner = [(b, a) for a, b in to_heads]
    w_heads = lax.all_gather(
        lax.ppermute(w_qkv.astype(BF), ALL, to_heads), ("xy", "zh"), axis=1, tiled=True
    )
    ff_local = w_up.shape[1]
    local = jnp.concatenate([w_proj.T, w_up, w_down.T], axis=1).astype(BF)
    shared = lax.all_gather(
        lax.all_gather(local, TENSOR, axis=0), DP, axis=1, tiled=True
    )
    heads_cols = w_proj.shape[0]
    proj_full = shared[:, :, :heads_cols]
    up_full = shared[:, :, heads_cols : heads_cols + ff_local]
    down_full = shared[:, :, heads_cols + ff_local :]

    small_local = jnp.concatenate([rel_bias, ln_gain.reshape(-1), ln_shift.reshape(-1)])
    small = lax.all_gather(small_local, ALL, axis=0)
    n_bias, n_gain = rel_bias.shape[0], ln_gain.shape[1]

    def columns_of(start):
        part = small[:, start : start + 2 * n_gain].reshape(devices, 2, n_gain)
        return part.transpose(1, 0, 2).reshape(2, width)

    table_flat = small[:, :n_bias].reshape(-1)
    gains, shifts = columns_of(n_bias), columns_of(n_bias + 2 * n_gain)

    swap = [(k * 2 + h, h * 2 + k) for k in range(2) for h in range(2)]
    group_rows = lax.all_gather(
        lax.ppermute(tokens, ("core", "zh"), swap), ("core", "zl"), axis=0, tiled=True
    )
    other_len = lax.ppermute(item_len, "core", [(0, 1), (1, 0)])
    split = jnp.where(zh == core, item_len, other_len)[0, 0:1]

    normed_all, _ = norm_parts(group_rows.astype(F32))
    a_first = (normed_all * gains[0] + shifts[0]).astype(BF)
    qkv = lax.dot_general(
        w_heads, a_first, (((1,), (1,)), ((), ())), preferred_element_type=F32
    ).astype(BF).reshape(3 * heads * DH, tok)

    table = lax.dynamic_slice_in_dim(
        table_flat.reshape(BUCKETS, H), head_block * heads, heads, 1
    )
    one_hot = (jnp.arange(BUCKETS)[:, None] == bucket_table[None, :]).astype(F32)
    dist_bias = lax.dot_general(
        table, one_hot, (((0,), (0,)), ((), ())), precision=HIGHEST, preferred_element_type=F32
    )
    pattern = jnp.concatenate(
        [dist_bias * LOG2E, jnp.full((heads, BLK), NEG, F32)], axis=1
    )[:, None, :]
    out, lse = attend(qkv, pattern, split, heads)

    attn_rows = exchange(shape, out, True, 0)
    x_rows = tokens.astype(F32)
    mixed = lax.dot_general(
        attn_rows, proj_full, (((0, 1), (0, 2)), ((), ())), preferred_element_type=F32
    )
    middle = x_rows + mixed
    normed_two, inverse_two = norm_parts(middle)
    a_second = (normed_two * gains[1] + shifts[1]).astype(BF)
    hidden_pre = jnp.einsum("nd,zdf->znf", a_second, up_full, preferred_element_type=F32)
    hidden = gelu_exact(hidden_pre).astype(BF)
    ffn = jnp.einsum("znf,zdf->nd", hidden, down_full, preferred_element_type=F32)
    block_out = (middle + ffn).astype(BF)
    _, gelu_back = jax.vjp(gelu_exact, hidden_pre)
    grad_down = jnp.einsum("nd,znf->zdf", cotangent, hidden, preferred_element_type=F32).astype(BF)
    grad_hidden = jnp.einsum("nd,zdf->znf", cotangent, down_full, preferred_element_type=F32)
    grad_pre = gelu_back(grad_hidden)[0].astype(BF)
    grad_up = jnp.einsum("nd,znf->zdf", a_second, grad_pre, preferred_element_type=F32).astype(BF)
    grad_second = jnp.einsum("znf,zdf->nd", grad_pre, up_full, preferred_element_type=F32)
    grad_middle = cotangent.astype(F32) + norm_back(normed_two, inverse_two, gains[1], grad_second)
    gain_two, shift_two = jnp.sum(grad_second * normed_two, axis=0), jnp.sum(grad_second, axis=0)
    grad_mid_low = grad_middle.astype(BF)
    grad_attn = jnp.einsum(
        "nd,tde->ten", grad_mid_low, proj_full, preferred_element_type=F32
    ).astype(BF)
    grad_proj = jnp.einsum(
        "nd,ten->tde", grad_mid_low, attn_rows, preferred_element_type=F32
    ).astype(BF)

    grad_out = exchange(shape, grad_attn, False, 1)
    grad_q, grad_k, grad_v, grad_pattern = attend_back(
        qkv, out, grad_out, lse, pattern, split, heads
    )
    grad_heads = jnp.stack([grad_q, grad_k, grad_v])
    grad_qkv = jnp.einsum("td,cet->cde", a_first, grad_heads, preferred_element_type=F32).astype(BF)
    grad_first = jnp.einsum(
        "cet,cde->td", grad_heads, w_heads, preferred_element_type=F32
    )
    gain_one, shift_one = jnp.sum(grad_first * normed_all, axis=0), jnp.sum(grad_first, axis=0)
    first_rows = lax.ppermute(
        lax.psum_scatter(grad_first.astype(BF), ("core", "zl"), scatter_dimension=0, tiled=True),
        ("core", "zh"),
        swap,
    ).astype(F32)
    normed_one, inverse_one = norm_parts(x_rows)
    grad_tokens = (
        grad_middle + norm_back(normed_one, inverse_one, gains[0], first_rows)
    ).astype(BF)

    def scatter(grad):
        part = lax.psum_scatter(grad, DP, scatter_dimension=1, tiled=True)
        return lax.psum_scatter(part, TENSOR, scatter_dimension=0, tiled=False).astype(F32)

    sum_down, sum_up, sum_proj = scatter(grad_down).T, scatter(grad_up), scatter(grad_proj).T
    sum_qkv = lax.ppermute(
        lax.psum_scatter(grad_qkv, ("xy", "zh"), scatter_dimension=1, tiled=True), ALL, to_owner
    ).astype(F32)
    bias_grad = lax.dot_general(
        one_hot, grad_pattern[:, 0, :tok], (((1,), (1,)), ((), ())),
        precision=HIGHEST, preferred_element_type=F32,
    )
    table_grad = lax.dynamic_update_slice(
        jnp.zeros((BUCKETS, H), F32), bias_grad, (0, head_block * heads)
    ).reshape(-1)
    small_sum = lax.psum(
        jnp.concatenate([table_grad, gain_one, gain_two, shift_one, shift_two]), ALL
    )
    full_table = small_sum[: BUCKETS * H]
    full_gain = small_sum[BUCKETS * H : BUCKETS * H + 2 * width].reshape(2, width)
    full_shift = small_sum[BUCKETS * H + 2 * width :].reshape(2, width)
    sum_table = lax.dynamic_slice_in_dim(full_table, me * n_bias, n_bias, 0)
    sum_gain = lax.dynamic_slice_in_dim(full_gain, me * n_gain, n_gain, 1)
    sum_shift = lax.dynamic_slice_in_dim(full_shift, me * n_gain, n_gain, 1)

    params = (w_qkv, w_proj, w_up, w_down, rel_bias, ln_gain, ln_shift)
    grads = (sum_qkv, sum_proj, sum_up, sum_down, sum_table, sum_gain, sum_shift)
    means = (mean_qkv, mean_proj, mean_up, mean_down, mean_bias, mean_gain, mean_shift)
    squares = (
        square_qkv, square_proj, square_up, square_down, square_bias, square_gain, square_shift,
    )
    sq_weight = lax.psum(
        jnp.concatenate([squares_of(params[:4]), small_squares(*params[4:])]), ALL
    )
    sq_grad = jnp.concatenate(
        [lax.psum(squares_of(grads[:4]), ALL), small_squares(full_table, full_gain, full_shift)]
    )
    grad_norm = jnp.sqrt(jnp.sum(sq_grad))
    clip = jnp.minimum(1.0, 1.0 / grad_norm)
    new_means = [0.5 * m + 0.5 * (clip * g) for m, g in zip(means, grads)]
    new_squares = [0.5 * s + 0.5 * (clip * g) * (clip * g) for s, g in zip(squares, grads)]
    updates = [
        nm / (jnp.sqrt(ns) + 1e-06) + 0.01 * w for nm, ns, w in zip(new_means, new_squares, params)
    ]
    sq_update = lax.psum(
        jnp.concatenate([squares_of(updates[:4]), small_squares(*updates[4:])]), ALL
    )
    trust = jnp.sqrt(sq_weight) / jnp.sqrt(sq_update)
    factors = expand(trust)
    new_weights = [w - 0.3 * f * u for w, f, u in zip(params, factors, updates)]
    param_norms = jnp.stack([jnp.sqrt(sq_weight), jnp.sqrt(sq_update)])
    return (block_out, grad_tokens, grad_norm, param_norms, *new_weights, *new_means, *new_squares)


def solution(mesh):
    shape = {"xy": mesh.shape["dp"] // 2, "core": 2, "zh": 2, "zl": mesh.shape["tensor"] // 2}
    split_mesh = Mesh(mesh.devices.reshape(tuple(shape[axis] for axis in ALL)), ALL)
    weights = (
        P(None, DP, TENSOR),
        P(TENSOR, DP),
        P(DP, TENSOR),
        P(TENSOR, DP),
        P(ALL),
        P(None, ALL),
        P(None, ALL),
    )
    rows = P(ALL, None)
    return jax.shard_map(
        functools.partial(per_device, shape),
        mesh=split_mesh,
        in_specs=(rows, rows, P(DP, None), P(), *weights, *weights, *weights),
        out_specs=(rows, rows, P(), P(), *weights, *weights, *weights),
        check_vma=False,
    )
```

```python
import functools

import jax
import jax.numpy as jnp
from jax import lax
from jax.experimental import pallas as pl
from jax.experimental.pallas import tpu as pltpu
from jax.sharding import Mesh
from jax.sharding import PartitionSpec as P

H = 16
DH = 64
BUCKETS = 32
BLK = 512
NEG = -1e30
LOG2E = 1.4426950408889634
F32 = jnp.float32
BF = jnp.bfloat16
MESH = pl.DeviceIdType.MESH
HIGHEST = lax.Precision.HIGHEST
ALL = ("xy", "core", "zh", "zl")
DP = ("xy", "core")
TENSOR = ("zh", "zl")


def dot(left, right, left_dim, right_dim):
    return lax.dot_general(
        left, right, (((left_dim,), (right_dim,)), ((), ())), preferred_element_type=F32
    )


def make_slab(pattern, slab):
    width = slab.shape[1]
    slab[0:8, :] = pltpu.roll(jnp.broadcast_to(pattern, (8, width)), 0, 1, stride=1, stride_axis=0)
    done = 8
    while done < slab.shape[0]:
        slab[done : 2 * done, :] = pltpu.roll(slab[0:done, :], done, 1)
        done *= 2


def fold_slab(slab):
    width = slab.shape[1]
    half = slab.shape[0] // 2
    while half >= 8:
        slab[0:half, :] = slab[0:half, :] + pltpu.roll(slab[half : 2 * half, :], width - half, 1)
        half //= 2
    total = slab[0:1, :]
    for row in range(1, 8):
        total = total + pltpu.roll(slab[row : row + 1, :], width - row, 1)
    return total


def split_three(values):
    high = values.astype(BF).astype(F32)
    rest = values - high
    middle = rest.astype(BF).astype(F32)
    return high, middle, (rest - middle).astype(BF).astype(F32)


def put_queries(queries, split, minus, tok, dst):
    scaled = queries.astype(F32) * (DH**-0.5 * LOG2E)
    high = scaled.astype(BF)
    dst[0:DH, :] = high
    dst[DH : 2 * DH, :] = (scaled - high.astype(F32)).astype(BF)
    position = lax.broadcasted_iota(jnp.int32, (16, tok), 1)
    row = lax.broadcasted_iota(jnp.int32, (16, tok), 0)
    extra = jnp.where((row == 0) & (position >= split), 1.0, 0.0)
    if minus is not None:
        first, second, third = split_three(minus)
        extra = jnp.where(
            row == 1, first, jnp.where(row == 2, second, jnp.where(row == 3, third, extra))
        )
    dst[2 * DH : 2 * DH + 16, :] = extra.astype(BF)


def put_keys(keys, split, tok, dst):
    for start in range(0, tok, BLK):
        position = start + lax.broadcasted_iota(jnp.int32, (16, BLK), 1)
        row = lax.broadcasted_iota(jnp.int32, (16, BLK), 0)
        extra = jnp.where(
            row == 0, jnp.where(position < split, NEG, 0.0), jnp.where(row < 4, 1.0, 0.0)
        )
        block = keys[:, start : start + BLK].astype(F32)
        whole = jnp.concatenate([block, block, extra], axis=0)
        dst[start : start + BLK, :] = whole.T.astype(BF)


def block_at(index):
    return pl.ds(pl.multiple_of(index * BLK, BLK), BLK)


def attend_kernel(
    shape, split_ref, pattern_ref, q_ref, k_ref, v_ref, out_ref, rows_ref, lse_ref,
    slab, kx, qx, outs, local_sem, send_sem, recv_sem,
):
    head = pl.program_id(0)
    tok = q_ref.shape[1]
    split = split_ref[0]
    trade = Trade(shape, tok)

    @pl.when(head == 0)
    def _():
        greet_column(shape)

    make_slab(pattern_ref[0], slab)
    put_queries(q_ref[...], split, None, tok, qx)
    put_keys(k_ref, split, tok, kx)

    def step(i, j, top, total, out):
        scores = dot(kx[block_at(j), :], qx[:, block_at(i)], 1, 0) + slab[:, block_at(i - j)]
        new_top = jnp.maximum(top, jnp.max(scores, axis=0, keepdims=True))
        weights = jnp.exp2(scores - new_top)
        scale = jnp.exp2(top - new_top)
        total = total * scale + jnp.sum(weights, axis=0, keepdims=True)
        out = out * scale + dot(v_ref[:, block_at(j)], weights.astype(BF), 1, 0)
        return new_top, total, out

    def row(i, carry):
        start = (
            jnp.full((1, BLK), NEG, F32),
            jnp.zeros((1, BLK), F32),
            jnp.zeros((DH, BLK), F32),
        )
        top, total, out = lax.fori_loop(0, i + 1, lambda t, c: step(i, i - t, *c), start)
        outs[head, :, block_at(i)] = (out / total).astype(BF)
        lse_ref[0, :, block_at(i)] = top + jnp.log2(total)
        return carry

    lax.fori_loop(0, tok // BLK, row, 0)

    def keep(h):
        return pltpu.make_async_copy(outs.at[h], out_ref.at[h], local_sem.at[0, h])

    def piece(h, n):
        return outs.at[h, :, pl.ds(pl.multiple_of(n * trade.rows, trade.rows), trade.rows)]

    def slot(h, n):
        return rows_ref.at[n, h]

    keep(head).start()
    trade.give(head, piece, slot, trade.owner, trade.head, local_sem.at[1, head], send_sem, recv_sem)

    @pl.when(head == pl.num_programs(0) - 1)
    def _():
        for h in range(rows_ref.shape[1]):
            keep(h).wait()
            trade.given(h, piece, slot, trade.owner, trade.head, local_sem.at[1, h], send_sem, recv_sem)
            trade.take(h, piece, slot, trade.header, send_sem, recv_sem)


def attend(shape, qkv, pattern, split, heads):
    tok = qkv.shape[1]
    width = pattern.shape[-1]
    parts = shape["zh"] * shape["zl"]
    dma = pltpu.SemaphoreType.DMA
    return pl.pallas_call(
        functools.partial(attend_kernel, shape),
        grid=(heads,),
        in_specs=[
            pl.BlockSpec(memory_space=pltpu.SMEM),
            pl.BlockSpec((1, 1, width), lambda h: (h, 0, 0)),
            pl.BlockSpec((DH, tok), lambda h: (h, 0)),
            pl.BlockSpec((DH, tok), lambda h: (h + heads, 0)),
            pl.BlockSpec((DH, tok), lambda h: (h + 2 * heads, 0)),
        ],
        out_specs=[
            pl.BlockSpec(memory_space=pl.ANY),
            pl.BlockSpec(memory_space=pl.ANY),
            pl.BlockSpec((1, 1, tok), lambda h: (h, 0, 0)),
        ],
        out_shape=[
            jax.ShapeDtypeStruct((heads, DH, tok), BF),
            jax.ShapeDtypeStruct((parts, heads, DH, tok // parts), BF),
            jax.ShapeDtypeStruct((heads, 1, tok), F32),
        ],
        scratch_shapes=[
            pltpu.VMEM((BLK, width), F32),
            pltpu.VMEM((tok, 2 * DH + 16), BF),
            pltpu.VMEM((2 * DH + 16, tok), BF),
            pltpu.VMEM((heads, DH, tok), BF),
            dma((2, heads)),
            dma((heads, parts)),
            dma((heads, parts)),
        ],
        compiler_params=pltpu.CompilerParams(
            vmem_limit_bytes=56 * 2**20, collective_id=0, has_side_effects=True
        ),
        name="attend",
    )(split, pattern, qkv, qkv, qkv)


def attend_back_kernel(
    shape, first_head, split_ref, pattern_ref, q_ref, k_ref, v_ref, o_ref, lse_ref, given_ref,
    grads_ref, dpattern_ref,
    slab, dslab, kx, qx, vx, dox, qn, don, dk, dv, taken,
    local_sem, in_send, in_recv,
):
    head = pl.program_id(0)
    tok = q_ref.shape[1]
    split = split_ref[0]
    trade = Trade(shape, tok)
    heads = taken.shape[0]

    def in_piece(h, n):
        return given_ref.at[n, first_head + h]

    def in_slot(h, n):
        return taken.at[h, :, pl.ds(pl.multiple_of(n * trade.rows, trade.rows), trade.rows)]

    @pl.when(head == 0)
    def _():
        greet_column(shape)
        for h in range(heads):
            trade.give(
                h, in_piece, in_slot, trade.header, trade.row, local_sem.at[h], in_send, in_recv
            )

    make_slab(pattern_ref[0], slab)
    put_queries(q_ref[...], split, -lse_ref[0], tok, qx)
    put_keys(k_ref, split, tok, kx)
    dslab[...] = jnp.zeros_like(dslab)
    dk[...] = jnp.zeros_like(dk)
    dv[...] = jnp.zeros_like(dv)
    row = lax.broadcasted_iota(jnp.int32, (16, BLK), 0)
    ones = jnp.where(row < 3, 1.0, 0.0)
    trade.given(
        head, in_piece, in_slot, trade.header, trade.row, local_sem.at[head], in_send, in_recv
    )
    trade.take(head, in_piece, in_slot, trade.owner, in_send, in_recv)
    for start in range(0, tok, BLK):
        here = slice(start, start + BLK)
        low_grad = taken[head, :, here]
        grad = low_grad.astype(F32)
        inner = jnp.sum(grad * o_ref[0, :, here].astype(F32), axis=0, keepdims=True)
        first, second, third = split_three(-inner)
        extra = jnp.where(
            row == 0, first, jnp.where(row == 1, second, jnp.where(row == 2, third, 0.0))
        )
        dox[0:DH, here] = low_grad
        dox[DH : DH + 16, here] = extra.astype(BF)
        vx[here, :] = jnp.concatenate([v_ref[:, here].astype(F32), ones], axis=0).T.astype(BF)
        both = jnp.concatenate([q_ref[:, here].astype(F32), grad], axis=0).T
        qn[here, :] = both[:, 0:DH].astype(BF)
        don[here, :] = both[:, DH : 2 * DH].astype(BF)

    def tile(i, j):
        qs, ks, diagonal = block_at(i), block_at(j), block_at(i - j)
        shares = jnp.exp2(dot(kx[ks, :], qx[:, qs], 1, 0) + slab[:, diagonal])
        grad_scores = shares * dot(vx[ks, :], dox[:, qs], 1, 0)
        dslab[:, diagonal] += grad_scores
        low = grad_scores.astype(BF)
        dv[ks, :] += dot(shares.astype(BF), don[qs, :], 1, 0)
        dk[ks, :] += dot(low, qn[qs, :], 1, 0)
        return dot(k_ref[:, ks], low, 1, 0)

    def query_row(i, carry):
        total = lax.fori_loop(
            0, i + 1, lambda t, c: c + tile(i, i - t), jnp.zeros((DH, BLK), F32)
        )
        grads_ref[0, 0, :, block_at(i)] = (total * DH**-0.5).astype(BF)
        return carry

    lax.fori_loop(0, tok // BLK, query_row, 0)
    for start in range(0, tok, BLK):
        here = slice(start, start + BLK)
        grads_ref[1, 0, :, here] = (dk[here, :] * DH**-0.5).T.astype(BF)
        grads_ref[2, 0, :, here] = dv[here, :].T.astype(BF)
    dpattern_ref[0] = fold_slab(dslab)


def attend_back(shape, qkv, out, given, lse, pattern, split, heads, first_head, count, collective_id):
    tok = qkv.shape[1]
    width = pattern.shape[-1]
    parts = shape["zh"] * shape["zl"]
    anywhere = pl.BlockSpec(memory_space=pl.ANY)
    dma = pltpu.SemaphoreType.DMA
    return pl.pallas_call(
        functools.partial(attend_back_kernel, shape, first_head),
        grid=(count,),
        in_specs=[
            pl.BlockSpec(memory_space=pltpu.SMEM),
            pl.BlockSpec((1, 1, width), lambda h: (first_head + h, 0, 0)),
            pl.BlockSpec((DH, tok), lambda h: (first_head + h, 0)),
            pl.BlockSpec((DH, tok), lambda h: (first_head + h + heads, 0)),
            pl.BlockSpec((DH, tok), lambda h: (first_head + h + 2 * heads, 0)),
            pl.BlockSpec((1, DH, tok), lambda h: (first_head + h, 0, 0)),
            pl.BlockSpec((1, 1, tok), lambda h: (first_head + h, 0, 0)),
            anywhere,
        ],
        out_specs=[
            pl.BlockSpec((3, 1, DH, tok), lambda h: (0, h, 0, 0)),
            pl.BlockSpec((1, 1, width), lambda h: (h, 0, 0)),
        ],
        out_shape=[
            jax.ShapeDtypeStruct((3, count, DH, tok), BF),
            jax.ShapeDtypeStruct((count, 1, width), F32),
        ],
        scratch_shapes=[
            pltpu.VMEM((BLK, width), F32),
            pltpu.VMEM((BLK, width), F32),
            pltpu.VMEM((tok, 2 * DH + 16), BF),
            pltpu.VMEM((2 * DH + 16, tok), BF),
            pltpu.VMEM((tok, DH + 16), BF),
            pltpu.VMEM((DH + 16, tok), BF),
            pltpu.VMEM((tok, DH), BF),
            pltpu.VMEM((tok, DH), BF),
            pltpu.VMEM((tok, DH), F32),
            pltpu.VMEM((tok, DH), F32),
            pltpu.VMEM((count, DH, tok), BF),
            dma((count,)),
            dma((count, parts)),
            dma((count, parts)),
        ],
        compiler_params=pltpu.CompilerParams(
            vmem_limit_bytes=60 * 2**20, collective_id=collective_id, has_side_effects=True
        ),
        name="attend_back",
    )(split, pattern, qkv, qkv, qkv, out, lse, given)


def place():
    return tuple(lax.axis_index(axis) for axis in ALL)


class Trade:
    def __init__(self, shape, tok):
        self.places = shape["zl"]
        self.parts = shape["zh"] * self.places
        self.rows = tok // self.parts
        self.me = place()
        _, core, zh, zl = self.me
        self.row = zh * self.places + zl
        self.head = zl * 2 + core

    def owner(self, n):
        return (self.me[0], self.me[2], lax.div(n, self.places), lax.rem(n, self.places))

    def header(self, n):
        return (self.me[0], lax.rem(n, 2), self.me[1], lax.div(n, 2))

    def each(self, device_of, local, remote):
        for index in range(self.parts):
            n = jnp.where(self.me[2] == 1, index, self.parts - 1 - index)
            device = device_of(n)
            if local is not None:

                @pl.when(is_same(device, self.me))
                def _():
                    local(n)

            @pl.when(jnp.logical_not(is_same(device, self.me)))
            def _():
                remote(n, device)

    def give(self, h, piece, slot, device_of, mine, local_sem, send_sem, recv_sem):
        def local(n):
            pltpu.make_async_copy(piece(h, n), slot(h, mine), local_sem).start()

        def remote(n, device):
            send(piece(h, n), slot(h, mine), send_sem.at[h, n], recv_sem.at[h, mine], device).start()

        self.each(device_of, local, remote)

    def given(self, h, piece, slot, device_of, mine, local_sem, send_sem, recv_sem):
        def local(n):
            pltpu.make_async_copy(piece(h, n), slot(h, mine), local_sem).wait()

        def remote(n, device):
            send(piece(h, n), slot(h, mine), send_sem.at[h, n], recv_sem.at[h, mine], device).wait_send()

        self.each(device_of, local, remote)

    def take(self, h, piece, slot, device_of, send_sem, recv_sem):
        def remote(n, device):
            send(piece(h, n), slot(h, n), send_sem.at[h, n], recv_sem.at[h, n], device).wait_recv()

        self.each(device_of, None, remote)


def is_same(left, right):
    same = left[0] == right[0]
    for one, other in zip(left[1:], right[1:]):
        same = same & (one == other)
    return same


def column_peers(shape, device):
    xy, core, zh, zl = device
    places = shape["zl"]
    total = 4 * places
    mine = (core * 2 + zh) * places + zl
    for step in range(1, total):
        there = lax.rem(mine + step, total)
        yield step, there, (xy, there // (2 * places), lax.rem(there // places, 2), lax.rem(there, places))


def plane_peers(shape, device):
    xy, core, zh, zl = device
    for step in range(1, shape["xy"]):
        there = lax.rem(xy + step, shape["xy"])
        yield step, there, (there, core, zh, zl)


def greet(shape):
    device = place()
    barrier = pltpu.get_barrier_semaphore()
    peers = [peer for _, _, peer in column_peers(shape, device)]
    peers += [peer for _, _, peer in plane_peers(shape, device)]
    for peer in peers:
        pl.semaphore_signal(barrier, inc=1, device_id=peer, device_id_type=MESH)
    pl.semaphore_wait(barrier, len(peers))


def greet_column(shape):
    barrier = pltpu.get_barrier_semaphore()
    peers = [peer for _, _, peer in column_peers(shape, place())]
    for peer in peers:
        pl.semaphore_signal(barrier, inc=1, device_id=peer, device_id_type=MESH)
    pl.semaphore_wait(barrier, len(peers))


def send(src, dst, send_sem, recv_sem, device):
    return pltpu.make_async_remote_copy(
        src_ref=src, dst_ref=dst, send_sem=send_sem, recv_sem=recv_sem,
        device_id=device, device_id_type=MESH,
    )


CHUNKS = 4


def gather_kernel(
    shape, tokens_ref, wq_ref, small_ref, wide_ref, rows_ref, heads_ref, all_small_ref, all_wide_ref,
    local_sems, in_send, fwd_send, share_send, x_recv, xs_recv,
    z_send, z_recv, p_send, p_recv, s_send, s_recv, w_send, w_recv, q_send, q_recv,
):
    me = place()
    xy, core, zh, zl = me
    places = shape["zl"]
    parts = 2 * places
    columns = shape["xy"]
    z = zh * places + zl
    sibling = (xy, 1 - core, zh, zl)
    size = tokens_ref.shape[0] // (2 * CHUNKS)
    dp = xy * 2 + core
    inside = core == zh
    outside = jnp.logical_not(inside)
    entry = jnp.where(zh < core, 0, places - 1)

    def chunk_of(ref, half, chunk):
        return ref.at[pl.ds(pl.multiple_of((half * CHUNKS + chunk) * size, size), size), :]

    def beside(step):
        there = z + step
        return (xy, core, there // places, lax.rem(there, places))

    greet(shape)

    depth = wq_ref.shape[1]
    head_block = zl * 2 + core

    def depth_of(index, count):
        return heads_ref.at[:, pl.ds(pl.multiple_of(index * depth, depth), count * depth), :]

    def wq_target(half):
        return (xy, lax.rem(z, 2), half, lax.div(z, 2))

    def wq_source(c):
        return (xy, c, lax.div(head_block, places), lax.rem(head_block, places))

    own_wq = pltpu.make_async_copy(wq_ref, depth_of(dp, 1), local_sems.at[1])
    own_small = pltpu.make_async_copy(small_ref, all_small_ref.at[dp, z], local_sems.at[2])
    own_wide = pltpu.make_async_copy(wide_ref, all_wide_ref.at[z], local_sems.at[3])
    own_small.start()
    for n in range(2):

        @pl.when(is_same(wq_target(n), me))
        def _():
            own_wq.start()

        @pl.when(jnp.logical_not(is_same(wq_target(n), me)))
        def _():
            send(wq_ref, depth_of(dp, 1), q_send.at[n], q_recv.at[core], wq_target(n)).start()

    for step in range(1, parts):
        there = lax.rem(z + step, parts)
        device = (xy, core, there // places, lax.rem(there, places))
        send(small_ref, all_small_ref.at[dp, z], z_send.at[step], z_recv.at[z], device).start()

    @pl.when(outside)
    def _():
        for chunk in range(CHUNKS):
            for half in range(2):
                send(
                    chunk_of(tokens_ref, half, chunk), chunk_of(rows_ref.at[z], half, chunk),
                    in_send.at[half, chunk], x_recv.at[z, chunk], (xy, half, core, entry),
                ).start()

    @pl.when(inside)
    def _():
        for chunk in range(CHUNKS):
            send(
                chunk_of(tokens_ref, 1 - core, chunk), chunk_of(rows_ref.at[z], 1 - core, chunk),
                in_send.at[0, chunk], x_recv.at[z, chunk], sibling,
            ).start()
        pltpu.make_async_copy(tokens_ref, rows_ref.at[z], local_sems.at[0]).start()

    def ways(shard):
        from_half, from_place = shard // places, lax.rem(shard, places)
        start = jnp.where(from_half == zh, from_place, jnp.where(from_half < zh, 0, places - 1))
        return (zl >= start) & (zl < places - 1), (zl <= start) & (zl > 0)

    def pass_on(shard, chunk, source):
        mine = chunk_of(rows_ref.at[shard], core, chunk)
        for n, (way, step) in enumerate(zip(ways(shard), (1, -1))):

            @pl.when(way)
            def _():
                send(
                    source, mine, fwd_send.at[n, shard, chunk], x_recv.at[shard, chunk],
                    (xy, core, zh, zl + step),
                ).start()

    def share(shard, chunk, source):
        mine = chunk_of(rows_ref.at[shard], core, chunk)
        send(source, mine, share_send.at[shard, chunk], xs_recv.at[shard, chunk], sibling).start()

    def got(shard, chunk):
        mine = chunk_of(rows_ref.at[shard], core, chunk)
        send(mine, mine, share_send.at[shard, chunk], x_recv.at[shard, chunk], sibling).wait_recv()

    @pl.when(inside)
    def _():
        for chunk in range(CHUNKS):
            mine = chunk_of(tokens_ref, core, chunk)
            pass_on(z, chunk, mine)
            share(z, chunk, mine)

    own_wide.start()
    for n, step in enumerate((1, -1)):

        @pl.when((z + step >= 0) & (z + step < parts))
        def _():
            send(
                wide_ref, all_wide_ref.at[z], w_send.at[n, z], w_recv.at[z], beside(step)
            ).start()

    @pl.when(outside)
    def _():
        for chunk in range(CHUNKS):
            got(z, chunk)
            pass_on(z, chunk, chunk_of(rows_ref.at[z], core, chunk))

    own_small.wait()
    for step in range(1, parts):
        there = lax.rem(z + step, parts)
        send(small_ref, all_small_ref.at[dp, there], z_send.at[step], z_recv.at[there], sibling).wait_recv()
    for c in range(2):

        @pl.when(is_same(wq_source(c), me))
        def _():
            own_wq.wait()

        @pl.when(jnp.logical_not(is_same(wq_source(c), me)))
        def _():
            here = depth_of(xy * 2 + c, 1)
            send(here, here, q_send.at[0], q_recv.at[c], wq_source(c)).wait_recv()

    def arrays_at(column):
        return depth_of(column * 2, 2), all_small_ref.at[column * 2 + core]

    for step, there, device in plane_peers(shape, me):
        for n, ref in enumerate(arrays_at(xy)):
            send(ref, ref, p_send.at[n, step], p_recv.at[n, xy], device).start()
    ref = all_small_ref.at[dp]
    send(ref, ref, s_send.at[xy], s_recv.at[xy], sibling).start()

    for distance in range(1, parts):
        for chunk in range(CHUNKS):
            for shard in (z + distance, z - distance):

                @pl.when((shard >= 0) & (shard < parts))
                def _():
                    got(shard, chunk)
                    mine = chunk_of(rows_ref.at[shard], core, chunk)
                    pass_on(shard, chunk, mine)
                    share(shard, chunk, mine)

        for n, step in enumerate((1, -1)):
            shard = z - step * distance

            @pl.when((shard >= 0) & (shard < parts))
            def _():
                piece = all_wide_ref.at[shard]
                send(piece, piece, w_send.at[n, shard], w_recv.at[shard], sibling).wait_recv()

            @pl.when((shard >= 0) & (shard < parts) & (z + step >= 0) & (z + step < parts))
            def _():
                piece = all_wide_ref.at[shard]
                send(piece, piece, w_send.at[n, shard], w_recv.at[shard], beside(step)).start()

    for step in range(1, columns):
        there = lax.rem(xy + columns - step, columns)
        for n, ref in enumerate(arrays_at(there)):
            send(ref, ref, p_send.at[n, step], p_recv.at[n, there], sibling).wait_recv()
        ref = all_small_ref.at[there * 2 + core]
        send(ref, ref, s_send.at[there], s_recv.at[there], sibling).start()

    for column in range(columns):
        ref = all_small_ref.at[column * 2 + 1 - core]
        copy = send(ref, ref, s_send.at[column], s_recv.at[column], sibling)
        copy.wait_recv()
        copy.wait_send()
    for step in range(1, columns):
        for n, ref in enumerate(arrays_at(xy)):
            send(ref, ref, p_send.at[n, step], p_recv.at[n, xy], sibling).wait_send()
    for step in range(1, parts):
        send(small_ref, all_small_ref.at[dp, z], z_send.at[step], z_recv.at[z], sibling).wait_send()
    for n in range(2):

        @pl.when(jnp.logical_not(is_same(wq_target(n), me)))
        def _():
            send(wq_ref, depth_of(dp, 1), q_send.at[n], q_recv.at[core], sibling).wait_send()

    own_wide.wait()
    for n, step in enumerate((1, -1)):
        for distance in range(parts):
            shard = z - step * distance

            @pl.when((shard >= 0) & (shard < parts) & (z + step >= 0) & (z + step < parts))
            def _():
                piece = all_wide_ref.at[shard]
                send(piece, piece, w_send.at[n, shard], w_recv.at[shard], beside(step)).wait_send()

    for shard in range(parts):
        for chunk in range(CHUNKS):
            mine = chunk_of(rows_ref.at[shard], core, chunk)
            other = chunk_of(rows_ref.at[shard], 1 - core, chunk)
            copy = send(mine, other, share_send.at[shard, chunk], xs_recv.at[shard, chunk], sibling)

            @pl.when(jnp.logical_not((shard == z) & outside))
            def _():
                copy.wait_send()

            @pl.when(jnp.logical_not((shard == z) & inside))
            def _():
                copy.wait_recv()

            for n, way in enumerate(ways(shard)):

                @pl.when(way)
                def _():
                    send(
                        mine, mine, fwd_send.at[n, shard, chunk], x_recv.at[shard, chunk], sibling
                    ).wait_send()

    for chunk in range(CHUNKS):
        first = chunk_of(tokens_ref, 0, chunk)
        send(first, first, in_send.at[0, chunk], x_recv.at[z, chunk], sibling).wait_send()

        @pl.when(outside)
        def _():
            send(first, first, in_send.at[1, chunk], x_recv.at[z, chunk], sibling).wait_send()

    @pl.when(inside)
    def _():
        pltpu.make_async_copy(tokens_ref, rows_ref.at[z], local_sems.at[0]).wait()


def gather(shape, tokens, wq, small, wide):
    parts, columns = shape["zh"] * shape["zl"], shape["xy"]
    anywhere = pl.BlockSpec(memory_space=pl.ANY)
    dma = pltpu.SemaphoreType.DMA
    return pl.pallas_call(
        functools.partial(gather_kernel, shape),
        out_shape=[
            jax.ShapeDtypeStruct((parts, *tokens.shape), tokens.dtype),
            jax.ShapeDtypeStruct((3, 2 * columns * wq.shape[1], wq.shape[2]), wq.dtype),
            jax.ShapeDtypeStruct((2 * columns, parts, *small.shape), small.dtype),
            jax.ShapeDtypeStruct((parts, *wide.shape), wide.dtype),
        ],
        in_specs=[anywhere] * 4,
        out_specs=[anywhere] * 4,
        scratch_shapes=[
            dma((4,)), dma((2, CHUNKS)), dma((2, parts, CHUNKS)), dma((parts, CHUNKS)),
            dma((parts, CHUNKS)), dma((parts, CHUNKS)),
            dma((parts,)), dma((parts,)), dma((2, columns)), dma((2, columns)), dma((columns,)),
            dma((columns,)), dma((2, parts)), dma((parts,)), dma((2,)), dma((2,)),
        ],
        compiler_params=pltpu.CompilerParams(collective_id=2, has_side_effects=True),
        name="gather",
    )(tokens, wq, small, wide)


def add_over_devices(shape, me, value, column_slots, plane_slots, sems):
    xy, core, zh, zl = me
    mine = (core * 2 + zh) * shape["zl"] + zl
    column_slots[mine] = value
    sent = []
    for step, there, device in column_peers(shape, me):
        copy = send(
            column_slots.at[mine], column_slots.at[mine], sems.at[0, step], sems.at[1, mine], device
        )
        copy.start()
        sent.append(copy)
    for step, there, device in column_peers(shape, me):
        send(
            column_slots.at[there], column_slots.at[there], sems.at[0, step], sems.at[1, there], device
        ).wait_recv()
    for copy in sent:
        copy.wait_send()
    total = column_slots[0]
    for slot in range(1, 4 * shape["zl"]):
        total = total + column_slots[slot]
    plane_slots[xy] = total
    sent = []
    for step, there, device in plane_peers(shape, me):
        copy = send(plane_slots.at[xy], plane_slots.at[xy], sems.at[2, step], sems.at[3, xy], device)
        copy.start()
        sent.append(copy)
    for step, there, device in plane_peers(shape, me):
        send(
            plane_slots.at[there], plane_slots.at[there], sems.at[2, step], sems.at[3, there], device
        ).wait_recv()
    for copy in sent:
        copy.wait_send()
    total = plane_slots[0]
    for slot in range(1, shape["xy"]):
        total = total + plane_slots[slot]
    return total


LANES = 256


def lane_sums(values, ranges):
    lane = lax.broadcasted_iota(jnp.int32, values.shape, 1)
    return [
        jnp.sum(jnp.where((lane >= low) & (lane < high), values, 0.0)) for low, high in ranges
    ]


def small_ranges(n_bias, n_gain):
    ends = [0, n_bias] + [n_bias + n_gain * (n + 1) for n in range(4)]
    return list(zip(ends[:-1], ends[1:]))


def row_of(values):
    lane = lax.broadcasted_iota(jnp.int32, (1, 128), 1)
    row = jnp.zeros((1, 128), F32)
    for n, value in enumerate(values):
        row = jnp.where(lane == n, value, row)
    return row


def sums_kernel(
    shape, n_bias, n_gain,
    grad_qkv_ref, small_ref, wide_ref, wq_ref, wp_ref, wu_ref, wd_ref, ws_ref,
    sum_ref, small_sum_ref, totals_ref,
    plane, both, pieces, small_column, small_plane, row_column, row_plane,
    p_send, p_recv, q_send, q_recv, local_sems, small_sems, row_sems,
):
    me = place()
    xy, core, zh, zl = me
    places, columns = shape["zl"], shape["xy"]
    z = zh * places + zl
    head_block = zl * 2 + core
    depth = both.shape[1] // 2
    greet(shape)

    def plane_part(column):
        return grad_qkv_ref.at[:, pl.ds(pl.multiple_of(column * 2 * depth, 2 * depth), 2 * depth), :]

    keep_part = pltpu.make_async_copy(plane_part(xy), plane.at[xy], local_sems.at[0])
    keep_part.start()
    for step, there, device in plane_peers(shape, me):
        send(plane_part(there), plane.at[xy], p_send.at[step], p_recv.at[xy], device).start()

    def square(values):
        wide = values.astype(F32)
        return jnp.sum(wide * wide)

    up, down, proj = parts_of(wide_ref, wu_ref, wp_ref)
    values = [square(proj), square(up), square(down)]
    values += [square(wq_ref[c]) for c in range(3)]
    values += [square(ref[...]) for ref in (wp_ref, wu_ref, wd_ref)]
    ranges = small_ranges(n_bias, n_gain)
    values += lane_sums(ws_ref[...] * ws_ref[...], ranges)

    keep_part.wait()
    for step, there, device in plane_peers(shape, me):
        send(plane_part(there), plane.at[there], p_send.at[step], p_recv.at[there], device).wait_recv()
    for c in range(3):
        total = plane[0, c].astype(F32)
        for n in range(1, columns):
            total = total + plane[n, c].astype(F32)
        both[c] = total.astype(BF)

    def target(c):
        return (xy, c, lax.div(head_block, places), lax.rem(head_block, places))

    def source(n):
        return (xy, lax.rem(z, 2), n, lax.div(z, 2))

    def part(c):
        return both.at[:, c * depth : (c + 1) * depth, :]

    for c in range(2):

        @pl.when(is_same(target(c), me))
        def _():
            pltpu.make_async_copy(part(c), pieces.at[zh], local_sems.at[1]).start()

        @pl.when(jnp.logical_not(is_same(target(c), me)))
        def _():
            send(part(c), pieces.at[zh], q_send.at[c], q_recv.at[zh], target(c)).start()

    small = add_over_devices(shape, me, small_ref[...], small_column, small_plane, small_sems)
    small_sum_ref[...] = small
    for n in range(2):

        @pl.when(is_same(target(n), me))
        def _():
            pltpu.make_async_copy(part(n), pieces.at[zh], local_sems.at[1]).wait()

        @pl.when(jnp.logical_not(is_same(target(n), me)))
        def _():
            send(part(n), pieces.at[zh], q_send.at[n], q_recv.at[zh], target(n)).wait_send()

        @pl.when(jnp.logical_not(is_same(source(n), me)))
        def _():
            send(part(n), pieces.at[n], q_send.at[n], q_recv.at[n], source(n)).wait_recv()

    squares = []
    for c in range(3):
        total = pieces[0, c].astype(F32) + pieces[1, c].astype(F32)
        sum_ref[c] = total
        squares.append(square(total))
    row = add_over_devices(shape, me, row_of(squares + values), row_column, row_plane, row_sems)
    lane = lax.broadcasted_iota(jnp.int32, (1, 128), 1)
    for n, value in enumerate(lane_sums(small * small, ranges)):
        row = jnp.where(lane == 17 + n, value, row)
    totals_ref[...] = row

    for step, there, device in plane_peers(shape, me):
        send(plane_part(there), plane.at[xy], p_send.at[step], p_recv.at[xy], device).wait_send()


def parts_of(wide_ref, up_like, proj_like):
    ff, heads = up_like.shape[1], proj_like.shape[0]
    return wide_ref[:, :ff], wide_ref[:, ff : 2 * ff], wide_ref[:, 2 * ff : 2 * ff + heads]


def sums(shape, n_bias, n_gain, grad_qkv, small, wide, weights):
    columns = shape["xy"]
    members = 4 * shape["zl"]
    depth = grad_qkv.shape[1] // (2 * columns)
    heads_cols = grad_qkv.shape[2]
    vmem = pl.BlockSpec(memory_space=pltpu.VMEM)
    dma = pltpu.SemaphoreType.DMA
    slots = max(members, columns)
    return pl.pallas_call(
        functools.partial(sums_kernel, shape, n_bias, n_gain),
        out_shape=[
            jax.ShapeDtypeStruct((3, depth, heads_cols), F32),
            jax.ShapeDtypeStruct(small.shape, F32),
            jax.ShapeDtypeStruct((1, 128), F32),
        ],
        in_specs=[pl.BlockSpec(memory_space=pl.ANY)] + [vmem] * 7,
        out_specs=[vmem] * 3,
        scratch_shapes=[
            pltpu.VMEM((columns, 3, 2 * depth, heads_cols), BF),
            pltpu.VMEM((3, 2 * depth, heads_cols), BF),
            pltpu.VMEM((2, 3, depth, heads_cols), BF),
            pltpu.VMEM((members, *small.shape), F32),
            pltpu.VMEM((columns, *small.shape), F32),
            pltpu.VMEM((members, 1, 128), F32),
            pltpu.VMEM((columns, 1, 128), F32),
            dma((columns,)), dma((columns,)), dma((2,)), dma((2,)), dma((2,)),
            dma((4, slots)), dma((4, slots)),
        ],
        compiler_params=pltpu.CompilerParams(
            collective_id=3, has_side_effects=True, vmem_limit_bytes=48 * 2**20
        ),
        name="sums",
    )(grad_qkv, small, wide, *weights)


def reduce_kernel(shape, row_ref, total_ref, row_column, row_plane, row_sems):
    greet(shape)
    total_ref[...] = add_over_devices(shape, place(), row_ref[...], row_column, row_plane, row_sems)


def reduce_row(shape, row):
    members = 4 * shape["zl"]
    vmem = pl.BlockSpec(memory_space=pltpu.VMEM)
    return pl.pallas_call(
        functools.partial(reduce_kernel, shape),
        out_shape=jax.ShapeDtypeStruct((1, 128), F32),
        in_specs=[vmem],
        out_specs=vmem,
        scratch_shapes=[
            pltpu.VMEM((members, 1, 128), F32),
            pltpu.VMEM((shape["xy"], 1, 128), F32),
            pltpu.SemaphoreType.DMA((4, max(members, shape["xy"]))),
        ],
        compiler_params=pltpu.CompilerParams(collective_id=4, has_side_effects=True),
        name="reduce_row",
    )(row)


def moments_kernel(
    n_bias, n_gain, spot_ref, totals_ref, small_ref,
    gq, wide, wq, wp, wu, wd, ws, mq, mp, mu, md, ms, sq, sp, su, sd, ss,
    nmq, nmp, nmu, nmd, nmb, nmg, nmt, nsq, nsp, nsu, nsd, nsb, nsg, nst, uq, up, uu, ud, us, row_ref,
):
    totals = totals_ref[...]
    lane = lax.broadcasted_iota(jnp.int32, (1, 128), 1)
    grads_here = (lane < 6) | ((lane >= 17) & (lane < 22))
    norm = jnp.sqrt(jnp.sum(jnp.where(grads_here, totals, 0.0), axis=1, keepdims=True))
    clip = jnp.minimum(1.0, 1.0 / norm)
    values = []

    def step(grad, weight, mean, square):
        scaled = clip * grad
        new_mean = 0.5 * mean + 0.5 * scaled
        new_square = 0.5 * square + 0.5 * scaled * scaled
        update = new_mean / (jnp.sqrt(new_square) + 1e-06) + 0.01 * weight
        return new_mean, new_square, update

    for c in range(3):
        nmq[c], nsq[c], update = step(gq[c], wq[c], mq[c], sq[c])
        uq[c] = update
        values.append(jnp.sum(update * update))
    grad_up, grad_down, grad_proj = parts_of(wide, wu, wp)
    for turned, g, w, m, s, nm, ns, u in (
        (True, grad_proj, wp, mp, sp, nmp, nsp, up),
        (False, grad_up, wu, mu, su, nmu, nsu, uu),
        (True, grad_down, wd, md, sd, nmd, nsd, ud),
    ):
        grad = g.astype(F32)
        nm[...], ns[...], update = step(grad.T if turned else grad, w[...], m[...], s[...])
        u[...] = update
        values.append(jnp.sum(update * update))
    spot = spot_ref[0]
    grad = small_ref[pl.ds(spot, 1), :]
    new_mean, new_square, update = step(grad, ws[...], ms[...], ss[...])
    us[...] = update
    ranges = small_ranges(n_bias, n_gain)
    values += lane_sums(update * update, ranges)
    row_ref[...] = row_of(values)
    put_small(ranges, new_mean, nmb, nmg, nmt)
    put_small(ranges, new_square, nsb, nsg, nst)


def put_small(ranges, row, bias, gain, shift):
    bias[...] = row[:, ranges[0][0] : ranges[0][1]]
    for n in range(2):
        gain[n : n + 1, :] = row[:, ranges[1 + n][0] : ranges[1 + n][1]]
        shift[n : n + 1, :] = row[:, ranges[3 + n][0] : ranges[3 + n][1]]


def weights_kernel(
    n_bias, n_gain, totals_ref, update_ref, wq, wp, wu, wd, ws, uq, up, uu, ud, us,
    nwq, nwp, nwu, nwd, nwb, nwg, nwt, norms_ref, norm_ref,
):
    totals, updates = totals_ref[...], update_ref[...]
    lane = lax.broadcasted_iota(jnp.int32, (1, 128), 1)
    grads_here = (lane < 6) | ((lane >= 17) & (lane < 22))
    norm_ref[...] = jnp.sqrt(jnp.sum(jnp.where(grads_here, totals, 0.0), axis=1, keepdims=True))
    weight_norm, update_norm = jnp.sqrt(totals), jnp.sqrt(updates)
    norms_ref[0:1, :] = weight_norm[:, 6:17]
    norms_ref[1:2, :] = update_norm[:, 0:11]

    def factor(n):
        return 0.3 * (weight_norm[:, 6 + n : 7 + n] / update_norm[:, n : n + 1])

    for c in range(3):
        nwq[c] = wq[c] - factor(c) * uq[c]
    for n, (w, u, out) in enumerate(((wp, up, nwp), (wu, uu, nwu), (wd, ud, nwd))):
        out[...] = w[...] - factor(3 + n) * u[...]
    ranges = small_ranges(n_bias, n_gain)
    column = lax.broadcasted_iota(jnp.int32, (1, LANES), 1)
    factors = jnp.zeros((1, LANES), F32)
    for n, (low, high) in enumerate(ranges):
        factors = jnp.where((column >= low) & (column < high), factor(6 + n), factors)
    put_small(ranges, ws[...] - factors * us[...], nwb, nwg, nwt)


def shapes_of(arrays):
    return [jax.ShapeDtypeStruct(array.shape, F32) for array in arrays]


def optimizer(shape, n_bias, n_gain, spot, totals, small, grads, weights, means, squares, small_like):
    vmem = pl.BlockSpec(memory_space=pltpu.VMEM)
    big = list(weights[:4])
    results = shapes_of(big) + shapes_of(small_like)
    row = jax.ShapeDtypeStruct((1, 128), F32)
    params = pltpu.CompilerParams(vmem_limit_bytes=48 * 2**20)
    out = pl.pallas_call(
        functools.partial(moments_kernel, n_bias, n_gain),
        out_shape=results * 2 + shapes_of(weights) + [row],
        in_specs=[pl.BlockSpec(memory_space=pltpu.SMEM)] + [vmem] * 19,
        out_specs=[vmem] * 20,
        compiler_params=params,
        name="moments",
    )(spot, totals, small, *grads, *weights, *means, *squares)
    new_means, new_squares, updates, row_here = out[:7], out[7:14], out[14:19], out[19]
    updates_total = reduce_row(shape, row_here)
    out = pl.pallas_call(
        functools.partial(weights_kernel, n_bias, n_gain),
        out_shape=results
        + [jax.ShapeDtypeStruct((2, 11), F32), jax.ShapeDtypeStruct((1, 1), F32)],
        in_specs=[vmem] * 12,
        out_specs=[vmem] * 9,
        compiler_params=params,
        name="weights",
    )(totals, updates_total, *weights, *updates)
    return updates_total, out[8], out[7], out[:7], new_means, new_squares


def turn_own_first(shape, core, src, dst):
    columns = shape["xy"]
    width = src.shape[1]
    depth = width // (2 * columns)
    for start in range(0, width, 128):
        turned = src[:, start : start + 128].T
        for offset in range(0, 128, depth):
            block = (start + offset) // depth
            slot = block // 2 + jnp.where(core == block % 2, 0, columns)
            dst[pl.ds(pl.multiple_of(slot * depth, depth), depth), :] = turned[offset : offset + depth]


def feed_kernel(
    shape, ff_local, x_ref, c_ref, attn_ref, norm_ref, proj_ref, up_ref, down_ref,
    block_ref, middle_ref, given_ref, wide_ref, sums_ref,
    middle, total, second, a_second, a_turned, c_turned, own, other, taken, proj_own, proj_other, proj_taken,
    out_sems, own_sems, swap_send, swap_recv, proj_sems,
):
    me = place()
    xy, core, zh, zl = me
    sibling = (xy, 1 - core, zh, zl)
    step = pl.program_id(0)
    steps = pl.num_programs(0)
    parts = attn_ref.shape[0]
    heads_cols = attn_ref.shape[1]
    half, chunk = own.shape[2], own.shape[3]
    per = ff_local // chunk
    wide = 2 * ff_local + heads_cols
    slot = lax.rem(step, 2)

    def swap(at, index):
        return send(other.at[at], taken.at[index], swap_send.at[index], swap_recv.at[index], sibling)

    def columns(index, which):
        start = lax.div(index, per) * wide + which * ff_local + lax.rem(index, per) * chunk
        return wide_ref.at[:, pl.ds(pl.multiple_of(start, 128), chunk)]

    def keep(at, index, which):
        return pltpu.make_async_copy(own.at[at, which], columns(index, which), own_sems.at[at, which])

    def add_swapped(at, index):
        swap(at, index).wait_recv()
        for which in range(2):
            own[at, which] = (
                own[at, which].astype(F32) + taken[index, which].astype(F32)
            ).astype(BF)
            keep(at, index, which).start()

    def normed():
        values = middle[...]
        center = values - jnp.mean(values, axis=-1, keepdims=True)
        inverse = lax.rsqrt(jnp.mean(center * center, axis=-1, keepdims=True) + 1e-05)
        return center * inverse, inverse

    @pl.when(step == 0)
    def _():
        barrier = pltpu.get_barrier_semaphore()
        pl.semaphore_signal(barrier, inc=1, device_id=sibling, device_id_type=MESH)
        mixed = x_ref[...].astype(F32)
        for part in range(parts):
            mixed = mixed + dot(attn_ref[part].T, proj_ref[part], 1, 1)
        middle[...] = mixed
        value, _ = normed()
        a_second[...] = (value * norm_ref[0:1, :] + norm_ref[1:2, :]).astype(BF)
        turn_own_first(shape, core, a_second, a_turned)
        turn_own_first(shape, core, c_ref, c_turned)
        total[...] = jnp.zeros_like(total)
        second[...] = jnp.zeros_like(second)
        pl.semaphore_wait(barrier, 1)

    @pl.when(step >= 2)
    def _():
        swap(slot, step - 2).wait_send()
        for which in range(2):
            keep(slot, step - 2, which).wait()

    up, down = up_ref[0], down_ref[0]
    pre = dot(a_second[...], up, 1, 0)
    grad_hidden = dot(c_ref[...], down, 1, 0)
    normal = 0.5 * (1.0 + lax.erf(pre * 2.0**-0.5))
    hidden = (pre * normal).astype(BF)
    slope = normal + pre * jnp.exp(-0.5 * pre * pre) * 0.3989422804014327
    grad_pre = (slope * grad_hidden).astype(BF)
    total[...] += dot(hidden, down, 1, 1)
    grad_down = dot(c_turned[...], hidden, 1, 0).astype(BF)
    own[slot, 1] = grad_down[:half]
    other[slot, 1] = grad_down[half:]
    second[...] += dot(grad_pre, up, 1, 1)
    grad_up = dot(a_turned[...], grad_pre, 1, 0).astype(BF)
    own[slot, 0] = grad_up[:half]
    other[slot, 0] = grad_up[half:]
    swap(slot, step).start()

    @pl.when(step >= 1)
    def _():
        add_swapped(1 - slot, step - 1)

    @pl.when(step == steps - 1)
    def _():
        a_second[...] = (middle[...] + total[...]).astype(BF)
        out_block = pltpu.make_async_copy(a_second, block_ref, out_sems.at[0])
        out_block.start()
        value, inverse = normed()
        grad = second[...]
        sums_ref[0:1, :] = jnp.sum(grad * value, axis=0, keepdims=True)
        sums_ref[1:2, :] = jnp.sum(grad, axis=0, keepdims=True)
        inner = grad * norm_ref[0:1, :]
        second[...] = c_ref[...].astype(F32) + inverse * (
            inner
            - jnp.mean(inner, axis=-1, keepdims=True)
            - value * jnp.mean(inner * value, axis=-1, keepdims=True)
        )
        out_middle = pltpu.make_async_copy(second, middle_ref, out_sems.at[1])
        out_middle.start()
        low = second[...].astype(BF)
        turn_own_first(shape, core, low, a_turned)
        for part in range(parts):
            grad_proj = dot(a_turned[...], attn_ref[part], 1, 1).astype(BF)
            proj_own[part] = grad_proj[:half]
            proj_other[part] = grad_proj[half:]
        swap_proj = send(proj_other, proj_taken, proj_sems.at[0], proj_sems.at[1], sibling)
        swap_proj.start()
        for part in range(parts):
            rows = pl.ds(part * heads_cols, heads_cols)
            c_turned[rows, :] = dot(low, proj_ref[part], 1, 0).T.astype(BF)
        out_given = pltpu.make_async_copy(c_turned, given_ref, out_sems.at[2])
        out_given.start()
        add_swapped(slot, step)
        swap_proj.wait_recv()
        kept = []
        for part in range(parts):
            proj_own[part] = (proj_own[part].astype(F32) + proj_taken[part].astype(F32)).astype(BF)
            there = wide_ref.at[:, pl.ds(part * wide + 2 * ff_local, heads_cols)]
            kept.append(pltpu.make_async_copy(proj_own.at[part], there, out_sems.at[3 + part]))
            kept[-1].start()

        @pl.when(step >= 1)
        def _():
            swap(1 - slot, step - 1).wait_send()
            for which in range(2):
                keep(1 - slot, step - 1, which).wait()

        swap(slot, step).wait_send()
        for which in range(2):
            keep(slot, step, which).wait()
        swap_proj.wait_send()
        for copy in (out_block, out_middle, out_given, *kept):
            copy.wait()


def feed_forward(shape, tokens, cotangent, attn_rows, norm, shared, ff_local):
    rows, width = tokens.shape
    parts, heads_cols = attn_rows.shape[:2]
    chunk = min(512, ff_local)
    per = ff_local // chunk
    steps = parts * per
    half = width // 2
    anywhere = pl.BlockSpec(memory_space=pl.ANY)

    def once(block, *index):
        return pl.BlockSpec(block, lambda s: index, pipeline_mode=pl.Buffered(1))

    dma = pltpu.SemaphoreType.DMA
    return pl.pallas_call(
        functools.partial(feed_kernel, shape, ff_local),
        grid=(steps,),
        in_specs=[
            once((rows, width), 0, 0),
            once((rows, width), 0, 0),
            once((parts, heads_cols, rows), 0, 0, 0),
            once((2, width), 0, 0),
            once((parts, width, heads_cols), 0, 0, 2 * ff_local // heads_cols),
            pl.BlockSpec((1, width, chunk), lambda s: (s // per, 0, s % per)),
            pl.BlockSpec((1, width, chunk), lambda s: (s // per, 0, per + s % per)),
        ],
        out_specs=[anywhere] * 4 + [pl.BlockSpec((2, width), lambda s: (0, 0))],
        out_shape=[
            jax.ShapeDtypeStruct((rows, width), BF),
            jax.ShapeDtypeStruct((rows, width), F32),
            jax.ShapeDtypeStruct((parts * heads_cols, rows), BF),
            jax.ShapeDtypeStruct((half, parts * (2 * ff_local + heads_cols)), BF),
            jax.ShapeDtypeStruct((2, width), F32),
        ],
        scratch_shapes=[
            pltpu.VMEM((rows, width), F32),
            pltpu.VMEM((rows, width), F32),
            pltpu.VMEM((rows, width), F32),
            pltpu.VMEM((rows, width), BF),
            pltpu.VMEM((width, rows), BF),
            pltpu.VMEM((width, rows), BF),
            pltpu.VMEM((2, 2, half, chunk), BF),
            pltpu.VMEM((2, 2, half, chunk), BF),
            pltpu.VMEM((steps, 2, half, chunk), BF),
            pltpu.VMEM((parts, half, heads_cols), BF),
            pltpu.VMEM((parts, half, heads_cols), BF),
            pltpu.VMEM((parts, half, heads_cols), BF),
            dma((3 + parts,)),
            dma((2, 2)),
            dma((steps,)),
            dma((steps,)),
            dma((2,)),
        ],
        compiler_params=pltpu.CompilerParams(
            vmem_limit_bytes=60 * 2**20, collective_id=5, has_side_effects=True
        ),
        name="feed_forward",
    )(tokens, cotangent, attn_rows, norm, shared, shared, shared)


def norm_parts(values):
    center = values - jnp.mean(values, axis=-1, keepdims=True)
    inverse = lax.rsqrt(jnp.mean(center * center, axis=-1, keepdims=True) + 1e-05)
    return center * inverse, inverse


def norm_back(normed, inverse, gain, grad):
    inner = grad * gain
    return inverse * (
        inner
        - jnp.mean(inner, axis=-1, keepdims=True)
        - normed * jnp.mean(inner * normed, axis=-1, keepdims=True)
    )


def per_device(
    shape,
    tokens, cotangent, item_len, bucket_table,
    w_qkv, w_proj, w_up, w_down, rel_bias, ln_gain, ln_shift,
    mean_qkv, mean_proj, mean_up, mean_down, mean_bias, mean_gain, mean_shift,
    square_qkv, square_proj, square_up, square_down, square_bias, square_gain, square_shift,
):
    columns, places = shape["xy"], shape["zl"]
    parts = 2 * places
    devices = columns * 2 * parts
    rows, width = tokens.shape
    heads = w_qkv.shape[2] // DH
    tok = rows * parts
    xy, core, zh, zl = place()
    me = ((xy * 2 + core) * 2 + zh) * places + zl
    head_block = zl * 2 + core

    ff_local, heads_cols = w_up.shape[1], w_proj.shape[0]
    local = jnp.concatenate([w_up, w_down.T, w_proj.T], axis=1).astype(BF)

    n_bias, n_gain = rel_bias.shape[0], ln_gain.shape[1]
    n_small = n_bias + 4 * n_gain

    def pack(bias, gain, shift):
        row = jnp.concatenate([bias, gain.reshape(-1), shift.reshape(-1)])
        return jnp.pad(row, (0, LANES - n_small))[None, :]

    small_weights = pack(rel_bias, ln_gain, ln_shift)
    group_rows, w_heads, small, wide = gather(
        shape, tokens, w_qkv.astype(BF), small_weights, local
    )
    shared = lax.all_gather(wide, DP, axis=1, tiled=True)
    small = small.reshape(devices, LANES)

    def columns_of(start):
        part = small[:, start : start + 2 * n_gain].reshape(devices, 2, n_gain)
        return part.transpose(1, 0, 2).reshape(2, width)

    table_flat = small[:, :n_bias].reshape(-1)
    gains, shifts = columns_of(n_bias), columns_of(n_bias + 2 * n_gain)
    other_len = lax.ppermute(item_len, "core", [(0, 1), (1, 0)])
    split = jnp.where(zh == core, item_len, other_len)[0, 0:1]

    normed_all, _ = norm_parts(group_rows.reshape(tok, width).astype(F32))
    a_first = (normed_all * gains[0] + shifts[0]).astype(BF)
    qkv = lax.dot_general(
        w_heads, a_first, (((1,), (1,)), ((), ())), preferred_element_type=F32
    ).astype(BF).reshape(3 * heads * DH, tok)

    table = lax.dynamic_slice_in_dim(
        table_flat.reshape(BUCKETS, H), head_block * heads, heads, 1
    )
    one_hot = (jnp.arange(BUCKETS)[:, None] == bucket_table[None, :]).astype(F32)
    dist_bias = lax.dot_general(
        table, one_hot, (((0,), (0,)), ((), ())), precision=HIGHEST, preferred_element_type=F32
    )
    pattern = jnp.concatenate(
        [dist_bias * LOG2E, jnp.full((heads, BLK), NEG, F32)], axis=1
    )[:, None, :]
    out, attn_rows, lse = attend(shape, qkv, pattern, split, heads)

    attn_rows = attn_rows.reshape(parts, heads * DH, rows)
    x_rows = tokens.astype(F32)
    norm_two = jnp.stack([gains[1], shifts[1]])
    block_out, grad_middle, grad_attn, wide_grad, sums_two = feed_forward(
        shape, tokens, cotangent, attn_rows, norm_two, shared, ff_local
    )
    gain_two, shift_two = sums_two[0], sums_two[1]
    given = grad_attn.reshape(parts, heads, DH, rows)
    early = heads - 1
    heads_early, pattern_early = attend_back(
        shape, qkv, out, given, lse, pattern, split, heads, 0, early, 1
    )
    heads_late, pattern_late = attend_back(
        shape, qkv, out, given, lse, pattern, split, heads, early, heads - early, 6
    )
    grad_pattern = jnp.concatenate([pattern_early, pattern_late])
    grad_heads = jnp.concatenate([heads_early, heads_late], axis=1).reshape(3, heads * DH, tok)

    half = width // 2

    def first_half(which):
        here = lax.dynamic_slice_in_dim(w_heads, which * half, half, 1)
        return lax.dot_general(
            grad_heads, here, (((0, 1), (0, 2)), ((), ())), preferred_element_type=F32
        )

    other_half = lax.ppermute(first_half(1 - core).astype(BF), "core", [(0, 1), (1, 0)])
    half_sum = (first_half(core) + other_half.astype(F32)).astype(BF)
    arrived = []
    for turn in range(parts):
        route = [
            (((c * 2 + b % 2) * 2 + g) * places + b // 2, (c * 2 + g) * parts + (b + turn) % parts)
            for c in range(columns)
            for g in range(2)
            for b in range(parts)
        ]
        shard = lax.rem(head_block + turn, parts)
        piece = lax.dynamic_slice_in_dim(half_sum, shard * rows, rows, 0)
        arrived.append(lax.ppermute(piece, ALL, route))

    grad_qkv = jnp.einsum("td,cet->cde", a_first, grad_heads, preferred_element_type=F32)
    head_sums = jnp.sum(grad_heads.astype(F32), axis=2)
    wide_heads = w_heads.astype(F32)
    shift_one = jnp.sum(wide_heads * head_sums[:, None, :], axis=(0, 2))
    gain_one = (
        jnp.sum(wide_heads * grad_qkv, axis=(0, 2)) - shifts[0] * shift_one
    ) / gains[0]
    grad_qkv = grad_qkv.astype(BF)

    part = lax.psum_scatter(wide_grad, "xy", scatter_dimension=0, tiled=True)
    part, heads_early = lax.optimization_barrier((part, heads_early))
    wide_sum = lax.psum_scatter(part, TENSOR, scatter_dimension=1, tiled=True)
    bias_grad = lax.dot_general(
        one_hot, grad_pattern[:, 0, :tok], (((1,), (1,)), ((), ())),
        precision=HIGHEST, preferred_element_type=F32,
    )
    table_grad = lax.dynamic_update_slice(
        jnp.zeros((BUCKETS, H), F32), bias_grad, (0, head_block * heads)
    )

    def by_device(*vectors):
        return jnp.stack(vectors).reshape(2, devices, n_gain).transpose(1, 0, 2).reshape(devices, -1)

    small_grad = jnp.concatenate(
        [
            table_grad.reshape(devices, n_bias),
            by_device(gain_one, gain_two),
            by_device(shift_one, shift_two),
            jnp.zeros((devices, LANES - n_small), F32),
        ],
        axis=1,
    )
    weights = (w_qkv, w_proj, w_up, w_down, small_weights)
    sum_qkv, small_sum, totals = sums(
        shape, n_bias, n_gain, grad_qkv, small_grad, wide_sum, weights
    )
    small_like = [rel_bias[None, :], ln_gain, ln_shift]
    updates_total, grad_norm, param_norms, *results = optimizer(
        shape, n_bias, n_gain, me[None].astype(jnp.int32), totals, small_sum,
        (sum_qkv, wide_sum), weights,
        (mean_qkv, mean_proj, mean_up, mean_down, pack(mean_bias, mean_gain, mean_shift)),
        (square_qkv, square_proj, square_up, square_down, pack(square_bias, square_gain, square_shift)),
        small_like,
    )
    arrived, _ = lax.optimization_barrier((arrived, updates_total))
    rounds = [sum(piece.astype(F32) for piece in arrived[n::2]) for n in range(2)]
    even = lax.rem(zh * places + zl, 2) == 0
    first_rows = jnp.concatenate(
        [jnp.where(even, rounds[0], rounds[1]), jnp.where(even, rounds[1], rounds[0])], axis=1
    )
    normed_one, inverse_one = norm_parts(x_rows)
    grad_tokens = (
        grad_middle + norm_back(normed_one, inverse_one, gains[0], first_rows)
    ).astype(BF)
    new = [array if n % 7 != 4 else array[0] for group in results for n, array in enumerate(group)]
    return (block_out, grad_tokens, grad_norm[0, 0], param_norms, *new)


def solution(mesh):
    shape = {"xy": mesh.shape["dp"] // 2, "core": 2, "zh": 2, "zl": mesh.shape["tensor"] // 2}
    split_mesh = Mesh(mesh.devices.reshape(tuple(shape[axis] for axis in ALL)), ALL)
    weights = (
        P(None, DP, TENSOR),
        P(TENSOR, DP),
        P(DP, TENSOR),
        P(TENSOR, DP),
        P(ALL),
        P(None, ALL),
        P(None, ALL),
    )
    rows = P(ALL, None)
    return jax.shard_map(
        functools.partial(per_device, shape),
        mesh=split_mesh,
        in_specs=(rows, rows, P(DP, None), P(), *weights, *weights, *weights),
        out_specs=(rows, rows, P(), P(), *weights, *weights, *weights),
        check_vma=False,
    )
```

```python
import functools
import math

import jax
import jax.numpy as jnp
from jax import lax
from jax.experimental import pallas as pl
from jax.experimental.pallas import tpu as pltpu
from jax.sharding import Mesh
from jax.sharding import PartitionSpec as P

H = 16
DH = 64
BUCKETS = 32
BLK = 512
NEG = -1e30
LOG2E = 1.4426950408889634
F32 = jnp.float32
BF = jnp.bfloat16
MESH = pl.DeviceIdType.MESH
HIGHEST = lax.Precision.HIGHEST
ALL = ("xy", "core", "zh", "zl")
DP = ("xy", "core")
TENSOR = ("zh", "zl")


def dot(left, right, left_dim, right_dim):
    return lax.dot_general(
        left, right, (((left_dim,), (right_dim,)), ((), ())), preferred_element_type=F32
    )


def project_kernel(x_ref, norm_ref, w_ref, a_ref, qkv_ref, turned):
    @pl.when(pl.program_id(0) == 0)
    def _():
        for c in range(3):
            turned[c] = w_ref[c].T

    values = x_ref[...].astype(F32)
    center = values - jnp.mean(values, axis=-1, keepdims=True)
    inverse = lax.rsqrt(jnp.mean(center * center, axis=-1, keepdims=True) + 1e-05)
    a_ref[...] = (center * inverse * norm_ref[0:1, :] + norm_ref[1:2, :]).astype(BF)
    for c in range(3):
        qkv_ref[c] = dot(turned[c], a_ref[...], 1, 1).astype(BF)


def project(rows, norm, weights):
    tok, width = rows.shape
    cols = weights.shape[2]
    return pl.pallas_call(
        project_kernel,
        grid=(tok // BLK,),
        in_specs=[
            pl.BlockSpec((BLK, width), lambda s: (s, 0)),
            pl.BlockSpec((2, width), lambda s: (0, 0)),
            pl.BlockSpec((3, width, cols), lambda s: (0, 0, 0)),
        ],
        out_specs=[
            pl.BlockSpec((BLK, width), lambda s: (s, 0)),
            pl.BlockSpec((3, cols, BLK), lambda s: (0, 0, s)),
        ],
        out_shape=[
            jax.ShapeDtypeStruct((tok, width), BF),
            jax.ShapeDtypeStruct((3, cols, tok), BF),
        ],
        scratch_shapes=[pltpu.VMEM((3, cols, width), BF)],
        compiler_params=pltpu.CompilerParams(vmem_limit_bytes=40 * 2**20),
        name="project",
    )(rows, norm, weights)


def make_slab(pattern, slab):
    width = slab.shape[1]
    slab[0:8, :] = pltpu.roll(jnp.broadcast_to(pattern, (8, width)), 0, 1, stride=1, stride_axis=0)
    done = 8
    while done < slab.shape[0]:
        slab[done : 2 * done, :] = pltpu.roll(slab[0:done, :], done, 1)
        done *= 2


def fold_slab(slab):
    width = slab.shape[1]
    half = slab.shape[0] // 2
    while half >= 8:
        slab[0:half, :] = slab[0:half, :] + pltpu.roll(slab[half : 2 * half, :], width - half, 1)
        half //= 2
    total = slab[0:1, :]
    for row in range(1, 8):
        total = total + pltpu.roll(slab[row : row + 1, :], width - row, 1)
    return total


def split_three(values):
    high = values.astype(BF).astype(F32)
    rest = values - high
    middle = rest.astype(BF).astype(F32)
    return high, middle, (rest - middle).astype(BF).astype(F32)


def put_queries(queries, split, minus, tok, dst):
    scaled = queries.astype(F32) * (DH**-0.5 * LOG2E)
    high = scaled.astype(BF)
    dst[0:DH, :] = high
    dst[DH : 2 * DH, :] = (scaled - high.astype(F32)).astype(BF)
    position = lax.broadcasted_iota(jnp.int32, (16, tok), 1)
    row = lax.broadcasted_iota(jnp.int32, (16, tok), 0)
    extra = jnp.where((row == 0) & (position >= split), 1.0, 0.0)
    if minus is not None:
        first, second, third = split_three(minus)
        extra = jnp.where(
            row == 1, first, jnp.where(row == 2, second, jnp.where(row == 3, third, extra))
        )
    dst[2 * DH : 2 * DH + 16, :] = extra.astype(BF)


def put_keys(keys, split, tok, dst):
    for start in range(0, tok, BLK):
        position = start + lax.broadcasted_iota(jnp.int32, (16, BLK), 1)
        row = lax.broadcasted_iota(jnp.int32, (16, BLK), 0)
        extra = jnp.where(
            row == 0, jnp.where(position < split, NEG, 0.0), jnp.where(row < 4, 1.0, 0.0)
        )
        block = keys[:, start : start + BLK].astype(F32)
        whole = jnp.concatenate([block, block, extra], axis=0)
        dst[start : start + BLK, :] = whole.T.astype(BF)


def block_at(index):
    return pl.ds(pl.multiple_of(index * BLK, BLK), BLK)


def attend_kernel(
    shape, split_ref, pattern_ref, q_ref, k_ref, v_ref, out_ref, rows_ref, lse_ref,
    slab, kx, qx, outs, local_sem, send_sem, recv_sem,
):
    head = pl.program_id(0)
    tok = q_ref.shape[1]
    split = split_ref[0]
    trade = Trade(shape, tok)

    @pl.when(head == 0)
    def _():
        greet_column(shape)

    make_slab(pattern_ref[0], slab)
    put_queries(q_ref[...], split, None, tok, qx)
    put_keys(k_ref, split, tok, kx)

    def step(i, j, top, total, out):
        scores = dot(kx[block_at(j), :], qx[:, block_at(i)], 1, 0) + slab[:, block_at(i - j)]
        new_top = jnp.maximum(top, jnp.max(scores, axis=0, keepdims=True))
        weights = jnp.exp2(scores - new_top)
        scale = jnp.exp2(top - new_top)
        total = total * scale + jnp.sum(weights, axis=0, keepdims=True)
        out = out * scale + dot(v_ref[:, block_at(j)], weights.astype(BF), 1, 0)
        return new_top, total, out

    def row(i, carry):
        start = (
            jnp.full((1, BLK), NEG, F32),
            jnp.zeros((1, BLK), F32),
            jnp.zeros((DH, BLK), F32),
        )
        top, total, out = lax.fori_loop(0, i + 1, lambda t, c: step(i, i - t, *c), start)
        outs[head, :, block_at(i)] = (out / total).astype(BF)
        lse_ref[0, :, block_at(i)] = top + jnp.log2(total)
        return carry

    lax.fori_loop(0, tok // BLK, row, 0)

    def keep(h):
        return pltpu.make_async_copy(outs.at[h], out_ref.at[h], local_sem.at[0, h])

    def piece(h, n):
        return outs.at[h, :, pl.ds(pl.multiple_of(n * trade.rows, trade.rows), trade.rows)]

    def slot(h, n):
        return rows_ref.at[n, h]

    keep(head).start()
    trade.give(head, piece, slot, trade.owner, trade.head, local_sem.at[1, head], send_sem, recv_sem)

    @pl.when(head == pl.num_programs(0) - 1)
    def _():
        for h in range(rows_ref.shape[1]):
            keep(h).wait()
            trade.given(h, piece, slot, trade.owner, trade.head, local_sem.at[1, h], send_sem, recv_sem)
            trade.take(h, piece, slot, trade.header, send_sem, recv_sem)


def attend(shape, qkv, pattern, split, heads):
    tok = qkv.shape[1]
    width = pattern.shape[-1]
    parts = shape["zh"] * shape["zl"]
    dma = pltpu.SemaphoreType.DMA
    return pl.pallas_call(
        functools.partial(attend_kernel, shape),
        grid=(heads,),
        in_specs=[
            pl.BlockSpec(memory_space=pltpu.SMEM),
            pl.BlockSpec((1, 1, width), lambda h: (h, 0, 0)),
            pl.BlockSpec((DH, tok), lambda h: (h, 0)),
            pl.BlockSpec((DH, tok), lambda h: (h + heads, 0)),
            pl.BlockSpec((DH, tok), lambda h: (h + 2 * heads, 0)),
        ],
        out_specs=[
            pl.BlockSpec(memory_space=pl.ANY),
            pl.BlockSpec(memory_space=pl.ANY),
            pl.BlockSpec((1, 1, tok), lambda h: (h, 0, 0)),
        ],
        out_shape=[
            jax.ShapeDtypeStruct((heads, DH, tok), BF),
            jax.ShapeDtypeStruct((parts, heads, DH, tok // parts), BF),
            jax.ShapeDtypeStruct((heads, 1, tok), F32),
        ],
        scratch_shapes=[
            pltpu.VMEM((BLK, width), F32),
            pltpu.VMEM((tok, 2 * DH + 16), BF),
            pltpu.VMEM((2 * DH + 16, tok), BF),
            pltpu.VMEM((heads, DH, tok), BF),
            dma((2, heads)),
            dma((heads, parts)),
            dma((heads, parts)),
        ],
        compiler_params=pltpu.CompilerParams(
            vmem_limit_bytes=56 * 2**20, collective_id=0, has_side_effects=True
        ),
        name="attend",
    )(split, pattern, qkv, qkv, qkv)


def attend_back_kernel(
    shape, segments, split_ref, pattern_ref, q_ref, k_ref, v_ref, o_ref, lse_ref, given_ref, wide_ref,
    grads_ref, wide_parts_ref, dpattern_ref,
    slab, dslab, kx, qx, vx, dox, qn, don, dk, dv, taken, wide_own, wide_in,
    local_sem, in_send, in_recv, wide_sem, z_send, z_recv, w_send, w_recv,
):
    head = pl.program_id(0)
    tok = q_ref.shape[1]
    split = split_ref[0]
    trade = Trade(shape, tok)
    heads = taken.shape[0]

    def in_piece(h, n):
        return given_ref.at[n, h]

    def in_slot(h, n):
        return taken.at[h, :, pl.ds(pl.multiple_of(n * trade.rows, trade.rows), trade.rows)]

    xy, core, zh, zl = trade.me
    side = math.isqrt(shape["xy"])

    def column_copies():
        at = (lax.div(xy, side), lax.rem(xy, side))
        for step in range(1, side):
            for n, (start, size, axis) in enumerate(segments):
                there = lax.rem(at[axis] + step, side)
                column = there * side + at[1] if axis == 0 else at[0] * side + there
                here = pl.ds(start, size)
                yield send(
                    wide_ref.at[step, :, here], wide_in.at[step - 1, :, here],
                    w_send.at[step - 1, n], w_recv.at[step - 1, n], (column, core, zh, zl),
                )

    bring = pltpu.make_async_copy(wide_ref.at[0], wide_own, wide_sem.at[1])

    @pl.when(head == 0)
    def _():
        greet(shape)
        bring.start()
        for copy in column_copies():
            copy.start()
        for h in range(heads):
            trade.give(
                h, in_piece, in_slot, trade.header, trade.row, local_sem.at[h], in_send, in_recv
            )

    size = wide_parts_ref.shape[2]

    def wide_part(n):
        return wide_own.at[:, pl.ds(pl.multiple_of(n * size, size), size)]

    def along_z(step):
        there = lax.rem(trade.row + step, trade.parts)
        return there, (
            trade.me[0], trade.me[1], lax.div(there, trade.places), lax.rem(there, trade.places),
        )

    def wide_copy(step):
        there, device = along_z(step)
        return send(
            wide_part(there), wide_parts_ref.at[trade.row], z_send.at[step], z_recv.at[trade.row], device
        )

    keep_wide = pltpu.make_async_copy(
        wide_part(trade.row), wide_parts_ref.at[trade.row], wide_sem.at[0]
    )

    @pl.when(head == min(1, heads - 1))
    def _():
        bring.wait()
        for copy in column_copies():
            copy.wait_recv()
            copy.wait_send()
        for n in range(trade.parts):
            here = slice(n * size, (n + 1) * size)
            total = wide_own[:, here].astype(F32)
            for step in range(side - 1):
                total = total + wide_in[step, :, here].astype(F32)
            wide_own[:, here] = total.astype(BF)
        keep_wide.start()
        for step in range(1, trade.parts):
            wide_copy(step).start()

    make_slab(pattern_ref[0], slab)
    put_queries(q_ref[...], split, -lse_ref[0], tok, qx)
    put_keys(k_ref, split, tok, kx)
    dslab[...] = jnp.zeros_like(dslab)
    dk[...] = jnp.zeros_like(dk)
    dv[...] = jnp.zeros_like(dv)
    row = lax.broadcasted_iota(jnp.int32, (16, BLK), 0)
    ones = jnp.where(row < 3, 1.0, 0.0)
    trade.given(
        head, in_piece, in_slot, trade.header, trade.row, local_sem.at[head], in_send, in_recv
    )
    trade.take(head, in_piece, in_slot, trade.owner, in_send, in_recv)
    for start in range(0, tok, BLK):
        here = slice(start, start + BLK)
        low_grad = taken[head, :, here]
        grad = low_grad.astype(F32)
        inner = jnp.sum(grad * o_ref[0, :, here].astype(F32), axis=0, keepdims=True)
        first, second, third = split_three(-inner)
        extra = jnp.where(
            row == 0, first, jnp.where(row == 1, second, jnp.where(row == 2, third, 0.0))
        )
        dox[0:DH, here] = low_grad
        dox[DH : DH + 16, here] = extra.astype(BF)
        vx[here, :] = jnp.concatenate([v_ref[:, here].astype(F32), ones], axis=0).T.astype(BF)
        both = jnp.concatenate([q_ref[:, here].astype(F32), grad], axis=0).T
        qn[here, :] = both[:, 0:DH].astype(BF)
        don[here, :] = both[:, DH : 2 * DH].astype(BF)

    def tile(i, j):
        qs, ks, diagonal = block_at(i), block_at(j), block_at(i - j)
        shares = jnp.exp2(dot(kx[ks, :], qx[:, qs], 1, 0) + slab[:, diagonal])
        grad_scores = shares * dot(vx[ks, :], dox[:, qs], 1, 0)
        dslab[:, diagonal] += grad_scores
        low = grad_scores.astype(BF)
        dv[ks, :] += dot(shares.astype(BF), don[qs, :], 1, 0)
        dk[ks, :] += dot(low, qn[qs, :], 1, 0)
        return dot(k_ref[:, ks], low, 1, 0)

    def query_row(i, carry):
        total = lax.fori_loop(
            0, i + 1, lambda t, c: c + tile(i, i - t), jnp.zeros((DH, BLK), F32)
        )
        grads_ref[0, 0, :, block_at(i)] = (total * DH**-0.5).astype(BF)
        return carry

    lax.fori_loop(0, tok // BLK, query_row, 0)
    for start in range(0, tok, BLK):
        here = slice(start, start + BLK)
        grads_ref[1, 0, :, here] = (dk[here, :] * DH**-0.5).T.astype(BF)
        grads_ref[2, 0, :, here] = dv[here, :].T.astype(BF)
    dpattern_ref[0] = fold_slab(dslab)

    @pl.when(head == heads - 1)
    def _():
        keep_wide.wait()
        for step in range(1, trade.parts):
            there, device = along_z(step)
            here = wide_parts_ref.at[there]
            wide_copy(step).wait_send()
            send(here, here, z_send.at[step], z_recv.at[there], device).wait_recv()


def attend_back(shape, segments, qkv, out, given, wide, lse, pattern, split, heads):
    tok = qkv.shape[1]
    width = pattern.shape[-1]
    parts = shape["zh"] * shape["zl"]
    anywhere = pl.BlockSpec(memory_space=pl.ANY)
    dma = pltpu.SemaphoreType.DMA
    return pl.pallas_call(
        functools.partial(attend_back_kernel, shape, segments),
        grid=(heads,),
        in_specs=[
            pl.BlockSpec(memory_space=pltpu.SMEM),
            pl.BlockSpec((1, 1, width), lambda h: (h, 0, 0)),
            pl.BlockSpec((DH, tok), lambda h: (h, 0)),
            pl.BlockSpec((DH, tok), lambda h: (h + heads, 0)),
            pl.BlockSpec((DH, tok), lambda h: (h + 2 * heads, 0)),
            pl.BlockSpec((1, DH, tok), lambda h: (h, 0, 0)),
            pl.BlockSpec((1, 1, tok), lambda h: (h, 0, 0)),
            anywhere,
            anywhere,
        ],
        out_specs=[
            pl.BlockSpec((3, 1, DH, tok), lambda h: (0, h, 0, 0)),
            anywhere,
            pl.BlockSpec((1, 1, width), lambda h: (h, 0, 0)),
        ],
        out_shape=[
            jax.ShapeDtypeStruct((3, heads, DH, tok), BF),
            jax.ShapeDtypeStruct((parts, wide.shape[1], wide.shape[2] // parts), BF),
            jax.ShapeDtypeStruct((heads, 1, width), F32),
        ],
        scratch_shapes=[
            pltpu.VMEM((BLK, width), F32),
            pltpu.VMEM((BLK, width), F32),
            pltpu.VMEM((tok, 2 * DH + 16), BF),
            pltpu.VMEM((2 * DH + 16, tok), BF),
            pltpu.VMEM((tok, DH + 16), BF),
            pltpu.VMEM((DH + 16, tok), BF),
            pltpu.VMEM((tok, DH), BF),
            pltpu.VMEM((tok, DH), BF),
            pltpu.VMEM((tok, DH), F32),
            pltpu.VMEM((tok, DH), F32),
            pltpu.VMEM((heads, DH, tok), BF),
            pltpu.VMEM(wide.shape[1:], BF),
            pltpu.VMEM((wide.shape[0] - 1, *wide.shape[1:]), BF),
            dma((heads,)),
            dma((heads, parts)),
            dma((heads, parts)),
            dma((2,)), dma((parts,)), dma((parts,)),
            *[dma((wide.shape[0] - 1, len(segments)))] * 2,
        ],
        compiler_params=pltpu.CompilerParams(
            vmem_limit_bytes=60 * 2**20, collective_id=1, has_side_effects=True
        ),
        name="attend_back",
    )(split, pattern, qkv, qkv, qkv, out, lse, given, wide)


def place():
    return tuple(lax.axis_index(axis) for axis in ALL)


class Trade:
    def __init__(self, shape, tok):
        self.places = shape["zl"]
        self.parts = shape["zh"] * self.places
        self.rows = tok // self.parts
        self.me = place()
        _, core, zh, zl = self.me
        self.row = zh * self.places + zl
        self.head = zl * 2 + core

    def owner(self, n):
        return (self.me[0], self.me[2], lax.div(n, self.places), lax.rem(n, self.places))

    def header(self, n):
        return (self.me[0], lax.rem(n, 2), self.me[1], lax.div(n, 2))

    def each(self, device_of, local, remote):
        for index in range(self.parts):
            n = jnp.where(self.me[2] == 1, index, self.parts - 1 - index)
            device = device_of(n)
            if local is not None:

                @pl.when(is_same(device, self.me))
                def _():
                    local(n)

            @pl.when(jnp.logical_not(is_same(device, self.me)))
            def _():
                remote(n, device)

    def give(self, h, piece, slot, device_of, mine, local_sem, send_sem, recv_sem):
        def local(n):
            pltpu.make_async_copy(piece(h, n), slot(h, mine), local_sem).start()

        def remote(n, device):
            send(piece(h, n), slot(h, mine), send_sem.at[h, n], recv_sem.at[h, mine], device).start()

        self.each(device_of, local, remote)

    def given(self, h, piece, slot, device_of, mine, local_sem, send_sem, recv_sem):
        def local(n):
            pltpu.make_async_copy(piece(h, n), slot(h, mine), local_sem).wait()

        def remote(n, device):
            send(piece(h, n), slot(h, mine), send_sem.at[h, n], recv_sem.at[h, mine], device).wait_send()

        self.each(device_of, local, remote)

    def take(self, h, piece, slot, device_of, send_sem, recv_sem):
        def remote(n, device):
            send(piece(h, n), slot(h, n), send_sem.at[h, n], recv_sem.at[h, n], device).wait_recv()

        self.each(device_of, None, remote)


def is_same(left, right):
    same = left[0] == right[0]
    for one, other in zip(left[1:], right[1:]):
        same = same & (one == other)
    return same


def column_peers(shape, device):
    xy, core, zh, zl = device
    places = shape["zl"]
    total = 4 * places
    mine = (core * 2 + zh) * places + zl
    for step in range(1, total):
        there = lax.rem(mine + step, total)
        yield step, there, (xy, there // (2 * places), lax.rem(there // places, 2), lax.rem(there, places))


def plane_peers(shape, device):
    xy, core, zh, zl = device
    for step in range(1, shape["xy"]):
        there = lax.rem(xy + step, shape["xy"])
        yield step, there, (there, core, zh, zl)


def greet(shape):
    device = place()
    barrier = pltpu.get_barrier_semaphore()
    peers = [peer for _, _, peer in column_peers(shape, device)]
    peers += [peer for _, _, peer in plane_peers(shape, device)]
    for peer in peers:
        pl.semaphore_signal(barrier, inc=1, device_id=peer, device_id_type=MESH)
    pl.semaphore_wait(barrier, len(peers))


def greet_column(shape):
    barrier = pltpu.get_barrier_semaphore()
    peers = [peer for _, _, peer in column_peers(shape, place())]
    for peer in peers:
        pl.semaphore_signal(barrier, inc=1, device_id=peer, device_id_type=MESH)
    pl.semaphore_wait(barrier, len(peers))


def send(src, dst, send_sem, recv_sem, device):
    return pltpu.make_async_remote_copy(
        src_ref=src, dst_ref=dst, send_sem=send_sem, recv_sem=recv_sem,
        device_id=device, device_id_type=MESH,
    )


CHUNKS = 4


def gather_kernel(
    shape, tokens_ref, wq_ref, small_ref, wide_ref, rows_ref, heads_ref, all_small_ref, all_wide_ref,
    local_sems, in_send, fwd_send, share_send, x_recv, xs_recv,
    z_send, z_recv, p_send, p_recv, s_send, s_recv, w_send, w_recv, q_send, q_recv,
):
    me = place()
    xy, core, zh, zl = me
    places = shape["zl"]
    parts = 2 * places
    columns = shape["xy"]
    z = zh * places + zl
    sibling = (xy, 1 - core, zh, zl)
    size = tokens_ref.shape[0] // (2 * CHUNKS)
    dp = xy * 2 + core
    inside = core == zh
    outside = jnp.logical_not(inside)
    entry = jnp.where(zh < core, 0, places - 1)

    def chunk_of(ref, half, chunk):
        return ref.at[pl.ds(pl.multiple_of((half * CHUNKS + chunk) * size, size), size), :]

    def beside(step):
        there = z + step
        return (xy, core, there // places, lax.rem(there, places))

    greet(shape)

    depth = wq_ref.shape[1]
    head_block = zl * 2 + core

    def depth_of(index, count):
        return heads_ref.at[:, pl.ds(pl.multiple_of(index * depth, depth), count * depth), :]

    def wq_target(half):
        return (xy, lax.rem(z, 2), half, lax.div(z, 2))

    def wq_source(c):
        return (xy, c, lax.div(head_block, places), lax.rem(head_block, places))

    own_wq = pltpu.make_async_copy(wq_ref, depth_of(dp, 1), local_sems.at[1])
    own_small = pltpu.make_async_copy(small_ref, all_small_ref.at[dp, z], local_sems.at[2])
    own_wide = pltpu.make_async_copy(wide_ref, all_wide_ref.at[z], local_sems.at[3])
    own_small.start()
    for n in range(2):

        @pl.when(is_same(wq_target(n), me))
        def _():
            own_wq.start()

        @pl.when(jnp.logical_not(is_same(wq_target(n), me)))
        def _():
            send(wq_ref, depth_of(dp, 1), q_send.at[n], q_recv.at[core], wq_target(n)).start()

    for step in range(1, parts):
        there = lax.rem(z + step, parts)
        device = (xy, core, there // places, lax.rem(there, places))
        send(small_ref, all_small_ref.at[dp, z], z_send.at[step], z_recv.at[z], device).start()

    @pl.when(outside)
    def _():
        for chunk in range(CHUNKS):
            for half in range(2):
                send(
                    chunk_of(tokens_ref, half, chunk), chunk_of(rows_ref.at[z], half, chunk),
                    in_send.at[half, chunk], x_recv.at[z, chunk], (xy, half, core, entry),
                ).start()

    @pl.when(inside)
    def _():
        for chunk in range(CHUNKS):
            send(
                chunk_of(tokens_ref, 1 - core, chunk), chunk_of(rows_ref.at[z], 1 - core, chunk),
                in_send.at[0, chunk], x_recv.at[z, chunk], sibling,
            ).start()
        pltpu.make_async_copy(tokens_ref, rows_ref.at[z], local_sems.at[0]).start()

    def ways(shard):
        from_half, from_place = shard // places, lax.rem(shard, places)
        start = jnp.where(from_half == zh, from_place, jnp.where(from_half < zh, 0, places - 1))
        return (zl >= start) & (zl < places - 1), (zl <= start) & (zl > 0)

    def pass_on(shard, chunk, source):
        mine = chunk_of(rows_ref.at[shard], core, chunk)
        for n, (way, step) in enumerate(zip(ways(shard), (1, -1))):

            @pl.when(way)
            def _():
                send(
                    source, mine, fwd_send.at[n, shard, chunk], x_recv.at[shard, chunk],
                    (xy, core, zh, zl + step),
                ).start()

    def share(shard, chunk, source):
        mine = chunk_of(rows_ref.at[shard], core, chunk)
        send(source, mine, share_send.at[shard, chunk], xs_recv.at[shard, chunk], sibling).start()

    def got(shard, chunk):
        mine = chunk_of(rows_ref.at[shard], core, chunk)
        send(mine, mine, share_send.at[shard, chunk], x_recv.at[shard, chunk], sibling).wait_recv()

    @pl.when(inside)
    def _():
        for chunk in range(CHUNKS):
            mine = chunk_of(tokens_ref, core, chunk)
            pass_on(z, chunk, mine)
            share(z, chunk, mine)

    own_wide.start()
    for n, step in enumerate((1, -1)):

        @pl.when((z + step >= 0) & (z + step < parts))
        def _():
            send(
                wide_ref, all_wide_ref.at[z], w_send.at[n, z], w_recv.at[z], beside(step)
            ).start()

    @pl.when(outside)
    def _():
        for chunk in range(CHUNKS):
            got(z, chunk)
            pass_on(z, chunk, chunk_of(rows_ref.at[z], core, chunk))

    own_small.wait()
    for step in range(1, parts):
        there = lax.rem(z + step, parts)
        send(small_ref, all_small_ref.at[dp, there], z_send.at[step], z_recv.at[there], sibling).wait_recv()
    for c in range(2):

        @pl.when(is_same(wq_source(c), me))
        def _():
            own_wq.wait()

        @pl.when(jnp.logical_not(is_same(wq_source(c), me)))
        def _():
            here = depth_of(xy * 2 + c, 1)
            send(here, here, q_send.at[0], q_recv.at[c], wq_source(c)).wait_recv()

    def arrays_at(column):
        return depth_of(column * 2, 2), all_small_ref.at[column * 2 + core]

    for step, there, device in plane_peers(shape, me):
        for n, ref in enumerate(arrays_at(xy)):
            send(ref, ref, p_send.at[n, step], p_recv.at[n, xy], device).start()
    ref = all_small_ref.at[dp]
    send(ref, ref, s_send.at[xy], s_recv.at[xy], sibling).start()

    for distance in range(1, parts):
        for chunk in range(CHUNKS):
            for shard in (z + distance, z - distance):

                @pl.when((shard >= 0) & (shard < parts))
                def _():
                    got(shard, chunk)
                    mine = chunk_of(rows_ref.at[shard], core, chunk)
                    pass_on(shard, chunk, mine)
                    share(shard, chunk, mine)

        for n, step in enumerate((1, -1)):
            shard = z - step * distance

            @pl.when((shard >= 0) & (shard < parts))
            def _():
                piece = all_wide_ref.at[shard]
                send(piece, piece, w_send.at[n, shard], w_recv.at[shard], sibling).wait_recv()

            @pl.when((shard >= 0) & (shard < parts) & (z + step >= 0) & (z + step < parts))
            def _():
                piece = all_wide_ref.at[shard]
                send(piece, piece, w_send.at[n, shard], w_recv.at[shard], beside(step)).start()

    for step in range(1, columns):
        there = lax.rem(xy + columns - step, columns)
        for n, ref in enumerate(arrays_at(there)):
            send(ref, ref, p_send.at[n, step], p_recv.at[n, there], sibling).wait_recv()
        ref = all_small_ref.at[there * 2 + core]
        send(ref, ref, s_send.at[there], s_recv.at[there], sibling).start()

    for column in range(columns):
        ref = all_small_ref.at[column * 2 + 1 - core]
        copy = send(ref, ref, s_send.at[column], s_recv.at[column], sibling)
        copy.wait_recv()
        copy.wait_send()
    for step in range(1, columns):
        for n, ref in enumerate(arrays_at(xy)):
            send(ref, ref, p_send.at[n, step], p_recv.at[n, xy], sibling).wait_send()
    for step in range(1, parts):
        send(small_ref, all_small_ref.at[dp, z], z_send.at[step], z_recv.at[z], sibling).wait_send()
    for n in range(2):

        @pl.when(jnp.logical_not(is_same(wq_target(n), me)))
        def _():
            send(wq_ref, depth_of(dp, 1), q_send.at[n], q_recv.at[core], sibling).wait_send()

    own_wide.wait()
    for n, step in enumerate((1, -1)):
        for distance in range(parts):
            shard = z - step * distance

            @pl.when((shard >= 0) & (shard < parts) & (z + step >= 0) & (z + step < parts))
            def _():
                piece = all_wide_ref.at[shard]
                send(piece, piece, w_send.at[n, shard], w_recv.at[shard], beside(step)).wait_send()

    for shard in range(parts):
        for chunk in range(CHUNKS):
            mine = chunk_of(rows_ref.at[shard], core, chunk)
            other = chunk_of(rows_ref.at[shard], 1 - core, chunk)
            copy = send(mine, other, share_send.at[shard, chunk], xs_recv.at[shard, chunk], sibling)

            @pl.when(jnp.logical_not((shard == z) & outside))
            def _():
                copy.wait_send()

            @pl.when(jnp.logical_not((shard == z) & inside))
            def _():
                copy.wait_recv()

            for n, way in enumerate(ways(shard)):

                @pl.when(way)
                def _():
                    send(
                        mine, mine, fwd_send.at[n, shard, chunk], x_recv.at[shard, chunk], sibling
                    ).wait_send()

    for chunk in range(CHUNKS):
        first = chunk_of(tokens_ref, 0, chunk)
        send(first, first, in_send.at[0, chunk], x_recv.at[z, chunk], sibling).wait_send()

        @pl.when(outside)
        def _():
            send(first, first, in_send.at[1, chunk], x_recv.at[z, chunk], sibling).wait_send()

    @pl.when(inside)
    def _():
        pltpu.make_async_copy(tokens_ref, rows_ref.at[z], local_sems.at[0]).wait()


def gather(shape, tokens, wq, small, wide):
    parts, columns = shape["zh"] * shape["zl"], shape["xy"]
    anywhere = pl.BlockSpec(memory_space=pl.ANY)
    dma = pltpu.SemaphoreType.DMA
    return pl.pallas_call(
        functools.partial(gather_kernel, shape),
        out_shape=[
            jax.ShapeDtypeStruct((parts, *tokens.shape), tokens.dtype),
            jax.ShapeDtypeStruct((3, 2 * columns * wq.shape[1], wq.shape[2]), wq.dtype),
            jax.ShapeDtypeStruct((2 * columns, parts, *small.shape), small.dtype),
            jax.ShapeDtypeStruct((parts, *wide.shape), wide.dtype),
        ],
        in_specs=[anywhere] * 4,
        out_specs=[anywhere] * 4,
        scratch_shapes=[
            dma((4,)), dma((2, CHUNKS)), dma((2, parts, CHUNKS)), dma((parts, CHUNKS)),
            dma((parts, CHUNKS)), dma((parts, CHUNKS)),
            dma((parts,)), dma((parts,)), dma((2, columns)), dma((2, columns)), dma((columns,)),
            dma((columns,)), dma((2, parts)), dma((parts,)), dma((2,)), dma((2,)),
        ],
        compiler_params=pltpu.CompilerParams(collective_id=2, has_side_effects=True),
        name="gather",
    )(tokens, wq, small, wide)


class AllSum:
    def __init__(self, shape, column_slots, plane_slots, sems):
        self.shape, self.me = shape, place()
        self.slots, self.sems = (column_slots, plane_slots), sems
        xy, core, zh, zl = self.me
        self.mine = ((core * 2 + zh) * shape["zl"] + zl, xy)

    def peers(self, turn):
        return (column_peers if turn == 0 else plane_peers)(self.shape, self.me)

    def start(self, turn, value):
        slots, mine = self.slots[turn], self.mine[turn]
        slots[mine] = value
        for step, _, device in self.peers(turn):
            self.copy(turn, step, mine, device).start()

    def copy(self, turn, step, slot, device):
        here = self.slots[turn].at[slot]
        return send(
            here, here, self.sems.at[2 * turn, step], self.sems.at[2 * turn + 1, slot], device
        )

    def finish(self, turn):
        slots = self.slots[turn]
        for step, there, device in self.peers(turn):
            self.copy(turn, step, there, device).wait_recv()
        for step, _, device in self.peers(turn):
            self.copy(turn, step, self.mine[turn], device).wait_send()
        total = slots[0]
        for slot in range(1, slots.shape[0]):
            total = total + slots[slot]
        return total


LANES = 256


def lane_sums(values, ranges):
    lane = lax.broadcasted_iota(jnp.int32, values.shape, 1)
    return [
        jnp.sum(jnp.where((lane >= low) & (lane < high), values, 0.0)) for low, high in ranges
    ]


def small_ranges(n_bias, n_gain):
    ends = [0, n_bias] + [n_bias + n_gain * (n + 1) for n in range(4)]
    return list(zip(ends[:-1], ends[1:]))


def row_of(values):
    lane = lax.broadcasted_iota(jnp.int32, (1, 128), 1)
    row = jnp.zeros((1, 128), F32)
    for n, value in enumerate(values):
        row = jnp.where(lane == n, value, row)
    return row


class Rows:
    def __init__(self, shape):
        self.me = place()
        self.places = shape["zl"]

    def shard_at(self, index):
        return jnp.where(self.me[2] == 1, index, 2 * self.places - 1 - index)

    def early(self, group):
        return jnp.where(group == 1, 0, 2 * self.places - 1)

    def owner(self, shard):
        return (self.me[0], self.me[2], lax.div(shard, self.places), lax.rem(shard, self.places))

    def copy(self, src, dst, half, shard, send_sems, recv_sems):
        xy, core, zh, zl = self.me
        there = dst.at[zl, :, pl.ds(pl.multiple_of(core * half, half), half)]
        return send(src, there, send_sems.at[shard], recv_sems.at[zl, core], self.owner(shard))

    def take(self, dst, half, send_sems, recv_sems):
        xy, core, zh, zl = self.me
        for n in range(self.places):
            for c in range(2):
                here = dst.at[n, :, c * half : (c + 1) * half]
                copy = send(here, here, send_sems.at[0], recv_sems.at[n, c], (xy, c, core, n))

                @pl.when(jnp.logical_not(is_same((xy, c, core, n), self.me)))
                def _():
                    copy.wait_recv()


def sums_kernel(
    shape, n_bias, n_gain,
    first_ref, grad_qkv_ref, small_ref, parts_ref, wq_ref, wp_ref, wu_ref, wd_ref, ws_ref,
    rows_ref, added_ref, sum_ref, wide_ref, small_sum_ref, totals_ref,
    taken, added, plane, both, pieces, small_column, small_plane, row_column, row_plane,
    t_send, t_recv, o_send, o_recv, p_send, p_recv, q_send, q_recv, local_sems, small_sems, row_sems,
):
    me = place()
    xy, core, zh, zl = me
    places, columns = shape["zl"], shape["xy"]
    parts = 2 * places
    z = zh * places + zl
    sibling = (xy, 1 - core, zh, zl)
    head_block = zl * 2 + core
    rows, half = taken.shape[1], taken.shape[2]
    moves = Rows(shape)
    shard_at = moves.shard_at
    depth = both.shape[1] // 2
    small_all = AllSum(shape, small_column, small_plane, small_sems)
    row_all = AllSum(shape, row_column, row_plane, row_sems)

    def columns_at(which):
        return pl.ds(pl.multiple_of(which * half, half), half)

    def to_sibling(shard):
        part = first_ref.at[pl.ds(pl.multiple_of(shard * rows, rows), rows), columns_at(1 - core)]
        return send(part, taken.at[shard], t_send.at[shard], t_recv.at[shard], sibling)

    def to_owner():
        shard = shard_at(0)
        return moves.copy(added.at[shard], rows_ref, half, shard, o_send, o_recv)

    keep_added = pltpu.make_async_copy(added, added_ref, local_sems.at[0])

    def add_rows(index):
        shard = shard_at(index)
        to_sibling(shard).wait_recv()
        here = first_ref[pl.ds(pl.multiple_of(shard * rows, rows), rows), columns_at(core)]
        added[shard] = (here.astype(F32) + taken[shard].astype(F32)).astype(BF)

    def plane_part(column):
        return grad_qkv_ref.at[:, pl.ds(pl.multiple_of(column * 2 * depth, 2 * depth), 2 * depth), :]

    def target(c):
        return (xy, c, lax.div(head_block, places), lax.rem(head_block, places))

    def source(n):
        return (xy, lax.rem(z, 2), n, lax.div(z, 2))

    def part(c):
        return both.at[:, c * depth : (c + 1) * depth, :]

    greet(shape)
    to_sibling(shard_at(0)).start()
    small_all.start(0, small_ref[...])
    keep_part = pltpu.make_async_copy(plane_part(xy), plane.at[xy], local_sems.at[1])
    keep_part.start()
    for step, there, device in plane_peers(shape, me):
        send(plane_part(there), plane.at[xy], p_send.at[step], p_recv.at[xy], device).start()
    for index in range(1, parts):
        to_sibling(shard_at(index)).start()
    add_rows(0)
    to_owner().start()

    def square(values):
        wide = values.astype(F32)
        return jnp.sum(wide * wide)

    wide = parts_ref[0].astype(F32)
    for n in range(1, parts):
        wide = wide + parts_ref[n].astype(F32)
    wide_ref[...] = wide
    up, down, proj = parts_of(wide_ref, wu_ref, wp_ref)
    values = [square(proj), square(up), square(down)]
    values += [square(wq_ref[c]) for c in range(3)]
    values += [square(ref[...]) for ref in (wp_ref, wu_ref, wd_ref)]
    ranges = small_ranges(n_bias, n_gain)
    values += lane_sums(ws_ref[...] * ws_ref[...], ranges)
    small_all.start(1, small_all.finish(0))

    keep_part.wait()
    for step, there, device in plane_peers(shape, me):
        send(plane_part(there), plane.at[there], p_send.at[step], p_recv.at[there], device).wait_recv()
    for c in range(3):
        total = plane[0, c].astype(F32)
        for n in range(1, columns):
            total = total + plane[n, c].astype(F32)
        both[c] = total.astype(BF)
    for c in range(2):

        @pl.when(is_same(target(c), me))
        def _():
            pltpu.make_async_copy(part(c), pieces.at[zh], local_sems.at[2]).start()

        @pl.when(jnp.logical_not(is_same(target(c), me)))
        def _():
            send(part(c), pieces.at[zh], q_send.at[c], q_recv.at[zh], target(c)).start()

    for index in range(1, parts):
        add_rows(index)
    keep_added.start()
    small = small_all.finish(1)
    small_sum_ref[...] = small
    for n in range(2):

        @pl.when(is_same(target(n), me))
        def _():
            pltpu.make_async_copy(part(n), pieces.at[zh], local_sems.at[2]).wait()

        @pl.when(jnp.logical_not(is_same(target(n), me)))
        def _():
            send(part(n), pieces.at[zh], q_send.at[n], q_recv.at[zh], target(n)).wait_send()

        @pl.when(jnp.logical_not(is_same(source(n), me)))
        def _():
            send(part(n), pieces.at[n], q_send.at[n], q_recv.at[n], source(n)).wait_recv()

    squares = []
    for c in range(3):
        total = pieces[0, c].astype(F32) + pieces[1, c].astype(F32)
        sum_ref[c] = total
        squares.append(square(total))
    row_all.start(0, row_of(squares + values))
    row_all.start(1, row_all.finish(0))
    row = row_all.finish(1)
    lane = lax.broadcasted_iota(jnp.int32, (1, 128), 1)
    for n, value in enumerate(lane_sums(small * small, ranges)):
        row = jnp.where(lane == 17 + n, value, row)
    totals_ref[...] = row

    for step, there, device in plane_peers(shape, me):
        send(plane_part(there), plane.at[xy], p_send.at[step], p_recv.at[xy], device).wait_send()
    for shard in range(parts):
        to_sibling(shard).wait_send()
    keep_added.wait()
    to_owner().wait_send()

    @pl.when(z == moves.early(core))
    def _():
        moves.take(rows_ref, half, o_send, o_recv)


def rows_kernel(
    shape, added_ref, early_ref, x_ref, middle_ref, gain_ref, out_ref,
    got, e_sem, keep_sem, o_send, o_recv,
):
    me = place()
    xy, core, zh, zl = me
    moves = Rows(shape)
    parts = added_ref.shape[0]
    half = added_ref.shape[2]
    z = zh * moves.places + zl
    is_early = z == moves.early(core)
    early = pltpu.make_async_copy(early_ref, got, e_sem)
    mine = got.at[zl, :, pl.ds(pl.multiple_of(core * half, half), half)]
    keep = pltpu.make_async_copy(added_ref.at[z], mine, keep_sem)

    def each(act):
        for index in range(1, parts):
            shard = moves.shard_at(index)

            @pl.when(jnp.logical_not(is_same(moves.owner(shard), me)))
            def _():
                act(moves.copy(added_ref.at[shard], got, half, shard, o_send, o_recv))

    greet_column(shape)
    each(lambda copy: copy.start())

    @pl.when(is_early)
    def _():
        early.start()

    @pl.when(zh == core)
    def _():
        keep.start()

    value, inverse = normed_of(x_ref[...].astype(F32))

    @pl.when(zh == core)
    def _():
        keep.wait()

    @pl.when(is_early)
    def _():
        early.wait()

    @pl.when(jnp.logical_not(is_early))
    def _():
        moves.take(got, half, o_send, o_recv)

    grad = got[0].astype(F32)
    for n in range(1, moves.places):
        grad = grad + got[n].astype(F32)
    inner = grad * gain_ref[...]
    out_ref[...] = (
        middle_ref[...]
        + inverse
        * (
            inner
            - jnp.mean(inner, axis=-1, keepdims=True)
            - value * jnp.mean(inner * value, axis=-1, keepdims=True)
        )
    ).astype(BF)
    each(lambda copy: copy.wait_send())


def finish_rows(shape, added, early, tokens, grad_middle, gain):
    places = shape["zl"]
    vmem = pl.BlockSpec(memory_space=pltpu.VMEM)
    anywhere = pl.BlockSpec(memory_space=pl.ANY)
    dma = pltpu.SemaphoreType.DMA
    return pl.pallas_call(
        functools.partial(rows_kernel, shape),
        out_shape=jax.ShapeDtypeStruct(tokens.shape, BF),
        in_specs=[anywhere, anywhere, vmem, vmem, vmem],
        out_specs=vmem,
        scratch_shapes=[
            pltpu.VMEM((places, *tokens.shape), BF),
            dma, dma, dma((2 * places,)), dma((places, 2)),
        ],
        compiler_params=pltpu.CompilerParams(
            collective_id=6, has_side_effects=True, vmem_limit_bytes=56 * 2**20
        ),
        name="finish_rows",
    )(added, early, tokens, grad_middle, gain)


def parts_of(wide_ref, up_like, proj_like):
    ff, heads = up_like.shape[1], proj_like.shape[0]
    return wide_ref[:, :ff], wide_ref[:, ff : 2 * ff], wide_ref[:, 2 * ff : 2 * ff + heads]


def sums(shape, n_bias, n_gain, first, grad_qkv, small, wide, weights):
    places, columns = shape["zl"], shape["xy"]
    members, parts = 4 * places, 2 * places
    rows, width = first.shape[0] // parts, first.shape[1]
    depth = grad_qkv.shape[1] // (2 * columns)
    heads_cols = grad_qkv.shape[2]
    vmem = pl.BlockSpec(memory_space=pltpu.VMEM)
    anywhere = pl.BlockSpec(memory_space=pl.ANY)
    dma = pltpu.SemaphoreType.DMA
    slots = max(members, columns)
    return pl.pallas_call(
        functools.partial(sums_kernel, shape, n_bias, n_gain),
        out_shape=[
            jax.ShapeDtypeStruct((places, rows, width), BF),
            jax.ShapeDtypeStruct((parts, rows, width // 2), BF),
            jax.ShapeDtypeStruct((3, depth, heads_cols), F32),
            jax.ShapeDtypeStruct(wide.shape[1:], F32),
            jax.ShapeDtypeStruct(small.shape, F32),
            jax.ShapeDtypeStruct((1, 128), F32),
        ],
        in_specs=[vmem, anywhere] + [vmem] * 7,
        out_specs=[anywhere] * 2 + [vmem] * 4,
        scratch_shapes=[
            pltpu.VMEM((parts, rows, width // 2), BF),
            pltpu.VMEM((parts, rows, width // 2), BF),
            pltpu.VMEM((columns, 3, 2 * depth, heads_cols), BF),
            pltpu.VMEM((3, 2 * depth, heads_cols), BF),
            pltpu.VMEM((2, 3, depth, heads_cols), BF),
            pltpu.VMEM((members, *small.shape), F32),
            pltpu.VMEM((columns, *small.shape), F32),
            pltpu.VMEM((members, 1, 128), F32),
            pltpu.VMEM((columns, 1, 128), F32),
            dma((parts,)), dma((parts,)), dma((parts,)), dma((places, 2)),
            dma((columns,)), dma((columns,)), dma((2,)), dma((2,)), dma((3,)),
            dma((4, slots)), dma((4, slots)),
        ],
        compiler_params=pltpu.CompilerParams(
            collective_id=3, has_side_effects=True, vmem_limit_bytes=56 * 2**20
        ),
        name="sums",
    )(first, grad_qkv, small, wide, *weights)


def reduce_kernel(shape, row_ref, total_ref, row_column, row_plane, row_sems):
    greet(shape)
    both = AllSum(shape, row_column, row_plane, row_sems)
    both.start(0, row_ref[...])
    both.start(1, both.finish(0))
    total_ref[...] = both.finish(1)


def reduce_row(shape, row):
    members = 4 * shape["zl"]
    vmem = pl.BlockSpec(memory_space=pltpu.VMEM)
    return pl.pallas_call(
        functools.partial(reduce_kernel, shape),
        out_shape=jax.ShapeDtypeStruct((1, 128), F32),
        in_specs=[vmem],
        out_specs=vmem,
        scratch_shapes=[
            pltpu.VMEM((members, 1, 128), F32),
            pltpu.VMEM((shape["xy"], 1, 128), F32),
            pltpu.SemaphoreType.DMA((4, max(members, shape["xy"]))),
        ],
        compiler_params=pltpu.CompilerParams(collective_id=4, has_side_effects=True),
        name="reduce_row",
    )(row)


def moments_kernel(
    n_bias, n_gain, spot_ref, totals_ref, small_ref,
    gq, wide, wq, wp, wu, wd, ws, mq, mp, mu, md, ms, sq, sp, su, sd, ss,
    nmq, nmp, nmu, nmd, nmb, nmg, nmt, nsq, nsp, nsu, nsd, nsb, nsg, nst, uq, up, uu, ud, us, row_ref,
):
    totals = totals_ref[...]
    lane = lax.broadcasted_iota(jnp.int32, (1, 128), 1)
    grads_here = (lane < 6) | ((lane >= 17) & (lane < 22))
    norm = jnp.sqrt(jnp.sum(jnp.where(grads_here, totals, 0.0), axis=1, keepdims=True))
    clip = jnp.minimum(1.0, 1.0 / norm)
    values = []

    def step(grad, weight, mean, square):
        scaled = clip * grad
        new_mean = 0.5 * mean + 0.5 * scaled
        new_square = 0.5 * square + 0.5 * scaled * scaled
        update = new_mean / (jnp.sqrt(new_square) + 1e-06) + 0.01 * weight
        return new_mean, new_square, update

    for c in range(3):
        nmq[c], nsq[c], update = step(gq[c], wq[c], mq[c], sq[c])
        uq[c] = update
        values.append(jnp.sum(update * update))
    grad_up, grad_down, grad_proj = parts_of(wide, wu, wp)
    for turned, g, w, m, s, nm, ns, u in (
        (True, grad_proj, wp, mp, sp, nmp, nsp, up),
        (False, grad_up, wu, mu, su, nmu, nsu, uu),
        (True, grad_down, wd, md, sd, nmd, nsd, ud),
    ):
        grad = g.astype(F32)
        nm[...], ns[...], update = step(grad.T if turned else grad, w[...], m[...], s[...])
        u[...] = update
        values.append(jnp.sum(update * update))
    spot = spot_ref[0]
    grad = small_ref[pl.ds(spot, 1), :]
    new_mean, new_square, update = step(grad, ws[...], ms[...], ss[...])
    us[...] = update
    ranges = small_ranges(n_bias, n_gain)
    values += lane_sums(update * update, ranges)
    row_ref[...] = row_of(values)
    put_small(ranges, new_mean, nmb, nmg, nmt)
    put_small(ranges, new_square, nsb, nsg, nst)


def put_small(ranges, row, bias, gain, shift):
    bias[...] = row[:, ranges[0][0] : ranges[0][1]]
    for n in range(2):
        gain[n : n + 1, :] = row[:, ranges[1 + n][0] : ranges[1 + n][1]]
        shift[n : n + 1, :] = row[:, ranges[3 + n][0] : ranges[3 + n][1]]


def weights_kernel(
    n_bias, n_gain, totals_ref, update_ref, wq, wp, wu, wd, ws, uq, up, uu, ud, us,
    nwq, nwp, nwu, nwd, nwb, nwg, nwt, norms_ref, norm_ref,
):
    totals, updates = totals_ref[...], update_ref[...]
    lane = lax.broadcasted_iota(jnp.int32, (1, 128), 1)
    grads_here = (lane < 6) | ((lane >= 17) & (lane < 22))
    norm_ref[...] = jnp.sqrt(jnp.sum(jnp.where(grads_here, totals, 0.0), axis=1, keepdims=True))
    weight_norm, update_norm = jnp.sqrt(totals), jnp.sqrt(updates)
    norms_ref[0:1, :] = weight_norm[:, 6:17]
    norms_ref[1:2, :] = update_norm[:, 0:11]

    def factor(n):
        return 0.3 * (weight_norm[:, 6 + n : 7 + n] / update_norm[:, n : n + 1])

    for c in range(3):
        nwq[c] = wq[c] - factor(c) * uq[c]
    for n, (w, u, out) in enumerate(((wp, up, nwp), (wu, uu, nwu), (wd, ud, nwd))):
        out[...] = w[...] - factor(3 + n) * u[...]
    ranges = small_ranges(n_bias, n_gain)
    column = lax.broadcasted_iota(jnp.int32, (1, LANES), 1)
    factors = jnp.zeros((1, LANES), F32)
    for n, (low, high) in enumerate(ranges):
        factors = jnp.where((column >= low) & (column < high), factor(6 + n), factors)
    put_small(ranges, ws[...] - factors * us[...], nwb, nwg, nwt)


def shapes_of(arrays):
    return [jax.ShapeDtypeStruct(array.shape, F32) for array in arrays]


def optimizer(shape, n_bias, n_gain, spot, totals, small, grads, weights, means, squares, small_like):
    vmem = pl.BlockSpec(memory_space=pltpu.VMEM)
    big = list(weights[:4])
    results = shapes_of(big) + shapes_of(small_like)
    row = jax.ShapeDtypeStruct((1, 128), F32)
    params = pltpu.CompilerParams(vmem_limit_bytes=48 * 2**20)
    out = pl.pallas_call(
        functools.partial(moments_kernel, n_bias, n_gain),
        out_shape=results * 2 + shapes_of(weights) + [row],
        in_specs=[pl.BlockSpec(memory_space=pltpu.SMEM)] + [vmem] * 19,
        out_specs=[vmem] * 20,
        compiler_params=params,
        name="moments",
    )(spot, totals, small, *grads, *weights, *means, *squares)
    new_means, new_squares, updates, row_here = out[:7], out[7:14], out[14:19], out[19]
    updates_total = reduce_row(shape, row_here)
    out = pl.pallas_call(
        functools.partial(weights_kernel, n_bias, n_gain),
        out_shape=results
        + [jax.ShapeDtypeStruct((2, 11), F32), jax.ShapeDtypeStruct((1, 1), F32)],
        in_specs=[vmem] * 12,
        out_specs=[vmem] * 9,
        compiler_params=params,
        name="weights",
    )(totals, updates_total, *weights, *updates)
    return updates_total, out[8], out[7], out[:7], new_means, new_squares


def turn_own_first(shape, core, src, dst):
    columns = shape["xy"]
    width = src.shape[1]
    depth = width // (2 * columns)
    for start in range(0, width, 128):
        turned = src[:, start : start + 128].T
        for offset in range(0, 128, depth):
            block = (start + offset) // depth
            slot = block // 2 + jnp.where(core == block % 2, 0, columns)
            dst[pl.ds(pl.multiple_of(slot * depth, depth), depth), :] = turned[offset : offset + depth]


def normed_of(values):
    center = values - jnp.mean(values, axis=-1, keepdims=True)
    inverse = lax.rsqrt(jnp.mean(center * center, axis=-1, keepdims=True) + 1e-05)
    return center * inverse, inverse


class Adder:
    def __init__(self, side, taken, first, sems):
        xy, core, zh, zl = place()
        self.side, self.taken, self.first = side, taken, first
        self.swap_send, self.swap_recv, *self.sems = sems
        self.at = (lax.div(xy, side), lax.rem(xy, side))
        self.rest = (core, zh, zl)
        self.sibling = (xy, 1 - core, zh, zl)

    def peers(self):
        xy = self.at[0] * self.side + self.at[1]
        columns = self.side * self.side
        return [self.sibling] + [
            (lax.rem(xy + step, columns), *self.rest) for step in range(1, columns)
        ]

    def swap(self, other, index):
        return send(other, self.taken.at[index], self.swap_send.at[index], self.swap_recv.at[index], self.sibling)

    def block(self, index, axis, there):
        return self.taken.at[index, :, there] if axis == 0 else self.taken.at[index, :, :, there]

    def owned(self, index, axis, step):
        there = lax.rem(self.at[1 - axis] + step, self.side)
        if axis == 0:
            return self.taken.at[index, :, self.at[0], there]
        return self.taken.at[index, :, there, self.at[1]]

    def copies(self, index, axis):
        for step in range(1, self.side):
            there = lax.rem(self.at[axis] + step, self.side)
            member = (there, self.at[1]) if axis == 0 else (self.at[0], there)
            yield send(
                self.block(index, axis, there), self.first.at[index, step - 1],
                self.sems[0].at[index, step - 1], self.sems[1].at[index, step - 1],
                (member[0] * self.side + member[1], *self.rest),
            )

    def by_parity(self, index, act):
        if isinstance(index, int):
            act(index % 2)
            return
        for parity in range(2):

            @pl.when(lax.rem(index, 2) == parity)
            def _():
                act(parity)

    def add_core(self, own, other, index):
        self.swap(other, index).wait_recv()
        for which in range(2):
            self.taken[index, which] = (
                own[which].astype(F32) + self.taken[index, which].astype(F32)
            ).astype(BF)

        def start(axis):
            for copy in self.copies(index, axis):
                copy.start()

        self.by_parity(index, start)

    def add_first(self, index, keep):
        def act(axis):
            mine = self.block(index, axis, self.at[axis])
            total = mine[...].astype(F32)
            for step, copy in enumerate(self.copies(index, axis)):
                copy.wait_recv()
                total = total + self.first[index, step].astype(F32)
            mine[...] = total.astype(BF)
            for copy in keep(index, axis):
                copy.start()

        self.by_parity(index, act)

    def end(self, index, keep):
        def act(axis):
            for copy in self.copies(index, axis):
                copy.wait_send()
            for copy in keep(index, axis):
                copy.wait()

        self.by_parity(index, act)


def feed_kernel(
    shape, ff_local, x_ref, c_ref, attn_ref, norm_ref, proj_ref, up_ref, down_ref,
    block_ref, middle_ref, given_ref, wide_ref, sums_ref,
    middle, total, second, a_second, a_turned, c_turned, own, other, taken, first_in,
    out_sems, keep_sems, proj_sems, *sems,
):
    step = pl.program_id(0)
    steps = taken.shape[0] - 1
    parts, heads_cols = attn_ref.shape[:2]
    side, chunk = own.shape[2], own.shape[5]
    half = c_turned.shape[0] // 2
    per = ff_local // chunk
    wide = 2 * ff_local + heads_cols
    slot = lax.rem(step, 2)
    adder = Adder(side, taken, first_in, sems)
    halves = own.shape[2:5]

    def keep(index, axis):
        for step in range(side):
            for which in range(2):
                start = index // per * wide + which * ff_local + index % per * chunk
                if not isinstance(index, int):
                    start = lax.div(index, per) * wide + which * ff_local + lax.rem(index, per) * chunk
                    start = pl.multiple_of(start, 128)
                yield pltpu.make_async_copy(
                    adder.owned(index, axis, step).at[which], wide_ref.at[step, :, pl.ds(start, chunk)],
                    keep_sems.at[index, step, which],
                )

    def keep_proj(index, axis):
        for step in range(side):
            for part in range(parts):
                which, place_in = part // (parts // 2), part % (parts // 2)
                yield pltpu.make_async_copy(
                    adder.owned(index, axis, step).at[which, :, pl.ds(place_in * heads_cols, heads_cols)],
                    wide_ref.at[step, :, pl.ds(part * wide + 2 * ff_local, heads_cols)],
                    proj_sems.at[step, part],
                )

    def put(at, which, grad):
        own[at, which] = grad[:half].reshape(*halves, grad.shape[1])
        other[at, which] = grad[half:].reshape(*halves, grad.shape[1])

    @pl.when(step == 0)
    def _():
        barrier = pltpu.get_barrier_semaphore()
        for peer in adder.peers():
            pl.semaphore_signal(barrier, inc=1, device_id=peer, device_id_type=MESH)
        core = lax.axis_index("core")
        mixed = x_ref[...].astype(F32)
        for part in range(parts):
            mixed = mixed + dot(attn_ref[part].T, proj_ref[part], 1, 1)
        middle[...] = mixed
        value, _ = normed_of(mixed)
        a_second[...] = (value * norm_ref[0:1, :] + norm_ref[1:2, :]).astype(BF)
        turn_own_first(shape, core, a_second, a_turned)
        turn_own_first(shape, core, c_ref, c_turned)
        total[...] = jnp.zeros_like(total)
        second[...] = jnp.zeros_like(second)
        pl.semaphore_wait(barrier, len(adder.peers()))

    @pl.when(step >= 2)
    def _():
        adder.swap(other.at[slot], step - 2).wait_send()

    up, down = up_ref[0], down_ref[0]
    pre = dot(a_second[...], up, 1, 0)
    grad_hidden = dot(c_ref[...], down, 1, 0)
    normal = 0.5 * (1.0 + lax.erf(pre * 2.0**-0.5))
    hidden = (pre * normal).astype(BF)
    slope = normal + pre * jnp.exp(-0.5 * pre * pre) * 0.3989422804014327
    grad_pre = (slope * grad_hidden).astype(BF)
    total[...] += dot(hidden, down, 1, 1)
    put(slot, 1, dot(c_turned[...], hidden, 1, 0).astype(BF))
    second[...] += dot(grad_pre, up, 1, 1)
    put(slot, 0, dot(a_turned[...], grad_pre, 1, 0).astype(BF))
    adder.swap(other.at[slot], step).start()

    @pl.when(step >= 1)
    def _():
        adder.add_core(own.at[1 - slot], other.at[1 - slot], step - 1)

    @pl.when(step >= 3)
    def _():
        adder.add_first(step - 3, keep)

    @pl.when(step == steps - 1)
    def _():
        core = lax.axis_index("core")
        last = steps - 1
        here, free = last % 2, 1 - last % 2
        adder.add_core(own.at[here], other.at[here], last)
        adder.add_first(last - 2, keep)
        a_second[...] = (middle[...] + total[...]).astype(BF)
        out_block = pltpu.make_async_copy(a_second, block_ref, out_sems.at[0])
        out_block.start()
        value, inverse = normed_of(middle[...])
        grad = second[...]
        sums_ref[0:1, :] = jnp.sum(grad * value, axis=0, keepdims=True)
        sums_ref[1:2, :] = jnp.sum(grad, axis=0, keepdims=True)
        inner = grad * norm_ref[0:1, :]
        second[...] = c_ref[...].astype(F32) + inverse * (
            inner
            - jnp.mean(inner, axis=-1, keepdims=True)
            - value * jnp.mean(inner * value, axis=-1, keepdims=True)
        )
        out_middle = pltpu.make_async_copy(second, middle_ref, out_sems.at[1])
        out_middle.start()
        low = second[...].astype(BF)
        turn_own_first(shape, core, low, a_turned)
        adder.swap(other.at[free], last - 1).wait_send()
        in_one = parts // 2
        for which in range(2):
            grads = [
                dot(a_turned[...], attn_ref[which * in_one + n], 1, 1).astype(BF) for n in range(in_one)
            ]
            put(free, which, jnp.concatenate(grads, axis=1))
        adder.swap(other.at[free], steps).start()
        adder.add_first(last - 1, keep)
        for part in range(parts):
            rows = pl.ds(part * heads_cols, heads_cols)
            c_turned[rows, :] = dot(low, proj_ref[part], 1, 0).T.astype(BF)
        out_given = pltpu.make_async_copy(c_turned, given_ref, out_sems.at[2])
        out_given.start()
        adder.add_core(own.at[free], other.at[free], steps)
        adder.add_first(last, keep)
        adder.add_first(steps, keep_proj)
        adder.swap(other.at[here], last).wait_send()
        adder.swap(other.at[free], steps).wait_send()
        for index in range(steps + 1):
            adder.end(index, keep if index < steps else keep_proj)
        for copy in (out_block, out_middle, out_given):
            copy.wait()


def column_segments(parts, ff_local, heads_cols):
    chunk = min(512, ff_local)
    per = ff_local // chunk
    wide = 2 * ff_local + heads_cols
    segments = [
        (part * wide + which * ff_local + n * chunk, chunk, 1 - (part * per + n) % 2)
        for part in range(parts)
        for which in range(2)
        for n in range(per)
    ]
    return segments + [
        (part * wide + 2 * ff_local, heads_cols, 1 - parts * per % 2) for part in range(parts)
    ]


def feed_forward(shape, tokens, cotangent, attn_rows, norm, shared, ff_local):
    rows, width = tokens.shape
    parts, heads_cols = attn_rows.shape[:2]
    chunk = min(512, ff_local)
    per = ff_local // chunk
    steps = parts * per
    side = math.isqrt(shape["xy"])
    depth = width // (2 * shape["xy"])
    anywhere = pl.BlockSpec(memory_space=pl.ANY)

    def once(block, *index):
        return pl.BlockSpec(block, lambda s: index, pipeline_mode=pl.Buffered(1))

    dma = pltpu.SemaphoreType.DMA
    return pl.pallas_call(
        functools.partial(feed_kernel, shape, ff_local),
        grid=(steps,),
        in_specs=[
            once((rows, width), 0, 0),
            once((rows, width), 0, 0),
            once((parts, heads_cols, rows), 0, 0, 0),
            once((2, width), 0, 0),
            once((parts, width, heads_cols), 0, 0, 2 * ff_local // heads_cols),
            pl.BlockSpec((1, width, chunk), lambda s: (s // per, 0, s % per)),
            pl.BlockSpec((1, width, chunk), lambda s: (s // per, 0, per + s % per)),
        ],
        out_specs=[anywhere] * 4 + [pl.BlockSpec((2, width), lambda s: (0, 0))],
        out_shape=[
            jax.ShapeDtypeStruct((rows, width), BF),
            jax.ShapeDtypeStruct((rows, width), F32),
            jax.ShapeDtypeStruct((parts * heads_cols, rows), BF),
            jax.ShapeDtypeStruct((side, depth, parts * (2 * ff_local + heads_cols)), BF),
            jax.ShapeDtypeStruct((2, width), F32),
        ],
        scratch_shapes=[
            pltpu.VMEM((rows, width), F32),
            pltpu.VMEM((rows, width), F32),
            pltpu.VMEM((rows, width), F32),
            pltpu.VMEM((rows, width), BF),
            pltpu.VMEM((width, rows), BF),
            pltpu.VMEM((width, rows), BF),
            pltpu.VMEM((2, 2, side, side, depth, chunk), BF),
            pltpu.VMEM((2, 2, side, side, depth, chunk), BF),
            pltpu.VMEM((steps + 1, 2, side, side, depth, chunk), BF),
            pltpu.VMEM((steps + 1, side - 1, 2, side, depth, chunk), BF),
            dma((3,)),
            dma((steps, side, 2)),
            dma((side, parts)),
            dma((steps + 1,)),
            dma((steps + 1,)),
            dma((steps + 1, side - 1)),
            dma((steps + 1, side - 1)),
        ],
        compiler_params=pltpu.CompilerParams(
            vmem_limit_bytes=62 * 2**20, collective_id=5, has_side_effects=True
        ),
        name="feed_forward",
    )(tokens, cotangent, attn_rows, norm, shared, shared, shared)


def norm_parts(values):
    center = values - jnp.mean(values, axis=-1, keepdims=True)
    inverse = lax.rsqrt(jnp.mean(center * center, axis=-1, keepdims=True) + 1e-05)
    return center * inverse, inverse


def norm_back(normed, inverse, gain, grad):
    inner = grad * gain
    return inverse * (
        inner
        - jnp.mean(inner, axis=-1, keepdims=True)
        - normed * jnp.mean(inner * normed, axis=-1, keepdims=True)
    )


def per_device(
    shape,
    tokens, cotangent, item_len, bucket_table,
    w_qkv, w_proj, w_up, w_down, rel_bias, ln_gain, ln_shift,
    mean_qkv, mean_proj, mean_up, mean_down, mean_bias, mean_gain, mean_shift,
    square_qkv, square_proj, square_up, square_down, square_bias, square_gain, square_shift,
):
    columns, places = shape["xy"], shape["zl"]
    parts = 2 * places
    devices = columns * 2 * parts
    rows, width = tokens.shape
    heads = w_qkv.shape[2] // DH
    tok = rows * parts
    xy, core, zh, zl = place()
    me = ((xy * 2 + core) * 2 + zh) * places + zl
    head_block = zl * 2 + core

    ff_local, heads_cols = w_up.shape[1], w_proj.shape[0]
    local = jnp.concatenate([w_up, w_down.T, w_proj.T], axis=1).astype(BF)

    n_bias, n_gain = rel_bias.shape[0], ln_gain.shape[1]
    n_small = n_bias + 4 * n_gain

    def pack(bias, gain, shift):
        row = jnp.concatenate([bias, gain.reshape(-1), shift.reshape(-1)])
        return jnp.pad(row, (0, LANES - n_small))[None, :]

    small_weights = pack(rel_bias, ln_gain, ln_shift)
    group_rows, w_heads, small, wide = gather(
        shape, tokens, w_qkv.astype(BF), small_weights, local
    )
    shared = lax.all_gather(wide, DP, axis=1, tiled=True)
    small = small.reshape(devices, LANES)

    def columns_of(start):
        part = small[:, start : start + 2 * n_gain].reshape(devices, 2, n_gain)
        return part.transpose(1, 0, 2).reshape(2, width)

    table_flat = small[:, :n_bias].reshape(-1)
    gains, shifts = columns_of(n_bias), columns_of(n_bias + 2 * n_gain)
    other_len = lax.ppermute(item_len, "core", [(0, 1), (1, 0)])
    split = jnp.where(zh == core, item_len, other_len)[0, 0:1]

    a_first, qkv = project(
        group_rows.reshape(tok, width), jnp.stack([gains[0], shifts[0]]), w_heads
    )
    qkv = qkv.reshape(3 * heads * DH, tok)

    table = lax.dynamic_slice_in_dim(
        table_flat.reshape(BUCKETS, H), head_block * heads, heads, 1
    )
    one_hot = (jnp.arange(BUCKETS)[:, None] == bucket_table[None, :]).astype(F32)
    dist_bias = lax.dot_general(
        table, one_hot, (((0,), (0,)), ((), ())), precision=HIGHEST, preferred_element_type=F32
    )
    pattern = jnp.concatenate(
        [dist_bias * LOG2E, jnp.full((heads, BLK), NEG, F32)], axis=1
    )[:, None, :]
    out, attn_rows, lse = attend(shape, qkv, pattern, split, heads)

    attn_rows = attn_rows.reshape(parts, heads * DH, rows)
    norm_two = jnp.stack([gains[1], shifts[1]])
    block_out, grad_middle, grad_attn, wide_grad, sums_two = feed_forward(
        shape, tokens, cotangent, attn_rows, norm_two, shared, ff_local
    )
    gain_two, shift_two = sums_two[0], sums_two[1]
    given = grad_attn.reshape(parts, heads, DH, rows)
    grad_heads, wide_parts, grad_pattern = attend_back(
        shape, column_segments(parts, ff_local, w_proj.shape[0]), qkv, out, given, wide_grad, lse, pattern,
        split, heads,
    )
    grad_heads = grad_heads.reshape(3, heads * DH, tok)

    first = lax.dot_general(
        grad_heads, w_heads, (((0, 1), (0, 2)), ((), ())), preferred_element_type=F32
    ).astype(BF)
    grad_qkv = jnp.einsum("td,cet->cde", a_first, grad_heads, preferred_element_type=F32)
    head_sums = jnp.sum(grad_heads.astype(F32), axis=2)
    wide_heads = w_heads.astype(F32)
    shift_one = jnp.sum(wide_heads * head_sums[:, None, :], axis=(0, 2))
    gain_one = (
        jnp.sum(wide_heads * grad_qkv, axis=(0, 2)) - shifts[0] * shift_one
    ) / gains[0]
    grad_qkv = grad_qkv.astype(BF)

    bias_grad = lax.dot_general(
        one_hot, grad_pattern[:, 0, :tok], (((1,), (1,)), ((), ())),
        precision=HIGHEST, preferred_element_type=F32,
    )
    table_grad = lax.dynamic_update_slice(
        jnp.zeros((BUCKETS, H), F32), bias_grad, (0, head_block * heads)
    )

    def by_device(*vectors):
        return jnp.stack(vectors).reshape(2, devices, n_gain).transpose(1, 0, 2).reshape(devices, -1)

    small_grad = jnp.concatenate(
        [
            table_grad.reshape(devices, n_bias),
            by_device(gain_one, gain_two),
            by_device(shift_one, shift_two),
            jnp.zeros((devices, LANES - n_small), F32),
        ],
        axis=1,
    )
    weights = (w_qkv, w_proj, w_up, w_down, small_weights)
    early_rows, added, sum_qkv, wide_sum, small_sum, totals = sums(
        shape, n_bias, n_gain, first, grad_qkv, small_grad, wide_parts, weights
    )
    small_like = [rel_bias[None, :], ln_gain, ln_shift]
    updates_total, grad_norm, param_norms, *results = optimizer(
        shape, n_bias, n_gain, me[None].astype(jnp.int32), totals, small_sum,
        (sum_qkv, wide_sum), weights,
        (mean_qkv, mean_proj, mean_up, mean_down, pack(mean_bias, mean_gain, mean_shift)),
        (square_qkv, square_proj, square_up, square_down, pack(square_bias, square_gain, square_shift)),
        small_like,
    )
    added, _ = lax.optimization_barrier((added, updates_total))
    grad_tokens = finish_rows(shape, added, early_rows, tokens, grad_middle, gains[0:1])
    new = [array if n % 7 != 4 else array[0] for group in results for n, array in enumerate(group)]
    return (block_out, grad_tokens, grad_norm[0, 0], param_norms, *new)


def solution(mesh):
    shape = {"xy": mesh.shape["dp"] // 2, "core": 2, "zh": 2, "zl": mesh.shape["tensor"] // 2}
    split_mesh = Mesh(mesh.devices.reshape(tuple(shape[axis] for axis in ALL)), ALL)
    weights = (
        P(None, DP, TENSOR),
        P(TENSOR, DP),
        P(DP, TENSOR),
        P(TENSOR, DP),
        P(ALL),
        P(None, ALL),
        P(None, ALL),
    )
    rows = P(ALL, None)
    return jax.shard_map(
        functools.partial(per_device, shape),
        mesh=split_mesh,
        in_specs=(rows, rows, P(DP, None), P(), *weights, *weights, *weights),
        out_specs=(rows, rows, P(), P(), *weights, *weights, *weights),
        check_vma=False,
    )
```

```python
import functools
import math

import jax
import jax.numpy as jnp
from jax import lax
from jax.experimental import pallas as pl
from jax.experimental.pallas import tpu as pltpu
from jax.sharding import Mesh
from jax.sharding import PartitionSpec as P

H = 16
DH = 64
BUCKETS = 32
BLK = 512
NEG = -1e30
LOG2E = 1.4426950408889634
F32 = jnp.float32
BF = jnp.bfloat16
MESH = pl.DeviceIdType.MESH
HIGHEST = lax.Precision.HIGHEST
ALL = ("xy", "core", "zh", "zl")
DP = ("xy", "core")
TENSOR = ("zh", "zl")


def dot(left, right, left_dim, right_dim):
    return lax.dot_general(
        left, right, (((left_dim,), (right_dim,)), ((), ())), preferred_element_type=F32
    )


def project_kernel(x_ref, norm_ref, w_ref, a_ref, qkv_ref, turned):
    @pl.when(pl.program_id(0) == 0)
    def _():
        for c in range(3):
            turned[c] = w_ref[c].T

    values = x_ref[...].astype(F32)
    center = values - jnp.mean(values, axis=-1, keepdims=True)
    inverse = lax.rsqrt(jnp.mean(center * center, axis=-1, keepdims=True) + 1e-05)
    a_ref[...] = (center * inverse * norm_ref[0:1, :] + norm_ref[1:2, :]).astype(BF)
    for c in range(3):
        qkv_ref[c] = dot(turned[c], a_ref[...], 1, 1).astype(BF)


def project(rows, norm, weights):
    tok, width = rows.shape
    cols = weights.shape[2]
    return pl.pallas_call(
        project_kernel,
        grid=(tok // BLK,),
        in_specs=[
            pl.BlockSpec((BLK, width), lambda s: (s, 0)),
            pl.BlockSpec((2, width), lambda s: (0, 0)),
            pl.BlockSpec((3, width, cols), lambda s: (0, 0, 0)),
        ],
        out_specs=[
            pl.BlockSpec((BLK, width), lambda s: (s, 0)),
            pl.BlockSpec((3, cols, BLK), lambda s: (0, 0, s)),
        ],
        out_shape=[
            jax.ShapeDtypeStruct((tok, width), BF),
            jax.ShapeDtypeStruct((3, cols, tok), BF),
        ],
        scratch_shapes=[pltpu.VMEM((3, cols, width), BF)],
        compiler_params=pltpu.CompilerParams(vmem_limit_bytes=62 * 2**20),
        name="project",
    )(rows, norm, weights)


def project_back_kernel(a_ref, grads_ref, w_ref, first_ref, grad_ref, sums_ref, low_ref, total, turned):
    step = pl.program_id(0)

    @pl.when(step == 0)
    def _():
        total[...] = jnp.zeros_like(total)
        sums_ref[...] = jnp.zeros_like(sums_ref)
        for c in range(3):
            turned[c] = w_ref[c].T

    first = jnp.zeros(first_ref.shape, F32)
    for c in range(3):
        grads = grads_ref[c]
        first = first + dot(grads.T, turned[c], 1, 0)
        total[c] += dot(grads, a_ref[...], 1, 0)
        sums_ref[c] += jnp.sum(grads.astype(F32), axis=1, keepdims=True)
    first_ref[...] = first.astype(BF)

    @pl.when(step == pl.num_programs(0) - 1)
    def _():
        for c in range(3):
            grad = total[c].T
            grad_ref[c] = grad.astype(BF)
            low_ref[:, c : c + 1] = jnp.sum(grad * w_ref[c].astype(F32), axis=1, keepdims=True)


def project_back(a_first, grads, weights):
    tok, width = a_first.shape
    cols = grads.shape[1]
    return pl.pallas_call(
        project_back_kernel,
        grid=(tok // BLK,),
        in_specs=[
            pl.BlockSpec((BLK, width), lambda s: (s, 0)),
            pl.BlockSpec((3, cols, BLK), lambda s: (0, 0, s)),
            pl.BlockSpec((3, width, cols), lambda s: (0, 0, 0)),
        ],
        out_specs=[
            pl.BlockSpec((BLK, width), lambda s: (s, 0)),
            pl.BlockSpec((3, width, cols), lambda s: (0, 0, 0)),
            pl.BlockSpec((3, cols, 1), lambda s: (0, 0, 0)),
            pl.BlockSpec((width, 3), lambda s: (0, 0)),
        ],
        out_shape=[
            jax.ShapeDtypeStruct((tok, width), BF),
            jax.ShapeDtypeStruct((3, width, cols), BF),
            jax.ShapeDtypeStruct((3, cols, 1), F32),
            jax.ShapeDtypeStruct((width, 3), F32),
        ],
        scratch_shapes=[pltpu.VMEM((3, cols, width), F32), pltpu.VMEM((3, cols, width), BF)],
        compiler_params=pltpu.CompilerParams(vmem_limit_bytes=62 * 2**20),
        name="project_back",
    )(a_first, grads, weights)


def make_slab(pattern, slab):
    width = slab.shape[1]
    slab[0:8, :] = pltpu.roll(jnp.broadcast_to(pattern, (8, width)), 0, 1, stride=1, stride_axis=0)
    done = 8
    while done < slab.shape[0]:
        slab[done : 2 * done, :] = pltpu.roll(slab[0:done, :], done, 1)
        done *= 2


def fold_slab(slab):
    width = slab.shape[1]
    half = slab.shape[0] // 2
    while half >= 8:
        slab[0:half, :] = slab[0:half, :] + pltpu.roll(slab[half : 2 * half, :], width - half, 1)
        half //= 2
    total = slab[0:1, :]
    for row in range(1, 8):
        total = total + pltpu.roll(slab[row : row + 1, :], width - row, 1)
    return total


def split_three(values):
    high = values.astype(BF).astype(F32)
    rest = values - high
    middle = rest.astype(BF).astype(F32)
    return high, middle, (rest - middle).astype(BF).astype(F32)


def put_queries(queries, split, minus, tok, dst):
    scaled = queries.astype(F32) * (DH**-0.5 * LOG2E)
    high = scaled.astype(BF)
    dst[0:DH, :] = high
    dst[DH : 2 * DH, :] = (scaled - high.astype(F32)).astype(BF)
    position = lax.broadcasted_iota(jnp.int32, (16, tok), 1)
    row = lax.broadcasted_iota(jnp.int32, (16, tok), 0)
    extra = jnp.where((row == 0) & (position >= split), 1.0, 0.0)
    if minus is not None:
        first, second, third = split_three(minus)
        extra = jnp.where(
            row == 1, first, jnp.where(row == 2, second, jnp.where(row == 3, third, extra))
        )
    dst[2 * DH : 2 * DH + 16, :] = extra.astype(BF)


def put_keys(keys, split, tok, dst):
    for start in range(0, tok, BLK):
        position = start + lax.broadcasted_iota(jnp.int32, (16, BLK), 1)
        row = lax.broadcasted_iota(jnp.int32, (16, BLK), 0)
        extra = jnp.where(
            row == 0, jnp.where(position < split, NEG, 0.0), jnp.where(row < 4, 1.0, 0.0)
        )
        block = keys[:, start : start + BLK].astype(F32)
        whole = jnp.concatenate([block, block, extra], axis=0)
        dst[start : start + BLK, :] = whole.T.astype(BF)


def block_at(index):
    return pl.ds(pl.multiple_of(index * BLK, BLK), BLK)


def attend_kernel(
    shape, split_ref, pattern_ref, q_ref, k_ref, v_ref, out_ref, rows_ref, lse_ref,
    slab, kx, qx, outs, local_sem, send_sem, recv_sem,
):
    head = pl.program_id(0)
    tok = q_ref.shape[1]
    split = split_ref[0]
    trade = Trade(shape, tok)

    @pl.when(head == 0)
    def _():
        greet_column(shape)

    make_slab(pattern_ref[0], slab)
    put_queries(q_ref[...], split, None, tok, qx)
    put_keys(k_ref, split, tok, kx)

    def steps(i, blocks, top, total, out):
        scores = [
            dot(kx[block_at(j), :], qx[:, block_at(i)], 1, 0) + slab[:, block_at(i - j)] for j in blocks
        ]
        new_top = top
        for score in scores:
            new_top = jnp.maximum(new_top, jnp.max(score, axis=0, keepdims=True))
        scale = jnp.exp2(top - new_top)
        total, out = total * scale, out * scale
        for j, score in zip(blocks, scores):
            weights = jnp.exp2(score - new_top)
            total = total + jnp.sum(weights, axis=0, keepdims=True)
            out = out + dot(v_ref[:, block_at(j)], weights.astype(BF), 1, 0)
        return new_top, total, out

    def row(i, carry):
        start = (
            jnp.full((1, BLK), NEG, F32),
            jnp.zeros((1, BLK), F32),
            jnp.zeros((DH, BLK), F32),
        )
        pairs = lax.fori_loop(
            0, (i + 1) // 2, lambda t, c: steps(i, (i - 2 * t, i - 2 * t - 1), *c), start
        )
        top, total, out = lax.fori_loop(0, (i + 1) % 2, lambda t, c: steps(i, (0,), *c), pairs)
        outs[head, :, block_at(i)] = (out / total).astype(BF)
        lse_ref[0, :, block_at(i)] = top + jnp.log2(total)
        return carry

    lax.fori_loop(0, tok // BLK, row, 0)

    def keep(h):
        return pltpu.make_async_copy(outs.at[h], out_ref.at[h], local_sem.at[0, h])

    def piece(h, n):
        return outs.at[h, :, pl.ds(pl.multiple_of(n * trade.rows, trade.rows), trade.rows)]

    def slot(h, n):
        return rows_ref.at[n, h]

    keep(head).start()
    trade.give(head, piece, slot, trade.owner, trade.head, local_sem.at[1, head], send_sem, recv_sem)

    @pl.when(head == pl.num_programs(0) - 1)
    def _():
        for h in range(rows_ref.shape[1]):
            keep(h).wait()
            trade.given(h, piece, slot, trade.owner, trade.head, local_sem.at[1, h], send_sem, recv_sem)
            trade.take(h, piece, slot, trade.header, send_sem, recv_sem)


def attend(shape, qkv, pattern, split, heads):
    tok = qkv.shape[1]
    width = pattern.shape[-1]
    parts = shape["zh"] * shape["zl"]
    dma = pltpu.SemaphoreType.DMA
    return pl.pallas_call(
        functools.partial(attend_kernel, shape),
        grid=(heads,),
        in_specs=[
            pl.BlockSpec(memory_space=pltpu.SMEM),
            pl.BlockSpec((1, 1, width), lambda h: (h, 0, 0)),
            pl.BlockSpec((DH, tok), lambda h: (h, 0)),
            pl.BlockSpec((DH, tok), lambda h: (h + heads, 0)),
            pl.BlockSpec((DH, tok), lambda h: (h + 2 * heads, 0)),
        ],
        out_specs=[
            pl.BlockSpec(memory_space=pl.ANY),
            pl.BlockSpec(memory_space=pl.ANY),
            pl.BlockSpec((1, 1, tok), lambda h: (h, 0, 0)),
        ],
        out_shape=[
            jax.ShapeDtypeStruct((heads, DH, tok), BF),
            jax.ShapeDtypeStruct((parts, heads, DH, tok // parts), BF),
            jax.ShapeDtypeStruct((heads, 1, tok), F32),
        ],
        scratch_shapes=[
            pltpu.VMEM((BLK, width), F32),
            pltpu.VMEM((tok, 2 * DH + 16), BF),
            pltpu.VMEM((2 * DH + 16, tok), BF),
            pltpu.VMEM((heads, DH, tok), BF),
            dma((2, heads)),
            dma((heads, parts)),
            dma((heads, parts)),
        ],
        compiler_params=pltpu.CompilerParams(
            vmem_limit_bytes=56 * 2**20, collective_id=0, has_side_effects=True
        ),
        name="attend",
    )(split, pattern, qkv, qkv, qkv)


def attend_back_kernel(
    shape, segments, split_ref, pattern_ref, q_ref, k_ref, v_ref, o_ref, lse_ref, given_ref, wide_ref,
    grads_ref, wide_parts_ref, dpattern_ref,
    slab, dslab, kx, qx, vx, dox, qn, don, dk, dv, taken, wide_own, wide_in,
    local_sem, in_send, in_recv, wide_sem, z_send, z_recv, w_send, w_recv,
):
    head = pl.program_id(0)
    tok = q_ref.shape[1]
    split = split_ref[0]
    trade = Trade(shape, tok)
    heads = taken.shape[0]

    def in_piece(h, n):
        return given_ref.at[n, h]

    def in_slot(h, n):
        return taken.at[h, :, pl.ds(pl.multiple_of(n * trade.rows, trade.rows), trade.rows)]

    xy, core, zh, zl = trade.me
    side = math.isqrt(shape["xy"])

    def column_copies():
        at = (lax.div(xy, side), lax.rem(xy, side))
        for step in range(1, side):
            for n, (distance, start, count, axis) in enumerate(segments):
                there = lax.rem(at[axis] + step, side)
                column = there * side + at[1] if axis == 0 else at[0] * side + there
                part = lax.rem(trade.row + distance, trade.parts)
                here = pl.ds(pl.multiple_of(part * wide_parts_ref.shape[2] + start, 128), count)
                yield send(
                    wide_ref.at[step, :, here], wide_in.at[step - 1, :, here],
                    w_send.at[step - 1, n], w_recv.at[step - 1, n], (column, core, zh, zl),
                )

    bring = pltpu.make_async_copy(wide_ref.at[0], wide_own, wide_sem.at[1])

    @pl.when(head == 0)
    def _():
        greet(shape)
        bring.start()
        for copy in column_copies():
            copy.start()
        for h in range(heads):
            trade.give(
                h, in_piece, in_slot, trade.header, trade.row, local_sem.at[h], in_send, in_recv
            )

    size = wide_parts_ref.shape[2]

    def wide_part(n):
        return wide_own.at[:, pl.ds(pl.multiple_of(n * size, size), size)]

    def along_z(step):
        there = lax.rem(trade.row + step, trade.parts)
        return there, (
            trade.me[0], trade.me[1], lax.div(there, trade.places), lax.rem(there, trade.places),
        )

    def wide_copy(step):
        there, device = along_z(step)
        return send(
            wide_part(there), wide_parts_ref.at[trade.row], z_send.at[step], z_recv.at[trade.row], device
        )

    keep_wide = pltpu.make_async_copy(
        wide_part(trade.row), wide_parts_ref.at[trade.row], wide_sem.at[0]
    )

    @pl.when(head == min(1, heads - 1))
    def _():
        bring.wait()
        for copy in column_copies():
            copy.wait_recv()
            copy.wait_send()
        for n in range(trade.parts):
            here = slice(n * size, (n + 1) * size)
            total = wide_own[:, here].astype(F32)
            for step in range(side - 1):
                total = total + wide_in[step, :, here].astype(F32)
            wide_own[:, here] = total.astype(BF)
        keep_wide.start()
        for step in range(1, trade.parts):
            wide_copy(step).start()

    make_slab(pattern_ref[0], slab)
    put_queries(q_ref[...], split, -lse_ref[0], tok, qx)
    put_keys(k_ref, split, tok, kx)
    dslab[...] = jnp.zeros_like(dslab)
    dk[...] = jnp.zeros_like(dk)
    dv[...] = jnp.zeros_like(dv)
    row = lax.broadcasted_iota(jnp.int32, (16, BLK), 0)
    ones = jnp.where(row < 3, 1.0, 0.0)
    trade.given(
        head, in_piece, in_slot, trade.header, trade.row, local_sem.at[head], in_send, in_recv
    )
    trade.take(head, in_piece, in_slot, trade.owner, in_send, in_recv)
    for start in range(0, tok, BLK):
        here = slice(start, start + BLK)
        low_grad = taken[head, :, here]
        grad = low_grad.astype(F32)
        inner = jnp.sum(grad * o_ref[0, :, here].astype(F32), axis=0, keepdims=True)
        first, second, third = split_three(-inner)
        extra = jnp.where(
            row == 0, first, jnp.where(row == 1, second, jnp.where(row == 2, third, 0.0))
        )
        dox[0:DH, here] = low_grad
        dox[DH : DH + 16, here] = extra.astype(BF)
        vx[here, :] = jnp.concatenate([v_ref[:, here].astype(F32), ones], axis=0).T.astype(BF)
        both = jnp.concatenate([q_ref[:, here].astype(F32), grad], axis=0).T
        qn[here, :] = both[:, 0:DH].astype(BF)
        don[here, :] = both[:, DH : 2 * DH].astype(BF)

    def tile(i, j):
        qs, ks, diagonal = block_at(i), block_at(j), block_at(i - j)
        shares = jnp.exp2(dot(kx[ks, :], qx[:, qs], 1, 0) + slab[:, diagonal])
        grad_scores = shares * dot(vx[ks, :], dox[:, qs], 1, 0)
        dslab[:, diagonal] += grad_scores
        low = grad_scores.astype(BF)
        dv[ks, :] += dot(shares.astype(BF), don[qs, :], 1, 0)
        dk[ks, :] += dot(low, qn[qs, :], 1, 0)
        return dot(k_ref[:, ks], low, 1, 0)

    def query_row(i, carry):
        total = lax.fori_loop(
            0,
            (i + 1) // 2,
            lambda t, c: c + tile(i, i - 2 * t) + tile(i, i - 2 * t - 1),
            jnp.zeros((DH, BLK), F32),
        )
        total = lax.fori_loop(0, (i + 1) % 2, lambda t, c: c + tile(i, 0), total)
        grads_ref[0, 0, :, block_at(i)] = (total * DH**-0.5).astype(BF)
        return carry

    lax.fori_loop(0, tok // BLK, query_row, 0)
    for start in range(0, tok, BLK):
        here = slice(start, start + BLK)
        grads_ref[1, 0, :, here] = (dk[here, :] * DH**-0.5).T.astype(BF)
        grads_ref[2, 0, :, here] = dv[here, :].T.astype(BF)
    dpattern_ref[0] = fold_slab(dslab)

    @pl.when(head == heads - 1)
    def _():
        keep_wide.wait()
        for step in range(1, trade.parts):
            there, device = along_z(step)
            here = wide_parts_ref.at[there]
            wide_copy(step).wait_send()
            send(here, here, z_send.at[step], z_recv.at[there], device).wait_recv()


def attend_back(shape, segments, qkv, out, given, wide, lse, pattern, split, heads):
    tok = qkv.shape[1]
    width = pattern.shape[-1]
    parts = shape["zh"] * shape["zl"]
    anywhere = pl.BlockSpec(memory_space=pl.ANY)
    dma = pltpu.SemaphoreType.DMA
    return pl.pallas_call(
        functools.partial(attend_back_kernel, shape, segments),
        grid=(heads,),
        in_specs=[
            pl.BlockSpec(memory_space=pltpu.SMEM),
            pl.BlockSpec((1, 1, width), lambda h: (h, 0, 0)),
            pl.BlockSpec((DH, tok), lambda h: (h, 0)),
            pl.BlockSpec((DH, tok), lambda h: (h + heads, 0)),
            pl.BlockSpec((DH, tok), lambda h: (h + 2 * heads, 0)),
            pl.BlockSpec((1, DH, tok), lambda h: (h, 0, 0)),
            pl.BlockSpec((1, 1, tok), lambda h: (h, 0, 0)),
            anywhere,
            anywhere,
        ],
        out_specs=[
            pl.BlockSpec((3, 1, DH, tok), lambda h: (0, h, 0, 0)),
            anywhere,
            pl.BlockSpec((1, 1, width), lambda h: (h, 0, 0)),
        ],
        out_shape=[
            jax.ShapeDtypeStruct((3, heads, DH, tok), BF),
            jax.ShapeDtypeStruct((parts, wide.shape[1], wide.shape[2] // parts), BF),
            jax.ShapeDtypeStruct((heads, 1, width), F32),
        ],
        scratch_shapes=[
            pltpu.VMEM((BLK, width), F32),
            pltpu.VMEM((BLK, width), F32),
            pltpu.VMEM((tok, 2 * DH + 16), BF),
            pltpu.VMEM((2 * DH + 16, tok), BF),
            pltpu.VMEM((tok, DH + 16), BF),
            pltpu.VMEM((DH + 16, tok), BF),
            pltpu.VMEM((tok, DH), BF),
            pltpu.VMEM((tok, DH), BF),
            pltpu.VMEM((tok, DH), F32),
            pltpu.VMEM((tok, DH), F32),
            pltpu.VMEM((heads, DH, tok), BF),
            pltpu.VMEM(wide.shape[1:], BF),
            pltpu.VMEM((wide.shape[0] - 1, *wide.shape[1:]), BF),
            dma((heads,)),
            dma((heads, parts)),
            dma((heads, parts)),
            dma((2,)), dma((parts,)), dma((parts,)),
            *[dma((wide.shape[0] - 1, len(segments)))] * 2,
        ],
        compiler_params=pltpu.CompilerParams(
            vmem_limit_bytes=60 * 2**20, collective_id=1, has_side_effects=True
        ),
        name="attend_back",
    )(split, pattern, qkv, qkv, qkv, out, lse, given, wide)


def place():
    return tuple(lax.axis_index(axis) for axis in ALL)


class Trade:
    def __init__(self, shape, tok):
        self.places = shape["zl"]
        self.parts = shape["zh"] * self.places
        self.rows = tok // self.parts
        self.me = place()
        _, core, zh, zl = self.me
        self.row = zh * self.places + zl
        self.head = zl * 2 + core

    def owner(self, n):
        return (self.me[0], self.me[2], lax.div(n, self.places), lax.rem(n, self.places))

    def header(self, n):
        return (self.me[0], lax.rem(n, 2), self.me[1], lax.div(n, 2))

    def each(self, device_of, local, remote):
        for index in range(self.parts):
            n = jnp.where(self.me[2] == 1, index, self.parts - 1 - index)
            device = device_of(n)
            if local is not None:

                @pl.when(is_same(device, self.me))
                def _():
                    local(n)

            @pl.when(jnp.logical_not(is_same(device, self.me)))
            def _():
                remote(n, device)

    def give(self, h, piece, slot, device_of, mine, local_sem, send_sem, recv_sem):
        def local(n):
            pltpu.make_async_copy(piece(h, n), slot(h, mine), local_sem).start()

        def remote(n, device):
            send(piece(h, n), slot(h, mine), send_sem.at[h, n], recv_sem.at[h, mine], device).start()

        self.each(device_of, local, remote)

    def given(self, h, piece, slot, device_of, mine, local_sem, send_sem, recv_sem):
        def local(n):
            pltpu.make_async_copy(piece(h, n), slot(h, mine), local_sem).wait()

        def remote(n, device):
            send(piece(h, n), slot(h, mine), send_sem.at[h, n], recv_sem.at[h, mine], device).wait_send()

        self.each(device_of, local, remote)

    def take(self, h, piece, slot, device_of, send_sem, recv_sem):
        def remote(n, device):
            send(piece(h, n), slot(h, n), send_sem.at[h, n], recv_sem.at[h, n], device).wait_recv()

        self.each(device_of, None, remote)


def is_same(left, right):
    same = left[0] == right[0]
    for one, other in zip(left[1:], right[1:]):
        same = same & (one == other)
    return same


def column_peers(shape, device):
    xy, core, zh, zl = device
    places = shape["zl"]
    total = 4 * places
    mine = (core * 2 + zh) * places + zl
    for step in range(1, total):
        there = lax.rem(mine + step, total)
        yield step, there, (xy, there // (2 * places), lax.rem(there // places, 2), lax.rem(there, places))


def plane_peers(shape, device):
    xy, core, zh, zl = device
    for step in range(1, shape["xy"]):
        there = lax.rem(xy + step, shape["xy"])
        yield step, there, (there, core, zh, zl)


def greet(shape):
    device = place()
    barrier = pltpu.get_barrier_semaphore()
    peers = [peer for _, _, peer in column_peers(shape, device)]
    peers += [peer for _, _, peer in plane_peers(shape, device)]
    for peer in peers:
        pl.semaphore_signal(barrier, inc=1, device_id=peer, device_id_type=MESH)
    pl.semaphore_wait(barrier, len(peers))


def greet_column(shape):
    barrier = pltpu.get_barrier_semaphore()
    peers = [peer for _, _, peer in column_peers(shape, place())]
    for peer in peers:
        pl.semaphore_signal(barrier, inc=1, device_id=peer, device_id_type=MESH)
    pl.semaphore_wait(barrier, len(peers))


def send(src, dst, send_sem, recv_sem, device):
    return pltpu.make_async_remote_copy(
        src_ref=src, dst_ref=dst, send_sem=send_sem, recv_sem=recv_sem,
        device_id=device, device_id_type=MESH,
    )


CHUNKS = 4


def gather_kernel(
    shape, tokens_ref, wq_ref, small_ref, wide_ref, rows_ref, heads_ref, all_small_ref, all_wide_ref,
    local_sems, in_send, fwd_send, share_send, x_recv, xs_recv,
    z_send, z_recv, p_send, p_recv, s_send, s_recv, w_send, w_recv, q_send, q_recv,
):
    me = place()
    xy, core, zh, zl = me
    places = shape["zl"]
    parts = 2 * places
    columns = shape["xy"]
    z = zh * places + zl
    sibling = (xy, 1 - core, zh, zl)
    size = tokens_ref.shape[0] // (2 * CHUNKS)
    dp = xy * 2 + core
    inside = core == zh
    outside = jnp.logical_not(inside)
    entry = jnp.where(zh < core, 0, places - 1)

    def chunk_of(ref, half, chunk):
        return ref.at[pl.ds(pl.multiple_of((half * CHUNKS + chunk) * size, size), size), :]

    def beside(step):
        there = z + step
        return (xy, core, there // places, lax.rem(there, places))

    greet(shape)

    depth = wq_ref.shape[1]
    head_block = zl * 2 + core

    def depth_of(index, count):
        return heads_ref.at[:, pl.ds(pl.multiple_of(index * depth, depth), count * depth), :]

    def wq_target(half):
        return (xy, lax.rem(z, 2), half, lax.div(z, 2))

    def wq_source(c):
        return (xy, c, lax.div(head_block, places), lax.rem(head_block, places))

    own_wq = pltpu.make_async_copy(wq_ref, depth_of(dp, 1), local_sems.at[1])
    own_small = pltpu.make_async_copy(small_ref, all_small_ref.at[dp, z], local_sems.at[2])

    def wide_at(shard, device_z):
        return all_wide_ref.at[lax.rem(shard + parts - device_z, parts) - 1]

    own_small.start()
    for n in range(2):

        @pl.when(is_same(wq_target(n), me))
        def _():
            own_wq.start()

        @pl.when(jnp.logical_not(is_same(wq_target(n), me)))
        def _():
            send(wq_ref, depth_of(dp, 1), q_send.at[n], q_recv.at[core], wq_target(n)).start()

    for step in range(1, parts):
        there = lax.rem(z + step, parts)
        device = (xy, core, there // places, lax.rem(there, places))
        send(small_ref, all_small_ref.at[dp, z], z_send.at[step], z_recv.at[z], device).start()

    @pl.when(outside)
    def _():
        for chunk in range(CHUNKS):
            for half in range(2):
                send(
                    chunk_of(tokens_ref, half, chunk), chunk_of(rows_ref.at[z], half, chunk),
                    in_send.at[half, chunk], x_recv.at[z, chunk], (xy, half, core, entry),
                ).start()

    @pl.when(inside)
    def _():
        for chunk in range(CHUNKS):
            send(
                chunk_of(tokens_ref, 1 - core, chunk), chunk_of(rows_ref.at[z], 1 - core, chunk),
                in_send.at[0, chunk], x_recv.at[z, chunk], sibling,
            ).start()
        pltpu.make_async_copy(tokens_ref, rows_ref.at[z], local_sems.at[0]).start()

    def ways(shard):
        from_half, from_place = shard // places, lax.rem(shard, places)
        start = jnp.where(from_half == zh, from_place, jnp.where(from_half < zh, 0, places - 1))
        return (zl >= start) & (zl < places - 1), (zl <= start) & (zl > 0)

    def pass_on(shard, chunk, source):
        mine = chunk_of(rows_ref.at[shard], core, chunk)
        for n, (way, step) in enumerate(zip(ways(shard), (1, -1))):

            @pl.when(way)
            def _():
                send(
                    source, mine, fwd_send.at[n, shard, chunk], x_recv.at[shard, chunk],
                    (xy, core, zh, zl + step),
                ).start()

    def share(shard, chunk, source):
        mine = chunk_of(rows_ref.at[shard], core, chunk)
        send(source, mine, share_send.at[shard, chunk], xs_recv.at[shard, chunk], sibling).start()

    def got(shard, chunk):
        mine = chunk_of(rows_ref.at[shard], core, chunk)
        send(mine, mine, share_send.at[shard, chunk], x_recv.at[shard, chunk], sibling).wait_recv()

    @pl.when(inside)
    def _():
        for chunk in range(CHUNKS):
            mine = chunk_of(tokens_ref, core, chunk)
            pass_on(z, chunk, mine)
            share(z, chunk, mine)

    for n, step in enumerate((1, -1)):

        @pl.when((z + step >= 0) & (z + step < parts))
        def _():
            send(
                wide_ref, wide_at(z, z + step), w_send.at[n, z], w_recv.at[z], beside(step)
            ).start()

    @pl.when(outside)
    def _():
        for chunk in range(CHUNKS):
            got(z, chunk)
            pass_on(z, chunk, chunk_of(rows_ref.at[z], core, chunk))

    def arrays_at(column):
        return depth_of(column * 2, 2), all_small_ref.at[column * 2 + core]

    def spread():
        own_small.wait()
        for step in range(1, parts):
            there = lax.rem(z + step, parts)
            send(small_ref, all_small_ref.at[dp, there], z_send.at[step], z_recv.at[there], sibling).wait_recv()
        for c in range(2):

            @pl.when(is_same(wq_source(c), me))
            def _():
                own_wq.wait()

            @pl.when(jnp.logical_not(is_same(wq_source(c), me)))
            def _():
                here = depth_of(xy * 2 + c, 1)
                send(here, here, q_send.at[0], q_recv.at[c], wq_source(c)).wait_recv()

        for step, there, device in plane_peers(shape, me):
            for n, ref in enumerate(arrays_at(xy)):
                send(ref, ref, p_send.at[n, step], p_recv.at[n, xy], device).start()
        ref = all_small_ref.at[dp]
        send(ref, ref, s_send.at[xy], s_recv.at[xy], sibling).start()

    for distance in range(1, parts):
        for chunk in range(CHUNKS):
            for shard in (z + distance, z - distance):

                @pl.when((shard >= 0) & (shard < parts))
                def _():
                    got(shard, chunk)
                    mine = chunk_of(rows_ref.at[shard], core, chunk)
                    pass_on(shard, chunk, mine)
                    share(shard, chunk, mine)

        if distance == 1:
            spread()
        for n, step in enumerate((1, -1)):
            shard = z - step * distance

            @pl.when((shard >= 0) & (shard < parts))
            def _():
                piece = wide_at(shard, z)
                send(piece, piece, w_send.at[n, shard], w_recv.at[shard], sibling).wait_recv()

            @pl.when((shard >= 0) & (shard < parts) & (z + step >= 0) & (z + step < parts))
            def _():
                send(
                    wide_at(shard, z), wide_at(shard, z + step), w_send.at[n, shard], w_recv.at[shard],
                    beside(step),
                ).start()

    for step in range(1, columns):
        there = lax.rem(xy + columns - step, columns)
        for n, ref in enumerate(arrays_at(there)):
            send(ref, ref, p_send.at[n, step], p_recv.at[n, there], sibling).wait_recv()
        ref = all_small_ref.at[there * 2 + core]
        send(ref, ref, s_send.at[there], s_recv.at[there], sibling).start()

    for column in range(columns):
        ref = all_small_ref.at[column * 2 + 1 - core]
        copy = send(ref, ref, s_send.at[column], s_recv.at[column], sibling)
        copy.wait_recv()
        copy.wait_send()
    for step in range(1, columns):
        for n, ref in enumerate(arrays_at(xy)):
            send(ref, ref, p_send.at[n, step], p_recv.at[n, xy], sibling).wait_send()
    for step in range(1, parts):
        send(small_ref, all_small_ref.at[dp, z], z_send.at[step], z_recv.at[z], sibling).wait_send()
    for n in range(2):

        @pl.when(jnp.logical_not(is_same(wq_target(n), me)))
        def _():
            send(wq_ref, depth_of(dp, 1), q_send.at[n], q_recv.at[core], sibling).wait_send()

    for n, step in enumerate((1, -1)):
        for distance in range(parts):
            shard = z - step * distance

            @pl.when((shard >= 0) & (shard < parts) & (z + step >= 0) & (z + step < parts))
            def _():
                send(
                    wide_ref, wide_ref, w_send.at[n, shard], w_recv.at[shard], beside(step)
                ).wait_send()

    for shard in range(parts):
        for chunk in range(CHUNKS):
            mine = chunk_of(rows_ref.at[shard], core, chunk)
            other = chunk_of(rows_ref.at[shard], 1 - core, chunk)
            copy = send(mine, other, share_send.at[shard, chunk], xs_recv.at[shard, chunk], sibling)

            @pl.when(jnp.logical_not((shard == z) & outside))
            def _():
                copy.wait_send()

            @pl.when(jnp.logical_not((shard == z) & inside))
            def _():
                copy.wait_recv()

            for n, way in enumerate(ways(shard)):

                @pl.when(way)
                def _():
                    send(
                        mine, mine, fwd_send.at[n, shard, chunk], x_recv.at[shard, chunk], sibling
                    ).wait_send()

    for chunk in range(CHUNKS):
        first = chunk_of(tokens_ref, 0, chunk)
        send(first, first, in_send.at[0, chunk], x_recv.at[z, chunk], sibling).wait_send()

        @pl.when(outside)
        def _():
            send(first, first, in_send.at[1, chunk], x_recv.at[z, chunk], sibling).wait_send()

    @pl.when(inside)
    def _():
        pltpu.make_async_copy(tokens_ref, rows_ref.at[z], local_sems.at[0]).wait()


def gather(shape, tokens, wq, small, wide):
    parts, columns = shape["zh"] * shape["zl"], shape["xy"]
    anywhere = pl.BlockSpec(memory_space=pl.ANY)
    dma = pltpu.SemaphoreType.DMA
    return pl.pallas_call(
        functools.partial(gather_kernel, shape),
        out_shape=[
            jax.ShapeDtypeStruct((parts, *tokens.shape), tokens.dtype),
            jax.ShapeDtypeStruct((3, 2 * columns * wq.shape[1], wq.shape[2]), wq.dtype),
            jax.ShapeDtypeStruct((2 * columns, parts, *small.shape), small.dtype),
            jax.ShapeDtypeStruct((parts - 1, *wide.shape), wide.dtype),
        ],
        in_specs=[anywhere] * 4,
        out_specs=[anywhere] * 4,
        scratch_shapes=[
            dma((3,)), dma((2, CHUNKS)), dma((2, parts, CHUNKS)), dma((parts, CHUNKS)),
            dma((parts, CHUNKS)), dma((parts, CHUNKS)),
            dma((parts,)), dma((parts,)), dma((2, columns)), dma((2, columns)), dma((columns,)),
            dma((columns,)), dma((2, parts)), dma((parts,)), dma((2,)), dma((2,)),
        ],
        compiler_params=pltpu.CompilerParams(collective_id=2, has_side_effects=True),
        name="gather",
    )(tokens, wq, small, wide)


class AllSum:
    def __init__(self, shape, column_slots, plane_slots, sems):
        self.shape, self.me = shape, place()
        self.slots, self.sems = (column_slots, plane_slots), sems
        xy, core, zh, zl = self.me
        self.mine = ((core * 2 + zh) * shape["zl"] + zl, xy)

    def peers(self, turn):
        return (column_peers if turn == 0 else plane_peers)(self.shape, self.me)

    def start(self, turn, value):
        slots, mine = self.slots[turn], self.mine[turn]
        slots[mine] = value
        for step, _, device in self.peers(turn):
            self.copy(turn, step, mine, device).start()

    def copy(self, turn, step, slot, device):
        here = self.slots[turn].at[slot]
        return send(
            here, here, self.sems.at[2 * turn, step], self.sems.at[2 * turn + 1, slot], device
        )

    def finish(self, turn):
        slots = self.slots[turn]
        for step, there, device in self.peers(turn):
            self.copy(turn, step, there, device).wait_recv()
        for step, _, device in self.peers(turn):
            self.copy(turn, step, self.mine[turn], device).wait_send()
        total = slots[0]
        for slot in range(1, slots.shape[0]):
            total = total + slots[slot]
        return total


LANES = 256


def lane_sums(values, ranges):
    lane = lax.broadcasted_iota(jnp.int32, values.shape, 1)
    return [
        jnp.sum(jnp.where((lane >= low) & (lane < high), values, 0.0)) for low, high in ranges
    ]


def small_ranges(n_bias, n_gain):
    ends = [0, n_bias] + [n_bias + n_gain * (n + 1) for n in range(4)]
    return list(zip(ends[:-1], ends[1:]))


def row_of(values):
    lane = lax.broadcasted_iota(jnp.int32, (1, 128), 1)
    row = jnp.zeros((1, 128), F32)
    for n, value in enumerate(values):
        row = jnp.where(lane == n, value, row)
    return row


class Rows:
    def __init__(self, shape):
        self.me = place()
        self.places = shape["zl"]

    def shard_at(self, index):
        return jnp.where(self.me[2] == 1, index, 2 * self.places - 1 - index)

    def early(self, group):
        return jnp.where(group == 1, 0, 2 * self.places - 1)

    def owner(self, shard):
        return (self.me[0], self.me[2], lax.div(shard, self.places), lax.rem(shard, self.places))

    def copy(self, src, dst, half, shard, send_sems, recv_sems):
        xy, core, zh, zl = self.me
        there = dst.at[zl, :, pl.ds(pl.multiple_of(core * half, half), half)]
        return send(src, there, send_sems.at[shard], recv_sems.at[zl, core], self.owner(shard))

    def take(self, dst, half, send_sems, recv_sems):
        xy, core, zh, zl = self.me
        for n in range(self.places):
            for c in range(2):
                here = dst.at[n, :, c * half : (c + 1) * half]
                copy = send(here, here, send_sems.at[0], recv_sems.at[n, c], (xy, c, core, n))

                @pl.when(jnp.logical_not(is_same((xy, c, core, n), self.me)))
                def _():
                    copy.wait_recv()


def sums_kernel(
    shape, n_bias, n_gain,
    first_ref, grad_qkv_ref, small_ref, parts_ref, wq_ref, wp_ref, wu_ref, wd_ref, ws_ref,
    rows_ref, added_ref, sum_ref, wide_ref, small_sum_ref, totals_ref,
    taken, added, plane, both, pieces, small_column, small_plane, row_column, row_plane,
    t_send, t_recv, o_send, o_recv, p_send, p_recv, q_send, q_recv, local_sems, small_sems, row_sems,
):
    me = place()
    xy, core, zh, zl = me
    places, columns = shape["zl"], shape["xy"]
    parts = 2 * places
    z = zh * places + zl
    sibling = (xy, 1 - core, zh, zl)
    head_block = zl * 2 + core
    rows, half = taken.shape[1], taken.shape[2]
    moves = Rows(shape)
    shard_at = moves.shard_at
    depth = both.shape[1] // 2
    small_all = AllSum(shape, small_column, small_plane, small_sems)
    row_all = AllSum(shape, row_column, row_plane, row_sems)

    def columns_at(which):
        return pl.ds(pl.multiple_of(which * half, half), half)

    def to_sibling(shard):
        part = first_ref.at[pl.ds(pl.multiple_of(shard * rows, rows), rows), columns_at(1 - core)]
        return send(part, taken.at[shard], t_send.at[shard], t_recv.at[shard], sibling)

    def to_owner():
        shard = shard_at(0)
        return moves.copy(added.at[shard], rows_ref, half, shard, o_send, o_recv)

    keep_added = pltpu.make_async_copy(added, added_ref, local_sems.at[0])

    def add_rows(index):
        shard = shard_at(index)
        to_sibling(shard).wait_recv()
        here = first_ref[pl.ds(pl.multiple_of(shard * rows, rows), rows), columns_at(core)]
        added[shard] = (here.astype(F32) + taken[shard].astype(F32)).astype(BF)

    def plane_part(column):
        return grad_qkv_ref.at[:, pl.ds(pl.multiple_of(column * 2 * depth, 2 * depth), 2 * depth), :]

    def target(c):
        return (xy, c, lax.div(head_block, places), lax.rem(head_block, places))

    def source(n):
        return (xy, lax.rem(z, 2), n, lax.div(z, 2))

    def part(c):
        return both.at[:, c * depth : (c + 1) * depth, :]

    greet(shape)
    to_sibling(shard_at(0)).start()
    small_all.start(0, small_ref[...])
    keep_part = pltpu.make_async_copy(plane_part(xy), plane.at[xy], local_sems.at[1])
    keep_part.start()
    for step, there, device in plane_peers(shape, me):
        send(plane_part(there), plane.at[xy], p_send.at[step], p_recv.at[xy], device).start()
    for index in range(1, parts):
        to_sibling(shard_at(index)).start()
    add_rows(0)
    to_owner().start()

    def square(values):
        wide = values.astype(F32)
        return jnp.sum(wide * wide)

    wide = parts_ref[0].astype(F32)
    for n in range(1, parts):
        wide = wide + parts_ref[n].astype(F32)
    wide_ref[...] = wide
    up, down, proj = parts_of(wide_ref, wu_ref, wp_ref)
    values = [square(proj), square(up), square(down)]
    values += [square(wq_ref[c]) for c in range(3)]
    values += [square(ref[...]) for ref in (wp_ref, wu_ref, wd_ref)]
    ranges = small_ranges(n_bias, n_gain)
    values += lane_sums(ws_ref[...] * ws_ref[...], ranges)
    small_all.start(1, small_all.finish(0))

    keep_part.wait()
    for step, there, device in plane_peers(shape, me):
        send(plane_part(there), plane.at[there], p_send.at[step], p_recv.at[there], device).wait_recv()
    for c in range(3):
        total = plane[0, c].astype(F32)
        for n in range(1, columns):
            total = total + plane[n, c].astype(F32)
        both[c] = total.astype(BF)
    for c in range(2):

        @pl.when(is_same(target(c), me))
        def _():
            pltpu.make_async_copy(part(c), pieces.at[zh], local_sems.at[2]).start()

        @pl.when(jnp.logical_not(is_same(target(c), me)))
        def _():
            send(part(c), pieces.at[zh], q_send.at[c], q_recv.at[zh], target(c)).start()

    for index in range(1, parts):
        add_rows(index)
    keep_added.start()
    small = small_all.finish(1)
    small_sum_ref[...] = small
    for n in range(2):

        @pl.when(is_same(target(n), me))
        def _():
            pltpu.make_async_copy(part(n), pieces.at[zh], local_sems.at[2]).wait()

        @pl.when(jnp.logical_not(is_same(target(n), me)))
        def _():
            send(part(n), pieces.at[zh], q_send.at[n], q_recv.at[zh], target(n)).wait_send()

        @pl.when(jnp.logical_not(is_same(source(n), me)))
        def _():
            send(part(n), pieces.at[n], q_send.at[n], q_recv.at[n], source(n)).wait_recv()

    squares = []
    for c in range(3):
        total = pieces[0, c].astype(F32) + pieces[1, c].astype(F32)
        sum_ref[c] = total
        squares.append(square(total))
    row_all.start(0, row_of(squares + values))
    row_all.start(1, row_all.finish(0))
    row = row_all.finish(1)
    lane = lax.broadcasted_iota(jnp.int32, (1, 128), 1)
    for n, value in enumerate(lane_sums(small * small, ranges)):
        row = jnp.where(lane == 17 + n, value, row)
    totals_ref[...] = row

    for step, there, device in plane_peers(shape, me):
        send(plane_part(there), plane.at[xy], p_send.at[step], p_recv.at[xy], device).wait_send()
    for shard in range(parts):
        to_sibling(shard).wait_send()
    keep_added.wait()
    to_owner().wait_send()

    @pl.when(z == moves.early(core))
    def _():
        moves.take(rows_ref, half, o_send, o_recv)


def rows_kernel(
    shape, added_ref, early_ref, x_ref, middle_ref, gain_ref, out_ref,
    got, e_sem, keep_sem, o_send, o_recv,
):
    me = place()
    xy, core, zh, zl = me
    moves = Rows(shape)
    parts = added_ref.shape[0]
    half = added_ref.shape[2]
    z = zh * moves.places + zl
    is_early = z == moves.early(core)
    early = pltpu.make_async_copy(early_ref, got, e_sem)
    mine = got.at[zl, :, pl.ds(pl.multiple_of(core * half, half), half)]
    keep = pltpu.make_async_copy(added_ref.at[z], mine, keep_sem)

    def each(act):
        for index in range(1, parts):
            shard = moves.shard_at(index)

            @pl.when(jnp.logical_not(is_same(moves.owner(shard), me)))
            def _():
                act(moves.copy(added_ref.at[shard], got, half, shard, o_send, o_recv))

    greet_column(shape)
    each(lambda copy: copy.start())

    @pl.when(is_early)
    def _():
        early.start()

    @pl.when(zh == core)
    def _():
        keep.start()

    value, inverse = normed_of(x_ref[...].astype(F32))

    @pl.when(zh == core)
    def _():
        keep.wait()

    @pl.when(is_early)
    def _():
        early.wait()

    @pl.when(jnp.logical_not(is_early))
    def _():
        moves.take(got, half, o_send, o_recv)

    grad = got[0].astype(F32)
    for n in range(1, moves.places):
        grad = grad + got[n].astype(F32)
    inner = grad * gain_ref[...]
    out_ref[...] = (
        middle_ref[...]
        + inverse
        * (
            inner
            - jnp.mean(inner, axis=-1, keepdims=True)
            - value * jnp.mean(inner * value, axis=-1, keepdims=True)
        )
    ).astype(BF)
    each(lambda copy: copy.wait_send())


def finish_rows(shape, added, early, tokens, grad_middle, gain):
    places = shape["zl"]
    vmem = pl.BlockSpec(memory_space=pltpu.VMEM)
    anywhere = pl.BlockSpec(memory_space=pl.ANY)
    dma = pltpu.SemaphoreType.DMA
    return pl.pallas_call(
        functools.partial(rows_kernel, shape),
        out_shape=jax.ShapeDtypeStruct(tokens.shape, BF),
        in_specs=[anywhere, anywhere, vmem, vmem, vmem],
        out_specs=vmem,
        scratch_shapes=[
            pltpu.VMEM((places, *tokens.shape), BF),
            dma, dma, dma((2 * places,)), dma((places, 2)),
        ],
        compiler_params=pltpu.CompilerParams(
            collective_id=6, has_side_effects=True, vmem_limit_bytes=56 * 2**20
        ),
        name="finish_rows",
    )(added, early, tokens, grad_middle, gain)


def parts_of(wide_ref, up_like, proj_like):
    ff, heads = up_like.shape[1], proj_like.shape[0]
    return wide_ref[:, :ff], wide_ref[:, ff : 2 * ff], wide_ref[:, 2 * ff : 2 * ff + heads]


def sums(shape, n_bias, n_gain, first, grad_qkv, small, wide, weights):
    places, columns = shape["zl"], shape["xy"]
    members, parts = 4 * places, 2 * places
    rows, width = first.shape[0] // parts, first.shape[1]
    depth = grad_qkv.shape[1] // (2 * columns)
    heads_cols = grad_qkv.shape[2]
    vmem = pl.BlockSpec(memory_space=pltpu.VMEM)
    anywhere = pl.BlockSpec(memory_space=pl.ANY)
    dma = pltpu.SemaphoreType.DMA
    slots = max(members, columns)
    return pl.pallas_call(
        functools.partial(sums_kernel, shape, n_bias, n_gain),
        out_shape=[
            jax.ShapeDtypeStruct((places, rows, width), BF),
            jax.ShapeDtypeStruct((parts, rows, width // 2), BF),
            jax.ShapeDtypeStruct((3, depth, heads_cols), F32),
            jax.ShapeDtypeStruct(wide.shape[1:], F32),
            jax.ShapeDtypeStruct(small.shape, F32),
            jax.ShapeDtypeStruct((1, 128), F32),
        ],
        in_specs=[vmem, anywhere] + [vmem] * 7,
        out_specs=[anywhere] * 2 + [vmem] * 4,
        scratch_shapes=[
            pltpu.VMEM((parts, rows, width // 2), BF),
            pltpu.VMEM((parts, rows, width // 2), BF),
            pltpu.VMEM((columns, 3, 2 * depth, heads_cols), BF),
            pltpu.VMEM((3, 2 * depth, heads_cols), BF),
            pltpu.VMEM((2, 3, depth, heads_cols), BF),
            pltpu.VMEM((members, *small.shape), F32),
            pltpu.VMEM((columns, *small.shape), F32),
            pltpu.VMEM((members, 1, 128), F32),
            pltpu.VMEM((columns, 1, 128), F32),
            dma((parts,)), dma((parts,)), dma((parts,)), dma((places, 2)),
            dma((columns,)), dma((columns,)), dma((2,)), dma((2,)), dma((3,)),
            dma((4, slots)), dma((4, slots)),
        ],
        compiler_params=pltpu.CompilerParams(
            collective_id=3, has_side_effects=True, vmem_limit_bytes=56 * 2**20
        ),
        name="sums",
    )(first, grad_qkv, small, wide, *weights)


def reduce_kernel(shape, row_ref, total_ref, row_column, row_plane, row_sems):
    greet(shape)
    both = AllSum(shape, row_column, row_plane, row_sems)
    both.start(0, row_ref[...])
    both.start(1, both.finish(0))
    total_ref[...] = both.finish(1)


def reduce_row(shape, row):
    members = 4 * shape["zl"]
    vmem = pl.BlockSpec(memory_space=pltpu.VMEM)
    return pl.pallas_call(
        functools.partial(reduce_kernel, shape),
        out_shape=jax.ShapeDtypeStruct((1, 128), F32),
        in_specs=[vmem],
        out_specs=vmem,
        scratch_shapes=[
            pltpu.VMEM((members, 1, 128), F32),
            pltpu.VMEM((shape["xy"], 1, 128), F32),
            pltpu.SemaphoreType.DMA((4, max(members, shape["xy"]))),
        ],
        compiler_params=pltpu.CompilerParams(collective_id=4, has_side_effects=True),
        name="reduce_row",
    )(row)


def moments_kernel(
    n_bias, n_gain, spot_ref, totals_ref, small_ref,
    gq, wide, wq, wp, wu, wd, ws, mq, mp, mu, md, ms, sq, sp, su, sd, ss,
    nmq, nmp, nmu, nmd, nmb, nmg, nmt, nsq, nsp, nsu, nsd, nsb, nsg, nst, uq, up, uu, ud, us, row_ref,
):
    totals = totals_ref[...]
    lane = lax.broadcasted_iota(jnp.int32, (1, 128), 1)
    grads_here = (lane < 6) | ((lane >= 17) & (lane < 22))
    norm = jnp.sqrt(jnp.sum(jnp.where(grads_here, totals, 0.0), axis=1, keepdims=True))
    clip = jnp.minimum(1.0, 1.0 / norm)
    values = []

    def step(grad, weight, mean, square):
        scaled = clip * grad
        new_mean = 0.5 * mean + 0.5 * scaled
        new_square = 0.5 * square + 0.5 * scaled * scaled
        update = new_mean / (jnp.sqrt(new_square) + 1e-06) + 0.01 * weight
        return new_mean, new_square, update

    for c in range(3):
        nmq[c], nsq[c], update = step(gq[c], wq[c], mq[c], sq[c])
        uq[c] = update
        values.append(jnp.sum(update * update))
    grad_up, grad_down, grad_proj = parts_of(wide, wu, wp)
    for turned, g, w, m, s, nm, ns, u in (
        (True, grad_proj, wp, mp, sp, nmp, nsp, up),
        (False, grad_up, wu, mu, su, nmu, nsu, uu),
        (True, grad_down, wd, md, sd, nmd, nsd, ud),
    ):
        grad = g.astype(F32)
        nm[...], ns[...], update = step(grad.T if turned else grad, w[...], m[...], s[...])
        u[...] = update
        values.append(jnp.sum(update * update))
    spot = spot_ref[0]
    grad = small_ref[pl.ds(spot, 1), :]
    new_mean, new_square, update = step(grad, ws[...], ms[...], ss[...])
    us[...] = update
    ranges = small_ranges(n_bias, n_gain)
    values += lane_sums(update * update, ranges)
    row_ref[...] = row_of(values)
    put_small(ranges, new_mean, nmb, nmg, nmt)
    put_small(ranges, new_square, nsb, nsg, nst)


def put_small(ranges, row, bias, gain, shift):
    bias[...] = row[:, ranges[0][0] : ranges[0][1]]
    for n in range(2):
        gain[n : n + 1, :] = row[:, ranges[1 + n][0] : ranges[1 + n][1]]
        shift[n : n + 1, :] = row[:, ranges[3 + n][0] : ranges[3 + n][1]]


def weights_kernel(
    n_bias, n_gain, totals_ref, update_ref, wq, wp, wu, wd, ws, uq, up, uu, ud, us,
    nwq, nwp, nwu, nwd, nwb, nwg, nwt, norms_ref, norm_ref,
):
    totals, updates = totals_ref[...], update_ref[...]
    lane = lax.broadcasted_iota(jnp.int32, (1, 128), 1)
    grads_here = (lane < 6) | ((lane >= 17) & (lane < 22))
    norm_ref[...] = jnp.sqrt(jnp.sum(jnp.where(grads_here, totals, 0.0), axis=1, keepdims=True))
    weight_norm, update_norm = jnp.sqrt(totals), jnp.sqrt(updates)
    norms_ref[0:1, :] = weight_norm[:, 6:17]
    norms_ref[1:2, :] = update_norm[:, 0:11]

    def factor(n):
        return 0.3 * (weight_norm[:, 6 + n : 7 + n] / update_norm[:, n : n + 1])

    for c in range(3):
        nwq[c] = wq[c] - factor(c) * uq[c]
    for n, (w, u, out) in enumerate(((wp, up, nwp), (wu, uu, nwu), (wd, ud, nwd))):
        out[...] = w[...] - factor(3 + n) * u[...]
    ranges = small_ranges(n_bias, n_gain)
    column = lax.broadcasted_iota(jnp.int32, (1, LANES), 1)
    factors = jnp.zeros((1, LANES), F32)
    for n, (low, high) in enumerate(ranges):
        factors = jnp.where((column >= low) & (column < high), factor(6 + n), factors)
    put_small(ranges, ws[...] - factors * us[...], nwb, nwg, nwt)


def shapes_of(arrays):
    return [jax.ShapeDtypeStruct(array.shape, F32) for array in arrays]


def optimizer(shape, n_bias, n_gain, spot, totals, small, grads, weights, means, squares, small_like):
    vmem = pl.BlockSpec(memory_space=pltpu.VMEM)
    big = list(weights[:4])
    results = shapes_of(big) + shapes_of(small_like)
    row = jax.ShapeDtypeStruct((1, 128), F32)
    params = pltpu.CompilerParams(vmem_limit_bytes=48 * 2**20)
    out = pl.pallas_call(
        functools.partial(moments_kernel, n_bias, n_gain),
        out_shape=results * 2 + shapes_of(weights) + [row],
        in_specs=[pl.BlockSpec(memory_space=pltpu.SMEM)] + [vmem] * 19,
        out_specs=[vmem] * 20,
        compiler_params=params,
        name="moments",
    )(spot, totals, small, *grads, *weights, *means, *squares)
    new_means, new_squares, updates, row_here = out[:7], out[7:14], out[14:19], out[19]
    updates_total = reduce_row(shape, row_here)
    out = pl.pallas_call(
        functools.partial(weights_kernel, n_bias, n_gain),
        out_shape=results
        + [jax.ShapeDtypeStruct((2, 11), F32), jax.ShapeDtypeStruct((1, 1), F32)],
        in_specs=[vmem] * 12,
        out_specs=[vmem] * 9,
        compiler_params=params,
        name="weights",
    )(totals, updates_total, *weights, *updates)
    return updates_total, out[8], out[7], out[:7], new_means, new_squares


def turn_own_first(shape, core, src, dst):
    columns = shape["xy"]
    width = src.shape[1]
    depth = width // (2 * columns)
    for start in range(0, width, 128):
        turned = src[:, start : start + 128].T
        for offset in range(0, 128, depth):
            block = (start + offset) // depth
            slot = block // 2 + jnp.where(core == block % 2, 0, columns)
            dst[pl.ds(pl.multiple_of(slot * depth, depth), depth), :] = turned[offset : offset + depth]


def normed_of(values):
    center = values - jnp.mean(values, axis=-1, keepdims=True)
    inverse = lax.rsqrt(jnp.mean(center * center, axis=-1, keepdims=True) + 1e-05)
    return center * inverse, inverse


class Adder:
    def __init__(self, side, taken, first, sems):
        xy, core, zh, zl = place()
        self.side, self.taken, self.first = side, taken, first
        self.swap_send, self.swap_recv, *self.sems = sems
        self.at = (lax.div(xy, side), lax.rem(xy, side))
        self.rest = (core, zh, zl)
        self.sibling = (xy, 1 - core, zh, zl)

    def peers(self):
        xy = self.at[0] * self.side + self.at[1]
        columns = self.side * self.side
        return [self.sibling] + [
            (lax.rem(xy + step, columns), *self.rest) for step in range(1, columns)
        ]

    def swap(self, other, index):
        return send(other, self.taken.at[index], self.swap_send.at[index], self.swap_recv.at[index], self.sibling)

    def block(self, index, axis, there):
        return self.taken.at[index, :, there] if axis == 0 else self.taken.at[index, :, :, there]

    def owned(self, index, axis, step):
        there = lax.rem(self.at[1 - axis] + step, self.side)
        if axis == 0:
            return self.taken.at[index, :, self.at[0], there]
        return self.taken.at[index, :, there, self.at[1]]

    def copies(self, index, axis):
        for step in range(1, self.side):
            there = lax.rem(self.at[axis] + step, self.side)
            member = (there, self.at[1]) if axis == 0 else (self.at[0], there)
            yield send(
                self.block(index, axis, there), self.first.at[index, step - 1],
                self.sems[0].at[index, step - 1], self.sems[1].at[index, step - 1],
                (member[0] * self.side + member[1], *self.rest),
            )

    def by_parity(self, index, act):
        if isinstance(index, int):
            act(index % 2)
            return
        for parity in range(2):

            @pl.when(lax.rem(index, 2) == parity)
            def _():
                act(parity)

    def add_core(self, own, other, index):
        self.swap(other, index).wait_recv()
        for which in range(2):
            self.taken[index, which] = (
                own[which].astype(F32) + self.taken[index, which].astype(F32)
            ).astype(BF)

        def start(axis):
            for copy in self.copies(index, axis):
                copy.start()

        self.by_parity(index, start)

    def add_first(self, index, keep):
        def act(axis):
            mine = self.block(index, axis, self.at[axis])
            total = mine[...].astype(F32)
            for step, copy in enumerate(self.copies(index, axis)):
                copy.wait_recv()
                total = total + self.first[index, step].astype(F32)
            mine[...] = total.astype(BF)
            for copy in keep(index, axis):
                copy.start()

        self.by_parity(index, act)

    def end(self, index, keep):
        def act(axis):
            for copy in self.copies(index, axis):
                copy.wait_send()
            for copy in keep(index, axis):
                copy.wait()

        self.by_parity(index, act)


def feed_kernel(
    shape, ff_local, x_ref, c_ref, attn_ref, norm_ref, own_proj, other_proj, own_up, own_down, other_up, other_down,
    block_ref, middle_ref, given_ref, wide_ref, sums_ref,
    middle, total, second, a_second, a_turned, c_turned, own, other, taken, first_in,
    out_sems, keep_sems, proj_sems, *sems,
):
    step = pl.program_id(0)
    steps = taken.shape[0] - 1
    parts, heads_cols = attn_ref.shape[:2]
    side, chunk = own.shape[2], own.shape[5]
    half = c_turned.shape[0] // 2
    per = ff_local // chunk
    wide = 2 * ff_local + heads_cols
    slot = lax.rem(step, 2)
    adder = Adder(side, taken, first_in, sems)
    halves = own.shape[2:5]
    _, _, zh, zl = place()
    z = zh * shape["zl"] + zl

    def part_at(distance):
        return lax.rem(z + distance, parts)

    def proj_at(distance):
        return own_proj[...] if distance == 0 else other_proj[distance - 1]

    def keep(index, axis):
        for step in range(side):
            for which in range(2):
                start = part_at(lax.div(index, per)) * wide + which * ff_local + lax.rem(index, per) * chunk
                start = pl.multiple_of(start, 128)
                yield pltpu.make_async_copy(
                    adder.owned(index, axis, step).at[which], wide_ref.at[step, :, pl.ds(start, chunk)],
                    keep_sems.at[index, step, which],
                )

    def keep_proj(index, axis):
        for step in range(side):
            for part in range(parts):
                which, place_in = part // (parts // 2), part % (parts // 2)
                yield pltpu.make_async_copy(
                    adder.owned(index, axis, step).at[which, :, pl.ds(place_in * heads_cols, heads_cols)],
                    wide_ref.at[step, :, pl.ds(part * wide + 2 * ff_local, heads_cols)],
                    proj_sems.at[step, part],
                )

    def put(at, which, grad):
        own[at, which] = grad[:half].reshape(*halves, grad.shape[1])
        other[at, which] = grad[half:].reshape(*halves, grad.shape[1])

    @pl.when(step == 0)
    def _():
        barrier = pltpu.get_barrier_semaphore()
        for peer in adder.peers():
            pl.semaphore_signal(barrier, inc=1, device_id=peer, device_id_type=MESH)
        core = lax.axis_index("core")
        mixed = x_ref[...].astype(F32)
        for distance in range(parts):
            mixed = mixed + dot(attn_ref[part_at(distance)].T, proj_at(distance), 1, 1)
        middle[...] = mixed
        value, _ = normed_of(mixed)
        a_second[...] = (value * norm_ref[0:1, :] + norm_ref[1:2, :]).astype(BF)
        turn_own_first(shape, core, a_second, a_turned)
        turn_own_first(shape, core, c_ref, c_turned)
        total[...] = jnp.zeros_like(total)
        second[...] = jnp.zeros_like(second)
        pl.semaphore_wait(barrier, len(adder.peers()))

    @pl.when(step >= 2)
    def _():
        adder.swap(other.at[slot], step - 2).wait_send()

    mine = step < per
    up = jnp.where(mine, own_up[...], other_up[0])
    down = jnp.where(mine, own_down[...], other_down[0])
    pre = dot(a_second[...], up, 1, 0)
    grad_hidden = dot(c_ref[...], down, 1, 0)
    normal = 0.5 * (1.0 + lax.erf(pre * 2.0**-0.5))
    hidden = (pre * normal).astype(BF)
    slope = normal + pre * jnp.exp(-0.5 * pre * pre) * 0.3989422804014327
    grad_pre = (slope * grad_hidden).astype(BF)
    total[...] += dot(hidden, down, 1, 1)
    put(slot, 1, dot(c_turned[...], hidden, 1, 0).astype(BF))
    second[...] += dot(grad_pre, up, 1, 1)
    put(slot, 0, dot(a_turned[...], grad_pre, 1, 0).astype(BF))
    adder.swap(other.at[slot], step).start()

    @pl.when(step >= 1)
    def _():
        adder.add_core(own.at[1 - slot], other.at[1 - slot], step - 1)

    @pl.when(step >= 3)
    def _():
        adder.add_first(step - 3, keep)

    @pl.when(step == steps - 1)
    def _():
        core = lax.axis_index("core")
        last = steps - 1
        here, free = last % 2, 1 - last % 2
        adder.add_core(own.at[here], other.at[here], last)
        adder.add_first(last - 2, keep)
        a_second[...] = (middle[...] + total[...]).astype(BF)
        out_block = pltpu.make_async_copy(a_second, block_ref, out_sems.at[0])
        out_block.start()
        value, inverse = normed_of(middle[...])
        grad = second[...]
        sums_ref[0:1, :] = jnp.sum(grad * value, axis=0, keepdims=True)
        sums_ref[1:2, :] = jnp.sum(grad, axis=0, keepdims=True)
        inner = grad * norm_ref[0:1, :]
        second[...] = c_ref[...].astype(F32) + inverse * (
            inner
            - jnp.mean(inner, axis=-1, keepdims=True)
            - value * jnp.mean(inner * value, axis=-1, keepdims=True)
        )
        out_middle = pltpu.make_async_copy(second, middle_ref, out_sems.at[1])
        out_middle.start()
        low = second[...].astype(BF)
        turn_own_first(shape, core, low, a_turned)
        adder.swap(other.at[free], last - 1).wait_send()
        in_one = parts // 2
        for which in range(2):
            grads = [
                dot(a_turned[...], attn_ref[which * in_one + n], 1, 1).astype(BF) for n in range(in_one)
            ]
            put(free, which, jnp.concatenate(grads, axis=1))
        adder.swap(other.at[free], steps).start()
        adder.add_first(last - 1, keep)
        for distance in range(parts):
            rows = pl.ds(pl.multiple_of(part_at(distance) * heads_cols, heads_cols), heads_cols)
            c_turned[rows, :] = dot(low, proj_at(distance), 1, 0).T.astype(BF)
        out_given = pltpu.make_async_copy(c_turned, given_ref, out_sems.at[2])
        out_given.start()
        adder.add_core(own.at[free], other.at[free], steps)
        adder.add_first(last, keep)
        adder.add_first(steps, keep_proj)
        adder.swap(other.at[here], last).wait_send()
        adder.swap(other.at[free], steps).wait_send()
        for index in range(steps + 1):
            adder.end(index, keep if index < steps else keep_proj)
        for copy in (out_block, out_middle, out_given):
            copy.wait()


def column_segments(parts, ff_local, heads_cols):
    chunk = min(512, ff_local)
    per = ff_local // chunk
    segments = [
        (distance, which * ff_local + n * chunk, chunk, 1 - (distance * per + n) % 2)
        for distance in range(parts)
        for which in range(2)
        for n in range(per)
    ]
    return segments + [
        (distance, 2 * ff_local, heads_cols, 1 - parts * per % 2) for distance in range(parts)
    ]


def feed_forward(shape, tokens, cotangent, attn_rows, norm, shared_own, shared_others, ff_local):
    rows, width = tokens.shape
    parts, heads_cols = attn_rows.shape[:2]
    chunk = min(512, ff_local)
    per = ff_local // chunk
    steps = parts * per
    side = math.isqrt(shape["xy"])
    depth = width // (2 * shape["xy"])
    anywhere = pl.BlockSpec(memory_space=pl.ANY)

    def once(block, *index):
        return pl.BlockSpec(block, lambda s: index, pipeline_mode=pl.Buffered(1))

    dma = pltpu.SemaphoreType.DMA
    return pl.pallas_call(
        functools.partial(feed_kernel, shape, ff_local),
        grid=(steps,),
        in_specs=[
            once((rows, width), 0, 0),
            once((rows, width), 0, 0),
            once((parts, heads_cols, rows), 0, 0, 0),
            once((2, width), 0, 0),
            once((width, heads_cols), 0, 2 * ff_local // heads_cols),
            once((parts - 1, width, heads_cols), 0, 0, 2 * ff_local // heads_cols),
            *[
                pl.BlockSpec((width, chunk), lambda s, at=at: (0, at + jnp.minimum(s, per - 1)))
                for at in (0, per)
            ],
            *[
                pl.BlockSpec(
                    (1, width, chunk),
                    lambda s, at=at: (jnp.maximum(s - per, 0) // per, 0, at + jnp.maximum(s - per, 0) % per),
                )
                for at in (0, per)
            ],
        ],
        out_specs=[anywhere] * 4 + [pl.BlockSpec((2, width), lambda s: (0, 0))],
        out_shape=[
            jax.ShapeDtypeStruct((rows, width), BF),
            jax.ShapeDtypeStruct((rows, width), F32),
            jax.ShapeDtypeStruct((parts * heads_cols, rows), BF),
            jax.ShapeDtypeStruct((side, depth, parts * (2 * ff_local + heads_cols)), BF),
            jax.ShapeDtypeStruct((2, width), F32),
        ],
        scratch_shapes=[
            pltpu.VMEM((rows, width), F32),
            pltpu.VMEM((rows, width), F32),
            pltpu.VMEM((rows, width), F32),
            pltpu.VMEM((rows, width), BF),
            pltpu.VMEM((width, rows), BF),
            pltpu.VMEM((width, rows), BF),
            pltpu.VMEM((2, 2, side, side, depth, chunk), BF),
            pltpu.VMEM((2, 2, side, side, depth, chunk), BF),
            pltpu.VMEM((steps + 1, 2, side, side, depth, chunk), BF),
            pltpu.VMEM((steps + 1, side - 1, 2, side, depth, chunk), BF),
            dma((3,)),
            dma((steps, side, 2)),
            dma((side, parts)),
            dma((steps + 1,)),
            dma((steps + 1,)),
            dma((steps + 1, side - 1)),
            dma((steps + 1, side - 1)),
        ],
        compiler_params=pltpu.CompilerParams(
            vmem_limit_bytes=62 * 2**20, collective_id=5, has_side_effects=True
        ),
        name="feed_forward",
    )(tokens, cotangent, attn_rows, norm, shared_own, shared_others, *[shared_own] * 2, *[shared_others] * 2)


def norm_parts(values):
    center = values - jnp.mean(values, axis=-1, keepdims=True)
    inverse = lax.rsqrt(jnp.mean(center * center, axis=-1, keepdims=True) + 1e-05)
    return center * inverse, inverse


def norm_back(normed, inverse, gain, grad):
    inner = grad * gain
    return inverse * (
        inner
        - jnp.mean(inner, axis=-1, keepdims=True)
        - normed * jnp.mean(inner * normed, axis=-1, keepdims=True)
    )


def per_device(
    shape,
    tokens, cotangent, item_len, bucket_table,
    w_qkv, w_proj, w_up, w_down, rel_bias, ln_gain, ln_shift,
    mean_qkv, mean_proj, mean_up, mean_down, mean_bias, mean_gain, mean_shift,
    square_qkv, square_proj, square_up, square_down, square_bias, square_gain, square_shift,
):
    columns, places = shape["xy"], shape["zl"]
    parts = 2 * places
    devices = columns * 2 * parts
    rows, width = tokens.shape
    heads = w_qkv.shape[2] // DH
    tok = rows * parts
    xy, core, zh, zl = place()
    me = ((xy * 2 + core) * 2 + zh) * places + zl
    head_block = zl * 2 + core

    ff_local, heads_cols = w_up.shape[1], w_proj.shape[0]
    local = jnp.concatenate([w_up, w_down.T, w_proj.T], axis=1).astype(BF)

    shared_own = lax.all_gather(local, DP, axis=0, tiled=True)
    n_bias, n_gain = rel_bias.shape[0], ln_gain.shape[1]
    n_small = n_bias + 4 * n_gain

    def pack(bias, gain, shift):
        row = jnp.concatenate([bias, gain.reshape(-1), shift.reshape(-1)])
        return jnp.pad(row, (0, LANES - n_small))[None, :]

    small_weights = pack(rel_bias, ln_gain, ln_shift)
    group_rows, w_heads, small, wide = gather(
        shape, tokens, w_qkv.astype(BF), small_weights, local
    )
    shared_others = lax.all_gather(wide, DP, axis=1, tiled=True)
    small = small.reshape(devices, LANES)

    def columns_of(start):
        part = small[:, start : start + 2 * n_gain].reshape(devices, 2, n_gain)
        return part.transpose(1, 0, 2).reshape(2, width)

    table_flat = small[:, :n_bias].reshape(-1)
    gains, shifts = columns_of(n_bias), columns_of(n_bias + 2 * n_gain)
    other_len = lax.ppermute(item_len, "core", [(0, 1), (1, 0)])
    split = jnp.where(zh == core, item_len, other_len)[0, 0:1]

    a_first, qkv = project(
        group_rows.reshape(tok, width), jnp.stack([gains[0], shifts[0]]), w_heads
    )
    qkv = qkv.reshape(3 * heads * DH, tok)

    table = lax.dynamic_slice_in_dim(
        table_flat.reshape(BUCKETS, H), head_block * heads, heads, 1
    )
    one_hot = (jnp.arange(BUCKETS)[:, None] == bucket_table[None, :]).astype(F32)
    dist_bias = lax.dot_general(
        table, one_hot, (((0,), (0,)), ((), ())), precision=HIGHEST, preferred_element_type=F32
    )
    pattern = jnp.concatenate(
        [dist_bias * LOG2E, jnp.full((heads, BLK), NEG, F32)], axis=1
    )[:, None, :]
    out, attn_rows, lse = attend(shape, qkv, pattern, split, heads)

    attn_rows = attn_rows.reshape(parts, heads * DH, rows)
    norm_two = jnp.stack([gains[1], shifts[1]])
    block_out, grad_middle, grad_attn, wide_grad, sums_two = feed_forward(
        shape, tokens, cotangent, attn_rows, norm_two, shared_own, shared_others, ff_local
    )
    gain_two, shift_two = sums_two[0], sums_two[1]
    given = grad_attn.reshape(parts, heads, DH, rows)
    grad_heads, wide_parts, grad_pattern = attend_back(
        shape, column_segments(parts, ff_local, w_proj.shape[0]), qkv, out, given, wide_grad, lse, pattern,
        split, heads,
    )
    grad_heads = grad_heads.reshape(3, heads * DH, tok)

    first, grad_qkv, head_sums, column_sums = project_back(a_first, grad_heads, w_heads)
    shift_one = jnp.sum(w_heads.astype(F32) * head_sums.reshape(3, 1, heads * DH), axis=(0, 2))
    gain_one = (jnp.sum(column_sums, axis=1) - shifts[0] * shift_one) / gains[0]

    bias_grad = lax.dot_general(
        one_hot, grad_pattern[:, 0, :tok], (((1,), (1,)), ((), ())),
        precision=HIGHEST, preferred_element_type=F32,
    )
    table_grad = lax.dynamic_update_slice(
        jnp.zeros((BUCKETS, H), F32), bias_grad, (0, head_block * heads)
    )

    def by_device(*vectors):
        return jnp.stack(vectors).reshape(2, devices, n_gain).transpose(1, 0, 2).reshape(devices, -1)

    small_grad = jnp.concatenate(
        [
            table_grad.reshape(devices, n_bias),
            by_device(gain_one, gain_two),
            by_device(shift_one, shift_two),
            jnp.zeros((devices, LANES - n_small), F32),
        ],
        axis=1,
    )
    weights = (w_qkv, w_proj, w_up, w_down, small_weights)
    early_rows, added, sum_qkv, wide_sum, small_sum, totals = sums(
        shape, n_bias, n_gain, first, grad_qkv, small_grad, wide_parts, weights
    )
    small_like = [rel_bias[None, :], ln_gain, ln_shift]
    updates_total, grad_norm, param_norms, *results = optimizer(
        shape, n_bias, n_gain, me[None].astype(jnp.int32), totals, small_sum,
        (sum_qkv, wide_sum), weights,
        (mean_qkv, mean_proj, mean_up, mean_down, pack(mean_bias, mean_gain, mean_shift)),
        (square_qkv, square_proj, square_up, square_down, pack(square_bias, square_gain, square_shift)),
        small_like,
    )
    added, _ = lax.optimization_barrier((added, updates_total))
    grad_tokens = finish_rows(shape, added, early_rows, tokens, grad_middle, gains[0:1])
    new = [array if n % 7 != 4 else array[0] for group in results for n, array in enumerate(group)]
    return (block_out, grad_tokens, grad_norm[0, 0], param_norms, *new)


def solution(mesh):
    shape = {"xy": mesh.shape["dp"] // 2, "core": 2, "zh": 2, "zl": mesh.shape["tensor"] // 2}
    split_mesh = Mesh(mesh.devices.reshape(tuple(shape[axis] for axis in ALL)), ALL)
    weights = (
        P(None, DP, TENSOR),
        P(TENSOR, DP),
        P(DP, TENSOR),
        P(TENSOR, DP),
        P(ALL),
        P(None, ALL),
        P(None, ALL),
    )
    rows = P(ALL, None)
    return jax.shard_map(
        functools.partial(per_device, shape),
        mesh=split_mesh,
        in_specs=(rows, rows, P(DP, None), P(), *weights, *weights, *weights),
        out_specs=(rows, rows, P(), P(), *weights, *weights, *weights),
        check_vma=False,
    )
```

```python
import functools
import math

import jax
import jax.numpy as jnp
from jax import lax
from jax.experimental import pallas as pl
from jax.experimental.pallas import tpu as pltpu
from jax.sharding import Mesh
from jax.sharding import PartitionSpec as P

H = 16
DH = 64
BUCKETS = 32
BLK = 512
NEG = -1e30
LOG2E = 1.4426950408889634
F32 = jnp.float32
BF = jnp.bfloat16
MESH = pl.DeviceIdType.MESH
HIGHEST = lax.Precision.HIGHEST
ALL = ("xy", "core", "zh", "zl")
DP = ("xy", "core")
TENSOR = ("zh", "zl")


def dot(left, right, left_dim, right_dim):
    return lax.dot_general(
        left, right, (((left_dim,), (right_dim,)), ((), ())), preferred_element_type=F32
    )


def project_kernel(x_ref, norm_ref, w_ref, a_ref, qkv_ref, turned):
    @pl.when(pl.program_id(0) == 0)
    def _():
        for c in range(3):
            turned[c] = w_ref[c].T

    values = x_ref[...].astype(F32)
    center = values - jnp.mean(values, axis=-1, keepdims=True)
    inverse = lax.rsqrt(jnp.mean(center * center, axis=-1, keepdims=True) + 1e-05)
    a_ref[...] = (center * inverse * norm_ref[0:1, :] + norm_ref[1:2, :]).astype(BF)
    for c in range(3):
        qkv_ref[c] = dot(turned[c], a_ref[...], 1, 1).astype(BF)


def project(rows, norm, weights):
    tok, width = rows.shape
    cols = weights.shape[2]
    return pl.pallas_call(
        project_kernel,
        grid=(tok // BLK,),
        in_specs=[
            pl.BlockSpec((BLK, width), lambda s: (s, 0)),
            pl.BlockSpec((2, width), lambda s: (0, 0)),
            pl.BlockSpec((3, width, cols), lambda s: (0, 0, 0)),
        ],
        out_specs=[
            pl.BlockSpec((BLK, width), lambda s: (s, 0)),
            pl.BlockSpec((3, cols, BLK), lambda s: (0, 0, s)),
        ],
        out_shape=[
            jax.ShapeDtypeStruct((tok, width), BF),
            jax.ShapeDtypeStruct((3, cols, tok), BF),
        ],
        scratch_shapes=[pltpu.VMEM((3, cols, width), BF)],
        compiler_params=pltpu.CompilerParams(vmem_limit_bytes=62 * 2**20),
        name="project",
    )(rows, norm, weights)


def make_slab(pattern, slab):
    width = slab.shape[1]
    slab[0:8, :] = pltpu.roll(jnp.broadcast_to(pattern, (8, width)), 0, 1, stride=1, stride_axis=0)
    done = 8
    while done < slab.shape[0]:
        slab[done : 2 * done, :] = pltpu.roll(slab[0:done, :], done, 1)
        done *= 2


def fold_slab(slab):
    width = slab.shape[1]
    half = slab.shape[0] // 2
    while half >= 8:
        slab[0:half, :] = slab[0:half, :] + pltpu.roll(slab[half : 2 * half, :], width - half, 1)
        half //= 2
    total = slab[0:1, :]
    for row in range(1, 8):
        total = total + pltpu.roll(slab[row : row + 1, :], width - row, 1)
    return total


def split_three(values):
    high = values.astype(BF).astype(F32)
    rest = values - high
    middle = rest.astype(BF).astype(F32)
    return high, middle, (rest - middle).astype(BF).astype(F32)


def put_queries(queries, split, minus, tok, dst):
    scaled = queries.astype(F32) * (DH**-0.5 * LOG2E)
    high = scaled.astype(BF)
    dst[0:DH, :] = high
    dst[DH : 2 * DH, :] = (scaled - high.astype(F32)).astype(BF)
    position = lax.broadcasted_iota(jnp.int32, (16, tok), 1)
    row = lax.broadcasted_iota(jnp.int32, (16, tok), 0)
    extra = jnp.where((row == 0) & (position >= split), 1.0, 0.0)
    if minus is not None:
        first, second, third = split_three(minus)
        extra = jnp.where(
            row == 1, first, jnp.where(row == 2, second, jnp.where(row == 3, third, extra))
        )
    dst[2 * DH : 2 * DH + 16, :] = extra.astype(BF)


def put_keys(keys, split, tok, dst):
    for start in range(0, tok, BLK):
        position = start + lax.broadcasted_iota(jnp.int32, (16, BLK), 1)
        row = lax.broadcasted_iota(jnp.int32, (16, BLK), 0)
        extra = jnp.where(
            row == 0, jnp.where(position < split, NEG, 0.0), jnp.where(row < 4, 1.0, 0.0)
        )
        block = keys[:, start : start + BLK].astype(F32)
        whole = jnp.concatenate([block, block, extra], axis=0)
        dst[start : start + BLK, :] = whole.T.astype(BF)


def block_at(index):
    return pl.ds(pl.multiple_of(index * BLK, BLK), BLK)


def attend_kernel(
    shape, split_ref, pattern_ref, q_ref, k_ref, v_ref, out_ref, rows_ref, lse_ref,
    slab, kx, qx, outs, local_sem, send_sem, recv_sem,
):
    head = pl.program_id(0)
    tok = q_ref.shape[1]
    split = split_ref[0]
    trade = Trade(shape, tok)

    @pl.when(head == 0)
    def _():
        greet_column(shape)

    make_slab(pattern_ref[0], slab)
    put_queries(q_ref[...], split, None, tok, qx)
    put_keys(k_ref, split, tok, kx)

    def steps(i, blocks, top, total, out):
        scores = [
            dot(kx[block_at(j), :], qx[:, block_at(i)], 1, 0) + slab[:, block_at(i - j)] for j in blocks
        ]
        new_top = top
        for score in scores:
            new_top = jnp.maximum(new_top, jnp.max(score, axis=0, keepdims=True))
        scale = jnp.exp2(top - new_top)
        total, out = total * scale, out * scale
        for j, score in zip(blocks, scores):
            weights = jnp.exp2(score - new_top)
            total = total + jnp.sum(weights, axis=0, keepdims=True)
            out = out + dot(v_ref[:, block_at(j)], weights.astype(BF), 1, 0)
        return new_top, total, out

    def row(i, carry):
        start = (
            jnp.full((1, BLK), NEG, F32),
            jnp.zeros((1, BLK), F32),
            jnp.zeros((DH, BLK), F32),
        )
        pairs = lax.fori_loop(
            0, (i + 1) // 2, lambda t, c: steps(i, (i - 2 * t, i - 2 * t - 1), *c), start
        )
        top, total, out = lax.fori_loop(0, (i + 1) % 2, lambda t, c: steps(i, (0,), *c), pairs)
        outs[head, :, block_at(i)] = (out / total).astype(BF)
        lse_ref[0, :, block_at(i)] = top + jnp.log2(total)
        return carry

    lax.fori_loop(0, tok // BLK, row, 0)

    def keep(h):
        return pltpu.make_async_copy(outs.at[h], out_ref.at[h], local_sem.at[0, h])

    def piece(h, n):
        return outs.at[h, :, pl.ds(pl.multiple_of(n * trade.rows, trade.rows), trade.rows)]

    def slot(h, n):
        return rows_ref.at[n, h]

    keep(head).start()
    trade.give(head, piece, slot, trade.owner, trade.head, local_sem.at[1, head], send_sem, recv_sem)

    @pl.when(head == pl.num_programs(0) - 1)
    def _():
        for h in range(rows_ref.shape[1]):
            keep(h).wait()
            trade.given(h, piece, slot, trade.owner, trade.head, local_sem.at[1, h], send_sem, recv_sem)
            trade.take(h, piece, slot, trade.header, send_sem, recv_sem)


def attend(shape, qkv, pattern, split, heads):
    tok = qkv.shape[1]
    width = pattern.shape[-1]
    parts = shape["zh"] * shape["zl"]
    dma = pltpu.SemaphoreType.DMA
    return pl.pallas_call(
        functools.partial(attend_kernel, shape),
        grid=(heads,),
        in_specs=[
            pl.BlockSpec(memory_space=pltpu.SMEM),
            pl.BlockSpec((1, 1, width), lambda h: (h, 0, 0)),
            pl.BlockSpec((DH, tok), lambda h: (h, 0)),
            pl.BlockSpec((DH, tok), lambda h: (h + heads, 0)),
            pl.BlockSpec((DH, tok), lambda h: (h + 2 * heads, 0)),
        ],
        out_specs=[
            pl.BlockSpec(memory_space=pl.ANY),
            pl.BlockSpec(memory_space=pl.ANY),
            pl.BlockSpec((1, 1, tok), lambda h: (h, 0, 0)),
        ],
        out_shape=[
            jax.ShapeDtypeStruct((heads, DH, tok), BF),
            jax.ShapeDtypeStruct((parts, heads, DH, tok // parts), BF),
            jax.ShapeDtypeStruct((heads, 1, tok), F32),
        ],
        scratch_shapes=[
            pltpu.VMEM((BLK, width), F32),
            pltpu.VMEM((tok, 2 * DH + 16), BF),
            pltpu.VMEM((2 * DH + 16, tok), BF),
            pltpu.VMEM((heads, DH, tok), BF),
            dma((2, heads)),
            dma((heads, parts)),
            dma((heads, parts)),
        ],
        compiler_params=pltpu.CompilerParams(
            vmem_limit_bytes=56 * 2**20, collective_id=0, has_side_effects=True
        ),
        name="attend",
    )(split, pattern, qkv, qkv, qkv)


def attend_back_kernel(
    shape, segments, split_ref, pattern_ref, q_ref, k_ref, v_ref, o_ref, lse_ref, given_ref, wide_ref,
    grads_ref, wide_parts_ref, dpattern_ref,
    slab, dslab, kx, qx, vx, dox, qn, don, dk, dv, taken, wide_own, wide_in,
    local_sem, in_send, in_recv, wide_sem, z_send, z_recv, w_send, w_recv,
):
    head = pl.program_id(0)
    tok = q_ref.shape[1]
    split = split_ref[0]
    trade = Trade(shape, tok)
    heads = taken.shape[0]

    def in_piece(h, n):
        return given_ref.at[n, h]

    def in_slot(h, n):
        return taken.at[h, :, pl.ds(pl.multiple_of(n * trade.rows, trade.rows), trade.rows)]

    xy, core, zh, zl = trade.me
    side = math.isqrt(shape["xy"])

    def column_copies():
        at = (lax.div(xy, side), lax.rem(xy, side))
        for step in range(1, side):
            for n, (distance, start, count, axis) in enumerate(segments):
                there = lax.rem(at[axis] + step, side)
                column = there * side + at[1] if axis == 0 else at[0] * side + there
                part = lax.rem(trade.row + distance, trade.parts)
                here = pl.ds(pl.multiple_of(part * wide_parts_ref.shape[2] + start, 128), count)
                yield send(
                    wide_ref.at[step, :, here], wide_in.at[step - 1, :, here],
                    w_send.at[step - 1, n], w_recv.at[step - 1, n], (column, core, zh, zl),
                )

    bring = pltpu.make_async_copy(wide_ref.at[0], wide_own, wide_sem.at[1])

    @pl.when(head == 0)
    def _():
        greet(shape)
        bring.start()
        for copy in column_copies():
            copy.start()
        for h in range(heads):
            trade.give(
                h, in_piece, in_slot, trade.header, trade.row, local_sem.at[h], in_send, in_recv
            )

    size = wide_parts_ref.shape[2]

    def wide_part(n):
        return wide_own.at[:, pl.ds(pl.multiple_of(n * size, size), size)]

    def along_z(step):
        there = lax.rem(trade.row + step, trade.parts)
        return there, (
            trade.me[0], trade.me[1], lax.div(there, trade.places), lax.rem(there, trade.places),
        )

    def wide_copy(step):
        there, device = along_z(step)
        return send(
            wide_part(there), wide_parts_ref.at[trade.row], z_send.at[step], z_recv.at[trade.row], device
        )

    keep_wide = pltpu.make_async_copy(
        wide_part(trade.row), wide_parts_ref.at[trade.row], wide_sem.at[0]
    )

    @pl.when(head == min(1, heads - 1))
    def _():
        bring.wait()
        for copy in column_copies():
            copy.wait_recv()
            copy.wait_send()
        for n in range(trade.parts):
            here = slice(n * size, (n + 1) * size)
            total = wide_own[:, here].astype(F32)
            for step in range(side - 1):
                total = total + wide_in[step, :, here].astype(F32)
            wide_own[:, here] = total.astype(BF)
        keep_wide.start()
        for step in range(1, trade.parts):
            wide_copy(step).start()

    make_slab(pattern_ref[0], slab)
    put_queries(q_ref[...], split, -lse_ref[0], tok, qx)
    put_keys(k_ref, split, tok, kx)
    dslab[...] = jnp.zeros_like(dslab)
    dk[...] = jnp.zeros_like(dk)
    dv[...] = jnp.zeros_like(dv)
    row = lax.broadcasted_iota(jnp.int32, (16, BLK), 0)
    ones = jnp.where(row < 3, 1.0, 0.0)
    trade.given(
        head, in_piece, in_slot, trade.header, trade.row, local_sem.at[head], in_send, in_recv
    )
    trade.take(head, in_piece, in_slot, trade.owner, in_send, in_recv)
    for start in range(0, tok, BLK):
        here = slice(start, start + BLK)
        low_grad = taken[head, :, here]
        grad = low_grad.astype(F32)
        inner = jnp.sum(grad * o_ref[0, :, here].astype(F32), axis=0, keepdims=True)
        first, second, third = split_three(-inner)
        extra = jnp.where(
            row == 0, first, jnp.where(row == 1, second, jnp.where(row == 2, third, 0.0))
        )
        dox[0:DH, here] = low_grad
        dox[DH : DH + 16, here] = extra.astype(BF)
        vx[here, :] = jnp.concatenate([v_ref[:, here].astype(F32), ones], axis=0).T.astype(BF)
        both = jnp.concatenate([q_ref[:, here].astype(F32), grad], axis=0).T
        qn[here, :] = both[:, 0:DH].astype(BF)
        don[here, :] = both[:, DH : 2 * DH].astype(BF)

    def tile(i, j):
        qs, ks, diagonal = block_at(i), block_at(j), block_at(i - j)
        shares = jnp.exp2(dot(kx[ks, :], qx[:, qs], 1, 0) + slab[:, diagonal])
        grad_scores = shares * dot(vx[ks, :], dox[:, qs], 1, 0)
        dslab[:, diagonal] += grad_scores
        low = grad_scores.astype(BF)
        dv[ks, :] += dot(shares.astype(BF), don[qs, :], 1, 0)
        dk[ks, :] += dot(low, qn[qs, :], 1, 0)
        return dot(k_ref[:, ks], low, 1, 0)

    def query_row(i, carry):
        total = lax.fori_loop(
            0,
            (i + 1) // 2,
            lambda t, c: c + tile(i, i - 2 * t) + tile(i, i - 2 * t - 1),
            jnp.zeros((DH, BLK), F32),
        )
        total = lax.fori_loop(0, (i + 1) % 2, lambda t, c: c + tile(i, 0), total)
        grads_ref[0, 0, :, block_at(i)] = (total * DH**-0.5).astype(BF)
        return carry

    lax.fori_loop(0, tok // BLK, query_row, 0)
    for start in range(0, tok, BLK):
        here = slice(start, start + BLK)
        grads_ref[1, 0, :, here] = (dk[here, :] * DH**-0.5).T.astype(BF)
        grads_ref[2, 0, :, here] = dv[here, :].T.astype(BF)
    dpattern_ref[0] = fold_slab(dslab)

    @pl.when(head == heads - 1)
    def _():
        keep_wide.wait()
        for step in range(1, trade.parts):
            there, device = along_z(step)
            here = wide_parts_ref.at[there]
            wide_copy(step).wait_send()
            send(here, here, z_send.at[step], z_recv.at[there], device).wait_recv()


def attend_back(shape, segments, qkv, out, given, wide, lse, pattern, split, heads):
    tok = qkv.shape[1]
    width = pattern.shape[-1]
    parts = shape["zh"] * shape["zl"]
    anywhere = pl.BlockSpec(memory_space=pl.ANY)
    dma = pltpu.SemaphoreType.DMA
    return pl.pallas_call(
        functools.partial(attend_back_kernel, shape, segments),
        grid=(heads,),
        in_specs=[
            pl.BlockSpec(memory_space=pltpu.SMEM),
            pl.BlockSpec((1, 1, width), lambda h: (h, 0, 0)),
            pl.BlockSpec((DH, tok), lambda h: (h, 0)),
            pl.BlockSpec((DH, tok), lambda h: (h + heads, 0)),
            pl.BlockSpec((DH, tok), lambda h: (h + 2 * heads, 0)),
            pl.BlockSpec((1, DH, tok), lambda h: (h, 0, 0)),
            pl.BlockSpec((1, 1, tok), lambda h: (h, 0, 0)),
            anywhere,
            anywhere,
        ],
        out_specs=[
            pl.BlockSpec((3, 1, DH, tok), lambda h: (0, h, 0, 0)),
            anywhere,
            pl.BlockSpec((1, 1, width), lambda h: (h, 0, 0)),
        ],
        out_shape=[
            jax.ShapeDtypeStruct((3, heads, DH, tok), BF),
            jax.ShapeDtypeStruct((parts, wide.shape[1], wide.shape[2] // parts), BF),
            jax.ShapeDtypeStruct((heads, 1, width), F32),
        ],
        scratch_shapes=[
            pltpu.VMEM((BLK, width), F32),
            pltpu.VMEM((BLK, width), F32),
            pltpu.VMEM((tok, 2 * DH + 16), BF),
            pltpu.VMEM((2 * DH + 16, tok), BF),
            pltpu.VMEM((tok, DH + 16), BF),
            pltpu.VMEM((DH + 16, tok), BF),
            pltpu.VMEM((tok, DH), BF),
            pltpu.VMEM((tok, DH), BF),
            pltpu.VMEM((tok, DH), F32),
            pltpu.VMEM((tok, DH), F32),
            pltpu.VMEM((heads, DH, tok), BF),
            pltpu.VMEM(wide.shape[1:], BF),
            pltpu.VMEM((wide.shape[0] - 1, *wide.shape[1:]), BF),
            dma((heads,)),
            dma((heads, parts)),
            dma((heads, parts)),
            dma((2,)), dma((parts,)), dma((parts,)),
            *[dma((wide.shape[0] - 1, len(segments)))] * 2,
        ],
        compiler_params=pltpu.CompilerParams(
            vmem_limit_bytes=60 * 2**20, collective_id=1, has_side_effects=True
        ),
        name="attend_back",
    )(split, pattern, qkv, qkv, qkv, out, lse, given, wide)


def place():
    return tuple(lax.axis_index(axis) for axis in ALL)


class Trade:
    def __init__(self, shape, tok):
        self.places = shape["zl"]
        self.parts = shape["zh"] * self.places
        self.rows = tok // self.parts
        self.me = place()
        _, core, zh, zl = self.me
        self.row = zh * self.places + zl
        self.head = zl * 2 + core

    def owner(self, n):
        return (self.me[0], self.me[2], lax.div(n, self.places), lax.rem(n, self.places))

    def header(self, n):
        return (self.me[0], lax.rem(n, 2), self.me[1], lax.div(n, 2))

    def each(self, device_of, local, remote):
        for index in range(self.parts):
            n = jnp.where(self.me[2] == 1, index, self.parts - 1 - index)
            device = device_of(n)
            if local is not None:

                @pl.when(is_same(device, self.me))
                def _():
                    local(n)

            @pl.when(jnp.logical_not(is_same(device, self.me)))
            def _():
                remote(n, device)

    def give(self, h, piece, slot, device_of, mine, local_sem, send_sem, recv_sem):
        def local(n):
            pltpu.make_async_copy(piece(h, n), slot(h, mine), local_sem).start()

        def remote(n, device):
            send(piece(h, n), slot(h, mine), send_sem.at[h, n], recv_sem.at[h, mine], device).start()

        self.each(device_of, local, remote)

    def given(self, h, piece, slot, device_of, mine, local_sem, send_sem, recv_sem):
        def local(n):
            pltpu.make_async_copy(piece(h, n), slot(h, mine), local_sem).wait()

        def remote(n, device):
            send(piece(h, n), slot(h, mine), send_sem.at[h, n], recv_sem.at[h, mine], device).wait_send()

        self.each(device_of, local, remote)

    def take(self, h, piece, slot, device_of, send_sem, recv_sem):
        def remote(n, device):
            send(piece(h, n), slot(h, n), send_sem.at[h, n], recv_sem.at[h, n], device).wait_recv()

        self.each(device_of, None, remote)


def is_same(left, right):
    same = left[0] == right[0]
    for one, other in zip(left[1:], right[1:]):
        same = same & (one == other)
    return same


def column_peers(shape, device):
    xy, core, zh, zl = device
    places = shape["zl"]
    total = 4 * places
    mine = (core * 2 + zh) * places + zl
    for step in range(1, total):
        there = lax.rem(mine + step, total)
        yield step, there, (xy, there // (2 * places), lax.rem(there // places, 2), lax.rem(there, places))


def plane_peers(shape, device):
    xy, core, zh, zl = device
    for step in range(1, shape["xy"]):
        there = lax.rem(xy + step, shape["xy"])
        yield step, there, (there, core, zh, zl)


def greet(shape):
    device = place()
    barrier = pltpu.get_barrier_semaphore()
    peers = [peer for _, _, peer in column_peers(shape, device)]
    peers += [peer for _, _, peer in plane_peers(shape, device)]
    for peer in peers:
        pl.semaphore_signal(barrier, inc=1, device_id=peer, device_id_type=MESH)
    pl.semaphore_wait(barrier, len(peers))


def greet_column(shape):
    barrier = pltpu.get_barrier_semaphore()
    peers = [peer for _, _, peer in column_peers(shape, place())]
    for peer in peers:
        pl.semaphore_signal(barrier, inc=1, device_id=peer, device_id_type=MESH)
    pl.semaphore_wait(barrier, len(peers))


def send(src, dst, send_sem, recv_sem, device):
    return pltpu.make_async_remote_copy(
        src_ref=src, dst_ref=dst, send_sem=send_sem, recv_sem=recv_sem,
        device_id=device, device_id_type=MESH,
    )


CHUNKS = 4


def gather_kernel(
    shape, tokens_ref, wq_ref, small_ref, wide_ref, rows_ref, heads_ref, all_small_ref, all_wide_ref,
    local_sems, in_send, fwd_send, share_send, x_recv, xs_recv,
    z_send, z_recv, p_send, p_recv, s_send, s_recv, w_send, w_recv, q_send, q_recv,
):
    me = place()
    xy, core, zh, zl = me
    places = shape["zl"]
    parts = 2 * places
    columns = shape["xy"]
    z = zh * places + zl
    sibling = (xy, 1 - core, zh, zl)
    size = tokens_ref.shape[0] // (2 * CHUNKS)
    dp = xy * 2 + core
    inside = core == zh
    outside = jnp.logical_not(inside)
    entry = jnp.where(zh < core, 0, places - 1)

    def chunk_of(ref, half, chunk):
        return ref.at[pl.ds(pl.multiple_of((half * CHUNKS + chunk) * size, size), size), :]

    def beside(step):
        there = z + step
        return (xy, core, there // places, lax.rem(there, places))

    greet(shape)

    depth = wq_ref.shape[1]
    head_block = zl * 2 + core

    def depth_of(index, count):
        return heads_ref.at[:, pl.ds(pl.multiple_of(index * depth, depth), count * depth), :]

    def wq_target(half):
        return (xy, lax.rem(z, 2), half, lax.div(z, 2))

    def wq_source(c):
        return (xy, c, lax.div(head_block, places), lax.rem(head_block, places))

    own_wq = pltpu.make_async_copy(wq_ref, depth_of(dp, 1), local_sems.at[1])
    own_small = pltpu.make_async_copy(small_ref, all_small_ref.at[dp, z], local_sems.at[2])

    def wide_at(shard, device_z):
        return all_wide_ref.at[lax.rem(shard + parts - device_z, parts) - 1]

    own_small.start()
    for n in range(2):

        @pl.when(is_same(wq_target(n), me))
        def _():
            own_wq.start()

        @pl.when(jnp.logical_not(is_same(wq_target(n), me)))
        def _():
            send(wq_ref, depth_of(dp, 1), q_send.at[n], q_recv.at[core], wq_target(n)).start()

    for step in range(1, parts):
        there = lax.rem(z + step, parts)
        device = (xy, core, there // places, lax.rem(there, places))
        send(small_ref, all_small_ref.at[dp, z], z_send.at[step], z_recv.at[z], device).start()

    @pl.when(outside)
    def _():
        for chunk in range(CHUNKS):
            for half in range(2):
                send(
                    chunk_of(tokens_ref, half, chunk), chunk_of(rows_ref.at[z], half, chunk),
                    in_send.at[half, chunk], x_recv.at[z, chunk], (xy, half, core, entry),
                ).start()

    @pl.when(inside)
    def _():
        for chunk in range(CHUNKS):
            send(
                chunk_of(tokens_ref, 1 - core, chunk), chunk_of(rows_ref.at[z], 1 - core, chunk),
                in_send.at[0, chunk], x_recv.at[z, chunk], sibling,
            ).start()
        pltpu.make_async_copy(tokens_ref, rows_ref.at[z], local_sems.at[0]).start()

    def ways(shard):
        from_half, from_place = shard // places, lax.rem(shard, places)
        start = jnp.where(from_half == zh, from_place, jnp.where(from_half < zh, 0, places - 1))
        return (zl >= start) & (zl < places - 1), (zl <= start) & (zl > 0)

    def pass_on(shard, chunk, source):
        mine = chunk_of(rows_ref.at[shard], core, chunk)
        for n, (way, step) in enumerate(zip(ways(shard), (1, -1))):

            @pl.when(way)
            def _():
                send(
                    source, mine, fwd_send.at[n, shard, chunk], x_recv.at[shard, chunk],
                    (xy, core, zh, zl + step),
                ).start()

    def share(shard, chunk, source):
        mine = chunk_of(rows_ref.at[shard], core, chunk)
        send(source, mine, share_send.at[shard, chunk], xs_recv.at[shard, chunk], sibling).start()

    def got(shard, chunk):
        mine = chunk_of(rows_ref.at[shard], core, chunk)
        send(mine, mine, share_send.at[shard, chunk], x_recv.at[shard, chunk], sibling).wait_recv()

    @pl.when(inside)
    def _():
        for chunk in range(CHUNKS):
            mine = chunk_of(tokens_ref, core, chunk)
            pass_on(z, chunk, mine)
            share(z, chunk, mine)

    for n, step in enumerate((1, -1)):

        @pl.when((z + step >= 0) & (z + step < parts))
        def _():
            send(
                wide_ref, wide_at(z, z + step), w_send.at[n, z], w_recv.at[z], beside(step)
            ).start()

    @pl.when(outside)
    def _():
        for chunk in range(CHUNKS):
            got(z, chunk)
            pass_on(z, chunk, chunk_of(rows_ref.at[z], core, chunk))

    def arrays_at(column):
        return depth_of(column * 2, 2), all_small_ref.at[column * 2 + core]

    def spread():
        own_small.wait()
        for step in range(1, parts):
            there = lax.rem(z + step, parts)
            send(small_ref, all_small_ref.at[dp, there], z_send.at[step], z_recv.at[there], sibling).wait_recv()
        for c in range(2):

            @pl.when(is_same(wq_source(c), me))
            def _():
                own_wq.wait()

            @pl.when(jnp.logical_not(is_same(wq_source(c), me)))
            def _():
                here = depth_of(xy * 2 + c, 1)
                send(here, here, q_send.at[0], q_recv.at[c], wq_source(c)).wait_recv()

        for step, there, device in plane_peers(shape, me):
            for n, ref in enumerate(arrays_at(xy)):
                send(ref, ref, p_send.at[n, step], p_recv.at[n, xy], device).start()
        ref = all_small_ref.at[dp]
        send(ref, ref, s_send.at[xy], s_recv.at[xy], sibling).start()

    for distance in range(1, parts):
        for chunk in range(CHUNKS):
            for shard in (z + distance, z - distance):

                @pl.when((shard >= 0) & (shard < parts))
                def _():
                    got(shard, chunk)
                    mine = chunk_of(rows_ref.at[shard], core, chunk)
                    pass_on(shard, chunk, mine)
                    share(shard, chunk, mine)

        if distance == 1:
            spread()
        for n, step in enumerate((1, -1)):
            shard = z - step * distance

            @pl.when((shard >= 0) & (shard < parts))
            def _():
                piece = wide_at(shard, z)
                send(piece, piece, w_send.at[n, shard], w_recv.at[shard], sibling).wait_recv()

            @pl.when((shard >= 0) & (shard < parts) & (z + step >= 0) & (z + step < parts))
            def _():
                send(
                    wide_at(shard, z), wide_at(shard, z + step), w_send.at[n, shard], w_recv.at[shard],
                    beside(step),
                ).start()

    for step in range(1, columns):
        there = lax.rem(xy + columns - step, columns)
        for n, ref in enumerate(arrays_at(there)):
            send(ref, ref, p_send.at[n, step], p_recv.at[n, there], sibling).wait_recv()
        ref = all_small_ref.at[there * 2 + core]
        send(ref, ref, s_send.at[there], s_recv.at[there], sibling).start()

    for column in range(columns):
        ref = all_small_ref.at[column * 2 + 1 - core]
        copy = send(ref, ref, s_send.at[column], s_recv.at[column], sibling)
        copy.wait_recv()
        copy.wait_send()
    for step in range(1, columns):
        for n, ref in enumerate(arrays_at(xy)):
            send(ref, ref, p_send.at[n, step], p_recv.at[n, xy], sibling).wait_send()
    for step in range(1, parts):
        send(small_ref, all_small_ref.at[dp, z], z_send.at[step], z_recv.at[z], sibling).wait_send()
    for n in range(2):

        @pl.when(jnp.logical_not(is_same(wq_target(n), me)))
        def _():
            send(wq_ref, depth_of(dp, 1), q_send.at[n], q_recv.at[core], sibling).wait_send()

    for n, step in enumerate((1, -1)):
        for distance in range(parts):
            shard = z - step * distance

            @pl.when((shard >= 0) & (shard < parts) & (z + step >= 0) & (z + step < parts))
            def _():
                send(
                    wide_ref, wide_ref, w_send.at[n, shard], w_recv.at[shard], beside(step)
                ).wait_send()

    for shard in range(parts):
        for chunk in range(CHUNKS):
            mine = chunk_of(rows_ref.at[shard], core, chunk)
            other = chunk_of(rows_ref.at[shard], 1 - core, chunk)
            copy = send(mine, other, share_send.at[shard, chunk], xs_recv.at[shard, chunk], sibling)

            @pl.when(jnp.logical_not((shard == z) & outside))
            def _():
                copy.wait_send()

            @pl.when(jnp.logical_not((shard == z) & inside))
            def _():
                copy.wait_recv()

            for n, way in enumerate(ways(shard)):

                @pl.when(way)
                def _():
                    send(
                        mine, mine, fwd_send.at[n, shard, chunk], x_recv.at[shard, chunk], sibling
                    ).wait_send()

    for chunk in range(CHUNKS):
        first = chunk_of(tokens_ref, 0, chunk)
        send(first, first, in_send.at[0, chunk], x_recv.at[z, chunk], sibling).wait_send()

        @pl.when(outside)
        def _():
            send(first, first, in_send.at[1, chunk], x_recv.at[z, chunk], sibling).wait_send()

    @pl.when(inside)
    def _():
        pltpu.make_async_copy(tokens_ref, rows_ref.at[z], local_sems.at[0]).wait()


def gather(shape, tokens, wq, small, wide):
    parts, columns = shape["zh"] * shape["zl"], shape["xy"]
    anywhere = pl.BlockSpec(memory_space=pl.ANY)
    dma = pltpu.SemaphoreType.DMA
    return pl.pallas_call(
        functools.partial(gather_kernel, shape),
        out_shape=[
            jax.ShapeDtypeStruct((parts, *tokens.shape), tokens.dtype),
            jax.ShapeDtypeStruct((3, 2 * columns * wq.shape[1], wq.shape[2]), wq.dtype),
            jax.ShapeDtypeStruct((2 * columns, parts, *small.shape), small.dtype),
            jax.ShapeDtypeStruct((parts - 1, *wide.shape), wide.dtype),
        ],
        in_specs=[anywhere] * 4,
        out_specs=[anywhere] * 4,
        scratch_shapes=[
            dma((3,)), dma((2, CHUNKS)), dma((2, parts, CHUNKS)), dma((parts, CHUNKS)),
            dma((parts, CHUNKS)), dma((parts, CHUNKS)),
            dma((parts,)), dma((parts,)), dma((2, columns)), dma((2, columns)), dma((columns,)),
            dma((columns,)), dma((2, parts)), dma((parts,)), dma((2,)), dma((2,)),
        ],
        compiler_params=pltpu.CompilerParams(collective_id=2, has_side_effects=True),
        name="gather",
    )(tokens, wq, small, wide)


class AllSum:
    def __init__(self, shape, column_slots, plane_slots, sems):
        self.shape, self.me = shape, place()
        self.slots, self.sems = (column_slots, plane_slots), sems
        xy, core, zh, zl = self.me
        self.mine = ((core * 2 + zh) * shape["zl"] + zl, xy)

    def peers(self, turn):
        return (column_peers if turn == 0 else plane_peers)(self.shape, self.me)

    def start(self, turn, value):
        slots, mine = self.slots[turn], self.mine[turn]
        slots[mine] = value
        for step, _, device in self.peers(turn):
            self.copy(turn, step, mine, device).start()

    def copy(self, turn, step, slot, device):
        here = self.slots[turn].at[slot]
        return send(
            here, here, self.sems.at[2 * turn, step], self.sems.at[2 * turn + 1, slot], device
        )

    def finish(self, turn):
        slots = self.slots[turn]
        for step, there, device in self.peers(turn):
            self.copy(turn, step, there, device).wait_recv()
        for step, _, device in self.peers(turn):
            self.copy(turn, step, self.mine[turn], device).wait_send()
        total = slots[0]
        for slot in range(1, slots.shape[0]):
            total = total + slots[slot]
        return total


LANES = 256


def lane_sums(values, ranges):
    lane = lax.broadcasted_iota(jnp.int32, values.shape, 1)
    return [
        jnp.sum(jnp.where((lane >= low) & (lane < high), values, 0.0)) for low, high in ranges
    ]


def small_ranges(n_bias, n_gain):
    ends = [0, n_bias] + [n_bias + n_gain * (n + 1) for n in range(4)]
    return list(zip(ends[:-1], ends[1:]))


def row_of(values):
    lane = lax.broadcasted_iota(jnp.int32, (1, 128), 1)
    row = jnp.zeros((1, 128), F32)
    for n, value in enumerate(values):
        row = jnp.where(lane == n, value, row)
    return row


class Rows:
    def __init__(self, shape):
        self.me = place()
        self.places = shape["zl"]

    def shard_at(self, index):
        return jnp.where(self.me[2] == 1, index, 2 * self.places - 1 - index)

    def early(self, group):
        return jnp.where(group == 1, 0, 2 * self.places - 1)

    def owner(self, shard):
        return (self.me[0], self.me[2], lax.div(shard, self.places), lax.rem(shard, self.places))

    def copy(self, src, dst, half, shard, send_sems, recv_sems):
        xy, core, zh, zl = self.me
        there = dst.at[zl, :, pl.ds(pl.multiple_of(core * half, half), half)]
        return send(src, there, send_sems.at[shard], recv_sems.at[zl, core], self.owner(shard))

    def take(self, dst, half, send_sems, recv_sems):
        xy, core, zh, zl = self.me
        for n in range(self.places):
            for c in range(2):
                here = dst.at[n, :, c * half : (c + 1) * half]
                copy = send(here, here, send_sems.at[0], recv_sems.at[n, c], (xy, c, core, n))

                @pl.when(jnp.logical_not(is_same((xy, c, core, n), self.me)))
                def _():
                    copy.wait_recv()


def sums_kernel(
    shape, n_bias, n_gain,
    a_ref, heads_ref, w_ref, norm_ref, small_ref, parts_ref, wq_ref, wp_ref, wu_ref, wd_ref, ws_ref,
    rows_ref, added_ref, sum_ref, wide_ref, small_sum_ref, totals_ref,
    first, total, turned, grad_qkv, small_all_ref, taken, added, plane, both, pieces, small_column, small_plane, row_column, row_plane,
    t_send, t_recv, o_send, o_recv, p_send, p_recv, q_send, q_recv, local_sems, small_sems, row_sems,
):
    me = place()
    xy, core, zh, zl = me
    places, columns = shape["zl"], shape["xy"]
    parts = 2 * places
    z = zh * places + zl
    sibling = (xy, 1 - core, zh, zl)
    head_block = zl * 2 + core
    rows, half = taken.shape[1], taken.shape[2]
    moves = Rows(shape)
    shard_at = moves.shard_at
    depth = both.shape[1] // 2
    small_all = AllSum(shape, small_column, small_plane, small_sems)
    row_all = AllSum(shape, row_column, row_plane, row_sems)

    def columns_at(which):
        return pl.ds(pl.multiple_of(which * half, half), half)

    def to_sibling(shard):
        part = first.at[shard, :, columns_at(1 - core)]
        return send(part, taken.at[shard], t_send.at[shard], t_recv.at[shard], sibling)

    def to_owner():
        shard = shard_at(0)
        return moves.copy(added.at[shard], rows_ref, half, shard, o_send, o_recv)

    keep_added = pltpu.make_async_copy(added, added_ref, local_sems.at[0])

    def add_rows(index):
        shard = shard_at(index)
        to_sibling(shard).wait_recv()
        here = first[shard, :, columns_at(core)]
        added[shard] = (here.astype(F32) + taken[shard].astype(F32)).astype(BF)

    def plane_part(c, column):
        return grad_qkv.at[c, pl.ds(pl.multiple_of(column * 2 * depth, 2 * depth), 2 * depth), :]

    def plane_copies(c):
        for step, there, device in plane_peers(shape, me):
            yield send(
                plane_part(c, there), plane.at[xy, c], p_send.at[c, step], p_recv.at[c, xy], device
            )

    def keep_part(c):
        return pltpu.make_async_copy(plane_part(c, xy), plane.at[xy, c], local_sems.at[3 + c])

    def back_of_shard(index):
        shard = shard_at(index)
        here = pl.ds(pl.multiple_of(shard * rows, rows), rows)
        part_sum = jnp.zeros((rows, 2 * half), F32)
        for c in range(3):
            part_sum = part_sum + dot(heads_ref[c, :, here].T, turned[c], 1, 0)
        first[shard] = part_sum.astype(BF)
        to_sibling(shard).start()

    def target(c):
        return (xy, c, lax.div(head_block, places), lax.rem(head_block, places))

    def source(n):
        return (xy, lax.rem(z, 2), n, lax.div(z, 2))

    def part(c):
        return both.at[:, c * depth : (c + 1) * depth, :]

    greet(shape)
    for c in range(3):
        turned[c] = w_ref[c].T
    back_of_shard(0)
    back_of_shard(1)
    add_rows(0)
    to_owner().start()

    shift_one = jnp.zeros((1, 2 * half), F32)
    gain_one = jnp.zeros((1, 2 * half), F32)
    for c in range(3):
        total[...] = jnp.zeros_like(total)
        for n in range(parts):
            here = slice(n * rows, (n + 1) * rows)
            total[...] += dot(heads_ref[c, :, here], a_ref[here, :], 1, 0)
        grad_qkv[c] = total[...].T.astype(BF)
        keep_part(c).start()
        for copy in plane_copies(c):
            copy.start()
        wide_turned = turned[c].astype(F32)
        head_sums = jnp.sum(heads_ref[c].astype(F32), axis=1, keepdims=True)
        shift_one = shift_one + jnp.sum(wide_turned * head_sums, axis=0, keepdims=True)
        gain_one = gain_one + jnp.sum(wide_turned * total[...], axis=0, keepdims=True)
    gain_one = (gain_one - norm_ref[1:2, :] * shift_one) / norm_ref[0:1, :]
    lines = [
        vector[:, n : n + LANES] for vector in (gain_one, shift_one) for n in range(0, 2 * half, LANES)
    ]
    small_all.start(0, jnp.concatenate([small_ref[...], *lines], axis=0))
    for index in range(2, parts):
        back_of_shard(index)

    def square(values):
        wide = values.astype(F32)
        return jnp.sum(wide * wide)

    wide = parts_ref[0].astype(F32)
    for n in range(1, parts):
        wide = wide + parts_ref[n].astype(F32)
    wide_ref[...] = wide
    up, down, proj = parts_of(wide_ref, wu_ref, wp_ref)
    values = [square(proj), square(up), square(down)]
    values += [square(wq_ref[c]) for c in range(3)]
    values += [square(ref[...]) for ref in (wp_ref, wu_ref, wd_ref)]
    ranges = small_ranges(n_bias, n_gain)
    values += lane_sums(ws_ref[...] * ws_ref[...], ranges)
    small_all.start(1, small_all.finish(0))

    for c in range(3):
        keep_part(c).wait()
        for step, there, device in plane_peers(shape, me):
            here = plane.at[there, c]
            send(here, here, p_send.at[c, step], p_recv.at[c, there], device).wait_recv()
        column_sum = plane[0, c].astype(F32)
        for n in range(1, columns):
            column_sum = column_sum + plane[n, c].astype(F32)
        both[c] = column_sum.astype(BF)
    for c in range(2):

        @pl.when(is_same(target(c), me))
        def _():
            pltpu.make_async_copy(part(c), pieces.at[zh], local_sems.at[2]).start()

        @pl.when(jnp.logical_not(is_same(target(c), me)))
        def _():
            send(part(c), pieces.at[zh], q_send.at[c], q_recv.at[zh], target(c)).start()

    for index in range(1, parts):
        add_rows(index)
    keep_added.start()
    small_all_ref[...] = small_all.finish(1)
    for n in range(2):

        @pl.when(is_same(target(n), me))
        def _():
            pltpu.make_async_copy(part(n), pieces.at[zh], local_sems.at[2]).wait()

        @pl.when(jnp.logical_not(is_same(target(n), me)))
        def _():
            send(part(n), pieces.at[zh], q_send.at[n], q_recv.at[zh], target(n)).wait_send()

        @pl.when(jnp.logical_not(is_same(source(n), me)))
        def _():
            send(part(n), pieces.at[n], q_send.at[n], q_recv.at[n], source(n)).wait_recv()

    squares = []
    for c in range(3):
        piece_sum = pieces[0, c].astype(F32) + pieces[1, c].astype(F32)
        sum_ref[c] = piece_sum
        squares.append(square(piece_sum))
    row_all.start(0, row_of(squares + values))
    row_all.start(1, row_all.finish(0))
    row = row_all.finish(1)
    lane = lax.broadcasted_iota(jnp.int32, (1, 128), 1)
    devices = small_ref.shape[0]
    count = 2 * half // LANES
    small = small_all_ref[0:devices, :]
    small_squares = lane_sums(small * small, ranges)
    for vector, spot in ((0, 1), (1, 3)):
        line = small_all_ref[devices + vector * count : devices + (vector + 1) * count, :]
        small_squares[spot] = jnp.sum(line * line)
    for n, value in enumerate(small_squares):
        row = jnp.where(lane == 17 + n, value, row)
    totals_ref[...] = row
    number = ((xy * 2 + core) * 2 + zh) * places + zl
    mine = small_all_ref[pl.ds(number, 1), :]
    column = lax.broadcasted_iota(jnp.int32, (1, LANES), 1)
    for vector, spot in ((0, 1), (1, 3)):
        low, high = ranges[spot]
        at = number * n_gain
        line = small_all_ref[pl.ds(devices + vector * count + lax.div(at, LANES), 1), :]
        line = pltpu.roll(line, lax.rem(low + LANES - lax.rem(at, LANES), LANES), 1)
        mine = jnp.where((column >= low) & (column < high), line, mine)
    small_sum_ref[...] = mine

    for c in range(3):
        for copy in plane_copies(c):
            copy.wait_send()
    for shard in range(parts):
        to_sibling(shard).wait_send()
    keep_added.wait()
    to_owner().wait_send()

    @pl.when(z == moves.early(core))
    def _():
        moves.take(rows_ref, half, o_send, o_recv)


def rows_kernel(
    shape, added_ref, early_ref, x_ref, middle_ref, gain_ref, out_ref,
    got, e_sem, keep_sem, o_send, o_recv,
):
    me = place()
    xy, core, zh, zl = me
    moves = Rows(shape)
    parts = added_ref.shape[0]
    half = added_ref.shape[2]
    z = zh * moves.places + zl
    is_early = z == moves.early(core)
    early = pltpu.make_async_copy(early_ref, got, e_sem)
    mine = got.at[zl, :, pl.ds(pl.multiple_of(core * half, half), half)]
    keep = pltpu.make_async_copy(added_ref.at[z], mine, keep_sem)

    def each(act):
        for index in range(1, parts):
            shard = moves.shard_at(index)

            @pl.when(jnp.logical_not(is_same(moves.owner(shard), me)))
            def _():
                act(moves.copy(added_ref.at[shard], got, half, shard, o_send, o_recv))

    greet_column(shape)
    each(lambda copy: copy.start())

    @pl.when(is_early)
    def _():
        early.start()

    @pl.when(zh == core)
    def _():
        keep.start()

    value, inverse = normed_of(x_ref[...].astype(F32))

    @pl.when(zh == core)
    def _():
        keep.wait()

    @pl.when(is_early)
    def _():
        early.wait()

    @pl.when(jnp.logical_not(is_early))
    def _():
        moves.take(got, half, o_send, o_recv)

    grad = got[0].astype(F32)
    for n in range(1, moves.places):
        grad = grad + got[n].astype(F32)
    inner = grad * gain_ref[...]
    out_ref[...] = (
        middle_ref[...]
        + inverse
        * (
            inner
            - jnp.mean(inner, axis=-1, keepdims=True)
            - value * jnp.mean(inner * value, axis=-1, keepdims=True)
        )
    ).astype(BF)
    each(lambda copy: copy.wait_send())


def finish_rows(shape, added, early, tokens, grad_middle, gain):
    places = shape["zl"]
    vmem = pl.BlockSpec(memory_space=pltpu.VMEM)
    anywhere = pl.BlockSpec(memory_space=pl.ANY)
    dma = pltpu.SemaphoreType.DMA
    return pl.pallas_call(
        functools.partial(rows_kernel, shape),
        out_shape=jax.ShapeDtypeStruct(tokens.shape, BF),
        in_specs=[anywhere, anywhere, vmem, vmem, vmem],
        out_specs=vmem,
        scratch_shapes=[
            pltpu.VMEM((places, *tokens.shape), BF),
            dma, dma, dma((2 * places,)), dma((places, 2)),
        ],
        compiler_params=pltpu.CompilerParams(
            collective_id=6, has_side_effects=True, vmem_limit_bytes=56 * 2**20
        ),
        name="finish_rows",
    )(added, early, tokens, grad_middle, gain)


def parts_of(wide_ref, up_like, proj_like):
    ff, heads = up_like.shape[1], proj_like.shape[0]
    return wide_ref[:, :ff], wide_ref[:, ff : 2 * ff], wide_ref[:, 2 * ff : 2 * ff + heads]


def sums(shape, n_bias, n_gain, a_first, grad_heads, w_heads, norm, small, wide, weights):
    places, columns = shape["zl"], shape["xy"]
    members, parts = 4 * places, 2 * places
    rows, width = a_first.shape[0] // parts, a_first.shape[1]
    depth = width // (2 * columns)
    heads_cols = w_heads.shape[2]
    lines = (small.shape[0] + 2 * width // LANES, LANES)
    vmem = pl.BlockSpec(memory_space=pltpu.VMEM)
    anywhere = pl.BlockSpec(memory_space=pl.ANY)
    dma = pltpu.SemaphoreType.DMA
    slots = max(members, columns)
    return pl.pallas_call(
        functools.partial(sums_kernel, shape, n_bias, n_gain),
        out_shape=[
            jax.ShapeDtypeStruct((places, rows, width), BF),
            jax.ShapeDtypeStruct((parts, rows, width // 2), BF),
            jax.ShapeDtypeStruct((3, depth, heads_cols), F32),
            jax.ShapeDtypeStruct(wide.shape[1:], F32),
            jax.ShapeDtypeStruct((1, LANES), F32),
            jax.ShapeDtypeStruct((1, 128), F32),
        ],
        in_specs=[vmem] * 11,
        out_specs=[anywhere] * 2 + [vmem] * 4,
        scratch_shapes=[
            pltpu.VMEM((parts, rows, width), BF),
            pltpu.VMEM((heads_cols, width), F32),
            pltpu.VMEM((3, heads_cols, width), BF),
            pltpu.VMEM((3, width, heads_cols), BF),
            pltpu.VMEM(lines, F32),
            pltpu.VMEM((parts, rows, width // 2), BF),
            pltpu.VMEM((parts, rows, width // 2), BF),
            pltpu.VMEM((columns, 3, 2 * depth, heads_cols), BF),
            pltpu.VMEM((3, 2 * depth, heads_cols), BF),
            pltpu.VMEM((2, 3, depth, heads_cols), BF),
            pltpu.VMEM((members, *lines), F32),
            pltpu.VMEM((columns, *lines), F32),
            pltpu.VMEM((members, 1, 128), F32),
            pltpu.VMEM((columns, 1, 128), F32),
            dma((parts,)), dma((parts,)), dma((parts,)), dma((places, 2)),
            dma((3, columns)), dma((3, columns)), dma((2,)), dma((2,)), dma((6,)),
            dma((4, slots)), dma((4, slots)),
        ],
        compiler_params=pltpu.CompilerParams(
            collective_id=3, has_side_effects=True, vmem_limit_bytes=50 * 2**20
        ),
        name="sums",
    )(a_first, grad_heads, w_heads, norm, small, wide, *weights)


def reduce_kernel(shape, row_ref, total_ref, row_column, row_plane, row_sems):
    greet(shape)
    both = AllSum(shape, row_column, row_plane, row_sems)
    both.start(0, row_ref[...])
    both.start(1, both.finish(0))
    total_ref[...] = both.finish(1)


def reduce_row(shape, row):
    members = 4 * shape["zl"]
    vmem = pl.BlockSpec(memory_space=pltpu.VMEM)
    return pl.pallas_call(
        functools.partial(reduce_kernel, shape),
        out_shape=jax.ShapeDtypeStruct((1, 128), F32),
        in_specs=[vmem],
        out_specs=vmem,
        scratch_shapes=[
            pltpu.VMEM((members, 1, 128), F32),
            pltpu.VMEM((shape["xy"], 1, 128), F32),
            pltpu.SemaphoreType.DMA((4, max(members, shape["xy"]))),
        ],
        compiler_params=pltpu.CompilerParams(collective_id=4, has_side_effects=True),
        name="reduce_row",
    )(row)


def moments_kernel(
    n_bias, n_gain, totals_ref, small_ref,
    gq, wide, wq, wp, wu, wd, ws, mq, mp, mu, md, ms, sq, sp, su, sd, ss,
    nmq, nmp, nmu, nmd, nmb, nmg, nmt, nsq, nsp, nsu, nsd, nsb, nsg, nst, uq, up, uu, ud, us, row_ref,
):
    totals = totals_ref[...]
    lane = lax.broadcasted_iota(jnp.int32, (1, 128), 1)
    grads_here = (lane < 6) | ((lane >= 17) & (lane < 22))
    norm = jnp.sqrt(jnp.sum(jnp.where(grads_here, totals, 0.0), axis=1, keepdims=True))
    clip = jnp.minimum(1.0, 1.0 / norm)
    values = []

    def step(grad, weight, mean, square):
        scaled = clip * grad
        new_mean = 0.5 * mean + 0.5 * scaled
        new_square = 0.5 * square + 0.5 * scaled * scaled
        update = new_mean / (jnp.sqrt(new_square) + 1e-06) + 0.01 * weight
        return new_mean, new_square, update

    for c in range(3):
        nmq[c], nsq[c], update = step(gq[c], wq[c], mq[c], sq[c])
        uq[c] = update
        values.append(jnp.sum(update * update))
    grad_up, grad_down, grad_proj = parts_of(wide, wu, wp)
    for turned, g, w, m, s, nm, ns, u in (
        (True, grad_proj, wp, mp, sp, nmp, nsp, up),
        (False, grad_up, wu, mu, su, nmu, nsu, uu),
        (True, grad_down, wd, md, sd, nmd, nsd, ud),
    ):
        grad = g.astype(F32)
        nm[...], ns[...], update = step(grad.T if turned else grad, w[...], m[...], s[...])
        u[...] = update
        values.append(jnp.sum(update * update))
    new_mean, new_square, update = step(small_ref[...], ws[...], ms[...], ss[...])
    us[...] = update
    ranges = small_ranges(n_bias, n_gain)
    values += lane_sums(update * update, ranges)
    row_ref[...] = row_of(values)
    put_small(ranges, new_mean, nmb, nmg, nmt)
    put_small(ranges, new_square, nsb, nsg, nst)


def put_small(ranges, row, bias, gain, shift):
    bias[...] = row[:, ranges[0][0] : ranges[0][1]]
    for n in range(2):
        gain[n : n + 1, :] = row[:, ranges[1 + n][0] : ranges[1 + n][1]]
        shift[n : n + 1, :] = row[:, ranges[3 + n][0] : ranges[3 + n][1]]


def weights_kernel(
    n_bias, n_gain, totals_ref, update_ref, wq, wp, wu, wd, ws, uq, up, uu, ud, us,
    nwq, nwp, nwu, nwd, nwb, nwg, nwt, norms_ref, norm_ref,
):
    totals, updates = totals_ref[...], update_ref[...]
    lane = lax.broadcasted_iota(jnp.int32, (1, 128), 1)
    grads_here = (lane < 6) | ((lane >= 17) & (lane < 22))
    norm_ref[...] = jnp.sqrt(jnp.sum(jnp.where(grads_here, totals, 0.0), axis=1, keepdims=True))
    weight_norm, update_norm = jnp.sqrt(totals), jnp.sqrt(updates)
    norms_ref[0:1, :] = weight_norm[:, 6:17]
    norms_ref[1:2, :] = update_norm[:, 0:11]

    def factor(n):
        return 0.3 * (weight_norm[:, 6 + n : 7 + n] / update_norm[:, n : n + 1])

    for c in range(3):
        nwq[c] = wq[c] - factor(c) * uq[c]
    for n, (w, u, out) in enumerate(((wp, up, nwp), (wu, uu, nwu), (wd, ud, nwd))):
        out[...] = w[...] - factor(3 + n) * u[...]
    ranges = small_ranges(n_bias, n_gain)
    column = lax.broadcasted_iota(jnp.int32, (1, LANES), 1)
    factors = jnp.zeros((1, LANES), F32)
    for n, (low, high) in enumerate(ranges):
        factors = jnp.where((column >= low) & (column < high), factor(6 + n), factors)
    put_small(ranges, ws[...] - factors * us[...], nwb, nwg, nwt)


def shapes_of(arrays):
    return [jax.ShapeDtypeStruct(array.shape, F32) for array in arrays]


def optimizer(shape, n_bias, n_gain, totals, small, grads, weights, means, squares, small_like):
    vmem = pl.BlockSpec(memory_space=pltpu.VMEM)
    big = list(weights[:4])
    results = shapes_of(big) + shapes_of(small_like)
    row = jax.ShapeDtypeStruct((1, 128), F32)
    params = pltpu.CompilerParams(vmem_limit_bytes=48 * 2**20)
    out = pl.pallas_call(
        functools.partial(moments_kernel, n_bias, n_gain),
        out_shape=results * 2 + shapes_of(weights) + [row],
        in_specs=[vmem] * 19,
        out_specs=[vmem] * 20,
        compiler_params=params,
        name="moments",
    )(totals, small, *grads, *weights, *means, *squares)
    new_means, new_squares, updates, row_here = out[:7], out[7:14], out[14:19], out[19]
    updates_total = reduce_row(shape, row_here)
    out = pl.pallas_call(
        functools.partial(weights_kernel, n_bias, n_gain),
        out_shape=results
        + [jax.ShapeDtypeStruct((2, 11), F32), jax.ShapeDtypeStruct((1, 1), F32)],
        in_specs=[vmem] * 12,
        out_specs=[vmem] * 9,
        compiler_params=params,
        name="weights",
    )(totals, updates_total, *weights, *updates)
    return updates_total, out[8], out[7], out[:7], new_means, new_squares


def turn_own_first(shape, core, src, dst):
    columns = shape["xy"]
    width = src.shape[1]
    depth = width // (2 * columns)
    for start in range(0, width, 128):
        turned = src[:, start : start + 128].T
        for offset in range(0, 128, depth):
            block = (start + offset) // depth
            slot = block // 2 + jnp.where(core == block % 2, 0, columns)
            dst[pl.ds(pl.multiple_of(slot * depth, depth), depth), :] = turned[offset : offset + depth]


def normed_of(values):
    center = values - jnp.mean(values, axis=-1, keepdims=True)
    inverse = lax.rsqrt(jnp.mean(center * center, axis=-1, keepdims=True) + 1e-05)
    return center * inverse, inverse


class Adder:
    def __init__(self, side, taken, first, sems):
        xy, core, zh, zl = place()
        self.side, self.taken, self.first = side, taken, first
        self.swap_send, self.swap_recv, *self.sems = sems
        self.at = (lax.div(xy, side), lax.rem(xy, side))
        self.rest = (core, zh, zl)
        self.sibling = (xy, 1 - core, zh, zl)

    def peers(self):
        xy = self.at[0] * self.side + self.at[1]
        columns = self.side * self.side
        return [self.sibling] + [
            (lax.rem(xy + step, columns), *self.rest) for step in range(1, columns)
        ]

    def swap(self, other, index):
        return send(other, self.taken.at[index], self.swap_send.at[index], self.swap_recv.at[index], self.sibling)

    def block(self, index, axis, there):
        return self.taken.at[index, :, there] if axis == 0 else self.taken.at[index, :, :, there]

    def owned(self, index, axis, step):
        there = lax.rem(self.at[1 - axis] + step, self.side)
        if axis == 0:
            return self.taken.at[index, :, self.at[0], there]
        return self.taken.at[index, :, there, self.at[1]]

    def copies(self, index, axis):
        for step in range(1, self.side):
            there = lax.rem(self.at[axis] + step, self.side)
            member = (there, self.at[1]) if axis == 0 else (self.at[0], there)
            yield send(
                self.block(index, axis, there), self.first.at[index, step - 1],
                self.sems[0].at[index, step - 1], self.sems[1].at[index, step - 1],
                (member[0] * self.side + member[1], *self.rest),
            )

    def by_parity(self, index, act):
        if isinstance(index, int):
            act(index % 2)
            return
        for parity in range(2):

            @pl.when(lax.rem(index, 2) == parity)
            def _():
                act(parity)

    def add_core(self, own, other, index):
        self.swap(other, index).wait_recv()
        for which in range(2):
            self.taken[index, which] = (
                own[which].astype(F32) + self.taken[index, which].astype(F32)
            ).astype(BF)

        def start(axis):
            for copy in self.copies(index, axis):
                copy.start()

        self.by_parity(index, start)

    def add_first(self, index, keep):
        def act(axis):
            mine = self.block(index, axis, self.at[axis])
            total = mine[...].astype(F32)
            for step, copy in enumerate(self.copies(index, axis)):
                copy.wait_recv()
                total = total + self.first[index, step].astype(F32)
            mine[...] = total.astype(BF)
            for copy in keep(index, axis):
                copy.start()

        self.by_parity(index, act)

    def end(self, index, keep):
        def act(axis):
            for copy in self.copies(index, axis):
                copy.wait_send()
            for copy in keep(index, axis):
                copy.wait()

        self.by_parity(index, act)


def feed_kernel(
    shape, ff_local, x_ref, c_ref, attn_ref, norm_ref, own_proj, other_proj, own_up, own_down, other_up, other_down,
    block_ref, middle_ref, given_ref, wide_ref, sums_ref,
    middle, total, second, a_second, a_turned, c_turned, own, other, taken, first_in,
    out_sems, keep_sems, proj_sems, *sems,
):
    step = pl.program_id(0)
    steps = taken.shape[0] - 1
    parts, heads_cols = attn_ref.shape[:2]
    side, chunk = own.shape[2], own.shape[5]
    half = c_turned.shape[0] // 2
    per = ff_local // chunk
    wide = 2 * ff_local + heads_cols
    slot = lax.rem(step, 2)
    adder = Adder(side, taken, first_in, sems)
    halves = own.shape[2:5]
    _, _, zh, zl = place()
    z = zh * shape["zl"] + zl

    def part_at(distance):
        return lax.rem(z + distance, parts)

    def proj_at(distance):
        return own_proj[...] if distance == 0 else other_proj[distance - 1]

    def keep(index, axis):
        for step in range(side):
            for which in range(2):
                start = part_at(lax.div(index, per)) * wide + which * ff_local + lax.rem(index, per) * chunk
                start = pl.multiple_of(start, 128)
                yield pltpu.make_async_copy(
                    adder.owned(index, axis, step).at[which], wide_ref.at[step, :, pl.ds(start, chunk)],
                    keep_sems.at[index, step, which],
                )

    def keep_proj(index, axis):
        for step in range(side):
            for part in range(parts):
                which, place_in = part // (parts // 2), part % (parts // 2)
                yield pltpu.make_async_copy(
                    adder.owned(index, axis, step).at[which, :, pl.ds(place_in * heads_cols, heads_cols)],
                    wide_ref.at[step, :, pl.ds(part * wide + 2 * ff_local, heads_cols)],
                    proj_sems.at[step, part],
                )

    def put(at, which, grad):
        own[at, which] = grad[:half].reshape(*halves, grad.shape[1])
        other[at, which] = grad[half:].reshape(*halves, grad.shape[1])

    @pl.when(step == 0)
    def _():
        barrier = pltpu.get_barrier_semaphore()
        for peer in adder.peers():
            pl.semaphore_signal(barrier, inc=1, device_id=peer, device_id_type=MESH)
        core = lax.axis_index("core")
        mixed = x_ref[...].astype(F32)
        for distance in range(parts):
            mixed = mixed + dot(attn_ref[part_at(distance)].T, proj_at(distance), 1, 1)
        middle[...] = mixed
        value, _ = normed_of(mixed)
        a_second[...] = (value * norm_ref[0:1, :] + norm_ref[1:2, :]).astype(BF)
        turn_own_first(shape, core, a_second, a_turned)
        turn_own_first(shape, core, c_ref, c_turned)
        total[...] = jnp.zeros_like(total)
        second[...] = jnp.zeros_like(second)
        pl.semaphore_wait(barrier, len(adder.peers()))

    @pl.when(step >= 2)
    def _():
        adder.swap(other.at[slot], step - 2).wait_send()

    mine = step < per
    up = jnp.where(mine, own_up[...], other_up[0])
    down = jnp.where(mine, own_down[...], other_down[0])
    pre = dot(a_second[...], up, 1, 0)
    grad_hidden = dot(c_ref[...], down, 1, 0)
    normal = 0.5 * (1.0 + lax.erf(pre * 2.0**-0.5))
    hidden = (pre * normal).astype(BF)
    slope = normal + pre * jnp.exp(-0.5 * pre * pre) * 0.3989422804014327
    grad_pre = (slope * grad_hidden).astype(BF)
    total[...] += dot(hidden, down, 1, 1)
    put(slot, 1, dot(c_turned[...], hidden, 1, 0).astype(BF))
    second[...] += dot(grad_pre, up, 1, 1)
    put(slot, 0, dot(a_turned[...], grad_pre, 1, 0).astype(BF))
    adder.swap(other.at[slot], step).start()

    @pl.when(step >= 1)
    def _():
        adder.add_core(own.at[1 - slot], other.at[1 - slot], step - 1)

    @pl.when(step >= 3)
    def _():
        adder.add_first(step - 3, keep)

    @pl.when(step == steps - 1)
    def _():
        core = lax.axis_index("core")
        last = steps - 1
        here, free = last % 2, 1 - last % 2
        adder.add_core(own.at[here], other.at[here], last)
        adder.add_first(last - 2, keep)
        a_second[...] = (middle[...] + total[...]).astype(BF)
        out_block = pltpu.make_async_copy(a_second, block_ref, out_sems.at[0])
        out_block.start()
        value, inverse = normed_of(middle[...])
        grad = second[...]
        sums_ref[0:1, :] = jnp.sum(grad * value, axis=0, keepdims=True)
        sums_ref[1:2, :] = jnp.sum(grad, axis=0, keepdims=True)
        inner = grad * norm_ref[0:1, :]
        second[...] = c_ref[...].astype(F32) + inverse * (
            inner
            - jnp.mean(inner, axis=-1, keepdims=True)
            - value * jnp.mean(inner * value, axis=-1, keepdims=True)
        )
        out_middle = pltpu.make_async_copy(second, middle_ref, out_sems.at[1])
        out_middle.start()
        low = second[...].astype(BF)
        turn_own_first(shape, core, low, a_turned)
        adder.swap(other.at[free], last - 1).wait_send()
        in_one = parts // 2
        for which in range(2):
            grads = [
                dot(a_turned[...], attn_ref[which * in_one + n], 1, 1).astype(BF) for n in range(in_one)
            ]
            put(free, which, jnp.concatenate(grads, axis=1))
        adder.swap(other.at[free], steps).start()
        adder.add_first(last - 1, keep)
        for distance in range(parts):
            rows = pl.ds(pl.multiple_of(part_at(distance) * heads_cols, heads_cols), heads_cols)
            c_turned[rows, :] = dot(low, proj_at(distance), 1, 0).T.astype(BF)
        out_given = pltpu.make_async_copy(c_turned, given_ref, out_sems.at[2])
        out_given.start()
        adder.add_core(own.at[free], other.at[free], steps)
        adder.add_first(last, keep)
        adder.add_first(steps, keep_proj)
        adder.swap(other.at[here], last).wait_send()
        adder.swap(other.at[free], steps).wait_send()
        for index in range(steps + 1):
            adder.end(index, keep if index < steps else keep_proj)
        for copy in (out_block, out_middle, out_given):
            copy.wait()


def column_segments(parts, ff_local, heads_cols):
    chunk = min(512, ff_local)
    per = ff_local // chunk
    segments = [
        (distance, which * ff_local + n * chunk, chunk, 1 - (distance * per + n) % 2)
        for distance in range(parts)
        for which in range(2)
        for n in range(per)
    ]
    return segments + [
        (distance, 2 * ff_local, heads_cols, 1 - parts * per % 2) for distance in range(parts)
    ]


def feed_forward(shape, tokens, cotangent, attn_rows, norm, shared_own, shared_others, ff_local):
    rows, width = tokens.shape
    parts, heads_cols = attn_rows.shape[:2]
    chunk = min(512, ff_local)
    per = ff_local // chunk
    steps = parts * per
    side = math.isqrt(shape["xy"])
    depth = width // (2 * shape["xy"])
    anywhere = pl.BlockSpec(memory_space=pl.ANY)

    def once(block, *index):
        return pl.BlockSpec(block, lambda s: index, pipeline_mode=pl.Buffered(1))

    dma = pltpu.SemaphoreType.DMA
    return pl.pallas_call(
        functools.partial(feed_kernel, shape, ff_local),
        grid=(steps,),
        in_specs=[
            once((rows, width), 0, 0),
            once((rows, width), 0, 0),
            once((parts, heads_cols, rows), 0, 0, 0),
            once((2, width), 0, 0),
            once((width, heads_cols), 0, 2 * ff_local // heads_cols),
            once((parts - 1, width, heads_cols), 0, 0, 2 * ff_local // heads_cols),
            *[
                pl.BlockSpec((width, chunk), lambda s, at=at: (0, at + jnp.minimum(s, per - 1)))
                for at in (0, per)
            ],
            *[
                pl.BlockSpec(
                    (1, width, chunk),
                    lambda s, at=at: (jnp.maximum(s - per, 0) // per, 0, at + jnp.maximum(s - per, 0) % per),
                )
                for at in (0, per)
            ],
        ],
        out_specs=[anywhere] * 4 + [pl.BlockSpec((2, width), lambda s: (0, 0))],
        out_shape=[
            jax.ShapeDtypeStruct((rows, width), BF),
            jax.ShapeDtypeStruct((rows, width), F32),
            jax.ShapeDtypeStruct((parts * heads_cols, rows), BF),
            jax.ShapeDtypeStruct((side, depth, parts * (2 * ff_local + heads_cols)), BF),
            jax.ShapeDtypeStruct((2, width), F32),
        ],
        scratch_shapes=[
            pltpu.VMEM((rows, width), F32),
            pltpu.VMEM((rows, width), F32),
            pltpu.VMEM((rows, width), F32),
            pltpu.VMEM((rows, width), BF),
            pltpu.VMEM((width, rows), BF),
            pltpu.VMEM((width, rows), BF),
            pltpu.VMEM((2, 2, side, side, depth, chunk), BF),
            pltpu.VMEM((2, 2, side, side, depth, chunk), BF),
            pltpu.VMEM((steps + 1, 2, side, side, depth, chunk), BF),
            pltpu.VMEM((steps + 1, side - 1, 2, side, depth, chunk), BF),
            dma((3,)),
            dma((steps, side, 2)),
            dma((side, parts)),
            dma((steps + 1,)),
            dma((steps + 1,)),
            dma((steps + 1, side - 1)),
            dma((steps + 1, side - 1)),
        ],
        compiler_params=pltpu.CompilerParams(
            vmem_limit_bytes=62 * 2**20, collective_id=5, has_side_effects=True
        ),
        name="feed_forward",
    )(tokens, cotangent, attn_rows, norm, shared_own, shared_others, *[shared_own] * 2, *[shared_others] * 2)


def norm_parts(values):
    center = values - jnp.mean(values, axis=-1, keepdims=True)
    inverse = lax.rsqrt(jnp.mean(center * center, axis=-1, keepdims=True) + 1e-05)
    return center * inverse, inverse


def norm_back(normed, inverse, gain, grad):
    inner = grad * gain
    return inverse * (
        inner
        - jnp.mean(inner, axis=-1, keepdims=True)
        - normed * jnp.mean(inner * normed, axis=-1, keepdims=True)
    )


def per_device(
    shape,
    tokens, cotangent, item_len, bucket_table,
    w_qkv, w_proj, w_up, w_down, rel_bias, ln_gain, ln_shift,
    mean_qkv, mean_proj, mean_up, mean_down, mean_bias, mean_gain, mean_shift,
    square_qkv, square_proj, square_up, square_down, square_bias, square_gain, square_shift,
):
    columns, places = shape["xy"], shape["zl"]
    parts = 2 * places
    devices = columns * 2 * parts
    rows, width = tokens.shape
    heads = w_qkv.shape[2] // DH
    tok = rows * parts
    xy, core, zh, zl = place()
    head_block = zl * 2 + core

    ff_local, heads_cols = w_up.shape[1], w_proj.shape[0]
    local = jnp.concatenate([w_up, w_down.T, w_proj.T], axis=1).astype(BF)

    shared_own = lax.all_gather(local, DP, axis=0, tiled=True)
    n_bias, n_gain = rel_bias.shape[0], ln_gain.shape[1]
    n_small = n_bias + 4 * n_gain

    def pack(bias, gain, shift):
        row = jnp.concatenate([bias, gain.reshape(-1), shift.reshape(-1)])
        return jnp.pad(row, (0, LANES - n_small))[None, :]

    small_weights = pack(rel_bias, ln_gain, ln_shift)
    group_rows, w_heads, small, wide = gather(
        shape, tokens, w_qkv.astype(BF), small_weights, local
    )
    shared_others = lax.all_gather(wide, DP, axis=1, tiled=True)
    small = small.reshape(devices, LANES)

    def columns_of(start):
        part = small[:, start : start + 2 * n_gain].reshape(devices, 2, n_gain)
        return part.transpose(1, 0, 2).reshape(2, width)

    table_flat = small[:, :n_bias].reshape(-1)
    gains, shifts = columns_of(n_bias), columns_of(n_bias + 2 * n_gain)
    other_len = lax.ppermute(item_len, "core", [(0, 1), (1, 0)])
    split = jnp.where(zh == core, item_len, other_len)[0, 0:1]

    norm_one = jnp.stack([gains[0], shifts[0]])
    a_first, qkv = project(group_rows.reshape(tok, width), norm_one, w_heads)
    qkv = qkv.reshape(3 * heads * DH, tok)

    table = lax.dynamic_slice_in_dim(
        table_flat.reshape(BUCKETS, H), head_block * heads, heads, 1
    )
    one_hot = (jnp.arange(BUCKETS)[:, None] == bucket_table[None, :]).astype(F32)
    dist_bias = lax.dot_general(
        table, one_hot, (((0,), (0,)), ((), ())), precision=HIGHEST, preferred_element_type=F32
    )
    pattern = jnp.concatenate(
        [dist_bias * LOG2E, jnp.full((heads, BLK), NEG, F32)], axis=1
    )[:, None, :]
    out, attn_rows, lse = attend(shape, qkv, pattern, split, heads)

    attn_rows = attn_rows.reshape(parts, heads * DH, rows)
    norm_two = jnp.stack([gains[1], shifts[1]])
    block_out, grad_middle, grad_attn, wide_grad, sums_two = feed_forward(
        shape, tokens, cotangent, attn_rows, norm_two, shared_own, shared_others, ff_local
    )
    gain_two, shift_two = sums_two[0], sums_two[1]
    given = grad_attn.reshape(parts, heads, DH, rows)
    grad_heads, wide_parts, grad_pattern = attend_back(
        shape, column_segments(parts, ff_local, w_proj.shape[0]), qkv, out, given, wide_grad, lse, pattern,
        split, heads,
    )
    grad_heads = grad_heads.reshape(3, heads * DH, tok)

    bias_grad = lax.dot_general(
        one_hot, grad_pattern[:, 0, :tok], (((1,), (1,)), ((), ())),
        precision=HIGHEST, preferred_element_type=F32,
    )
    table_grad = lax.dynamic_update_slice(
        jnp.zeros((BUCKETS, H), F32), bias_grad, (0, head_block * heads)
    )

    def by_device(*vectors):
        return jnp.stack(vectors).reshape(2, devices, n_gain).transpose(1, 0, 2).reshape(devices, -1)

    small_grad = jnp.concatenate(
        [
            table_grad.reshape(devices, n_bias),
            by_device(jnp.zeros_like(gain_two), gain_two),
            by_device(jnp.zeros_like(shift_two), shift_two),
            jnp.zeros((devices, LANES - n_small), F32),
        ],
        axis=1,
    )
    weights = (w_qkv, w_proj, w_up, w_down, small_weights)
    early_rows, added, sum_qkv, wide_sum, small_sum, totals = sums(
        shape, n_bias, n_gain, a_first, grad_heads, w_heads, norm_one, small_grad, wide_parts, weights
    )
    small_like = [rel_bias[None, :], ln_gain, ln_shift]
    updates_total, grad_norm, param_norms, *results = optimizer(
        shape, n_bias, n_gain, totals, small_sum,
        (sum_qkv, wide_sum), weights,
        (mean_qkv, mean_proj, mean_up, mean_down, pack(mean_bias, mean_gain, mean_shift)),
        (square_qkv, square_proj, square_up, square_down, pack(square_bias, square_gain, square_shift)),
        small_like,
    )
    added, _ = lax.optimization_barrier((added, updates_total))
    grad_tokens = finish_rows(shape, added, early_rows, tokens, grad_middle, gains[0:1])
    new = [array if n % 7 != 4 else array[0] for group in results for n, array in enumerate(group)]
    return (block_out, grad_tokens, grad_norm[0, 0], param_norms, *new)


def solution(mesh):
    shape = {"xy": mesh.shape["dp"] // 2, "core": 2, "zh": 2, "zl": mesh.shape["tensor"] // 2}
    split_mesh = Mesh(mesh.devices.reshape(tuple(shape[axis] for axis in ALL)), ALL)
    weights = (
        P(None, DP, TENSOR),
        P(TENSOR, DP),
        P(DP, TENSOR),
        P(TENSOR, DP),
        P(ALL),
        P(None, ALL),
        P(None, ALL),
    )
    rows = P(ALL, None)
    return jax.shard_map(
        functools.partial(per_device, shape),
        mesh=split_mesh,
        in_specs=(rows, rows, P(DP, None), P(), *weights, *weights, *weights),
        out_specs=(rows, rows, P(), P(), *weights, *weights, *weights),
        check_vma=False,
    )
```

```python
import functools
import math

import jax
import jax.numpy as jnp
from jax import lax
from jax.experimental import pallas as pl
from jax.experimental.pallas import tpu as pltpu
from jax.sharding import Mesh
from jax.sharding import PartitionSpec as P

H = 16
DH = 64
BUCKETS = 32
BLK = 512
NEG = -1e30
LOG2E = 1.4426950408889634
F32 = jnp.float32
BF = jnp.bfloat16
MESH = pl.DeviceIdType.MESH
HIGHEST = lax.Precision.HIGHEST
ALL = ("xy", "core", "zh", "zl")
DP = ("xy", "core")
TENSOR = ("zh", "zl")


def dot(left, right, left_dim, right_dim):
    return lax.dot_general(
        left, right, (((left_dim,), (right_dim,)), ((), ())), preferred_element_type=F32
    )


def project_kernel(x_ref, norm_ref, w_ref, a_ref, qkv_ref, turned):
    @pl.when(pl.program_id(0) == 0)
    def _():
        for c in range(3):
            turned[c] = w_ref[c].T

    values = x_ref[...].astype(F32)
    center = values - jnp.mean(values, axis=-1, keepdims=True)
    inverse = lax.rsqrt(jnp.mean(center * center, axis=-1, keepdims=True) + 1e-05)
    a_ref[...] = (center * inverse * norm_ref[0:1, :] + norm_ref[1:2, :]).astype(BF)
    for c in range(3):
        qkv_ref[c] = dot(turned[c], a_ref[...], 1, 1).astype(BF)


def project(rows, norm, weights):
    tok, width = rows.shape
    cols = weights.shape[2]
    return pl.pallas_call(
        project_kernel,
        grid=(tok // BLK,),
        in_specs=[
            pl.BlockSpec((BLK, width), lambda s: (s, 0)),
            pl.BlockSpec((2, width), lambda s: (0, 0)),
            pl.BlockSpec((3, width, cols), lambda s: (0, 0, 0)),
        ],
        out_specs=[
            pl.BlockSpec((BLK, width), lambda s: (s, 0)),
            pl.BlockSpec((3, cols, BLK), lambda s: (0, 0, s)),
        ],
        out_shape=[
            jax.ShapeDtypeStruct((tok, width), BF),
            jax.ShapeDtypeStruct((3, cols, tok), BF),
        ],
        scratch_shapes=[pltpu.VMEM((3, cols, width), BF)],
        compiler_params=pltpu.CompilerParams(vmem_limit_bytes=62 * 2**20),
        name="project",
    )(rows, norm, weights)


def make_slab(pattern, slab):
    width = slab.shape[1]
    slab[0:8, :] = pltpu.roll(jnp.broadcast_to(pattern, (8, width)), 0, 1, stride=1, stride_axis=0)
    done = 8
    while done < slab.shape[0]:
        slab[done : 2 * done, :] = pltpu.roll(slab[0:done, :], done, 1)
        done *= 2


def fold_slab(slab):
    width = slab.shape[1]
    half = slab.shape[0] // 2
    while half >= 8:
        slab[0:half, :] = slab[0:half, :] + pltpu.roll(slab[half : 2 * half, :], width - half, 1)
        half //= 2
    total = slab[0:1, :]
    for row in range(1, 8):
        total = total + pltpu.roll(slab[row : row + 1, :], width - row, 1)
    return total


def split_three(values):
    high = values.astype(BF).astype(F32)
    rest = values - high
    middle = rest.astype(BF).astype(F32)
    return high, middle, (rest - middle).astype(BF).astype(F32)


def put_queries(queries, split, minus, tok, dst):
    scaled = queries.astype(F32) * (DH**-0.5 * LOG2E)
    high = scaled.astype(BF)
    dst[0:DH, :] = high
    dst[DH : 2 * DH, :] = (scaled - high.astype(F32)).astype(BF)
    position = lax.broadcasted_iota(jnp.int32, (16, tok), 1)
    row = lax.broadcasted_iota(jnp.int32, (16, tok), 0)
    extra = jnp.where((row == 0) & (position >= split), 1.0, 0.0)
    if minus is not None:
        first, second, third = split_three(minus)
        extra = jnp.where(
            row == 1, first, jnp.where(row == 2, second, jnp.where(row == 3, third, extra))
        )
    dst[2 * DH : 2 * DH + 16, :] = extra.astype(BF)


def put_keys(keys, split, tok, dst):
    for start in range(0, tok, BLK):
        position = start + lax.broadcasted_iota(jnp.int32, (16, BLK), 1)
        row = lax.broadcasted_iota(jnp.int32, (16, BLK), 0)
        extra = jnp.where(
            row == 0, jnp.where(position < split, NEG, 0.0), jnp.where(row < 4, 1.0, 0.0)
        )
        block = keys[:, start : start + BLK].astype(F32)
        whole = jnp.concatenate([block, block, extra], axis=0)
        dst[start : start + BLK, :] = whole.T.astype(BF)


def block_at(index):
    return pl.ds(pl.multiple_of(index * BLK, BLK), BLK)


def attend_kernel(
    shape, split_ref, pattern_ref, q_ref, k_ref, v_ref, out_ref, rows_ref, lse_ref,
    slab, kx, qx, outs, local_sem, send_sem, recv_sem,
):
    head = pl.program_id(0)
    tok = q_ref.shape[1]
    split = split_ref[0]
    trade = Trade(shape, tok)

    @pl.when(head == 0)
    def _():
        greet_column(shape)

    make_slab(pattern_ref[0], slab)
    put_queries(q_ref[...], split, None, tok, qx)
    put_keys(k_ref, split, tok, kx)

    def steps(i, blocks, top, total, out):
        scores = [
            dot(kx[block_at(j), :], qx[:, block_at(i)], 1, 0) + slab[:, block_at(i - j)] for j in blocks
        ]
        new_top = top
        for score in scores:
            new_top = jnp.maximum(new_top, jnp.max(score, axis=0, keepdims=True))
        scale = jnp.exp2(top - new_top)
        total, out = total * scale, out * scale
        for j, score in zip(blocks, scores):
            weights = jnp.exp2(score - new_top)
            total = total + jnp.sum(weights, axis=0, keepdims=True)
            out = out + dot(v_ref[:, block_at(j)], weights.astype(BF), 1, 0)
        return new_top, total, out

    def row(i, carry):
        start = (
            jnp.full((1, BLK), NEG, F32),
            jnp.zeros((1, BLK), F32),
            jnp.zeros((DH, BLK), F32),
        )
        pairs = lax.fori_loop(
            0, (i + 1) // 2, lambda t, c: steps(i, (i - 2 * t, i - 2 * t - 1), *c), start
        )
        top, total, out = lax.fori_loop(0, (i + 1) % 2, lambda t, c: steps(i, (0,), *c), pairs)
        outs[head, :, block_at(i)] = (out / total).astype(BF)
        lse_ref[0, :, block_at(i)] = top + jnp.log2(total)
        return carry

    lax.fori_loop(0, tok // BLK, row, 0)

    def keep(h):
        return pltpu.make_async_copy(outs.at[h], out_ref.at[h], local_sem.at[0, h])

    def piece(h, n):
        return outs.at[h, :, pl.ds(pl.multiple_of(n * trade.rows, trade.rows), trade.rows)]

    def slot(h, n):
        return rows_ref.at[n, h]

    keep(head).start()
    trade.give(head, piece, slot, trade.owner, trade.head, local_sem.at[1, head], send_sem, recv_sem)

    @pl.when(head == pl.num_programs(0) - 1)
    def _():
        for h in range(rows_ref.shape[1]):
            keep(h).wait()
            trade.given(h, piece, slot, trade.owner, trade.head, local_sem.at[1, h], send_sem, recv_sem)
            trade.take(h, piece, slot, trade.header, send_sem, recv_sem)


def attend(shape, qkv, pattern, split, heads):
    tok = qkv.shape[1]
    width = pattern.shape[-1]
    parts = shape["zh"] * shape["zl"]
    dma = pltpu.SemaphoreType.DMA
    return pl.pallas_call(
        functools.partial(attend_kernel, shape),
        grid=(heads,),
        in_specs=[
            pl.BlockSpec(memory_space=pltpu.SMEM),
            pl.BlockSpec((1, 1, width), lambda h: (h, 0, 0)),
            pl.BlockSpec((DH, tok), lambda h: (h, 0)),
            pl.BlockSpec((DH, tok), lambda h: (h + heads, 0)),
            pl.BlockSpec((DH, tok), lambda h: (h + 2 * heads, 0)),
        ],
        out_specs=[
            pl.BlockSpec(memory_space=pl.ANY),
            pl.BlockSpec(memory_space=pl.ANY),
            pl.BlockSpec((1, 1, tok), lambda h: (h, 0, 0)),
        ],
        out_shape=[
            jax.ShapeDtypeStruct((heads, DH, tok), BF),
            jax.ShapeDtypeStruct((parts, heads, DH, tok // parts), BF),
            jax.ShapeDtypeStruct((heads, 1, tok), F32),
        ],
        scratch_shapes=[
            pltpu.VMEM((BLK, width), F32),
            pltpu.VMEM((tok, 2 * DH + 16), BF),
            pltpu.VMEM((2 * DH + 16, tok), BF),
            pltpu.VMEM((heads, DH, tok), BF),
            dma((2, heads)),
            dma((heads, parts)),
            dma((heads, parts)),
        ],
        compiler_params=pltpu.CompilerParams(
            vmem_limit_bytes=56 * 2**20, collective_id=0, has_side_effects=True
        ),
        name="attend",
    )(split, pattern, qkv, qkv, qkv)


def attend_back_kernel(
    shape, segments, split_ref, pattern_ref, q_ref, k_ref, v_ref, o_ref, lse_ref, given_ref, wide_ref,
    grads_ref, wide_parts_ref, dpattern_ref,
    slab, dslab, kx, qx, vx, dox, qn, don, dk, dv, taken, wide_own, wide_in,
    local_sem, in_send, in_recv, wide_sem, z_send, z_recv, w_send, w_recv,
):
    head = pl.program_id(0)
    tok = q_ref.shape[1]
    split = split_ref[0]
    trade = Trade(shape, tok)
    heads = taken.shape[0]

    def in_piece(h, n):
        return given_ref.at[n, h]

    def in_slot(h, n):
        return taken.at[h, :, pl.ds(pl.multiple_of(n * trade.rows, trade.rows), trade.rows)]

    xy, core, zh, zl = trade.me
    side = math.isqrt(shape["xy"])

    def column_copies():
        at = (lax.div(xy, side), lax.rem(xy, side))
        for step in range(1, side):
            for n, (distance, start, count, axis) in enumerate(segments):
                there = lax.rem(at[axis] + step, side)
                column = there * side + at[1] if axis == 0 else at[0] * side + there
                part = lax.rem(trade.row + distance, trade.parts)
                here = pl.ds(pl.multiple_of(part * wide_parts_ref.shape[2] + start, 128), count)
                yield send(
                    wide_ref.at[step, :, here], wide_in.at[step - 1, :, here],
                    w_send.at[step - 1, n], w_recv.at[step - 1, n], (column, core, zh, zl),
                )

    bring = pltpu.make_async_copy(wide_ref.at[0], wide_own, wide_sem.at[1])

    @pl.when(head == 0)
    def _():
        greet(shape)
        bring.start()
        for copy in column_copies():
            copy.start()
        for h in range(heads):
            trade.give(
                h, in_piece, in_slot, trade.header, trade.row, local_sem.at[h], in_send, in_recv
            )

    size = wide_parts_ref.shape[2]

    def wide_part(n):
        return wide_own.at[:, pl.ds(pl.multiple_of(n * size, size), size)]

    def along_z(step):
        there = lax.rem(trade.row + step, trade.parts)
        return there, (
            trade.me[0], trade.me[1], lax.div(there, trade.places), lax.rem(there, trade.places),
        )

    def wide_copy(step):
        there, device = along_z(step)
        return send(
            wide_part(there), wide_parts_ref.at[trade.row], z_send.at[step], z_recv.at[trade.row], device
        )

    keep_wide = pltpu.make_async_copy(
        wide_part(trade.row), wide_parts_ref.at[trade.row], wide_sem.at[0]
    )

    @pl.when(head == min(1, heads - 1))
    def _():
        bring.wait()
        for copy in column_copies():
            copy.wait_recv()
            copy.wait_send()
        for n in range(trade.parts):
            here = slice(n * size, (n + 1) * size)
            total = wide_own[:, here].astype(F32)
            for step in range(side - 1):
                total = total + wide_in[step, :, here].astype(F32)
            wide_own[:, here] = total.astype(BF)
        keep_wide.start()
        for step in range(1, trade.parts):
            wide_copy(step).start()

    make_slab(pattern_ref[0], slab)
    put_queries(q_ref[...], split, -lse_ref[0], tok, qx)
    put_keys(k_ref, split, tok, kx)
    dslab[...] = jnp.zeros_like(dslab)
    dk[...] = jnp.zeros_like(dk)
    dv[...] = jnp.zeros_like(dv)
    row = lax.broadcasted_iota(jnp.int32, (16, BLK), 0)
    ones = jnp.where(row < 3, 1.0, 0.0)
    trade.given(
        head, in_piece, in_slot, trade.header, trade.row, local_sem.at[head], in_send, in_recv
    )
    trade.take(head, in_piece, in_slot, trade.owner, in_send, in_recv)
    for start in range(0, tok, BLK):
        here = slice(start, start + BLK)
        low_grad = taken[head, :, here]
        grad = low_grad.astype(F32)
        inner = jnp.sum(grad * o_ref[0, :, here].astype(F32), axis=0, keepdims=True)
        first, second, third = split_three(-inner)
        extra = jnp.where(
            row == 0, first, jnp.where(row == 1, second, jnp.where(row == 2, third, 0.0))
        )
        dox[0:DH, here] = low_grad
        dox[DH : DH + 16, here] = extra.astype(BF)
        vx[here, :] = jnp.concatenate([v_ref[:, here].astype(F32), ones], axis=0).T.astype(BF)
        both = jnp.concatenate([q_ref[:, here].astype(F32), grad], axis=0).T
        qn[here, :] = both[:, 0:DH].astype(BF)
        don[here, :] = both[:, DH : 2 * DH].astype(BF)

    def tile(i, j):
        qs, ks, diagonal = block_at(i), block_at(j), block_at(i - j)
        shares = jnp.exp2(dot(kx[ks, :], qx[:, qs], 1, 0) + slab[:, diagonal])
        grad_scores = shares * dot(vx[ks, :], dox[:, qs], 1, 0)
        dslab[:, diagonal] += grad_scores
        low = grad_scores.astype(BF)
        dv[ks, :] += dot(shares.astype(BF), don[qs, :], 1, 0)
        dk[ks, :] += dot(low, qn[qs, :], 1, 0)
        return dot(k_ref[:, ks], low, 1, 0)

    def query_row(i, carry):
        total = lax.fori_loop(
            0,
            (i + 1) // 2,
            lambda t, c: c + tile(i, i - 2 * t) + tile(i, i - 2 * t - 1),
            jnp.zeros((DH, BLK), F32),
        )
        total = lax.fori_loop(0, (i + 1) % 2, lambda t, c: c + tile(i, 0), total)
        grads_ref[0, 0, :, block_at(i)] = (total * DH**-0.5).astype(BF)
        return carry

    lax.fori_loop(0, tok // BLK, query_row, 0)
    for start in range(0, tok, BLK):
        here = slice(start, start + BLK)
        grads_ref[1, 0, :, here] = (dk[here, :] * DH**-0.5).T.astype(BF)
        grads_ref[2, 0, :, here] = dv[here, :].T.astype(BF)
    dpattern_ref[0] = fold_slab(dslab)

    @pl.when(head == heads - 1)
    def _():
        keep_wide.wait()
        for step in range(1, trade.parts):
            there, device = along_z(step)
            here = wide_parts_ref.at[there]
            wide_copy(step).wait_send()
            send(here, here, z_send.at[step], z_recv.at[there], device).wait_recv()


def attend_back(shape, segments, qkv, out, given, wide, lse, pattern, split, heads):
    tok = qkv.shape[1]
    width = pattern.shape[-1]
    parts = shape["zh"] * shape["zl"]
    anywhere = pl.BlockSpec(memory_space=pl.ANY)
    dma = pltpu.SemaphoreType.DMA
    return pl.pallas_call(
        functools.partial(attend_back_kernel, shape, segments),
        grid=(heads,),
        in_specs=[
            pl.BlockSpec(memory_space=pltpu.SMEM),
            pl.BlockSpec((1, 1, width), lambda h: (h, 0, 0)),
            pl.BlockSpec((DH, tok), lambda h: (h, 0)),
            pl.BlockSpec((DH, tok), lambda h: (h + heads, 0)),
            pl.BlockSpec((DH, tok), lambda h: (h + 2 * heads, 0)),
            pl.BlockSpec((1, DH, tok), lambda h: (h, 0, 0)),
            pl.BlockSpec((1, 1, tok), lambda h: (h, 0, 0)),
            anywhere,
            anywhere,
        ],
        out_specs=[
            pl.BlockSpec((3, 1, DH, tok), lambda h: (0, h, 0, 0)),
            anywhere,
            pl.BlockSpec((1, 1, width), lambda h: (h, 0, 0)),
        ],
        out_shape=[
            jax.ShapeDtypeStruct((3, heads, DH, tok), BF),
            jax.ShapeDtypeStruct((parts, wide.shape[1], wide.shape[2] // parts), BF),
            jax.ShapeDtypeStruct((heads, 1, width), F32),
        ],
        scratch_shapes=[
            pltpu.VMEM((BLK, width), F32),
            pltpu.VMEM((BLK, width), F32),
            pltpu.VMEM((tok, 2 * DH + 16), BF),
            pltpu.VMEM((2 * DH + 16, tok), BF),
            pltpu.VMEM((tok, DH + 16), BF),
            pltpu.VMEM((DH + 16, tok), BF),
            pltpu.VMEM((tok, DH), BF),
            pltpu.VMEM((tok, DH), BF),
            pltpu.VMEM((tok, DH), F32),
            pltpu.VMEM((tok, DH), F32),
            pltpu.VMEM((heads, DH, tok), BF),
            pltpu.VMEM(wide.shape[1:], BF),
            pltpu.VMEM((wide.shape[0] - 1, *wide.shape[1:]), BF),
            dma((heads,)),
            dma((heads, parts)),
            dma((heads, parts)),
            dma((2,)), dma((parts,)), dma((parts,)),
            *[dma((wide.shape[0] - 1, len(segments)))] * 2,
        ],
        compiler_params=pltpu.CompilerParams(
            vmem_limit_bytes=60 * 2**20, collective_id=1, has_side_effects=True
        ),
        name="attend_back",
    )(split, pattern, qkv, qkv, qkv, out, lse, given, wide)


def place():
    return tuple(lax.axis_index(axis) for axis in ALL)


class Trade:
    def __init__(self, shape, tok):
        self.places = shape["zl"]
        self.parts = shape["zh"] * self.places
        self.rows = tok // self.parts
        self.me = place()
        _, core, zh, zl = self.me
        self.row = zh * self.places + zl
        self.head = zl * 2 + core

    def owner(self, n):
        return (self.me[0], self.me[2], lax.div(n, self.places), lax.rem(n, self.places))

    def header(self, n):
        return (self.me[0], lax.rem(n, 2), self.me[1], lax.div(n, 2))

    def each(self, device_of, local, remote):
        for index in range(self.parts):
            n = jnp.where(self.me[2] == 1, index, self.parts - 1 - index)
            device = device_of(n)
            if local is not None:

                @pl.when(is_same(device, self.me))
                def _():
                    local(n)

            @pl.when(jnp.logical_not(is_same(device, self.me)))
            def _():
                remote(n, device)

    def give(self, h, piece, slot, device_of, mine, local_sem, send_sem, recv_sem):
        def local(n):
            pltpu.make_async_copy(piece(h, n), slot(h, mine), local_sem).start()

        def remote(n, device):
            send(piece(h, n), slot(h, mine), send_sem.at[h, n], recv_sem.at[h, mine], device).start()

        self.each(device_of, local, remote)

    def given(self, h, piece, slot, device_of, mine, local_sem, send_sem, recv_sem):
        def local(n):
            pltpu.make_async_copy(piece(h, n), slot(h, mine), local_sem).wait()

        def remote(n, device):
            send(piece(h, n), slot(h, mine), send_sem.at[h, n], recv_sem.at[h, mine], device).wait_send()

        self.each(device_of, local, remote)

    def take(self, h, piece, slot, device_of, send_sem, recv_sem):
        def remote(n, device):
            send(piece(h, n), slot(h, n), send_sem.at[h, n], recv_sem.at[h, n], device).wait_recv()

        self.each(device_of, None, remote)


def is_same(left, right):
    same = left[0] == right[0]
    for one, other in zip(left[1:], right[1:]):
        same = same & (one == other)
    return same


def column_peers(shape, device):
    xy, core, zh, zl = device
    places = shape["zl"]
    total = 4 * places
    mine = (core * 2 + zh) * places + zl
    for step in range(1, total):
        there = lax.rem(mine + step, total)
        yield step, there, (xy, there // (2 * places), lax.rem(there // places, 2), lax.rem(there, places))


def plane_peers(shape, device):
    xy, core, zh, zl = device
    for step in range(1, shape["xy"]):
        there = lax.rem(xy + step, shape["xy"])
        yield step, there, (there, core, zh, zl)


def greet(shape):
    device = place()
    barrier = pltpu.get_barrier_semaphore()
    peers = [peer for _, _, peer in column_peers(shape, device)]
    peers += [peer for _, _, peer in plane_peers(shape, device)]
    for peer in peers:
        pl.semaphore_signal(barrier, inc=1, device_id=peer, device_id_type=MESH)
    pl.semaphore_wait(barrier, len(peers))


def greet_column(shape):
    barrier = pltpu.get_barrier_semaphore()
    peers = [peer for _, _, peer in column_peers(shape, place())]
    for peer in peers:
        pl.semaphore_signal(barrier, inc=1, device_id=peer, device_id_type=MESH)
    pl.semaphore_wait(barrier, len(peers))


def send(src, dst, send_sem, recv_sem, device):
    return pltpu.make_async_remote_copy(
        src_ref=src, dst_ref=dst, send_sem=send_sem, recv_sem=recv_sem,
        device_id=device, device_id_type=MESH,
    )


CHUNKS = 4


def gather_kernel(
    shape, tokens_ref, wq_ref, small_ref, wide_ref, rows_ref, heads_ref, all_small_ref, all_wide_ref,
    local_sems, in_send, fwd_send, share_send, x_recv, xs_recv,
    z_send, z_recv, p_send, p_recv, s_send, s_recv, w_send, w_recv, q_send, q_recv,
):
    me = place()
    xy, core, zh, zl = me
    places = shape["zl"]
    parts = 2 * places
    columns = shape["xy"]
    z = zh * places + zl
    sibling = (xy, 1 - core, zh, zl)
    size = tokens_ref.shape[0] // (2 * CHUNKS)
    dp = xy * 2 + core
    inside = core == zh
    outside = jnp.logical_not(inside)
    entry = jnp.where(zh < core, 0, places - 1)

    def chunk_of(ref, half, chunk):
        return ref.at[pl.ds(pl.multiple_of((half * CHUNKS + chunk) * size, size), size), :]

    def beside(step):
        there = z + step
        return (xy, core, there // places, lax.rem(there, places))

    greet(shape)

    depth = wq_ref.shape[1]
    head_block = zl * 2 + core

    def depth_of(index, count):
        return heads_ref.at[:, pl.ds(pl.multiple_of(index * depth, depth), count * depth), :]

    def wq_target(half):
        return (xy, lax.rem(z, 2), half, lax.div(z, 2))

    def wq_source(c):
        return (xy, c, lax.div(head_block, places), lax.rem(head_block, places))

    own_wq = pltpu.make_async_copy(wq_ref, depth_of(dp, 1), local_sems.at[1])
    own_small = pltpu.make_async_copy(small_ref, all_small_ref.at[dp, z], local_sems.at[2])

    def wide_at(shard, device_z):
        return all_wide_ref.at[lax.rem(shard + parts - device_z, parts) - 1]

    own_small.start()
    for n in range(2):

        @pl.when(is_same(wq_target(n), me))
        def _():
            own_wq.start()

        @pl.when(jnp.logical_not(is_same(wq_target(n), me)))
        def _():
            send(wq_ref, depth_of(dp, 1), q_send.at[n], q_recv.at[core], wq_target(n)).start()

    for step in range(1, parts):
        there = lax.rem(z + step, parts)
        device = (xy, core, there // places, lax.rem(there, places))
        send(small_ref, all_small_ref.at[dp, z], z_send.at[step], z_recv.at[z], device).start()

    @pl.when(outside)
    def _():
        for chunk in range(CHUNKS):
            for half in range(2):
                send(
                    chunk_of(tokens_ref, half, chunk), chunk_of(rows_ref.at[z], half, chunk),
                    in_send.at[half, chunk], x_recv.at[z, chunk], (xy, half, core, entry),
                ).start()

    @pl.when(inside)
    def _():
        for chunk in range(CHUNKS):
            send(
                chunk_of(tokens_ref, 1 - core, chunk), chunk_of(rows_ref.at[z], 1 - core, chunk),
                in_send.at[0, chunk], x_recv.at[z, chunk], sibling,
            ).start()
        pltpu.make_async_copy(tokens_ref, rows_ref.at[z], local_sems.at[0]).start()

    def ways(shard):
        from_half, from_place = shard // places, lax.rem(shard, places)
        start = jnp.where(from_half == zh, from_place, jnp.where(from_half < zh, 0, places - 1))
        return (zl >= start) & (zl < places - 1), (zl <= start) & (zl > 0)

    def pass_on(shard, chunk, source):
        mine = chunk_of(rows_ref.at[shard], core, chunk)
        for n, (way, step) in enumerate(zip(ways(shard), (1, -1))):

            @pl.when(way)
            def _():
                send(
                    source, mine, fwd_send.at[n, shard, chunk], x_recv.at[shard, chunk],
                    (xy, core, zh, zl + step),
                ).start()

    def share(shard, chunk, source):
        mine = chunk_of(rows_ref.at[shard], core, chunk)
        send(source, mine, share_send.at[shard, chunk], xs_recv.at[shard, chunk], sibling).start()

    def got(shard, chunk):
        mine = chunk_of(rows_ref.at[shard], core, chunk)
        send(mine, mine, share_send.at[shard, chunk], x_recv.at[shard, chunk], sibling).wait_recv()

    @pl.when(inside)
    def _():
        for chunk in range(CHUNKS):
            mine = chunk_of(tokens_ref, core, chunk)
            pass_on(z, chunk, mine)
            share(z, chunk, mine)

    for n, step in enumerate((1, -1)):

        @pl.when((z + step >= 0) & (z + step < parts))
        def _():
            send(
                wide_ref, wide_at(z, z + step), w_send.at[n, z], w_recv.at[z], beside(step)
            ).start()

    @pl.when(outside)
    def _():
        for chunk in range(CHUNKS):
            got(z, chunk)
            pass_on(z, chunk, chunk_of(rows_ref.at[z], core, chunk))

    def arrays_at(column):
        return depth_of(column * 2, 2), all_small_ref.at[column * 2 + core]

    def spread():
        own_small.wait()
        for step in range(1, parts):
            there = lax.rem(z + step, parts)
            send(small_ref, all_small_ref.at[dp, there], z_send.at[step], z_recv.at[there], sibling).wait_recv()
        for c in range(2):

            @pl.when(is_same(wq_source(c), me))
            def _():
                own_wq.wait()

            @pl.when(jnp.logical_not(is_same(wq_source(c), me)))
            def _():
                here = depth_of(xy * 2 + c, 1)
                send(here, here, q_send.at[0], q_recv.at[c], wq_source(c)).wait_recv()

        for step, there, device in plane_peers(shape, me):
            for n, ref in enumerate(arrays_at(xy)):
                send(ref, ref, p_send.at[n, step], p_recv.at[n, xy], device).start()
        ref = all_small_ref.at[dp]
        send(ref, ref, s_send.at[xy], s_recv.at[xy], sibling).start()

    for distance in range(1, parts):
        for chunk in range(CHUNKS):
            for shard in (z + distance, z - distance):

                @pl.when((shard >= 0) & (shard < parts))
                def _():
                    got(shard, chunk)
                    mine = chunk_of(rows_ref.at[shard], core, chunk)
                    pass_on(shard, chunk, mine)
                    share(shard, chunk, mine)

        if distance == 1:
            spread()
        for n, step in enumerate((1, -1)):
            shard = z - step * distance

            @pl.when((shard >= 0) & (shard < parts))
            def _():
                piece = wide_at(shard, z)
                send(piece, piece, w_send.at[n, shard], w_recv.at[shard], sibling).wait_recv()

            @pl.when((shard >= 0) & (shard < parts) & (z + step >= 0) & (z + step < parts))
            def _():
                send(
                    wide_at(shard, z), wide_at(shard, z + step), w_send.at[n, shard], w_recv.at[shard],
                    beside(step),
                ).start()

    for step in range(1, columns):
        there = lax.rem(xy + columns - step, columns)
        for n, ref in enumerate(arrays_at(there)):
            send(ref, ref, p_send.at[n, step], p_recv.at[n, there], sibling).wait_recv()
        ref = all_small_ref.at[there * 2 + core]
        send(ref, ref, s_send.at[there], s_recv.at[there], sibling).start()

    for column in range(columns):
        ref = all_small_ref.at[column * 2 + 1 - core]
        copy = send(ref, ref, s_send.at[column], s_recv.at[column], sibling)
        copy.wait_recv()
        copy.wait_send()
    for step in range(1, columns):
        for n, ref in enumerate(arrays_at(xy)):
            send(ref, ref, p_send.at[n, step], p_recv.at[n, xy], sibling).wait_send()
    for step in range(1, parts):
        send(small_ref, all_small_ref.at[dp, z], z_send.at[step], z_recv.at[z], sibling).wait_send()
    for n in range(2):

        @pl.when(jnp.logical_not(is_same(wq_target(n), me)))
        def _():
            send(wq_ref, depth_of(dp, 1), q_send.at[n], q_recv.at[core], sibling).wait_send()

    for n, step in enumerate((1, -1)):
        for distance in range(parts):
            shard = z - step * distance

            @pl.when((shard >= 0) & (shard < parts) & (z + step >= 0) & (z + step < parts))
            def _():
                send(
                    wide_ref, wide_ref, w_send.at[n, shard], w_recv.at[shard], beside(step)
                ).wait_send()

    for shard in range(parts):
        for chunk in range(CHUNKS):
            mine = chunk_of(rows_ref.at[shard], core, chunk)
            other = chunk_of(rows_ref.at[shard], 1 - core, chunk)
            copy = send(mine, other, share_send.at[shard, chunk], xs_recv.at[shard, chunk], sibling)

            @pl.when(jnp.logical_not((shard == z) & outside))
            def _():
                copy.wait_send()

            @pl.when(jnp.logical_not((shard == z) & inside))
            def _():
                copy.wait_recv()

            for n, way in enumerate(ways(shard)):

                @pl.when(way)
                def _():
                    send(
                        mine, mine, fwd_send.at[n, shard, chunk], x_recv.at[shard, chunk], sibling
                    ).wait_send()

    for chunk in range(CHUNKS):
        first = chunk_of(tokens_ref, 0, chunk)
        send(first, first, in_send.at[0, chunk], x_recv.at[z, chunk], sibling).wait_send()

        @pl.when(outside)
        def _():
            send(first, first, in_send.at[1, chunk], x_recv.at[z, chunk], sibling).wait_send()

    @pl.when(inside)
    def _():
        pltpu.make_async_copy(tokens_ref, rows_ref.at[z], local_sems.at[0]).wait()


def gather(shape, tokens, wq, small, wide):
    parts, columns = shape["zh"] * shape["zl"], shape["xy"]
    anywhere = pl.BlockSpec(memory_space=pl.ANY)
    dma = pltpu.SemaphoreType.DMA
    return pl.pallas_call(
        functools.partial(gather_kernel, shape),
        out_shape=[
            jax.ShapeDtypeStruct((parts, *tokens.shape), tokens.dtype),
            jax.ShapeDtypeStruct((3, 2 * columns * wq.shape[1], wq.shape[2]), wq.dtype),
            jax.ShapeDtypeStruct((2 * columns, parts, *small.shape), small.dtype),
            jax.ShapeDtypeStruct((parts - 1, *wide.shape), wide.dtype),
        ],
        in_specs=[anywhere] * 4,
        out_specs=[anywhere] * 4,
        scratch_shapes=[
            dma((3,)), dma((2, CHUNKS)), dma((2, parts, CHUNKS)), dma((parts, CHUNKS)),
            dma((parts, CHUNKS)), dma((parts, CHUNKS)),
            dma((parts,)), dma((parts,)), dma((2, columns)), dma((2, columns)), dma((columns,)),
            dma((columns,)), dma((2, parts)), dma((parts,)), dma((2,)), dma((2,)),
        ],
        compiler_params=pltpu.CompilerParams(collective_id=2, has_side_effects=True),
        name="gather",
    )(tokens, wq, small, wide)


class AllSum:
    def __init__(self, shape, column_slots, plane_slots, sems):
        self.shape, self.me = shape, place()
        self.slots, self.sems = (column_slots, plane_slots), sems
        xy, core, zh, zl = self.me
        self.mine = ((core * 2 + zh) * shape["zl"] + zl, xy)

    def peers(self, turn):
        return (column_peers if turn == 0 else plane_peers)(self.shape, self.me)

    def start(self, turn, value):
        slots, mine = self.slots[turn], self.mine[turn]
        slots[mine] = value
        for step, _, device in self.peers(turn):
            self.copy(turn, step, mine, device).start()

    def copy(self, turn, step, slot, device):
        here = self.slots[turn].at[slot]
        return send(
            here, here, self.sems.at[2 * turn, step], self.sems.at[2 * turn + 1, slot], device
        )

    def finish(self, turn):
        slots = self.slots[turn]
        for step, there, device in self.peers(turn):
            self.copy(turn, step, there, device).wait_recv()
        for step, _, device in self.peers(turn):
            self.copy(turn, step, self.mine[turn], device).wait_send()
        total = slots[0]
        for slot in range(1, slots.shape[0]):
            total = total + slots[slot]
        return total


LANES = 256


def lane_sums(values, ranges):
    lane = lax.broadcasted_iota(jnp.int32, values.shape, 1)
    return [
        jnp.sum(jnp.where((lane >= low) & (lane < high), values, 0.0)) for low, high in ranges
    ]


def small_ranges(n_bias, n_gain):
    ends = [0, n_bias] + [n_bias + n_gain * (n + 1) for n in range(4)]
    return list(zip(ends[:-1], ends[1:]))


def row_of(values):
    lane = lax.broadcasted_iota(jnp.int32, (1, 128), 1)
    row = jnp.zeros((1, 128), F32)
    for n, value in enumerate(values):
        row = jnp.where(lane == n, value, row)
    return row


class Rows:
    def __init__(self, shape):
        self.me = place()
        self.places = shape["zl"]

    def shard_at(self, index):
        return jnp.where(self.me[2] == 1, index, 2 * self.places - 1 - index)

    def early(self, group):
        return jnp.where(group == 1, 0, 2 * self.places - 1)

    def owner(self, shard):
        return (self.me[0], self.me[2], lax.div(shard, self.places), lax.rem(shard, self.places))

    def copy(self, src, dst, half, shard, send_sems, recv_sems):
        xy, core, zh, zl = self.me
        there = dst.at[zl, :, pl.ds(pl.multiple_of(core * half, half), half)]
        return send(src, there, send_sems.at[shard], recv_sems.at[zl, core], self.owner(shard))

    def take(self, dst, half, send_sems, recv_sems):
        xy, core, zh, zl = self.me
        for n in range(self.places):
            for c in range(2):
                here = dst.at[n, :, c * half : (c + 1) * half]
                copy = send(here, here, send_sems.at[0], recv_sems.at[n, c], (xy, c, core, n))

                @pl.when(jnp.logical_not(is_same((xy, c, core, n), self.me)))
                def _():
                    copy.wait_recv()


def sums_kernel(
    shape, n_bias, n_gain,
    a_ref, heads_ref, w_ref, norm_ref, small_ref, parts_ref, wq_ref, wp_ref, wu_ref, wd_ref, ws_ref,
    rows_ref, added_ref, sum_ref, wide_ref, small_sum_ref, totals_ref,
    first, total, turned, grad_qkv, small_all_ref, taken, added, plane, both, pieces, small_column, small_plane, row_column, row_plane,
    t_send, t_recv, o_send, o_recv, p_send, p_recv, q_send, q_recv, local_sems, small_sems, row_sems,
):
    me = place()
    xy, core, zh, zl = me
    places, columns = shape["zl"], shape["xy"]
    parts = 2 * places
    z = zh * places + zl
    sibling = (xy, 1 - core, zh, zl)
    head_block = zl * 2 + core
    rows, half = taken.shape[1], taken.shape[2]
    moves = Rows(shape)
    shard_at = moves.shard_at
    depth = both.shape[1] // 2
    small_all = AllSum(shape, small_column, small_plane, small_sems)
    row_all = AllSum(shape, row_column, row_plane, row_sems)

    def columns_at(which):
        return pl.ds(pl.multiple_of(which * half, half), half)

    def to_sibling(shard):
        part = first.at[shard, :, columns_at(1 - core)]
        return send(part, taken.at[shard], t_send.at[shard], t_recv.at[shard], sibling)

    def to_owner():
        shard = shard_at(0)
        return moves.copy(added.at[shard], rows_ref, half, shard, o_send, o_recv)

    keep_added = pltpu.make_async_copy(added, added_ref, local_sems.at[0])

    def add_rows(index):
        shard = shard_at(index)
        to_sibling(shard).wait_recv()
        here = first[shard, :, columns_at(core)]
        added[shard] = (here.astype(F32) + taken[shard].astype(F32)).astype(BF)

    def plane_part(c, column):
        return grad_qkv.at[c, pl.ds(pl.multiple_of(column * 2 * depth, 2 * depth), 2 * depth), :]

    def plane_copies(c):
        for step, there, device in plane_peers(shape, me):
            yield send(
                plane_part(c, there), plane.at[xy, c], p_send.at[c, step], p_recv.at[c, xy], device
            )

    def keep_part(c):
        return pltpu.make_async_copy(plane_part(c, xy), plane.at[xy, c], local_sems.at[3 + c])

    def back_of_shard(index):
        shard = shard_at(index)
        here = pl.ds(pl.multiple_of(shard * rows, rows), rows)
        part_sum = jnp.zeros((rows, 2 * half), F32)
        for c in range(3):
            part_sum = part_sum + dot(heads_ref[c, :, here].T, turned[c], 1, 0)
        first[shard] = part_sum.astype(BF)
        to_sibling(shard).start()

    def target(c):
        return (xy, c, lax.div(head_block, places), lax.rem(head_block, places))

    def source(n):
        return (xy, lax.rem(z, 2), n, lax.div(z, 2))

    def part(c):
        return both.at[:, c * depth : (c + 1) * depth, :]

    greet(shape)
    for c in range(3):
        turned[c] = w_ref[c].T
    back_of_shard(0)
    back_of_shard(1)
    add_rows(0)
    to_owner().start()

    shift_one = jnp.zeros((1, 2 * half), F32)
    gain_one = jnp.zeros((1, 2 * half), F32)
    for c in range(3):
        total[...] = jnp.zeros_like(total)
        for n in range(parts):
            here = slice(n * rows, (n + 1) * rows)
            total[...] += dot(heads_ref[c, :, here], a_ref[here, :], 1, 0)
        grad_qkv[c] = total[...].T.astype(BF)
        keep_part(c).start()
        for copy in plane_copies(c):
            copy.start()
        wide_turned = turned[c].astype(F32)
        head_sums = jnp.sum(heads_ref[c].astype(F32), axis=1, keepdims=True)
        shift_one = shift_one + jnp.sum(wide_turned * head_sums, axis=0, keepdims=True)
        gain_one = gain_one + jnp.sum(wide_turned * total[...], axis=0, keepdims=True)
    gain_one = (gain_one - norm_ref[1:2, :] * shift_one) / norm_ref[0:1, :]
    lines = [
        vector[:, n : n + LANES] for vector in (gain_one, shift_one) for n in range(0, 2 * half, LANES)
    ]
    small_all.start(0, jnp.concatenate([small_ref[...], *lines], axis=0))
    for index in range(2, parts):
        back_of_shard(index)

    def square(values):
        wide = values.astype(F32)
        return jnp.sum(wide * wide)

    wide = parts_ref[0].astype(F32)
    for n in range(1, parts):
        wide = wide + parts_ref[n].astype(F32)
    wide_ref[...] = wide
    up, down, proj = parts_of(wide_ref, wu_ref, wp_ref)
    values = [square(proj), square(up), square(down)]
    values += [square(wq_ref[c]) for c in range(3)]
    values += [square(ref[...]) for ref in (wp_ref, wu_ref, wd_ref)]
    ranges = small_ranges(n_bias, n_gain)
    values += lane_sums(ws_ref[...] * ws_ref[...], ranges)

    for c in range(3):
        keep_part(c).wait()
        for step, there, device in plane_peers(shape, me):
            here = plane.at[there, c]
            send(here, here, p_send.at[c, step], p_recv.at[c, there], device).wait_recv()
        column_sum = plane[0, c].astype(F32)
        for n in range(1, columns):
            column_sum = column_sum + plane[n, c].astype(F32)
        both[c] = column_sum.astype(BF)
    for c in range(2):

        @pl.when(is_same(target(c), me))
        def _():
            pltpu.make_async_copy(part(c), pieces.at[zh], local_sems.at[2]).start()

        @pl.when(jnp.logical_not(is_same(target(c), me)))
        def _():
            send(part(c), pieces.at[zh], q_send.at[c], q_recv.at[zh], target(c)).start()

    small_all.start(1, small_all.finish(0))
    for index in range(1, parts):
        add_rows(index)
    keep_added.start()
    small_all_ref[...] = small_all.finish(1)
    for n in range(2):

        @pl.when(is_same(target(n), me))
        def _():
            pltpu.make_async_copy(part(n), pieces.at[zh], local_sems.at[2]).wait()

        @pl.when(jnp.logical_not(is_same(target(n), me)))
        def _():
            send(part(n), pieces.at[zh], q_send.at[n], q_recv.at[zh], target(n)).wait_send()

        @pl.when(jnp.logical_not(is_same(source(n), me)))
        def _():
            send(part(n), pieces.at[n], q_send.at[n], q_recv.at[n], source(n)).wait_recv()

    squares = []
    for c in range(3):
        piece_sum = pieces[0, c].astype(F32) + pieces[1, c].astype(F32)
        sum_ref[c] = piece_sum
        squares.append(square(piece_sum))
    row_all.start(0, row_of(squares + values))
    row_all.start(1, row_all.finish(0))
    row = row_all.finish(1)
    lane = lax.broadcasted_iota(jnp.int32, (1, 128), 1)
    devices = small_ref.shape[0]
    count = 2 * half // LANES
    small = small_all_ref[0:devices, :]
    small_squares = lane_sums(small * small, ranges)
    for vector, spot in ((0, 1), (1, 3)):
        line = small_all_ref[devices + vector * count : devices + (vector + 1) * count, :]
        small_squares[spot] = jnp.sum(line * line)
    for n, value in enumerate(small_squares):
        row = jnp.where(lane == 17 + n, value, row)
    totals_ref[...] = row
    number = ((xy * 2 + core) * 2 + zh) * places + zl
    mine = small_all_ref[pl.ds(number, 1), :]
    column = lax.broadcasted_iota(jnp.int32, (1, LANES), 1)
    for vector, spot in ((0, 1), (1, 3)):
        low, high = ranges[spot]
        at = number * n_gain
        line = small_all_ref[pl.ds(devices + vector * count + lax.div(at, LANES), 1), :]
        line = pltpu.roll(line, lax.rem(low + LANES - lax.rem(at, LANES), LANES), 1)
        mine = jnp.where((column >= low) & (column < high), line, mine)
    small_sum_ref[...] = mine

    for c in range(3):
        for copy in plane_copies(c):
            copy.wait_send()
    for shard in range(parts):
        to_sibling(shard).wait_send()
    keep_added.wait()
    to_owner().wait_send()

    @pl.when(z == moves.early(core))
    def _():
        moves.take(rows_ref, half, o_send, o_recv)


def rows_kernel(
    shape, added_ref, early_ref, x_ref, middle_ref, gain_ref, out_ref,
    got, e_sem, keep_sem, o_send, o_recv,
):
    me = place()
    xy, core, zh, zl = me
    moves = Rows(shape)
    parts = added_ref.shape[0]
    half = added_ref.shape[2]
    z = zh * moves.places + zl
    is_early = z == moves.early(core)
    early = pltpu.make_async_copy(early_ref, got, e_sem)
    mine = got.at[zl, :, pl.ds(pl.multiple_of(core * half, half), half)]
    keep = pltpu.make_async_copy(added_ref.at[z], mine, keep_sem)

    def each(act):
        for index in range(1, parts):
            shard = moves.shard_at(index)

            @pl.when(jnp.logical_not(is_same(moves.owner(shard), me)))
            def _():
                act(moves.copy(added_ref.at[shard], got, half, shard, o_send, o_recv))

    greet_column(shape)
    each(lambda copy: copy.start())

    @pl.when(is_early)
    def _():
        early.start()

    @pl.when(zh == core)
    def _():
        keep.start()

    value, inverse = normed_of(x_ref[...].astype(F32))

    @pl.when(zh == core)
    def _():
        keep.wait()

    @pl.when(is_early)
    def _():
        early.wait()

    @pl.when(jnp.logical_not(is_early))
    def _():
        moves.take(got, half, o_send, o_recv)

    grad = got[0].astype(F32)
    for n in range(1, moves.places):
        grad = grad + got[n].astype(F32)
    inner = grad * gain_ref[...]
    out_ref[...] = (
        middle_ref[...]
        + inverse
        * (
            inner
            - jnp.mean(inner, axis=-1, keepdims=True)
            - value * jnp.mean(inner * value, axis=-1, keepdims=True)
        )
    ).astype(BF)
    each(lambda copy: copy.wait_send())


def finish_rows(shape, added, early, tokens, grad_middle, gain):
    places = shape["zl"]
    vmem = pl.BlockSpec(memory_space=pltpu.VMEM)
    anywhere = pl.BlockSpec(memory_space=pl.ANY)
    dma = pltpu.SemaphoreType.DMA
    return pl.pallas_call(
        functools.partial(rows_kernel, shape),
        out_shape=jax.ShapeDtypeStruct(tokens.shape, BF),
        in_specs=[anywhere, anywhere, vmem, vmem, vmem],
        out_specs=vmem,
        scratch_shapes=[
            pltpu.VMEM((places, *tokens.shape), BF),
            dma, dma, dma((2 * places,)), dma((places, 2)),
        ],
        compiler_params=pltpu.CompilerParams(
            collective_id=6, has_side_effects=True, vmem_limit_bytes=56 * 2**20
        ),
        name="finish_rows",
    )(added, early, tokens, grad_middle, gain)


def parts_of(wide_ref, up_like, proj_like):
    ff, heads = up_like.shape[1], proj_like.shape[0]
    return wide_ref[:, :ff], wide_ref[:, ff : 2 * ff], wide_ref[:, 2 * ff : 2 * ff + heads]


def sums(shape, n_bias, n_gain, a_first, grad_heads, w_heads, norm, small, wide, weights):
    places, columns = shape["zl"], shape["xy"]
    members, parts = 4 * places, 2 * places
    rows, width = a_first.shape[0] // parts, a_first.shape[1]
    depth = width // (2 * columns)
    heads_cols = w_heads.shape[2]
    lines = (small.shape[0] + 2 * width // LANES, LANES)
    vmem = pl.BlockSpec(memory_space=pltpu.VMEM)
    anywhere = pl.BlockSpec(memory_space=pl.ANY)
    dma = pltpu.SemaphoreType.DMA
    slots = max(members, columns)
    return pl.pallas_call(
        functools.partial(sums_kernel, shape, n_bias, n_gain),
        out_shape=[
            jax.ShapeDtypeStruct((places, rows, width), BF),
            jax.ShapeDtypeStruct((parts, rows, width // 2), BF),
            jax.ShapeDtypeStruct((3, depth, heads_cols), F32),
            jax.ShapeDtypeStruct(wide.shape[1:], F32),
            jax.ShapeDtypeStruct((1, LANES), F32),
            jax.ShapeDtypeStruct((1, 128), F32),
        ],
        in_specs=[vmem] * 11,
        out_specs=[anywhere] * 2 + [vmem] * 4,
        scratch_shapes=[
            pltpu.VMEM((parts, rows, width), BF),
            pltpu.VMEM((heads_cols, width), F32),
            pltpu.VMEM((3, heads_cols, width), BF),
            pltpu.VMEM((3, width, heads_cols), BF),
            pltpu.VMEM(lines, F32),
            pltpu.VMEM((parts, rows, width // 2), BF),
            pltpu.VMEM((parts, rows, width // 2), BF),
            pltpu.VMEM((columns, 3, 2 * depth, heads_cols), BF),
            pltpu.VMEM((3, 2 * depth, heads_cols), BF),
            pltpu.VMEM((2, 3, depth, heads_cols), BF),
            pltpu.VMEM((members, *lines), F32),
            pltpu.VMEM((columns, *lines), F32),
            pltpu.VMEM((members, 1, 128), F32),
            pltpu.VMEM((columns, 1, 128), F32),
            dma((parts,)), dma((parts,)), dma((parts,)), dma((places, 2)),
            dma((3, columns)), dma((3, columns)), dma((2,)), dma((2,)), dma((6,)),
            dma((4, slots)), dma((4, slots)),
        ],
        compiler_params=pltpu.CompilerParams(
            collective_id=3, has_side_effects=True, vmem_limit_bytes=50 * 2**20
        ),
        name="sums",
    )(a_first, grad_heads, w_heads, norm, small, wide, *weights)


def reduce_kernel(shape, row_ref, total_ref, row_column, row_plane, row_sems):
    greet(shape)
    both = AllSum(shape, row_column, row_plane, row_sems)
    both.start(0, row_ref[...])
    both.start(1, both.finish(0))
    total_ref[...] = both.finish(1)


def reduce_row(shape, row):
    members = 4 * shape["zl"]
    vmem = pl.BlockSpec(memory_space=pltpu.VMEM)
    return pl.pallas_call(
        functools.partial(reduce_kernel, shape),
        out_shape=jax.ShapeDtypeStruct((1, 128), F32),
        in_specs=[vmem],
        out_specs=vmem,
        scratch_shapes=[
            pltpu.VMEM((members, 1, 128), F32),
            pltpu.VMEM((shape["xy"], 1, 128), F32),
            pltpu.SemaphoreType.DMA((4, max(members, shape["xy"]))),
        ],
        compiler_params=pltpu.CompilerParams(collective_id=4, has_side_effects=True),
        name="reduce_row",
    )(row)


def moments_kernel(
    n_bias, n_gain, totals_ref, small_ref,
    gq, wide, wq, wp, wu, wd, ws, mq, mp, mu, md, ms, sq, sp, su, sd, ss,
    nmq, nmp, nmu, nmd, nmb, nmg, nmt, nsq, nsp, nsu, nsd, nsb, nsg, nst, uq, up, uu, ud, us, row_ref,
):
    totals = totals_ref[...]
    lane = lax.broadcasted_iota(jnp.int32, (1, 128), 1)
    grads_here = (lane < 6) | ((lane >= 17) & (lane < 22))
    norm = jnp.sqrt(jnp.sum(jnp.where(grads_here, totals, 0.0), axis=1, keepdims=True))
    clip = jnp.minimum(1.0, 1.0 / norm)
    values = []

    def step(grad, weight, mean, square):
        scaled = clip * grad
        new_mean = 0.5 * mean + 0.5 * scaled
        new_square = 0.5 * square + 0.5 * scaled * scaled
        update = new_mean / (jnp.sqrt(new_square) + 1e-06) + 0.01 * weight
        return new_mean, new_square, update

    for c in range(3):
        nmq[c], nsq[c], update = step(gq[c], wq[c], mq[c], sq[c])
        uq[c] = update
        values.append(jnp.sum(update * update))
    grad_up, grad_down, grad_proj = parts_of(wide, wu, wp)
    for turned, g, w, m, s, nm, ns, u in (
        (True, grad_proj, wp, mp, sp, nmp, nsp, up),
        (False, grad_up, wu, mu, su, nmu, nsu, uu),
        (True, grad_down, wd, md, sd, nmd, nsd, ud),
    ):
        grad = g.astype(F32)
        nm[...], ns[...], update = step(grad.T if turned else grad, w[...], m[...], s[...])
        u[...] = update
        values.append(jnp.sum(update * update))
    new_mean, new_square, update = step(small_ref[...], ws[...], ms[...], ss[...])
    us[...] = update
    ranges = small_ranges(n_bias, n_gain)
    values += lane_sums(update * update, ranges)
    row_ref[...] = row_of(values)
    put_small(ranges, new_mean, nmb, nmg, nmt)
    put_small(ranges, new_square, nsb, nsg, nst)


def put_small(ranges, row, bias, gain, shift):
    bias[...] = row[:, ranges[0][0] : ranges[0][1]]
    for n in range(2):
        gain[n : n + 1, :] = row[:, ranges[1 + n][0] : ranges[1 + n][1]]
        shift[n : n + 1, :] = row[:, ranges[3 + n][0] : ranges[3 + n][1]]


def weights_kernel(
    n_bias, n_gain, totals_ref, update_ref, wq, wp, wu, wd, ws, uq, up, uu, ud, us,
    nwq, nwp, nwu, nwd, nwb, nwg, nwt, norms_ref, norm_ref,
):
    totals, updates = totals_ref[...], update_ref[...]
    lane = lax.broadcasted_iota(jnp.int32, (1, 128), 1)
    grads_here = (lane < 6) | ((lane >= 17) & (lane < 22))
    norm_ref[...] = jnp.sqrt(jnp.sum(jnp.where(grads_here, totals, 0.0), axis=1, keepdims=True))
    weight_norm, update_norm = jnp.sqrt(totals), jnp.sqrt(updates)
    norms_ref[0:1, :] = weight_norm[:, 6:17]
    norms_ref[1:2, :] = update_norm[:, 0:11]

    def factor(n):
        return 0.3 * (weight_norm[:, 6 + n : 7 + n] / update_norm[:, n : n + 1])

    for c in range(3):
        nwq[c] = wq[c] - factor(c) * uq[c]
    for n, (w, u, out) in enumerate(((wp, up, nwp), (wu, uu, nwu), (wd, ud, nwd))):
        out[...] = w[...] - factor(3 + n) * u[...]
    ranges = small_ranges(n_bias, n_gain)
    column = lax.broadcasted_iota(jnp.int32, (1, LANES), 1)
    factors = jnp.zeros((1, LANES), F32)
    for n, (low, high) in enumerate(ranges):
        factors = jnp.where((column >= low) & (column < high), factor(6 + n), factors)
    put_small(ranges, ws[...] - factors * us[...], nwb, nwg, nwt)


def shapes_of(arrays):
    return [jax.ShapeDtypeStruct(array.shape, F32) for array in arrays]


def optimizer(shape, n_bias, n_gain, totals, small, grads, weights, means, squares, small_like):
    vmem = pl.BlockSpec(memory_space=pltpu.VMEM)
    big = list(weights[:4])
    results = shapes_of(big) + shapes_of(small_like)
    row = jax.ShapeDtypeStruct((1, 128), F32)
    params = pltpu.CompilerParams(vmem_limit_bytes=48 * 2**20)
    out = pl.pallas_call(
        functools.partial(moments_kernel, n_bias, n_gain),
        out_shape=results * 2 + shapes_of(weights) + [row],
        in_specs=[vmem] * 19,
        out_specs=[vmem] * 20,
        compiler_params=params,
        name="moments",
    )(totals, small, *grads, *weights, *means, *squares)
    new_means, new_squares, updates, row_here = out[:7], out[7:14], out[14:19], out[19]
    updates_total = reduce_row(shape, row_here)
    out = pl.pallas_call(
        functools.partial(weights_kernel, n_bias, n_gain),
        out_shape=results
        + [jax.ShapeDtypeStruct((2, 11), F32), jax.ShapeDtypeStruct((1, 1), F32)],
        in_specs=[vmem] * 12,
        out_specs=[vmem] * 9,
        compiler_params=params,
        name="weights",
    )(totals, updates_total, *weights, *updates)
    return updates_total, out[8], out[7], out[:7], new_means, new_squares


def turn_own_first(shape, core, src, dst):
    columns = shape["xy"]
    width = src.shape[1]
    depth = width // (2 * columns)
    for start in range(0, width, 128):
        turned = src[:, start : start + 128].T
        for offset in range(0, 128, depth):
            block = (start + offset) // depth
            slot = block // 2 + jnp.where(core == block % 2, 0, columns)
            dst[pl.ds(pl.multiple_of(slot * depth, depth), depth), :] = turned[offset : offset + depth]


def normed_of(values):
    center = values - jnp.mean(values, axis=-1, keepdims=True)
    inverse = lax.rsqrt(jnp.mean(center * center, axis=-1, keepdims=True) + 1e-05)
    return center * inverse, inverse


class Adder:
    def __init__(self, side, taken, first, sems):
        xy, core, zh, zl = place()
        self.side, self.taken, self.first = side, taken, first
        self.swap_send, self.swap_recv, *self.sems = sems
        self.at = (lax.div(xy, side), lax.rem(xy, side))
        self.rest = (core, zh, zl)
        self.sibling = (xy, 1 - core, zh, zl)

    def peers(self):
        xy = self.at[0] * self.side + self.at[1]
        columns = self.side * self.side
        return [self.sibling] + [
            (lax.rem(xy + step, columns), *self.rest) for step in range(1, columns)
        ]

    def swap(self, other, index):
        return send(other, self.taken.at[index], self.swap_send.at[index], self.swap_recv.at[index], self.sibling)

    def block(self, index, axis, there):
        return self.taken.at[index, :, there] if axis == 0 else self.taken.at[index, :, :, there]

    def owned(self, index, axis, step):
        there = lax.rem(self.at[1 - axis] + step, self.side)
        if axis == 0:
            return self.taken.at[index, :, self.at[0], there]
        return self.taken.at[index, :, there, self.at[1]]

    def copies(self, index, axis):
        for step in range(1, self.side):
            there = lax.rem(self.at[axis] + step, self.side)
            member = (there, self.at[1]) if axis == 0 else (self.at[0], there)
            yield send(
                self.block(index, axis, there), self.first.at[index, step - 1],
                self.sems[0].at[index, step - 1], self.sems[1].at[index, step - 1],
                (member[0] * self.side + member[1], *self.rest),
            )

    def by_parity(self, index, act):
        if isinstance(index, int):
            act(index % 2)
            return
        for parity in range(2):

            @pl.when(lax.rem(index, 2) == parity)
            def _():
                act(parity)

    def add_core(self, own, other, index):
        self.swap(other, index).wait_recv()
        for which in range(2):
            self.taken[index, which] = (
                own[which].astype(F32) + self.taken[index, which].astype(F32)
            ).astype(BF)

        def start(axis):
            for copy in self.copies(index, axis):
                copy.start()

        self.by_parity(index, start)

    def add_first(self, index, keep):
        def act(axis):
            mine = self.block(index, axis, self.at[axis])
            total = mine[...].astype(F32)
            for step, copy in enumerate(self.copies(index, axis)):
                copy.wait_recv()
                total = total + self.first[index, step].astype(F32)
            mine[...] = total.astype(BF)
            for copy in keep(index, axis):
                copy.start()

        self.by_parity(index, act)

    def end(self, index, keep):
        def act(axis):
            for copy in self.copies(index, axis):
                copy.wait_send()
            for copy in keep(index, axis):
                copy.wait()

        self.by_parity(index, act)


def feed_kernel(
    shape, ff_local, x_ref, c_ref, attn_ref, norm_ref, own_proj, other_proj, own_up, own_down, other_up, other_down,
    block_ref, middle_ref, given_ref, wide_ref, sums_ref,
    middle, total, second, a_second, a_turned, c_turned, own, other, taken, first_in,
    out_sems, keep_sems, proj_sems, *sems,
):
    step = pl.program_id(0)
    steps = taken.shape[0] - 1
    parts, heads_cols = attn_ref.shape[:2]
    side, chunk = own.shape[2], own.shape[5]
    half = c_turned.shape[0] // 2
    per = ff_local // chunk
    wide = 2 * ff_local + heads_cols
    slot = lax.rem(step, 2)
    adder = Adder(side, taken, first_in, sems)
    halves = own.shape[2:5]
    _, _, zh, zl = place()
    z = zh * shape["zl"] + zl

    def part_at(distance):
        return lax.rem(z + distance, parts)

    def proj_at(distance):
        return own_proj[...] if distance == 0 else other_proj[distance - 1]

    def keep(index, axis):
        for step in range(side):
            for which in range(2):
                start = part_at(lax.div(index, per)) * wide + which * ff_local + lax.rem(index, per) * chunk
                start = pl.multiple_of(start, 128)
                yield pltpu.make_async_copy(
                    adder.owned(index, axis, step).at[which], wide_ref.at[step, :, pl.ds(start, chunk)],
                    keep_sems.at[index, step, which],
                )

    def keep_proj(index, axis):
        for step in range(side):
            for part in range(parts):
                which, place_in = part // (parts // 2), part % (parts // 2)
                yield pltpu.make_async_copy(
                    adder.owned(index, axis, step).at[which, :, pl.ds(place_in * heads_cols, heads_cols)],
                    wide_ref.at[step, :, pl.ds(part * wide + 2 * ff_local, heads_cols)],
                    proj_sems.at[step, part],
                )

    def put(at, which, grad):
        own[at, which] = grad[:half].reshape(*halves, grad.shape[1])
        other[at, which] = grad[half:].reshape(*halves, grad.shape[1])

    @pl.when(step == 0)
    def _():
        barrier = pltpu.get_barrier_semaphore()
        for peer in adder.peers():
            pl.semaphore_signal(barrier, inc=1, device_id=peer, device_id_type=MESH)
        core = lax.axis_index("core")
        mixed = x_ref[...].astype(F32)
        for distance in range(parts):
            mixed = mixed + dot(attn_ref[part_at(distance)].T, proj_at(distance), 1, 1)
        middle[...] = mixed
        value, _ = normed_of(mixed)
        a_second[...] = (value * norm_ref[0:1, :] + norm_ref[1:2, :]).astype(BF)
        turn_own_first(shape, core, a_second, a_turned)
        turn_own_first(shape, core, c_ref, c_turned)
        total[...] = jnp.zeros_like(total)
        second[...] = jnp.zeros_like(second)
        pl.semaphore_wait(barrier, len(adder.peers()))

    @pl.when(step >= 2)
    def _():
        adder.swap(other.at[slot], step - 2).wait_send()

    mine = step < per
    up = jnp.where(mine, own_up[...], other_up[0])
    down = jnp.where(mine, own_down[...], other_down[0])
    pre = dot(a_second[...], up, 1, 0)
    grad_hidden = dot(c_ref[...], down, 1, 0)
    normal = 0.5 * (1.0 + lax.erf(pre * 2.0**-0.5))
    hidden = (pre * normal).astype(BF)
    slope = normal + pre * jnp.exp(-0.5 * pre * pre) * 0.3989422804014327
    grad_pre = (slope * grad_hidden).astype(BF)
    total[...] += dot(hidden, down, 1, 1)
    put(slot, 1, dot(c_turned[...], hidden, 1, 0).astype(BF))
    second[...] += dot(grad_pre, up, 1, 1)
    put(slot, 0, dot(a_turned[...], grad_pre, 1, 0).astype(BF))
    adder.swap(other.at[slot], step).start()

    @pl.when(step >= 1)
    def _():
        adder.add_core(own.at[1 - slot], other.at[1 - slot], step - 1)

    @pl.when(step >= 3)
    def _():
        adder.add_first(step - 3, keep)

    @pl.when(step == steps - 1)
    def _():
        core = lax.axis_index("core")
        last = steps - 1
        here, free = last % 2, 1 - last % 2
        adder.add_core(own.at[here], other.at[here], last)
        adder.add_first(last - 2, keep)
        a_second[...] = (middle[...] + total[...]).astype(BF)
        out_block = pltpu.make_async_copy(a_second, block_ref, out_sems.at[0])
        out_block.start()
        value, inverse = normed_of(middle[...])
        grad = second[...]
        sums_ref[0:1, :] = jnp.sum(grad * value, axis=0, keepdims=True)
        sums_ref[1:2, :] = jnp.sum(grad, axis=0, keepdims=True)
        inner = grad * norm_ref[0:1, :]
        second[...] = c_ref[...].astype(F32) + inverse * (
            inner
            - jnp.mean(inner, axis=-1, keepdims=True)
            - value * jnp.mean(inner * value, axis=-1, keepdims=True)
        )
        out_middle = pltpu.make_async_copy(second, middle_ref, out_sems.at[1])
        out_middle.start()
        low = second[...].astype(BF)
        turn_own_first(shape, core, low, a_turned)
        adder.swap(other.at[free], last - 1).wait_send()
        in_one = parts // 2
        for which in range(2):
            grads = [
                dot(a_turned[...], attn_ref[which * in_one + n], 1, 1).astype(BF) for n in range(in_one)
            ]
            put(free, which, jnp.concatenate(grads, axis=1))
        adder.swap(other.at[free], steps).start()
        adder.add_first(last - 1, keep)
        for distance in range(parts):
            rows = pl.ds(pl.multiple_of(part_at(distance) * heads_cols, heads_cols), heads_cols)
            c_turned[rows, :] = dot(low, proj_at(distance), 1, 0).T.astype(BF)
        out_given = pltpu.make_async_copy(c_turned, given_ref, out_sems.at[2])
        out_given.start()
        adder.add_core(own.at[free], other.at[free], steps)
        adder.add_first(last, keep)
        adder.add_first(steps, keep_proj)
        adder.swap(other.at[here], last).wait_send()
        adder.swap(other.at[free], steps).wait_send()
        for index in range(steps + 1):
            adder.end(index, keep if index < steps else keep_proj)
        for copy in (out_block, out_middle, out_given):
            copy.wait()


def column_segments(parts, ff_local, heads_cols):
    chunk = min(512, ff_local)
    per = ff_local // chunk
    segments = [
        (distance, which * ff_local + n * chunk, chunk, 1 - (distance * per + n) % 2)
        for distance in range(parts)
        for which in range(2)
        for n in range(per)
    ]
    return segments + [
        (distance, 2 * ff_local, heads_cols, 1 - parts * per % 2) for distance in range(parts)
    ]


def feed_forward(shape, tokens, cotangent, attn_rows, norm, shared_own, shared_others, ff_local):
    rows, width = tokens.shape
    parts, heads_cols = attn_rows.shape[:2]
    chunk = min(512, ff_local)
    per = ff_local // chunk
    steps = parts * per
    side = math.isqrt(shape["xy"])
    depth = width // (2 * shape["xy"])
    anywhere = pl.BlockSpec(memory_space=pl.ANY)

    def once(block, *index):
        return pl.BlockSpec(block, lambda s: index, pipeline_mode=pl.Buffered(1))

    dma = pltpu.SemaphoreType.DMA
    return pl.pallas_call(
        functools.partial(feed_kernel, shape, ff_local),
        grid=(steps,),
        in_specs=[
            once((rows, width), 0, 0),
            once((rows, width), 0, 0),
            once((parts, heads_cols, rows), 0, 0, 0),
            once((2, width), 0, 0),
            once((width, heads_cols), 0, 2 * ff_local // heads_cols),
            once((parts - 1, width, heads_cols), 0, 0, 2 * ff_local // heads_cols),
            *[
                pl.BlockSpec((width, chunk), lambda s, at=at: (0, at + jnp.minimum(s, per - 1)))
                for at in (0, per)
            ],
            *[
                pl.BlockSpec(
                    (1, width, chunk),
                    lambda s, at=at: (jnp.maximum(s - per, 0) // per, 0, at + jnp.maximum(s - per, 0) % per),
                )
                for at in (0, per)
            ],
        ],
        out_specs=[anywhere] * 4 + [pl.BlockSpec((2, width), lambda s: (0, 0))],
        out_shape=[
            jax.ShapeDtypeStruct((rows, width), BF),
            jax.ShapeDtypeStruct((rows, width), F32),
            jax.ShapeDtypeStruct((parts * heads_cols, rows), BF),
            jax.ShapeDtypeStruct((side, depth, parts * (2 * ff_local + heads_cols)), BF),
            jax.ShapeDtypeStruct((2, width), F32),
        ],
        scratch_shapes=[
            pltpu.VMEM((rows, width), F32),
            pltpu.VMEM((rows, width), F32),
            pltpu.VMEM((rows, width), F32),
            pltpu.VMEM((rows, width), BF),
            pltpu.VMEM((width, rows), BF),
            pltpu.VMEM((width, rows), BF),
            pltpu.VMEM((2, 2, side, side, depth, chunk), BF),
            pltpu.VMEM((2, 2, side, side, depth, chunk), BF),
            pltpu.VMEM((steps + 1, 2, side, side, depth, chunk), BF),
            pltpu.VMEM((steps + 1, side - 1, 2, side, depth, chunk), BF),
            dma((3,)),
            dma((steps, side, 2)),
            dma((side, parts)),
            dma((steps + 1,)),
            dma((steps + 1,)),
            dma((steps + 1, side - 1)),
            dma((steps + 1, side - 1)),
        ],
        compiler_params=pltpu.CompilerParams(
            vmem_limit_bytes=62 * 2**20, collective_id=5, has_side_effects=True
        ),
        name="feed_forward",
    )(tokens, cotangent, attn_rows, norm, shared_own, shared_others, *[shared_own] * 2, *[shared_others] * 2)


def norm_parts(values):
    center = values - jnp.mean(values, axis=-1, keepdims=True)
    inverse = lax.rsqrt(jnp.mean(center * center, axis=-1, keepdims=True) + 1e-05)
    return center * inverse, inverse


def norm_back(normed, inverse, gain, grad):
    inner = grad * gain
    return inverse * (
        inner
        - jnp.mean(inner, axis=-1, keepdims=True)
        - normed * jnp.mean(inner * normed, axis=-1, keepdims=True)
    )


def per_device(
    shape,
    tokens, cotangent, item_len, bucket_table,
    w_qkv, w_proj, w_up, w_down, rel_bias, ln_gain, ln_shift,
    mean_qkv, mean_proj, mean_up, mean_down, mean_bias, mean_gain, mean_shift,
    square_qkv, square_proj, square_up, square_down, square_bias, square_gain, square_shift,
):
    columns, places = shape["xy"], shape["zl"]
    parts = 2 * places
    devices = columns * 2 * parts
    rows, width = tokens.shape
    heads = w_qkv.shape[2] // DH
    tok = rows * parts
    xy, core, zh, zl = place()
    head_block = zl * 2 + core

    ff_local, heads_cols = w_up.shape[1], w_proj.shape[0]
    local = jnp.concatenate([w_up, w_down.T, w_proj.T], axis=1).astype(BF)

    shared_own = lax.all_gather(local, DP, axis=0, tiled=True)
    n_bias, n_gain = rel_bias.shape[0], ln_gain.shape[1]
    n_small = n_bias + 4 * n_gain

    def pack(bias, gain, shift):
        row = jnp.concatenate([bias, gain.reshape(-1), shift.reshape(-1)])
        return jnp.pad(row, (0, LANES - n_small))[None, :]

    small_weights = pack(rel_bias, ln_gain, ln_shift)
    group_rows, w_heads, small, wide = gather(
        shape, tokens, w_qkv.astype(BF), small_weights, local
    )
    shared_others = lax.all_gather(wide, DP, axis=1, tiled=True)
    small = small.reshape(devices, LANES)

    def columns_of(start):
        part = small[:, start : start + 2 * n_gain].reshape(devices, 2, n_gain)
        return part.transpose(1, 0, 2).reshape(2, width)

    table_flat = small[:, :n_bias].reshape(-1)
    gains, shifts = columns_of(n_bias), columns_of(n_bias + 2 * n_gain)
    other_len = lax.ppermute(item_len, "core", [(0, 1), (1, 0)])
    split = jnp.where(zh == core, item_len, other_len)[0, 0:1]

    norm_one = jnp.stack([gains[0], shifts[0]])
    a_first, qkv = project(group_rows.reshape(tok, width), norm_one, w_heads)
    qkv = qkv.reshape(3 * heads * DH, tok)

    table = lax.dynamic_slice_in_dim(
        table_flat.reshape(BUCKETS, H), head_block * heads, heads, 1
    )
    one_hot = (jnp.arange(BUCKETS)[:, None] == bucket_table[None, :]).astype(F32)
    dist_bias = lax.dot_general(
        table, one_hot, (((0,), (0,)), ((), ())), precision=HIGHEST, preferred_element_type=F32
    )
    pattern = jnp.concatenate(
        [dist_bias * LOG2E, jnp.full((heads, BLK), NEG, F32)], axis=1
    )[:, None, :]
    out, attn_rows, lse = attend(shape, qkv, pattern, split, heads)

    attn_rows = attn_rows.reshape(parts, heads * DH, rows)
    norm_two = jnp.stack([gains[1], shifts[1]])
    block_out, grad_middle, grad_attn, wide_grad, sums_two = feed_forward(
        shape, tokens, cotangent, attn_rows, norm_two, shared_own, shared_others, ff_local
    )
    gain_two, shift_two = sums_two[0], sums_two[1]
    given = grad_attn.reshape(parts, heads, DH, rows)
    grad_heads, wide_parts, grad_pattern = attend_back(
        shape, column_segments(parts, ff_local, w_proj.shape[0]), qkv, out, given, wide_grad, lse, pattern,
        split, heads,
    )
    grad_heads = grad_heads.reshape(3, heads * DH, tok)

    bias_grad = lax.dot_general(
        one_hot, grad_pattern[:, 0, :tok], (((1,), (1,)), ((), ())),
        precision=HIGHEST, preferred_element_type=F32,
    )
    table_grad = lax.dynamic_update_slice(
        jnp.zeros((BUCKETS, H), F32), bias_grad, (0, head_block * heads)
    )

    def by_device(*vectors):
        return jnp.stack(vectors).reshape(2, devices, n_gain).transpose(1, 0, 2).reshape(devices, -1)

    small_grad = jnp.concatenate(
        [
            table_grad.reshape(devices, n_bias),
            by_device(jnp.zeros_like(gain_two), gain_two),
            by_device(jnp.zeros_like(shift_two), shift_two),
            jnp.zeros((devices, LANES - n_small), F32),
        ],
        axis=1,
    )
    weights = (w_qkv, w_proj, w_up, w_down, small_weights)
    early_rows, added, sum_qkv, wide_sum, small_sum, totals = sums(
        shape, n_bias, n_gain, a_first, grad_heads, w_heads, norm_one, small_grad, wide_parts, weights
    )
    small_like = [rel_bias[None, :], ln_gain, ln_shift]
    updates_total, grad_norm, param_norms, *results = optimizer(
        shape, n_bias, n_gain, totals, small_sum,
        (sum_qkv, wide_sum), weights,
        (mean_qkv, mean_proj, mean_up, mean_down, pack(mean_bias, mean_gain, mean_shift)),
        (square_qkv, square_proj, square_up, square_down, pack(square_bias, square_gain, square_shift)),
        small_like,
    )
    added, _ = lax.optimization_barrier((added, updates_total))
    grad_tokens = finish_rows(shape, added, early_rows, tokens, grad_middle, gains[0:1])
    new = [array if n % 7 != 4 else array[0] for group in results for n, array in enumerate(group)]
    return (block_out, grad_tokens, grad_norm[0, 0], param_norms, *new)


def solution(mesh):
    shape = {"xy": mesh.shape["dp"] // 2, "core": 2, "zh": 2, "zl": mesh.shape["tensor"] // 2}
    split_mesh = Mesh(mesh.devices.reshape(tuple(shape[axis] for axis in ALL)), ALL)
    weights = (
        P(None, DP, TENSOR),
        P(TENSOR, DP),
        P(DP, TENSOR),
        P(TENSOR, DP),
        P(ALL),
        P(None, ALL),
        P(None, ALL),
    )
    rows = P(ALL, None)
    return jax.shard_map(
        functools.partial(per_device, shape),
        mesh=split_mesh,
        in_specs=(rows, rows, P(DP, None), P(), *weights, *weights, *weights),
        out_specs=(rows, rows, P(), P(), *weights, *weights, *weights),
        check_vma=False,
    )
```
